32 devices in a mesh: dp: 8 (over z, x), head: 4 (over y, core).
Axes of the slice: x: 2, y: 2, z: 4, core: 2. Of those that a mesh axis runs over, the one named last changes fastest.
Arguments:
- inputs: bfloat16 [8, 32, 32, 512], P('dp', 'head'), may hold values from -6 to 6
- embedding: bfloat16 [8, 1024], P('dp'), may hold values from -6 to 6
- extent: int32 [8, 2], P('dp'), may hold values from 12 to 32, as said below
- cotangent: bfloat16 [8, 32, 32, 512], P('dp', 'head'), may hold values from -6 to 6
- gains: float32 [2, 512], replicated, may hold values from 0.5 to 1.5
- biases: float32 [7, 512], replicated, may hold values from -3 to 3
- conv_first: float32 [2359296], P(('dp', 'head')), may hold values from -0.09375 to 0.09375
- conv_second: float32 [2359296], P(('dp', 'head')), may hold values from -0.09375 to 0.09375
- qkv_master: float32 [786432], P(('dp', 'head')), may hold values from -0.25 to 0.25
- ada_master: float32 [1048576], P(('dp', 'head')), may hold values from -0.1875 to 0.1875
- proj_master: float32 [262144], P(('dp', 'head')), may hold values from -2 to 2
Outputs:
- output: bfloat16 [8, 32, 32, 512], P('dp', 'head')
- grad_inputs: float32 [8, 32, 32, 512], P('dp', 'head')
- grad_embedding: float32 [8, 1024], P('dp')
- grad_gains: float32 [2, 512], replicated
- grad_biases: float32 [7, 512], replicated
- grad_conv_first: float32 [2359296], P(('dp', 'head'))
- grad_conv_second: float32 [2359296], P(('dp', 'head'))
- grad_qkv: float32 [786432], P(('dp', 'head'))
- grad_ada: float32 [1048576], P(('dp', 'head'))
- grad_proj: float32 [262144], P(('dp', 'head'))
The draws below stay inside these ranges and needn't reach their ends.
Inputs may be any that keep to these rules, and one draw needn't show every extreme that they name: `extent`: one side of each image is all 32 pixels.
All inputs are finite; a program needn't handle non-finite values.
Results may differ from the reference program's by a relative error of at most 0.013.
Values may be sent and summed in bfloat16 or wider, within the bound.
No kernel may reach another device: no remote copies, remote signals or barrier semaphores. Data moves between devices by JAX's collectives and lax.ppermute only.
A program may use at most 192 MiB of HBM per device.

```python
import math
import jax
import jax.numpy as jnp
from jax import lax

C = 512
EMB = 1024
HEADS = 8
HD = 64
GROUPS = 32
SIDE = 32
IMAGES = 8
PIX = 1024


def draw_extent(key, part):
    key = jax.random.fold_in(key, 11)
    key_side, key_length = jax.random.split(key)
    side_pick = jax.random.randint(key_side, (IMAGES, 1), 0, 2)
    short_side = jax.random.randint(key_length, (IMAGES, 1), SIDE * 3 // 8, SIDE + 1)
    full_side = jnp.full((IMAGES, 1), SIDE, jnp.int32)
    extent_rows = jnp.where(side_pick == 0, full_side, short_side)
    extent_cols = jnp.where(side_pick == 0, short_side, full_side)
    return jnp.concatenate([extent_rows, extent_cols], axis=1).astype(jnp.int32)


def steps_of(stream_key, shape, cuts, smallest, largest):
    def one(dim, blocks):
        heights = jax.random.uniform(jax.random.fold_in(jax.random.fold_in(stream_key, 6), dim), (blocks,), jnp.float32, smallest / len(cuts), largest / len(cuts))
        return jnp.repeat(jnp.exp(heights), shape[dim] // blocks).reshape((-1,) + (1,) * (len(shape) - dim - 1))

    loudness = one(*cuts[0])
    for cut in cuts[1:]:
        loudness = loudness * one(*cut)
    return loudness


def normal_values(rng, shape, width, bound, pieces=(), held_as=jnp.bfloat16):
    array = width * jax.random.normal(rng, shape, jnp.float32)
    if pieces:
        array = array * steps_of(rng, shape, pieces, -0.22, 0.18)
    return jnp.clip(array, -bound, bound).astype(held_as)


def setup_inputs(seed: int = 0) -> dict:
    splits = jax.random.split(jax.random.key(seed), 12)
    inputs = normal_values(splits[0], (IMAGES, SIDE, SIDE, C), 1.0, 6.0, ((0, 8), (1, 4)))
    embedding = normal_values(splits[1], (IMAGES, EMB), 1.0, 6.0, ((0, 8),))
    extent = draw_extent(jax.random.fold_in(splits[11], 71), 0)
    cotangent = normal_values(splits[3], (IMAGES, SIDE, SIDE, C), 1.0, 6.0, ((0, 8), (1, 4)))
    gains = jnp.clip(1.0 + 0.1 * jax.random.normal(splits[4], (2, C), jnp.float32), 0.5, 1.5)
    biases = normal_values(splits[5], (7, C), 0.5, 3.0, (), jnp.float32)
    conv_first = normal_values(splits[6], (9 * C * C,), (9 * C) ** -0.5, 0.09375, ((0, 32),), jnp.float32)
    conv_second = normal_values(splits[7], (9 * C * C,), (9 * C) ** -0.5, 0.09375, ((0, 32),), jnp.float32)
    qkv_master = normal_values(splits[8], (3 * C * C,), C ** -0.5, 0.25, ((0, 32),), jnp.float32)
    ada_master = normal_values(splits[9], (2 * EMB * C,), EMB ** -0.5, 0.1875, ((0, 32),), jnp.float32)
    proj_master = normal_values(splits[10], (C * C,), (C // 64) ** -0.5, 2.0, ((0, 32),), jnp.float32)
    return dict(inputs=inputs, embedding=embedding, extent=extent, cotangent=cotangent, gains=gains, biases=biases, conv_first=conv_first, conv_second=conv_second, qkv_master=qkv_master, ada_master=ada_master, proj_master=proj_master)


EPS = 1e-05
MASKED = -1e+30
HIGH = lax.Precision.HIGHEST

@jax.custom_vjp
def low(v):
    return lax.optimization_barrier(v.astype(jnp.bfloat16)).astype(jnp.float32)

@jax.custom_vjp
def low_back(v):
    return v

def low_keep(v):
    return (low(v), None)

def low_pass(kept, grad):
    return (grad,)

def back_keep(v):
    return (v, None)

def back_low(kept, grad):
    return (low(grad),)
low.defvjp(low_keep, low_pass)
low_back.defvjp(back_keep, back_low)

def image_mask(extent):
    index = jnp.arange(SIDE, dtype=jnp.int32)
    valid_rows = index[None, :] < extent[:, 0:1]
    valid_cols = index[None, :] < extent[:, 1:2]
    both = valid_rows[:, :, None] & valid_cols[:, None, :]
    return both.astype(jnp.float32)[..., None]

def group_norm(value, valid, count):
    grouped = value.reshape(value.shape[:-1] + (GROUPS, C // GROUPS))
    masked = grouped * valid[..., None]
    total_sum = lax.optimization_barrier(jnp.sum(masked, axis=(1, 2, 4)))
    square_sum = lax.optimization_barrier(jnp.sum(masked * grouped, axis=(1, 2, 4)))
    center = total_sum / count[:, None]
    inverse = lax.rsqrt(square_sum / count[:, None] - center * center + EPS)
    normed = (grouped - center[:, None, None, :, None]) * inverse[:, None, None, :, None]
    return normed.reshape(value.shape)

def conv_same(activation, kernel):
    return lax.conv_general_dilated(activation, kernel, (1, 1), 'SAME', dimension_numbers=('NHWC', 'HWIO', 'NHWC'), precision=HIGH)

def attend_image(items):
    packed, key_valid = items
    queries = packed[:, :, 0]
    key_heads = packed[:, :, 1]
    value_heads = packed[:, :, 2]
    scores = jnp.einsum('qhd,khd->hqk', queries, key_heads, precision=HIGH) * (1.0 / math.sqrt(HD))
    scores = low_back(scores)
    scores = jnp.where(key_valid[None, None, :], scores, MASKED)
    top_score = lax.optimization_barrier(jnp.max(scores, axis=-1, keepdims=True))
    expo_score = jnp.exp(scores - top_score)
    probs = expo_score / lax.optimization_barrier(jnp.sum(expo_score, axis=-1, keepdims=True))
    result = jnp.einsum('hqk,khd->qhd', low(probs), value_heads, precision=HIGH)
    return low_back(low(result)).reshape(PIX, C)

def forward(source, emb_value, weights, valid, count):
    gains, biases, conv_first, conv_second, qkv_master, ada_master, proj_master = weights
    kernel_first = low(conv_first).reshape(3, 3, C, C)
    kernel_second = low(conv_second).reshape(3, 3, C, C)
    qkv_weight = low(qkv_master).reshape(C, 3 * C)
    ada_weight = low(ada_master).reshape(EMB, 2 * C)
    proj_weight = low(proj_master).reshape(C, C)
    pre_first = group_norm(source, valid, count) * gains[0] + biases[0]
    act_first = low(jax.nn.silu(pre_first) * valid)
    hidden_first = low_back(conv_same(act_first, kernel_first) + biases[1])
    emb_act = low(jax.nn.silu(emb_value))
    modulation = low_back(jnp.dot(emb_act, ada_weight, precision=HIGH) + jnp.concatenate([biases[2], biases[3]]))
    scale = modulation[:, None, None, :C]
    shift = modulation[:, None, None, C:]
    pre_second = group_norm(hidden_first, valid, count) * (1.0 + scale) + shift
    act_second = low(jax.nn.silu(pre_second) * valid)
    hidden_third = low_back(conv_same(act_second, kernel_second) + biases[4])
    residual = source + valid * hidden_third
    attn_in = low(group_norm(residual, valid, count) * gains[1] + biases[5])
    qkv = low_back(low(jnp.einsum('nijc,cd->nijd', attn_in, qkv_weight, precision=HIGH)))
    images = source.shape[0]
    packed = qkv.reshape(images, PIX, HEADS, 3, HD)
    key_valid = valid.reshape(images, PIX) > 0
    attended = lax.map(jax.checkpoint(attend_image), (packed, key_valid))
    projected = low_back(jnp.einsum('npc,cd->npd', attended, proj_weight, precision=HIGH) + biases[6])
    return residual + projected.reshape(source.shape)

def reference(inputs, embedding, extent, cotangent, gains, biases, conv_first, conv_second, qkv_master, ada_master, proj_master):
    params = (gains, biases, conv_first, conv_second, qkv_master, ada_master, proj_master)
    blocks = IMAGES // 4

    def fold_block(carry, items):
        block_in, block_emb, block_ext, block_cot = items
        valid = image_mask(block_ext)
        count = (block_ext[:, 0] * block_ext[:, 1]).astype(jnp.float32) * (C // GROUPS)

        def run_block(source, emb_value, *weights):
            return forward(source, emb_value, weights, valid, count)
        result, pull = jax.vjp(run_block, block_in.astype(jnp.float32), block_emb.astype(jnp.float32), *params)
        grads = pull(block_cot.astype(jnp.float32))
        carry = tuple((running + update for running, update in zip(carry, grads[2:])))
        return (carry, (result.astype(jnp.bfloat16), grads[0], grads[1]))
    start = tuple((jnp.zeros_like(param) for param in params))
    stacked = (inputs.reshape(blocks, 4, SIDE, SIDE, C), embedding.reshape(blocks, 4, EMB), extent.reshape(blocks, 4, 2), cotangent.reshape(blocks, 4, SIDE, SIDE, C))
    totals, (outputs, grad_in, grad_emb) = lax.scan(fold_block, start, stacked)
    return (outputs.reshape(IMAGES, SIDE, SIDE, C), grad_in.reshape(IMAGES, SIDE, SIDE, C), grad_emb.reshape(IMAGES, EMB), totals[0], totals[1], totals[2], totals[3], totals[4], totals[5], totals[6])
```

```python
import functools
import math

import jax
import jax.numpy as jnp
from jax import lax
from jax.experimental import pallas as pl
from jax.experimental.pallas import tpu as pltpu
from jax.sharding import PartitionSpec as P

HD = 64
GROUPS = 32
EPS = 1e-05
MASKED = -1e30
LANES = 128
F32 = jnp.float32
BF16 = jnp.bfloat16
VMEM_SPEC = pl.BlockSpec(memory_space=pltpu.VMEM)
SMEM_SPEC = pl.BlockSpec(memory_space=pltpu.SMEM)


def sds(shape, dtype):
    return jax.ShapeDtypeStruct(shape, dtype)


def call(kernel, outs, scalars, *args, scratch=(), flops=0, vmem=48):
    moved = sum(math.prod(a.shape) * a.dtype.itemsize for a in tuple(args) + tuple(outs))
    return pl.pallas_call(
        kernel,
        out_shape=tuple(outs),
        in_specs=[SMEM_SPEC] + [VMEM_SPEC] * len(args),
        out_specs=tuple(VMEM_SPEC for _ in outs),
        scratch_shapes=list(scratch),
        compiler_params=pltpu.CompilerParams(vmem_limit_bytes=vmem * 1024 * 1024),
        cost_estimate=pl.CostEstimate(flops=flops, bytes_accessed=moved, transcendentals=0),
    )(scalars, *args)


def hop(value, axis, bit):
    count = lax.axis_size(axis)
    return lax.ppermute(value, axis, [(i, i ^ bit) for i in range(count)])


def head_gather(block):
    far = hop(block, "head", 2)
    near = hop(block, "head", 1)
    return (block, near, far, hop(far, "head", 1))


def head_exchange(pair, across):
    near = hop(pair, "head", 1)
    far = hop(jnp.stack([across, near[1]]), "head", 2)
    return (near, far)


def mm(left, right, left_dim, right_dim):
    return lax.dot_general(
        left, right, (((left_dim,), (right_dim,)), ((), ())), preferred_element_type=F32
    )


def lane_block(index):
    return pl.ds(pl.multiple_of(index * LANES, LANES), LANES)


def row_block(index, rows):
    return pl.ds(pl.multiple_of(index * rows, rows), rows)


def pixel_place(rows, lanes, cols, start=0):
    pixel = lax.broadcasted_iota(jnp.int32, (rows, lanes), 0) + start
    shift = cols.bit_length() - 1
    return (lax.shift_right_logical(pixel, shift), lax.bitwise_and(pixel, cols - 1))


def valid_of(scalars, rows, lanes, cols, start=0):
    place_row, place_col = pixel_place(rows, lanes, cols, start)
    inside = jnp.logical_and(place_row < scalars[2], place_col < scalars[3])
    return jnp.where(inside, 1.0, 0.0).astype(F32)


def group_total(first, second, width):
    lanes = first.shape[-1]
    pick = lax.broadcasted_iota(jnp.int32, (8, lanes), 0)
    both = jnp.where(pick == 0, first, jnp.where(pick == 1, second, 0.0))
    shift = width.bit_length() - 1
    left = lax.shift_right_logical(lax.broadcasted_iota(jnp.int32, (lanes, lanes), 0), shift)
    right = lax.shift_right_logical(lax.broadcasted_iota(jnp.int32, (lanes, lanes), 1), shift)
    same = jnp.where(left == right, 1.0, 0.0).astype(F32)
    total = lax.dot_general(
        both,
        same,
        (((1,), (0,)), ((), ())),
        precision=lax.Precision.HIGHEST,
        preferred_element_type=F32,
    )
    return (total[0:1], total[1:2])


def pixel_count(scalars, width):
    return (scalars[2] * scalars[3] * width).astype(F32)


def col_sum(value):
    return jnp.sum(value, axis=0, keepdims=True)


def norm_stats(value, valid, count, width):
    masked = value * valid
    total, square = group_total(col_sum(masked), col_sum(masked * value), width)
    center = total / count
    return (center, lax.rsqrt(square / count - center * center + EPS))


def norm_back(grad, normed, inverse, valid, count, width):
    first, second = group_total(col_sum(grad), col_sum(grad * normed), width)
    return (grad - valid * ((first + normed * second) * (1.0 / count))) * inverse


def silu_grad(value):
    gate = jax.nn.sigmoid(value)
    return gate * (1.0 + value * (1.0 - gate))


def place_pieces(dest, pieces, offsets, start, groups, rows):
    for k, piece in enumerate(pieces):
        for group in range(groups):
            begin = start + group * rows
            dest[group, pl.ds(pl.multiple_of(offsets[k] * rows, rows), rows), :] = piece[
                begin : begin + rows, :
            ]


def taps_side_by_side(flat, wide):
    channels = wide.shape[0]
    for tap in range(9):
        wide[:, tap * LANES : (tap + 1) * LANES] = flat[0, tap * channels : (tap + 1) * channels, :]


def conv_taps(act, wide, taps, cols):
    pixels = act.shape[0]
    lanes = wide.shape[1]
    taps[0:cols, :] = jnp.zeros((cols, lanes), F32)
    taps[pixels + cols :, :] = jnp.zeros((cols, lanes), F32)
    step = 256

    def one(i, carry):
        begin = pl.multiple_of(i * step, step)
        taps[pl.ds(pl.multiple_of(begin + cols, cols), step), :] = mm(
            act[pl.ds(begin, step), :], wide[...], 1, 0
        )
        return carry

    lax.fori_loop(0, pixels // step, one, 0)


def conv_sum(taps, begin, rows, cols):
    def column(side):
        return sum(
            taps[
                pl.ds(pl.multiple_of(begin + up * cols, cols), rows),
                (up * 3 + side) * LANES : (up * 3 + side + 1) * LANES,
            ]
            for up in range(3)
        )

    place_col = pixel_place(rows, LANES, cols)[1]
    left = jnp.where(place_col > 0, pltpu.roll(column(0), 1, 0), 0.0)
    right = jnp.where(place_col < cols - 1, pltpu.roll(column(2), rows - 1, 0), 0.0)
    return column(1) + left + right


def shifted_grads(grad, dest, cols):
    pixels = grad.shape[0]
    place_col = pixel_place(pixels, LANES, cols)[1]
    sides = (
        jnp.where(place_col < cols - 1, pltpu.roll(grad, pixels - 1, 0), 0.0),
        grad,
        jnp.where(place_col > 0, pltpu.roll(grad, 1, 0), 0.0),
    )
    blank = jnp.zeros((cols, LANES), BF16)
    for side, value in enumerate(sides):
        low = value.astype(BF16)
        for up in range(3):
            lanes = slice((up * 3 + side) * LANES, (up * 3 + side + 1) * LANES)
            if up == 0:
                dest[0 : pixels - cols, lanes] = low[cols:, :]
                dest[pixels - cols :, lanes] = blank
            elif up == 1:
                dest[:, lanes] = low
            else:
                dest[cols:, lanes] = low[0 : pixels - cols, :]
                dest[0:cols, lanes] = blank


def partial_sums(left, right, whole, rank, kept, pair, across):
    pixels = left.shape[0]
    step = 256

    def one(i, carry):
        rows = pl.ds(pl.multiple_of(i * step, step), step)
        whole[rows, :] = mm(left[rows, :], right[...], 1, 1)
        return carry

    lax.fori_loop(0, pixels // step, one, 0)
    kept[...] = whole[:, lane_block(rank)]
    pair[0] = whole[:, lane_block(rank ^ 1)].astype(BF16)
    pair[1] = whole[:, lane_block(rank ^ 3)].astype(BF16)
    across[...] = whole[:, lane_block(rank ^ 2)].astype(BF16)


def weights_out_kernel(sc, first, second, qkv, ada, proj, a0, a13, a2, b0, b13, b2, pj):
    rank = sc[0]
    rows_conv = first.shape[0] // 4
    rows_qkv = qkv.shape[0] // 12
    rows_ada = ada.shape[0] // 8
    rows_proj = proj.shape[0] // 4
    low_half = lax.broadcasted_iota(jnp.int32, (rows_qkv, LANES), 1) < HD
    places = ((0, a0, b0, None), (1, a13, b13, 0), (2, a2, b2, None), (3, a13, b13, 1))
    for k, a_dest, b_dest, slot in places:
        peer = rank ^ k

        def put(dest, begin, value, slot=slot):
            rows = value.shape[0]
            if slot is None:
                dest[begin : begin + rows, :] = value.astype(BF16)
            else:
                dest[slot, begin : begin + rows, :] = value.astype(BF16)

        put(a_dest, 0, first[pl.ds(peer, rows_conv, stride=4), :])
        for side in range(2):
            put(
                a_dest,
                rows_conv + side * rows_ada,
                ada[pl.ds(4 * side + peer, rows_ada, stride=8), :],
            )
        put(b_dest, 0, second[pl.ds(peer, rows_conv, stride=4), :])
        part = [qkv[pl.ds(peer * 3 + g, rows_qkv, stride=12), :] for g in range(3)]
        mixed = (
            jnp.where(low_half, part[0], part[1]),
            pltpu.roll(jnp.where(low_half, part[2], part[0]), HD, 1),
            jnp.where(low_half, part[1], part[2]),
        )
        for g in range(3):
            put(b_dest, rows_conv + g * rows_qkv, mixed[g])
    for g in range(4):
        pj[g * rows_proj : (g + 1) * rows_proj, :] = proj[
            pl.ds(g, rows_proj, stride=4), :
        ].astype(BF16)


def first_piece_kernel(sc, a0, near, far, emb, piece, *, rows_conv, rows_ada):
    rank = sc[0]
    for k, block in enumerate((a0, near.at[0], far.at[0], far.at[1])):
        peer = rank ^ k
        piece[row_block(peer, rows_conv), :] = block[0:rows_conv, :]
        for side in range(2):
            begin = 4 * rows_conv + side * 4 * rows_ada
            piece[pl.ds(pl.multiple_of(begin + peer * rows_ada, 16), rows_ada), :] = block[
                rows_conv + side * rows_ada : rows_conv + (side + 1) * rows_ada, :
            ]
    begin = 4 * rows_conv + 8 * rows_ada
    piece[begin : begin + 16, :] = jnp.zeros((16, LANES), BF16)
    piece[begin : begin + 8, :] = emb[...]


def second_piece_kernel(sc, b0, near, far, pj, piece, *, rows_conv, rows_qkv):
    rank = sc[0]
    for k, block in enumerate((b0, near.at[0], far.at[0], far.at[1])):
        peer = rank ^ k
        piece[row_block(peer, rows_conv), :] = block[0:rows_conv, :]
        for g in range(3):
            begin = 4 * rows_conv + g * 4 * rows_qkv
            piece[pl.ds(pl.multiple_of(begin + peer * rows_qkv, 16), rows_qkv), :] = block[
                rows_conv + g * rows_qkv : rows_conv + (g + 1) * rows_qkv, :
            ]
    begin = 4 * rows_conv + 12 * rows_qkv
    piece[begin : begin + pj.shape[0], :] = pj[...]


def dp_gather(piece):
    far = [piece] + [hop(piece, "dp", k) for k in (2, 4, 6)]
    near = [hop(value, "dp", 1) for value in far]
    return [value for pair in zip(far, near) for value in pair]


def norm_first_kernel(sc, gains, biases, *refs, cols, width):
    blocks = refs[0:4]
    act, own, stats, held = refs[4:]
    rank = sc[0]
    rows, channels = blocks[0].shape
    count = pixel_count(sc, width)
    total = jnp.zeros((1, channels), F32)
    square = jnp.zeros((1, channels), F32)
    for k, block in enumerate(blocks):
        value = block[...].astype(F32)
        masked = value * valid_of(sc, rows, channels, cols, (rank ^ k) * rows)
        total = total + col_sum(masked)
        square = square + col_sum(masked * value)
    total, square = group_total(total, square, width)
    center = total / count
    inverse = lax.rsqrt(square / count - center * center + EPS)
    held[0:1, :] = center
    held[1:2, :] = inverse
    for k, block in enumerate(blocks):
        peer = rank ^ k
        pre = (block[...].astype(F32) - center) * inverse * gains[0:1, :] + biases[0:1, :]
        valid = valid_of(sc, rows, channels, cols, peer * rows)
        act[row_block(peer, rows), :] = (pre * jax.nn.sigmoid(pre) * valid).astype(BF16)
        own[row_block(peer, rows), :] = block[:, lane_block(rank)]
    stats[...] = held[:, lane_block(rank)]


def conv_first_kernel(sc, offsets, biases, act, emb, *refs, cols, width, count_pieces, segments):
    pieces = refs[0:count_pieces]
    act_out, normed_out, aux, wide, ada, flat, taps, hidden = refs[count_pieces:]
    rank = sc[0]
    pixels = act.shape[0]
    place_pieces(flat, pieces, offsets, *segments[0])
    place_pieces(ada, pieces, offsets, *segments[1])
    taps_side_by_side(flat, wide)
    conv_taps(act, wide, taps, cols)
    bias = biases[1:2, lane_block(rank)]
    step = 256
    for i in range(pixels // step):
        hidden[i * step : (i + 1) * step, :] = conv_sum(taps, i * step, step, cols) + bias
    value = hidden[...]
    valid = valid_of(sc, pixels, LANES, cols)
    center, inverse = norm_stats(value, valid, pixel_count(sc, width), width)
    normed = (value - center) * inverse
    emb_value = emb[...].astype(F32)
    emb_act = (emb_value * jax.nn.sigmoid(emb_value)).astype(BF16)
    mods = []
    for side in range(2):
        mod = biases[2 + side : 3 + side, lane_block(rank)]
        for j in range(emb_act.shape[0]):
            row = jnp.broadcast_to(emb_act[j : j + 1, :].astype(F32), (16, LANES)).astype(BF16)
            mod = mod + mm(row, ada[side, j * LANES : (j + 1) * LANES, :], 1, 0)[0:1]
        mods.append(mod)
    pre = normed * (1.0 + mods[0]) + mods[1]
    act_out[...] = (pre * jax.nn.sigmoid(pre) * valid).astype(BF16)
    normed_out[...] = normed
    aux[...] = jnp.zeros(aux.shape, F32)
    aux[0:1, :] = inverse
    aux[1:2, :] = mods[0]
    aux[2:3, :] = mods[1]


def conv_second_kernel(sc, offsets, gains, biases, own, *refs, cols, width, count_pieces, segments):
    blocks = refs[0:4]
    pieces = refs[4 : 4 + count_pieces]
    attn_in, act, residual_out, normed_out, aux, wide, flat, taps = refs[4 + count_pieces :]
    rank = sc[0]
    pixels = act.shape[0]
    for k, block in enumerate(blocks):
        act[:, lane_block(rank ^ k)] = block[...]
    place_pieces(flat, pieces, offsets, *segments[0])
    taps_side_by_side(flat, wide)
    conv_taps(act, wide, taps, cols)
    bias = biases[4:5, lane_block(rank)]
    step = 256
    for i in range(pixels // step):
        rows = slice(i * step, (i + 1) * step)
        third = conv_sum(taps, i * step, step, cols) + bias
        valid = valid_of(sc, step, LANES, cols, i * step)
        residual_out[rows, :] = own[rows, :].astype(F32) + valid * third
    value = residual_out[...]
    valid = valid_of(sc, pixels, LANES, cols)
    center, inverse = norm_stats(value, valid, pixel_count(sc, width), width)
    normed = (value - center) * inverse
    normed_out[...] = normed
    attn_in[...] = (
        normed * gains[1:2, lane_block(rank)] + biases[5:6, lane_block(rank)]
    ).astype(BF16)
    aux[...] = jnp.broadcast_to(inverse, aux.shape)


def attention_kernel(sc, offsets, *refs, cols, count_pieces, segments):
    blocks = refs[0:4]
    cots = refs[4:8]
    pieces = refs[8 : 8 + count_pieces]
    (kept, pair, across, attn_full, grads, attended, cot_full, cot_own, rows_weight) = refs[
        8 + count_pieces : 17 + count_pieces
    ]
    (w_qkv, w_proj, wide, qkv, keys_t, values_t, cot_att, cot_att_t, grad_kv, whole) = refs[
        17 + count_pieces :
    ]
    rank = sc[0]
    pixels, channels = attn_full.shape
    rows = cots[0].shape[0]
    scale = 1.0 / math.sqrt(HD)
    for k in range(4):
        attn_full[:, lane_block(rank ^ k)] = blocks[k][...]
        cot_full[row_block(rank ^ k, rows), :] = cots[k][...]
        cot_own[row_block(rank ^ k, rows), :] = cots[k][:, lane_block(rank)]
    place_pieces(w_qkv, pieces, offsets, *segments[1])
    place_pieces(w_proj, pieces, offsets, *segments[2])
    for g in range(3):
        wide[:, g * LANES : (g + 1) * LANES] = w_qkv[g]
    for g in range(channels // LANES):
        rows_weight[:, g * LANES : (g + 1) * LANES] = w_proj[g]
    step = 256

    def project(i, carry):
        at = pl.ds(pl.multiple_of(i * step, step), step)
        qkv[at, :] = mm(attn_full[at, :], wide[...], 1, 0).astype(BF16)
        cot_att[at, :] = mm(cot_full[at, :], rows_weight[...], 1, 1).astype(BF16)
        return carry

    lax.fori_loop(0, pixels // step, project, 0)
    for i in range(pixels // step):
        at = slice(i * step, (i + 1) * step)
        keys_t[:, at] = qkv[at, LANES : 2 * LANES].astype(F32).T.astype(BF16)
        values_t[:, at] = qkv[at, 2 * LANES :].astype(F32).T.astype(BF16)
        cot_att_t[:, at] = cot_att[at, :].astype(F32).T
    grad_kv[...] = jnp.zeros(grad_kv.shape, F32)
    span = 256
    lane = lax.broadcasted_iota(jnp.int32, (span, LANES), 1)
    sublane = lax.broadcasted_iota(jnp.int32, (LANES, span), 0)
    sublane_all = lax.broadcasted_iota(jnp.int32, (LANES, pixels), 0)

    def attend(i, carry):
        at = pl.ds(pl.multiple_of(i * span, span), span)
        queries = qkv[at, 0:LANES]
        cot_rows = cot_att[at, :]
        cot_cols = cot_att_t[:, at]
        key_row, key_col = pixel_place(pixels, span, cols)
        key_valid = jnp.logical_and(key_row < sc[2], key_col < sc[3])
        att_sum = jnp.zeros((LANES, span), F32)
        query_sum = jnp.zeros((LANES, span), F32)
        for h in range(LANES // HD):
            mine = lax.shift_right_logical(lane, 6) == h
            mine_t = lax.shift_right_logical(sublane, 6) == h
            mine_all = lax.shift_right_logical(sublane_all, 6) == h
            query = jnp.where(mine, queries, jnp.zeros_like(queries))
            cot = jnp.where(mine, cot_rows, jnp.zeros_like(cot_rows))
            scores = mm(qkv[:, LANES : 2 * LANES], query, 1, 1) * scale
            scores = jnp.where(key_valid, scores, MASKED)
            top = jnp.max(scores, axis=0, keepdims=True)
            expo = jnp.exp(scores - top)
            probs = expo * (1.0 / col_sum(expo))
            probs_low = probs.astype(BF16)
            value_t = jnp.where(mine_all, values_t[...], jnp.zeros_like(values_t[...]))
            att = mm(value_t, probs_low, 1, 0)
            att_sum = att_sum + att
            row_dot = col_sum(att * cot_cols)
            grad_kv[:, LANES:] += mm(probs_low, cot, 1, 0)
            grad_probs = mm(qkv[:, 2 * LANES :], cot, 1, 1)
            grad_scores = (probs * (grad_probs - row_dot)).astype(BF16)
            grad_kv[:, 0:LANES] += mm(grad_scores, query, 1, 0)
            key_t = jnp.where(mine_all, keys_t[...], jnp.zeros_like(keys_t[...]))
            query_sum = query_sum + mm(key_t, grad_scores, 1, 0)
        attended[at, :] = att_sum.T.astype(BF16)
        grads[at, 0:LANES] = (query_sum.T * scale).astype(BF16)
        return carry

    lax.fori_loop(0, pixels // span, attend, 0)
    grads[:, LANES : 2 * LANES] = (grad_kv[:, 0:LANES] * scale).astype(BF16)
    grads[:, 2 * LANES :] = grad_kv[:, LANES:].astype(BF16)
    partial_sums(grads, wide, whole, rank, kept, pair, across)


def out_partial_kernel(sc, biases, attended, rows_weight, residual, kept, pair, across, whole):
    rank = sc[0]
    rows = kept.shape[0]
    bias = biases[6:7, lane_block(rank)]
    for i in range(4):
        at = slice(i * rows, (i + 1) * rows)
        whole[at, :] = mm(attended[at, :], rows_weight[...], 1, 0)
    whole[:, lane_block(rank)] += residual[...] + bias
    kept[...] = whole[row_block(rank, rows), :]
    pair[0] = whole[row_block(rank ^ 1, rows), :].astype(BF16)
    pair[1] = whole[row_block(rank ^ 3, rows), :].astype(BF16)
    across[...] = whole[row_block(rank ^ 2, rows), :].astype(BF16)


def norm_third_back_kernel(
    sc, gains, kept, near, far, normed_ref, inverse_ref, cot, wide,
    out_kept, out_pair, out_across, grad_res, shifted, sums, whole, *, cols, width,
):
    rank = sc[0]
    pixels = kept.shape[0]
    grad = kept[...] + near[0].astype(F32) + far[...].astype(F32)
    normed = normed_ref[...]
    valid = valid_of(sc, pixels, LANES, cols)
    back = norm_back(
        grad * gains[1:2, lane_block(rank)], normed, inverse_ref[0:1, :], valid,
        pixel_count(sc, width), width,
    )
    cot_value = cot[...].astype(F32)
    residual = cot_value + back
    grad_res[...] = residual
    third = (valid * residual).astype(BF16).astype(F32)
    shifted_grads(third, shifted, cols)
    sums[...] = jnp.zeros(sums.shape, F32)
    sums[0:1, :] = col_sum(grad * normed)
    sums[1:2, :] = col_sum(grad)
    sums[2:3, :] = col_sum(third)
    sums[3:4, :] = col_sum(cot_value)
    partial_sums(shifted, wide, whole, rank, out_kept, out_pair, out_across)


def norm_second_back_kernel(
    sc, kept, near, far, normed_ref, aux, wide,
    out_kept, out_pair, out_across, shifted, sums, whole, *, cols, width,
):
    rank = sc[0]
    pixels = kept.shape[0]
    grad_act = kept[...] + near[0].astype(F32) + far[...].astype(F32)
    normed = normed_ref[...]
    valid = valid_of(sc, pixels, LANES, cols)
    inverse, scale, shift = (aux[0:1, :], aux[1:2, :], aux[2:3, :])
    grad_pre = grad_act * valid * silu_grad(normed * (1.0 + scale) + shift)
    back = norm_back(
        grad_pre * (1.0 + scale), normed, inverse, valid, pixel_count(sc, width), width
    )
    first = back.astype(BF16).astype(F32)
    shifted_grads(first, shifted, cols)
    sums[...] = jnp.zeros(sums.shape, F32)
    sums[0:1, :] = col_sum(grad_pre * normed).astype(BF16).astype(F32)
    sums[1:2, :] = col_sum(grad_pre).astype(BF16).astype(F32)
    sums[2:3, :] = col_sum(first)
    partial_sums(shifted, wide, whole, rank, out_kept, out_pair, out_across)


def norm_first_back_kernel(
    sc, gains, biases, kept, near, far, own, stats, grad_res, sums_third, sums_second,
    out_kept, out_pair, out_across, table, held, *, cols, width,
):
    rank = sc[0]
    pixels = kept.shape[0]
    rows = out_kept.shape[0]
    grad_act = kept[...] + near[0].astype(F32) + far[...].astype(F32)
    valid = valid_of(sc, pixels, LANES, cols)
    center, inverse = (stats[0:1, :], stats[1:2, :])
    normed = (own[...].astype(F32) - center) * inverse
    gain = gains[0:1, lane_block(rank)]
    grad_pre = grad_act * valid * silu_grad(normed * gain + biases[0:1, lane_block(rank)])
    back = norm_back(grad_pre * gain, normed, inverse, valid, pixel_count(sc, width), width)
    held[...] = grad_res[...] + back
    out_kept[...] = held[row_block(rank, rows), :]
    out_pair[0] = held[row_block(rank ^ 1, rows), :].astype(BF16)
    out_pair[1] = held[row_block(rank ^ 3, rows), :].astype(BF16)
    out_across[...] = held[row_block(rank ^ 2, rows), :].astype(BF16)
    table[...] = jnp.zeros(table.shape, F32)
    table[0:1, :] = col_sum(grad_pre * normed)
    table[1:2, :] = sums_third[0:1, :]
    table[2:3, :] = col_sum(grad_pre)
    table[3:4, :] = sums_second[2:3, :]
    table[4:6, :] = sums_second[0:2, :]
    table[6:7, :] = sums_third[2:3, :]
    table[7:8, :] = sums_third[1:2, :]
    table[8:9, :] = sums_third[3:4, :]
    table[pl.ds(16 + 2 * sc[1], 2), :] = sums_second[0:2, :]


def rows_join_kernel(sc, kept, near, far, out):
    rank = sc[0]
    for k, block in enumerate((kept, near.at[0], far.at[0], far.at[1])):
        out[:, lane_block(rank ^ k)] = block[...].astype(F32)


def taps_grad(act, shifted, flat):
    channels = act.shape[1]
    for i in range(channels // LANES):
        part = mm(act[:, i * LANES : (i + 1) * LANES], shifted[...], 0, 0)
        for tap in range(9):
            flat[tap * channels + i * LANES : tap * channels + (i + 1) * LANES, :] = part[
                :, tap * LANES : (tap + 1) * LANES
            ]


def second_grads_kernel(sc, act, shifted, attn, grads, attended, cot, *refs, dp_count):
    dests = refs[0:dp_count]
    flat, qkv, proj = refs[dp_count:]
    place = sc[1]
    channels = act.shape[1]
    taps_grad(act, shifted, flat)
    part = mm(attn[...], grads[...], 0, 0)
    for g in range(3):
        qkv[g] = part[:, g * LANES : (g + 1) * LANES]
    part = mm(attended[...], cot[...], 0, 0)
    for g in range(channels // LANES):
        proj[g] = part[:, g * LANES : (g + 1) * LANES]
    sizes = (flat.shape[0] // dp_count, channels // dp_count, LANES // dp_count)
    for k, dest in enumerate(dests):
        peer = place ^ k
        dest[0 : sizes[0], :] = flat[row_block(peer, sizes[0]), :].astype(dest.dtype)
        at = sizes[0]
        for source, size in ((qkv, sizes[1]), (proj, sizes[2])):
            for g in range(source.shape[0]):
                dest[at : at + size, :] = source[g, row_block(peer, size), :].astype(dest.dtype)
                at += size


def first_grads_kernel(sc, act, shifted, sums, ada, *refs, dp_count):
    dests = refs[0:dp_count]
    emb_part, flat = refs[dp_count:]
    place = sc[1]
    taps_grad(act, shifted, flat)
    size = flat.shape[0] // dp_count
    for k, dest in enumerate(dests):
        dest[...] = flat[row_block(place ^ k, size), :].astype(dest.dtype)
    for j in range(emb_part.shape[0]):
        row = jnp.zeros((1, LANES), F32)
        for side in range(2):
            mod = jnp.broadcast_to(sums[side : side + 1, :], (16, LANES)).astype(BF16)
            row = row + mm(mod, ada[side, j * LANES : (j + 1) * LANES, :], 1, 1)[0:1]
        emb_part[j : j + 1, :] = row


def dp_scatter(blocks):
    near = {k: hop(blocks[k ^ 1], "dp", 1) for k in (2, 4, 6, 0)}
    far = [
        hop((blocks[k].astype(F32) + near[k].astype(F32)).astype(BF16), "dp", k) for k in (2, 4, 6)
    ]
    return (blocks[0], near[0], *far)


def split_second_kernel(sc, a, b, c, d, e, kept, pair, across, proj, held, *, rows_conv, rows_qkv):
    rank = sc[0]
    held[...] = a[...] + sum(part[...].astype(F32) for part in (b, c, d, e))

    def put(dest, peer):
        dest[0:rows_conv, :] = held[row_block(peer, rows_conv), :].astype(dest.dtype)
        for g in range(3):
            begin = 4 * rows_conv + g * 4 * rows_qkv
            dest[rows_conv + g * rows_qkv : rows_conv + (g + 1) * rows_qkv, :] = held[
                pl.ds(pl.multiple_of(begin + peer * rows_qkv, 8), rows_qkv), :
            ].astype(dest.dtype)

    put(kept, rank)
    put(pair.at[0], rank ^ 1)
    put(pair.at[1], rank ^ 3)
    put(across, rank ^ 2)
    proj[...] = held[4 * rows_conv + 12 * rows_qkv :, :].astype(BF16)


def split_first_kernel(sc, a, b, c, d, e, kept, pair, across, held, *, rows_conv):
    rank = sc[0]
    held[...] = a[...] + sum(part[...].astype(F32) for part in (b, c, d, e))
    kept[...] = held[row_block(rank, rows_conv), :]
    pair[0] = held[row_block(rank ^ 1, rows_conv), :].astype(BF16)
    pair[1] = held[row_block(rank ^ 3, rows_conv), :].astype(BF16)
    across[...] = held[row_block(rank ^ 2, rows_conv), :].astype(BF16)


def join_second_kernel(sc, kept, near, far, proj, conv_out, qkv_out, proj_out, *, rows_conv, rows_qkv):
    rank = sc[0]
    rows_proj = proj.shape[0] // 4
    low_half = lax.broadcasted_iota(jnp.int32, (rows_qkv, LANES), 1) < HD
    for k, block in enumerate((kept, near.at[0], far.at[0], far.at[1])):
        peer = rank ^ k
        conv_out[pl.ds(peer, rows_conv, stride=4), :] = block[0:rows_conv, :].astype(F32)
        part = [
            block[rows_conv + g * rows_qkv : rows_conv + (g + 1) * rows_qkv, :].astype(F32)
            for g in range(3)
        ]
        keys = pltpu.roll(part[1], HD, 1)
        mixed = (
            jnp.where(low_half, part[0], keys),
            jnp.where(low_half, part[2], part[0]),
            jnp.where(low_half, keys, part[2]),
        )
        for g in range(3):
            qkv_out[pl.ds(peer * 3 + g, rows_qkv, stride=12), :] = mixed[g]
    for g in range(4):
        proj_out[pl.ds(g, rows_proj, stride=4), :] = proj[
            g * rows_proj : (g + 1) * rows_proj, :
        ].astype(F32)


def join_first_kernel(sc, kept, near, far, conv_out, *, rows_conv):
    rank = sc[0]
    for k, block in enumerate((kept, near.at[0], far.at[0], far.at[1])):
        conv_out[pl.ds(rank ^ k, rows_conv, stride=4), :] = block[...].astype(F32)


def small_grads_kernel(sc, embs, t0, t1, t2, t3, gains_out, biases_out, ada_out, mods, table):
    rank = sc[0]
    images = embs.shape[0]
    for k, block in enumerate((t0, t1, t2, t3)):
        lanes = lane_block(rank ^ k)
        table[:, lanes] = block[0:16, :]
        for side in range(2):
            at = pl.ds(pl.multiple_of((side * 4 + (rank ^ k)) * LANES, LANES), LANES)
            mods[:, at] = block[pl.ds(16 + side, images, stride=2), :]
    gains_out[...] = table[0:2, :]
    biases_out[...] = table[2:9, :]
    part = mm(embs[...], mods[...].astype(BF16), 0, 0)
    rows = ada_out.shape[0] // 8
    for g in range(8):
        ada_out[pl.ds(g, rows, stride=8), :] = part[:, g * LANES : (g + 1) * LANES]


def body(
    inputs, embedding, extent, cotangent, gains, biases,
    conv_first, conv_second, qkv_master, ada_master, proj_master,
):
    heads = lax.axis_size("head")
    dps = lax.axis_size("dp")
    rank = lax.axis_index("head")
    place = lax.axis_index("dp")
    batch, row_count, cols, channels = inputs.shape
    rows = row_count * cols
    pixels = rows * heads
    width = channels // GROUPS
    emb_rows = embedding.shape[1] // LANES
    sc = jnp.stack([rank, place, extent[0, 0], extent[0, 1]]).astype(jnp.int32)
    direct = dps == 8
    flats = [
        master.reshape(-1, LANES)
        for master in (conv_first, conv_second, qkv_master, ada_master, proj_master)
    ]
    rows_conv = flats[0].shape[0] // 4
    rows_qkv = flats[2].shape[0] // 12
    rows_ada = flats[3].shape[0] // 8
    rows_proj = flats[4].shape[0] // 4
    emb_own = embedding.reshape(emb_rows, LANES)
    spread = [
        (i, (i % dps) * heads + i // dps) for i in range(dps * heads)
    ]
    if direct:
        rows_a = rows_conv + 2 * rows_ada
        rows_b = rows_conv + 3 * rows_qkv
        a0, a13, a2, b0, b13, b2, pj = call(
            weights_out_kernel,
            [
                sds(shape, BF16)
                for size in (rows_a, rows_b)
                for shape in ((size, LANES), (2, size, LANES), (size, LANES))
            ]
            + [sds((4 * rows_proj, LANES), BF16)],
            sc,
            *flats,
        )
        near, far = head_exchange(a13, a2)
        rows_first = 4 * rows_conv + 8 * rows_ada + 16
        (first_piece,) = call(
            functools.partial(first_piece_kernel, rows_conv=rows_conv, rows_ada=rows_ada),
            [sds((rows_first, LANES), BF16)],
            sc, a0, near, far, emb_own,
        )
        first_pieces = dp_gather(first_piece)
        near, far = head_exchange(b13, b2)
        pj = lax.ppermute(pj, ("dp", "head"), spread)
        rows_second = 4 * rows_conv + 12 * rows_qkv + 4 * rows_proj
        (second_piece,) = call(
            functools.partial(second_piece_kernel, rows_conv=rows_conv, rows_qkv=rows_qkv),
            [sds((rows_second, LANES), BF16)],
            sc, b0, near, far, pj,
        )
        second_pieces = dp_gather(second_piece)
        offsets = (place ^ jnp.arange(dps, dtype=jnp.int32)).astype(jnp.int32)
        first_segments = (
            (0, 1, 4 * rows_conv),
            (4 * rows_conv, 2, 4 * rows_ada),
        )
        second_segments = (
            (0, 1, 4 * rows_conv),
            (4 * rows_conv, 3, 4 * rows_qkv),
            (4 * rows_conv + 12 * rows_qkv, 4, rows_proj),
        )
    else:
        first_pieces, first_segments, second_pieces, second_segments, emb_table = gather_plain(
            flats, emb_own, spread, channels
        )
        offsets = jnp.zeros((1,), jnp.int32)

    blocks = head_gather(inputs.reshape(rows, channels))
    cots = head_gather(cotangent.reshape(rows, channels))
    act_first, own, stats_first = call(
        functools.partial(norm_first_kernel, cols=cols, width=width),
        [sds((pixels, channels), BF16), sds((pixels, LANES), BF16), sds((8, LANES), F32)],
        sc, gains, biases, *blocks,
        scratch=[pltpu.VMEM((8, channels), F32)],
        flops=20 * pixels * channels,
    )
    conv_flops = 2 * pixels * channels * 9 * LANES
    wide_shape = (channels, 9 * LANES)
    taps_scratch = pltpu.VMEM((pixels + 2 * cols, 9 * LANES), F32)
    flat_scratch = pltpu.VMEM((1, 9 * channels, LANES), BF16)
    n_pieces = len(first_pieces)

    def with_offsets(kernel, n_offsets=1):
        def run(sc_ref, *refs):
            return kernel(sc_ref, sc_ref.at[pl.ds(4, n_pieces)], *refs)

        return run

    sc_all = jnp.concatenate([sc, offsets])
    act_second_own, normed_second, aux_second, wide_first, ada_full = call(
        with_offsets(
            functools.partial(
                conv_first_kernel, cols=cols, width=width, count_pieces=n_pieces,
                segments=first_segments,
            )
        ),
        [
            sds((pixels, LANES), BF16), sds((pixels, LANES), F32), sds((8, LANES), F32),
            sds(wide_shape, BF16), sds((2, emb_rows * LANES, LANES), BF16),
        ],
        sc_all, biases, act_first, emb_own, *first_pieces,
        scratch=[flat_scratch, taps_scratch, pltpu.VMEM((pixels, LANES), F32)],
        flops=conv_flops,
    )
    blocks = head_gather(act_second_own)
    attn_own, act_second, residual, normed_third, aux_third, wide_second = call(
        with_offsets(
            functools.partial(
                conv_second_kernel, cols=cols, width=width, count_pieces=n_pieces,
                segments=second_segments,
            )
        ),
        [
            sds((pixels, LANES), BF16), sds((pixels, channels), BF16), sds((pixels, LANES), F32),
            sds((pixels, LANES), F32), sds((8, LANES), F32), sds(wide_shape, BF16),
        ],
        sc_all, gains, biases, own, *blocks, *second_pieces,
        scratch=[flat_scratch, taps_scratch],
        flops=conv_flops,
    )
    blocks = head_gather(attn_own)
    split_outs = [
        sds((pixels, LANES), F32), sds((2, pixels, LANES), BF16), sds((pixels, LANES), BF16)
    ]
    whole_scratch = pltpu.VMEM((pixels, channels), F32)
    kept, pair, across, attn_full, grads_qkv, attended, cot_full, cot_own, rows_weight = call(
        with_offsets(
            functools.partial(
                attention_kernel, cols=cols, count_pieces=n_pieces, segments=second_segments
            )
        ),
        split_outs
        + [
            sds((pixels, channels), BF16), sds((pixels, 3 * LANES), BF16),
            sds((pixels, LANES), BF16), sds((pixels, channels), BF16),
            sds((pixels, LANES), BF16), sds((LANES, channels), BF16),
        ],
        sc_all, *blocks, *cots, *second_pieces,
        scratch=[
            pltpu.VMEM((3, channels, LANES), BF16),
            pltpu.VMEM((channels // LANES, LANES, LANES), BF16),
            pltpu.VMEM((channels, 3 * LANES), BF16),
            pltpu.VMEM((pixels, 3 * LANES), BF16),
            pltpu.VMEM((LANES, pixels), BF16),
            pltpu.VMEM((LANES, pixels), BF16),
            pltpu.VMEM((pixels, LANES), BF16),
            pltpu.VMEM((LANES, pixels), F32),
            pltpu.VMEM((pixels, 2 * LANES), F32),
            whole_scratch,
        ],
        flops=12 * pixels * pixels * LANES * 2,
    )

    def reduce_send(pair, across):
        near = hop(pair, "head", 1)
        far = hop((across.astype(F32) + near[1].astype(F32)).astype(BF16), "head", 2)
        return (near, far)

    near, far = reduce_send(pair, across)
    out_kept, out_pair, out_across = call(
        out_partial_kernel,
        [
            sds((rows, channels), F32), sds((2, rows, channels), BF16),
            sds((rows, channels), BF16),
        ],
        sc, biases, attended, rows_weight, residual,
        scratch=[whole_scratch],
        flops=2 * pixels * channels * LANES,
    )
    out_near, out_far = reduce_send(out_pair, out_across)
    output = (out_kept + out_near[0].astype(F32) + out_far.astype(F32)).astype(BF16)

    kept, pair, across, grad_res, shifted_second, sums_third = call(
        functools.partial(norm_third_back_kernel, cols=cols, width=width),
        split_outs
        + [sds((pixels, LANES), F32), sds((pixels, 9 * LANES), BF16), sds((8, LANES), F32)],
        sc, gains, kept, near, far, normed_third, aux_third, cot_own, wide_second,
        scratch=[whole_scratch],
        flops=conv_flops,
    )
    near, far = reduce_send(pair, across)
    rows_second = 4 * rows_conv + 12 * rows_qkv + 4 * rows_proj
    n_dests = dps if direct else 1
    second_blocks = call(
        functools.partial(second_grads_kernel, dp_count=n_dests),
        [
            sds(((9 * channels + 3 * channels + channels) // n_dests, LANES), F32 if k == 0 else BF16)
            for k in range(n_dests)
        ],
        sc if direct else sc * jnp.array([1, 0, 1, 1], jnp.int32),
        act_second, shifted_second, attn_full, grads_qkv, attended, cot_full,
        scratch=[
            pltpu.VMEM((9 * channels, LANES), F32),
            pltpu.VMEM((3, channels, LANES), F32),
            pltpu.VMEM((channels // LANES, LANES, LANES), F32),
        ],
        flops=conv_flops + conv_flops // 2,
    )
    kept, pair, across, shifted_first, sums_second = call(
        functools.partial(norm_second_back_kernel, cols=cols, width=width),
        split_outs + [sds((pixels, 9 * LANES), BF16), sds((8, LANES), F32)],
        sc, kept, near, far, normed_second, aux_second, wide_first,
        scratch=[whole_scratch],
        flops=conv_flops,
    )
    near, far = reduce_send(pair, across)
    first_out = call(
        functools.partial(first_grads_kernel, dp_count=n_dests),
        [
            sds((9 * channels // n_dests, LANES), F32 if k == 0 else BF16) for k in range(n_dests)
        ]
        + [sds((emb_rows, LANES), F32)],
        sc if direct else sc * jnp.array([1, 0, 1, 1], jnp.int32),
        act_first, shifted_first, sums_second, ada_full,
        scratch=[pltpu.VMEM((9 * channels, LANES), F32)],
        flops=conv_flops,
    )
    first_blocks, emb_part = (first_out[:-1], first_out[-1])
    table_rows = 16 + 2 * dps
    kept, pair, across, table = call(
        functools.partial(norm_first_back_kernel, cols=cols, width=width),
        [
            sds((rows, LANES), F32), sds((2, rows, LANES), BF16), sds((rows, LANES), BF16),
            sds((table_rows, LANES), F32),
        ],
        sc, gains, biases, kept, near, far, own, stats_first, grad_res, sums_third, sums_second,
        scratch=[pltpu.VMEM((pixels, LANES), F32)],
        flops=20 * pixels * LANES,
    )
    near, far = head_exchange(pair, across)
    (grad_inputs,) = call(
        rows_join_kernel, [sds((rows, channels), F32)], sc, kept, near, far
    )

    if direct:
        for bit in (1, 2, 4):
            table = table + hop(table, "dp", bit)
    else:
        table = lax.psum(table, "dp")
    t0, t1, t2, t3 = head_gather(jnp.concatenate([table, emb_part]))
    emb_float = embedding.astype(F32)
    grad_embedding = (t0 + t1 + t2 + t3)[table_rows:].reshape(1, -1) * silu_grad(emb_float)
    if direct:
        emb_at = first_segments[1][0] + 8 * rows_ada
        emb_table = jnp.stack([piece[emb_at : emb_at + emb_rows] for piece in first_pieces])
        emb_table = emb_table[place ^ jnp.arange(dps)]
    mine = lax.dynamic_index_in_dim(
        emb_table.reshape(dps, -1, rows_ada), place * heads + rank, 1, False
    ).astype(F32)
    mine = (mine * jax.nn.sigmoid(mine)).astype(BF16)
    grad_gains, grad_biases, ada_grad = call(
        small_grads_kernel,
        [sds(gains.shape, F32), sds(biases.shape, F32), sds(flats[3].shape, F32)],
        sc, mine, t0, t1, t2, t3,
        scratch=[
            pltpu.VMEM((dps, 8 * LANES), F32),
            pltpu.VMEM((16, channels), F32),
        ],
    )

    if direct:
        parts = dp_scatter(second_blocks)
        kept, pair, across, pj = call(
            functools.partial(split_second_kernel, rows_conv=rows_conv, rows_qkv=rows_qkv),
            [
                sds((rows_b, LANES), F32), sds((2, rows_b, LANES), BF16), sds((rows_b, LANES), BF16),
                sds((4 * rows_proj, LANES), BF16),
            ],
            sc, *parts,
            scratch=[pltpu.VMEM((rows_second, LANES), F32)],
        )
        near, far = head_exchange(pair, across)
        pj = lax.ppermute(pj, ("dp", "head"), [(j, i) for i, j in spread])
        second_grad, qkv_grad, proj_grad = call(
            functools.partial(join_second_kernel, rows_conv=rows_conv, rows_qkv=rows_qkv),
            [sds(flats[i].shape, F32) for i in (1, 2, 4)],
            sc, kept, near, far, pj,
        )
        parts = dp_scatter(first_blocks)
        kept, pair, across = call(
            functools.partial(split_first_kernel, rows_conv=rows_conv),
            [sds((rows_conv, LANES), F32), sds((2, rows_conv, LANES), BF16), sds((rows_conv, LANES), BF16)],
            sc, *parts,
            scratch=[pltpu.VMEM((4 * rows_conv, LANES), F32)],
        )
        near, far = head_exchange(pair, across)
        (first_grad,) = call(
            functools.partial(join_first_kernel, rows_conv=rows_conv),
            [sds(flats[0].shape, F32)],
            sc, kept, near, far,
        )
    else:
        first_grad, second_grad, qkv_grad, proj_grad = scatter_plain(
            first_blocks[0], second_blocks[0], spread, channels
        )
    return (
        output.reshape(inputs.shape),
        grad_inputs.reshape(inputs.shape),
        grad_embedding,
        grad_gains,
        grad_biases,
        first_grad.reshape(-1),
        second_grad.reshape(-1),
        qkv_grad.reshape(-1),
        ada_grad.reshape(-1),
        proj_grad.reshape(-1),
    )


def gather_plain(flats, emb_own, spread, channels):
    heads = lax.axis_size("head")

    def columns(flat, groups):
        blocks = flat.astype(BF16).reshape(-1, groups, LANES)
        return blocks

    def own_columns(blocks):
        got = lax.all_to_all(blocks, "head", split_axis=1, concat_axis=0, tiled=True)
        return lax.all_gather(got[:, 0], "dp", axis=0, tiled=True)

    first, second = (own_columns(columns(flats[i], heads).reshape(-1, heads, 1, LANES))[:, 0] for i in (0, 1))
    qkv = columns(flats[2], 12).reshape(-1, heads, 2, 3, HD)
    qkv = jnp.swapaxes(qkv, 2, 3).reshape(-1, heads, 3, LANES)
    qkv = jnp.swapaxes(own_columns(qkv), 0, 1).reshape(-1, LANES)
    ada = columns(flats[3], 8).reshape(-1, 2, heads, LANES)
    ada = jnp.swapaxes(own_columns(jnp.swapaxes(ada, 1, 2)), 0, 1).reshape(-1, LANES)
    proj = lax.ppermute(flats[4].astype(BF16), ("dp", "head"), spread)
    proj = lax.all_gather(proj, "dp", axis=0, tiled=True).reshape(-1, channels // LANES, LANES)
    proj = jnp.swapaxes(proj, 0, 1).reshape(-1, LANES)
    emb_table = lax.all_gather(emb_own, "dp", axis=0)
    first_piece = jnp.concatenate([first, ada])
    second_piece = jnp.concatenate([second, qkv, proj])
    return (
        [first_piece],
        ((0, 1, 9 * channels), (9 * channels, 2, ada.shape[0] // 2)),
        [second_piece],
        (
            (0, 1, 9 * channels),
            (9 * channels, 3, channels),
            (12 * channels, channels // LANES, LANES),
        ),
        emb_table,
    )


def scatter_plain(first, second, spread, channels):
    heads = lax.axis_size("head")

    def rows_of(grad):
        part = lax.psum_scatter(grad, "dp", scatter_dimension=0, tiled=True)
        return lax.all_to_all(part[:, None], "head", split_axis=0, concat_axis=1, tiled=True)

    def conv(grad):
        return rows_of(grad[:, None])

    qkv = jnp.swapaxes(second[9 * channels : 12 * channels].reshape(3, channels, LANES), 0, 1)
    qkv = rows_of(qkv).reshape(-1, heads, 3, 2, HD)
    qkv = jnp.swapaxes(qkv, 2, 3)
    proj = jnp.swapaxes(second[12 * channels :].reshape(-1, LANES, LANES), 0, 1)
    proj = lax.psum_scatter(proj, "dp", scatter_dimension=0, tiled=True)
    proj = lax.ppermute(proj, ("dp", "head"), [(j, i) for i, j in spread])
    return (conv(first), conv(second[: 9 * channels]), qkv, proj)


def solution(mesh):
    flat = P(("dp", "head"))
    image = P("dp", "head", None, None)
    return jax.shard_map(
        body,
        mesh=mesh,
        in_specs=(image, P("dp", None), P("dp", None), image, P(), P(), flat, flat, flat, flat, flat),
        out_specs=(image, image, P("dp", None), P(), P(), flat, flat, flat, flat, flat),
        check_vma=False,
    )
```

```python
import functools
import math

import jax
import jax.numpy as jnp
from jax import lax
from jax.experimental import pallas as pl
from jax.experimental.pallas import tpu as pltpu
from jax.sharding import PartitionSpec as P

HD = 64
GROUPS = 32
EPS = 1e-05
MASKED = -1e30
LANES = 128
F32 = jnp.float32
BF16 = jnp.bfloat16
VMEM_SPEC = pl.BlockSpec(memory_space=pltpu.VMEM)
SMEM_SPEC = pl.BlockSpec(memory_space=pltpu.SMEM)


def sds(shape, dtype):
    return jax.ShapeDtypeStruct(shape, dtype)


class Far:
    def __init__(self, array, held=True, pinned=False):
        self.array = pltpu.with_memory_space_constraint(array, pltpu.HBM) if pinned else array
        self.held = held


class Fetch:
    def __init__(self, source, ref, sem):
        self.copy = pltpu.make_async_copy(source, ref, sem)
        self.ref = ref
        self.copy.start()

    def get(self):
        self.copy.wait()
        return self.ref


class Store:
    def __init__(self, dest, ref, sem):
        self.dest = dest
        self.ref = ref
        self.sem = sem
        self.copy = None

    def send(self, source=None):
        self.copy = pltpu.make_async_copy(self.ref if source is None else source, self.dest, self.sem)
        self.copy.start()


def call(kernel, outs, args, scratch=(), us=1.0, vmem=24, after=()):
    arrays = [arg.array if isinstance(arg, Far) else arg for arg in args]
    results = [out.array if isinstance(out, Far) else out for out in outs]
    far_in = [isinstance(arg, Far) for arg in args]
    far_out = [isinstance(out, Far) for out in outs]
    held = [
        pltpu.VMEM(x.array.shape, x.array.dtype)
        for x in list(args) + list(outs)
        if isinstance(x, Far) and x.held
    ]
    copies = sum(far_in) + sum(far_out)

    def run(*refs):
        ins = refs[: len(args)]
        begin = len(args) + len(after)
        dests = refs[begin : begin + len(outs)]
        begin += len(outs)
        buffers = iter(refs[begin : begin + len(held)])
        begin += len(held)
        sems = refs[begin] if copies else None
        rest = refs[begin + (1 if copies else 0) :]
        count = 0
        given = []
        for ref, far in zip(ins, far_in):
            if far:
                ref = Fetch(ref, next(buffers), sems.at[count])
                count += 1
            given.append(ref)
        stores = []
        for ref, out in zip(dests, outs):
            if isinstance(out, Far):
                ref = Store(ref, next(buffers) if out.held else None, sems.at[count])
                stores.append(ref)
                count += 1
            given.append(ref)
        kernel(*given, *rest)
        for store in stores:
            store.copy.wait()

    hbm = pl.BlockSpec(memory_space=pltpu.HBM)
    anywhere = pl.BlockSpec(memory_space=pl.ANY)
    return pl.pallas_call(
        run,
        out_shape=tuple(results),
        in_specs=[SMEM_SPEC]
        + [hbm if far else VMEM_SPEC for far in far_in[1:]]
        + [anywhere for _ in after],
        out_specs=tuple(hbm if far else VMEM_SPEC for far in far_out),
        scratch_shapes=held
        + ([pltpu.SemaphoreType.DMA((copies,))] if copies else [])
        + list(scratch),
        compiler_params=pltpu.CompilerParams(vmem_limit_bytes=vmem * 1024 * 1024),
        cost_estimate=pl.CostEstimate(
            flops=int(1.15e9 * us),
            bytes_accessed=1024,
            transcendentals=0,
        ),
    )(*arrays, *after)


def following(value, *earlier):
    return lax.optimization_barrier((value, *earlier))[0]


def hop(value, axis, bit):
    count = lax.axis_size(axis)
    return lax.ppermute(value, axis, [(i, i ^ bit) for i in range(count)])


def head_gather(block, *earlier):
    far = hop(block, "head", 2)
    near = hop(block, "head", 1)
    return (block, near, far, hop(following(far, *earlier) if earlier else far, "head", 1))


def head_exchange(near_block, far_pair):
    far = hop(far_pair, "head", 2)
    near = hop(near_block, "head", 1)
    return (near, far, hop(far, "head", 1))


def add_kernel(ext, first, second, out):
    out[...] = (first[...].astype(F32) + second[...].astype(F32)).astype(out.dtype)


def head_reduce(ext, blocks):
    kept, near_block, far_block, corner = blocks
    corner = hop(corner, "head", 1)
    (far_block,) = call(
        add_kernel, [sds(far_block.shape, BF16)], [ext, far_block, corner], us=0.7
    )
    return (kept, hop(near_block, "head", 1), hop(far_block, "head", 2))


def mm(left, right, left_dim, right_dim):
    return lax.dot_general(
        left, right, (((left_dim,), (right_dim,)), ((), ())), preferred_element_type=F32
    )


def lane_block(index):
    return pl.ds(pl.multiple_of(index * LANES, LANES), LANES)


def row_block(index, rows):
    return pl.ds(pl.multiple_of(index * rows, rows), rows)


def pixel_place(rows, lanes, cols, start=0):
    pixel = lax.broadcasted_iota(jnp.int32, (rows, lanes), 0) + start
    shift = cols.bit_length() - 1
    return (lax.shift_right_logical(pixel, shift), lax.bitwise_and(pixel, cols - 1))


def valid_of(ext, rows, lanes, cols, start=0):
    place_row, place_col = pixel_place(rows, lanes, cols, start)
    inside = jnp.logical_and(place_row < ext[0, 0], place_col < ext[0, 1])
    return jnp.where(inside, 1.0, 0.0).astype(F32)


def group_total(first, second, width):
    lanes = first.shape[-1]
    pick = lax.broadcasted_iota(jnp.int32, (8, lanes), 0)
    both = jnp.where(pick == 0, first, jnp.where(pick == 1, second, 0.0))
    shift = width.bit_length() - 1
    left = lax.shift_right_logical(lax.broadcasted_iota(jnp.int32, (lanes, lanes), 0), shift)
    right = lax.shift_right_logical(lax.broadcasted_iota(jnp.int32, (lanes, lanes), 1), shift)
    same = jnp.where(left == right, 1.0, 0.0).astype(F32)
    total = lax.dot_general(
        both,
        same,
        (((1,), (0,)), ((), ())),
        precision=lax.Precision.HIGHEST,
        preferred_element_type=F32,
    )
    return (total[0:1], total[1:2])


def pixel_count(ext, width):
    return (ext[0, 0] * ext[0, 1] * width).astype(F32)


def col_sum(value):
    return jnp.sum(value, axis=0, keepdims=True)


def head_rank():
    return lax.axis_index("head")


def norm_stats(value, valid, count, width):
    masked = value * valid
    total, square = group_total(col_sum(masked), col_sum(masked * value), width)
    center = total / count
    return (center, lax.rsqrt(square / count - center * center + EPS))


def norm_back(grad, normed, inverse, valid, count, width):
    first, second = group_total(col_sum(grad), col_sum(grad * normed), width)
    return (grad - valid * ((first + normed * second) * (1.0 / count))) * inverse


def silu_grad(value):
    gate = jax.nn.sigmoid(value)
    return gate * (1.0 + value * (1.0 - gate))


def place_pieces(dest, pieces, start, groups, rows):
    for k, piece in enumerate(pieces):
        part = lax.axis_index("dp") ^ k if len(pieces) > 1 else 0
        for group in range(groups):
            begin = start + group * rows
            dest[group, pl.ds(pl.multiple_of(part * rows, rows), rows), :] = piece[
                begin : begin + rows, :
            ]


def taps_side_by_side(flat, wide):
    channels = wide.shape[0]
    for tap in range(9):
        wide[:, tap * LANES : (tap + 1) * LANES] = flat[0, tap * channels : (tap + 1) * channels, :]


def conv_taps(act, wide, taps, cols):
    pixels = act.shape[0]
    lanes = wide.shape[1]
    taps[0:cols, :] = jnp.zeros((cols, lanes), F32)
    taps[pixels + cols :, :] = jnp.zeros((cols, lanes), F32)
    step = 256

    def one(i, carry):
        begin = pl.multiple_of(i * step, step)
        taps[pl.ds(pl.multiple_of(begin + cols, cols), step), :] = mm(
            act[pl.ds(begin, step), :], wide[...], 1, 0
        )
        return carry

    lax.fori_loop(0, pixels // step, one, 0)


def conv_sum(taps, begin, rows, cols):
    def column(side):
        return sum(
            taps[
                pl.ds(pl.multiple_of(begin + up * cols, cols), rows),
                (up * 3 + side) * LANES : (up * 3 + side + 1) * LANES,
            ]
            for up in range(3)
        )

    place_col = pixel_place(rows, LANES, cols)[1]
    left = jnp.where(place_col > 0, pltpu.roll(column(0), 1, 0), 0.0)
    right = jnp.where(place_col < cols - 1, pltpu.roll(column(2), rows - 1, 0), 0.0)
    return column(1) + left + right


def shifted_grads(grad, dest, cols):
    pixels = grad.shape[0]
    place_col = pixel_place(pixels, LANES, cols)[1]
    sides = (
        jnp.where(place_col < cols - 1, pltpu.roll(grad, pixels - 1, 0), 0.0),
        grad,
        jnp.where(place_col > 0, pltpu.roll(grad, 1, 0), 0.0),
    )
    blank = jnp.zeros((cols, LANES), BF16)
    for side, value in enumerate(sides):
        low = value.astype(BF16)
        for up in range(3):
            lanes = slice((up * 3 + side) * LANES, (up * 3 + side + 1) * LANES)
            if up == 0:
                dest[0 : pixels - cols, lanes] = low[cols:, :]
                dest[pixels - cols :, lanes] = blank
            elif up == 1:
                dest[:, lanes] = low
            else:
                dest[cols:, lanes] = low[0 : pixels - cols, :]
                dest[0:cols, lanes] = blank


def partial_sums(left, right, whole, outs):
    pixels = left.shape[0]
    step = 256

    def one(i, carry):
        rows = pl.ds(pl.multiple_of(i * step, step), step)
        whole[rows, :] = mm(left[rows, :], right[...], 1, 1)
        return carry

    lax.fori_loop(0, pixels // step, one, 0)
    rank = head_rank()
    for k, out in enumerate(outs):
        out[...] = whole[:, lane_block(rank ^ k)].astype(out.dtype)


def weights_out_kernel(ext, *refs):
    first, second, qkv, ada, proj = refs[0:5]
    a0, a1, a23, b0, b1, b23, pj = refs[5:]
    rank = head_rank()
    low_half = lax.broadcasted_iota(jnp.int32, (qkv.ref.shape[0] // 12, LANES), 1) < HD

    def strided(ref, begin, stride):
        return ref[pl.ds(begin, ref.shape[0] // stride, stride=stride), :]

    def put(dest, slot, begin, value):
        rows = value.shape[0]
        if slot is None:
            dest[begin : begin + rows, :] = value.astype(BF16)
        else:
            dest[slot, begin : begin + rows, :] = value.astype(BF16)
        return begin + rows

    first, ada = (first.get(), ada.get())
    for k, (dest, slot) in enumerate(((a0, None), (a1, None), (a23, 0), (a23, 1))):
        at = put(dest, slot, 0, strided(first, rank ^ k, 4))
        for side in range(2):
            at = put(dest, slot, at, strided(ada, 4 * side + (rank ^ k), 8))
    second, qkv, proj = (second.get(), qkv.get(), proj.get())
    for k, (dest, slot) in enumerate(((b0, None), (b1, None), (b23, 0), (b23, 1))):
        at = put(dest, slot, 0, strided(second, rank ^ k, 4))
        part = [strided(qkv, (rank ^ k) * 3 + g, 12) for g in range(3)]
        at = put(dest, slot, at, jnp.where(low_half, part[0], part[1]))
        at = put(dest, slot, at, pltpu.roll(jnp.where(low_half, part[2], part[0]), HD, 1))
        put(dest, slot, at, jnp.where(low_half, part[1], part[2]))
    at = 0
    for g in range(4):
        at = put(pj, None, at, strided(proj, g, 4))


def first_piece_kernel(ext, a0, near, far, corner, emb, piece, line, *, rows_conv, rows_ada):
    rank = head_rank()
    for k, block in enumerate((a0, near, far.at[0], corner.at[1])):
        peer = rank ^ k
        piece[row_block(peer, rows_conv), :] = block[0:rows_conv, :]
        for side in range(2):
            begin = 4 * rows_conv + side * 4 * rows_ada
            piece[pl.ds(pl.multiple_of(begin + peer * rows_ada, 16), rows_ada), :] = block[
                rows_conv + side * rows_ada : rows_conv + (side + 1) * rows_ada, :
            ]
    emb = emb.get()
    line[...] = jnp.zeros(line.shape, F32)
    for j in range(emb.shape[1] // LANES):
        line[j : j + 1, :] = emb[0:1, j * LANES : (j + 1) * LANES].astype(F32)
    piece[4 * rows_conv + 8 * rows_ada :, :] = line[...].astype(BF16)


def second_piece_kernel(ext, b0, near, far, corner, pj, piece, *, rows_conv, rows_qkv):
    rank = head_rank()
    for k, block in enumerate((b0, near, far.at[0], corner.at[1])):
        peer = rank ^ k
        piece[row_block(peer, rows_conv), :] = block[0:rows_conv, :]
        for g in range(3):
            begin = 4 * rows_conv + g * 4 * rows_qkv
            piece[pl.ds(pl.multiple_of(begin + peer * rows_qkv, 16), rows_qkv), :] = block[
                rows_conv + g * rows_qkv : rows_conv + (g + 1) * rows_qkv, :
            ]
    piece[4 * rows_conv + 12 * rows_qkv :, :] = pj[...]


def dp_straight(piece):
    two, six = (hop(piece, "dp", 2), hop(piece, "dp", 6))
    return [piece, two, hop(following(piece, two), "dp", 4), six]


def dp_beside(straight):
    own, two, four, six = straight
    near = [hop(value, "dp", 1) for value in (own, two, six)]
    near.insert(2, hop(following(four, *near), "dp", 1))
    return [value for pair in zip(straight, near) for value in pair]


def norm_first_kernel(ext, gains, biases, *refs, cols, width):
    blocks = refs[0:4]
    act, own_out, stats, held = refs[4:]
    own = own_out.ref
    rank = head_rank()
    rows, channels = blocks[0].shape
    count = pixel_count(ext, width)
    total = jnp.zeros((1, channels), F32)
    square = jnp.zeros((1, channels), F32)
    for k, block in enumerate(blocks):
        own[row_block(rank ^ k, rows), :] = block[:, lane_block(rank)]
    own_out.send()
    for k, block in enumerate(blocks):
        value = block[...].astype(F32)
        masked = value * valid_of(ext, rows, channels, cols, (rank ^ k) * rows)
        total = total + col_sum(masked)
        square = square + col_sum(masked * value)
    total, square = group_total(total, square, width)
    center = total / count
    inverse = lax.rsqrt(square / count - center * center + EPS)
    held[0:1, :] = center
    held[1:2, :] = inverse
    gain, bias = (gains.get()[0:1, :], biases.get()[0:1, :])
    for k, block in enumerate(blocks):
        peer = rank ^ k
        pre = (block[...].astype(F32) - center) * inverse * gain + bias
        valid = valid_of(ext, rows, channels, cols, peer * rows)
        act[row_block(peer, rows), :] = (pre * jax.nn.sigmoid(pre) * valid).astype(BF16)
    stats[...] = held[:, lane_block(rank)]


def conv_first_kernel(ext, biases, act, emb, *refs, cols, width, count_pieces, segments, emb_at):
    pieces = refs[0:count_pieces]
    act_out, normed_out, aux, wide_out, ada_out, act_far = refs[count_pieces : count_pieces + 6]
    flat, taps, hidden = refs[-3:]
    rank = head_rank()
    pixels = act.shape[0]
    act_far.send(act)
    place_pieces(flat, pieces, *segments[0])
    wide = wide_out.ref
    taps_side_by_side(flat, wide)
    wide_out.send()
    ada = ada_out.ref
    place_pieces(ada, pieces, *segments[1])
    ada_out.send()
    if emb_at is not None:
        table = refs[count_pieces + 6]
        place = lax.axis_index("dp")
        table[...] = jnp.zeros(table.shape, F32)
        for k, piece in enumerate(pieces):
            lines = piece[emb_at : emb_at + 16, :].astype(F32)
            mine = lax.broadcasted_iota(jnp.int32, lines.shape, 0) == place
            table[pl.ds(place ^ k, 1), :] = col_sum(jnp.where(mine, lines, 0.0))
    conv_taps(act, wide, taps, cols)
    biases = biases.get()
    bias = biases[1:2, lane_block(rank)]
    step = 256
    for i in range(pixels // step):
        hidden[i * step : (i + 1) * step, :] = conv_sum(taps, i * step, step, cols) + bias
    value = hidden[...]
    valid = valid_of(ext, pixels, LANES, cols)
    center, inverse = norm_stats(value, valid, pixel_count(ext, width), width)
    normed = (value - center) * inverse
    normed_out.ref[...] = normed
    normed_out.send()
    emb_value = emb.get()[...].astype(F32)
    emb_act = (emb_value * jax.nn.sigmoid(emb_value)).astype(BF16).astype(F32)
    mods = []
    for side in range(2):
        mod = biases[2 + side : 3 + side, lane_block(rank)]
        for j in range(emb_act.shape[1] // LANES):
            lanes = slice(j * LANES, (j + 1) * LANES)
            row = jnp.broadcast_to(emb_act[:, lanes], (16, LANES)).astype(BF16)
            mod = mod + mm(row, ada[side, lanes, :], 1, 0)[0:1]
        mods.append(mod)
    pre = normed * (1.0 + mods[0]) + mods[1]
    act_out[...] = (pre * jax.nn.sigmoid(pre) * valid).astype(BF16)
    aux[...] = jnp.zeros(aux.shape, F32)
    aux[0:1, :] = inverse
    aux[1:2, :] = mods[0]
    aux[2:3, :] = mods[1]


def conv_second_kernel(ext, gains, biases, own, *refs, cols, width, count_pieces, segments):
    blocks = refs[0:4]
    pieces = refs[4 : 4 + count_pieces]
    attn_in, act_out, residual_out, normed_out, aux, wide_out, w_qkv, w_proj = refs[
        4 + count_pieces : 12 + count_pieces
    ]
    flat, qkv, proj, taps = refs[12 + count_pieces :]
    rank = head_rank()
    act, wide, residual = (act_out.ref, wide_out.ref, residual_out.ref)
    pixels = act.shape[0]
    for k, block in enumerate(blocks):
        act[:, lane_block(rank ^ k)] = block[...]
    act_out.send()
    place_pieces(flat, pieces, *segments[0])
    taps_side_by_side(flat, wide)
    wide_out.send()
    place_pieces(qkv, pieces, *segments[1])
    place_pieces(proj, pieces, *segments[2])
    for source, dest in ((qkv, w_qkv), (proj, w_proj)):
        for g in range(source.shape[0]):
            dest[:, g * LANES : (g + 1) * LANES] = source[g]
    conv_taps(act, wide, taps, cols)
    gains, biases, own = (gains.get(), biases.get(), own.get())
    bias = biases[4:5, lane_block(rank)]
    step = 256
    for i in range(pixels // step):
        rows = slice(i * step, (i + 1) * step)
        third = conv_sum(taps, i * step, step, cols) + bias
        valid = valid_of(ext, step, LANES, cols, i * step)
        residual[rows, :] = own[rows, :].astype(F32) + valid * third
    residual_out.send()
    value = residual[...]
    valid = valid_of(ext, pixels, LANES, cols)
    center, inverse = norm_stats(value, valid, pixel_count(ext, width), width)
    normed = (value - center) * inverse
    normed_out.ref[...] = normed
    normed_out.send()
    attn_in[...] = (
        normed * gains[1:2, lane_block(rank)] + biases[5:6, lane_block(rank)]
    ).astype(BF16)
    aux[...] = jnp.broadcast_to(inverse, aux.shape)


def cotangent_kernel(ext, *refs):
    cots = refs[0:4]
    rows_weight, full_out, own_out, att, att_t = refs[4:]
    rank = head_rank()
    rows = cots[0].shape[0]
    for k, cot in enumerate(cots):
        at = row_block(rank ^ k, rows)
        full_out.ref[at, :] = cot[...]
        own_out.ref[at, :] = cot[:, lane_block(rank)]
    full_out.send()
    own_out.send()
    for i in range(4):
        at = slice(i * rows, (i + 1) * rows)
        grad = mm(full_out.ref[at, :], rows_weight[...], 1, 1).astype(BF16)
        att[at, :] = grad
        att_t[:, at] = grad.astype(F32).T


def attention_kernel(ext, *refs, cols):
    blocks = refs[0:4]
    wide, cot_att, cot_att_t = refs[4:7]
    outs = refs[7:11]
    full_out, grads_out, attended_out = refs[11:14]
    qkv, keys_t, values_t, grad_kv, whole = refs[14:]
    attn_full, grads, attended = (full_out.ref, grads_out.ref, attended_out.ref)
    rank = head_rank()
    pixels = attn_full.shape[0]
    scale = 1.0 / math.sqrt(HD)
    for k in range(4):
        attn_full[:, lane_block(rank ^ k)] = blocks[k][...]
    full_out.send()
    step = 256

    def project(i, carry):
        at = pl.ds(pl.multiple_of(i * step, step), step)
        qkv[at, :] = mm(attn_full[at, :], wide[...], 1, 0).astype(BF16)
        return carry

    lax.fori_loop(0, pixels // step, project, 0)
    for i in range(pixels // step):
        at = slice(i * step, (i + 1) * step)
        keys_t[:, at] = qkv[at, LANES : 2 * LANES].astype(F32).T.astype(BF16)
        values_t[:, at] = qkv[at, 2 * LANES :].astype(F32).T.astype(BF16)
    grad_kv[...] = jnp.zeros(grad_kv.shape, F32)
    span = 256
    lane = lax.broadcasted_iota(jnp.int32, (span, LANES), 1)
    sublane_all = lax.broadcasted_iota(jnp.int32, (LANES, pixels), 0)

    def attend(i, carry):
        at = pl.ds(pl.multiple_of(i * span, span), span)
        queries = qkv[at, 0:LANES]
        cot_rows = cot_att[at, :]
        cot_cols = cot_att_t[:, at]
        key_row, key_col = pixel_place(pixels, span, cols)
        key_valid = jnp.logical_and(key_row < ext[0, 0], key_col < ext[0, 1])
        att_sum = jnp.zeros((LANES, span), F32)
        query_sum = jnp.zeros((LANES, span), F32)
        for h in range(LANES // HD):
            mine = lax.shift_right_logical(lane, 6) == h
            mine_all = lax.shift_right_logical(sublane_all, 6) == h
            query = jnp.where(mine, queries, jnp.zeros_like(queries))
            cot = jnp.where(mine, cot_rows, jnp.zeros_like(cot_rows))
            scores = mm(qkv[:, LANES : 2 * LANES], query, 1, 1) * scale
            scores = jnp.where(key_valid, scores, MASKED)
            top = jnp.max(scores, axis=0, keepdims=True)
            expo = jnp.exp(scores - top)
            probs = expo * (1.0 / col_sum(expo))
            probs_low = probs.astype(BF16)
            value_t = jnp.where(mine_all, values_t[...], jnp.zeros_like(values_t[...]))
            att = mm(value_t, probs_low, 1, 0)
            att_sum = att_sum + att
            row_dot = col_sum(att * cot_cols)
            grad_kv[:, LANES:] += mm(probs_low, cot, 1, 0)
            grad_probs = mm(qkv[:, 2 * LANES :], cot, 1, 1)
            grad_scores = (probs * (grad_probs - row_dot)).astype(BF16)
            grad_kv[:, 0:LANES] += mm(grad_scores, query, 1, 0)
            key_t = jnp.where(mine_all, keys_t[...], jnp.zeros_like(keys_t[...]))
            query_sum = query_sum + mm(key_t, grad_scores, 1, 0)
        attended[at, :] = att_sum.T.astype(BF16)
        grads[at, 0:LANES] = (query_sum.T * scale).astype(BF16)
        return carry

    lax.fori_loop(0, pixels // span, attend, 0)
    attended_out.send()
    grads[:, LANES : 2 * LANES] = (grad_kv[:, 0:LANES] * scale).astype(BF16)
    grads[:, 2 * LANES :] = grad_kv[:, LANES:].astype(BF16)
    grads_out.send()
    partial_sums(grads, wide, whole, outs)


def out_partial_kernel(ext, biases, attended, rows_weight, residual, *refs):
    outs = refs[0:4]
    whole = refs[4]
    rank = head_rank()
    rows = outs[0].shape[0]
    attended = attended.get()
    for i in range(4):
        at = slice(i * rows, (i + 1) * rows)
        whole[at, :] = mm(attended[at, :], rows_weight[...], 1, 0)
    bias = biases.get()[6:7, lane_block(rank)]
    whole[:, lane_block(rank)] += residual.get()[...] + bias
    for k, out in enumerate(outs):
        out[...] = whole[row_block(rank ^ k, rows), :].astype(out.dtype)


def sum_kernel(ext, first, second, third, out):
    out[...] = (first[...] + second[...].astype(F32) + third[...].astype(F32)).astype(out.dtype)


def norm_third_back_kernel(ext, gains, kept, near, far, normed, inverse, cot, wide, *refs, cols, width):
    outs = refs[0:4]
    grad_res, third_out, sums, shifted, whole = refs[4:]
    rank = head_rank()
    pixels = kept.shape[0]
    grad = kept[...] + near[...].astype(F32) + far[...].astype(F32)
    normed, gains, cot = (normed.get()[...], gains.get(), cot.get())
    valid = valid_of(ext, pixels, LANES, cols)
    back = norm_back(
        grad * gains[1:2, lane_block(rank)], normed, inverse[0:1, :], valid,
        pixel_count(ext, width), width,
    )
    cot_value = cot[...].astype(F32)
    residual = cot_value + back
    grad_res.ref[...] = residual
    grad_res.send()
    third = (valid * residual).astype(BF16)
    third_out[...] = third
    third = third.astype(F32)
    shifted_grads(third, shifted, cols)
    sums[...] = jnp.zeros(sums.shape, F32)
    sums[0:1, :] = col_sum(grad * normed)
    sums[1:2, :] = col_sum(grad)
    sums[2:3, :] = col_sum(third)
    sums[3:4, :] = col_sum(cot_value)
    partial_sums(shifted, wide.get(), whole, outs)


def norm_second_back_kernel(ext, kept, near, far, normed, aux, wide, *refs, cols, width):
    outs = refs[0:4]
    first_out, sums, shifted, whole = refs[4:]
    pixels = kept.shape[0]
    grad_act = kept[...] + near[...].astype(F32) + far[...].astype(F32)
    normed = normed.get()[...]
    valid = valid_of(ext, pixels, LANES, cols)
    inverse, scale, shift = (aux[0:1, :], aux[1:2, :], aux[2:3, :])
    grad_pre = grad_act * valid * silu_grad(normed * (1.0 + scale) + shift)
    back = norm_back(
        grad_pre * (1.0 + scale), normed, inverse, valid, pixel_count(ext, width), width
    )
    first = back.astype(BF16)
    first_out[...] = first
    first = first.astype(F32)
    shifted_grads(first, shifted, cols)
    sums[...] = jnp.zeros(sums.shape, F32)
    sums[0:1, :] = col_sum(grad_pre * normed).astype(BF16).astype(F32)
    sums[1:2, :] = col_sum(grad_pre).astype(BF16).astype(F32)
    sums[2:3, :] = col_sum(first)
    partial_sums(shifted, wide.get(), whole, outs)


def norm_first_back_kernel(
    ext, gains, biases, kept, near, far, own, stats, grad_res, sums_third, sums_second,
    out_kept, out_near, out_pair, table, held, *, cols, width,
):
    rank = head_rank()
    pixels = kept.shape[0]
    rows = out_kept.shape[0]
    grad_act = kept[...] + near[...].astype(F32) + far[...].astype(F32)
    valid = valid_of(ext, pixels, LANES, cols)
    center, inverse = (stats[0:1, :], stats[1:2, :])
    normed = (own.get()[...].astype(F32) - center) * inverse
    gain = gains.get()[0:1, lane_block(rank)]
    bias = biases.get()[0:1, lane_block(rank)]
    grad_pre = grad_act * valid * silu_grad(normed * gain + bias)
    back = norm_back(grad_pre * gain, normed, inverse, valid, pixel_count(ext, width), width)
    held[...] = grad_res.get()[...] + back
    out_kept[...] = held[row_block(rank, rows), :]
    out_near[...] = held[row_block(rank ^ 1, rows), :].astype(BF16)
    for k in (2, 3):
        out_pair[k - 2] = held[row_block(rank ^ k, rows), :].astype(BF16)
    table[...] = jnp.zeros(table.shape, F32)
    table[0:1, :] = col_sum(grad_pre * normed)
    table[1:2, :] = sums_third[0:1, :]
    table[2:3, :] = col_sum(grad_pre)
    table[3:4, :] = sums_second[2:3, :]
    table[4:6, :] = sums_second[0:2, :]
    table[6:7, :] = sums_third[2:3, :]
    table[7:8, :] = sums_third[1:2, :]
    table[8:9, :] = sums_third[3:4, :]
    table[pl.ds(16 + 2 * lax.axis_index("dp"), 2), :] = sums_second[0:2, :]


def rows_join_kernel(ext, kept, near, far, corner, out):
    rank = head_rank()
    for k, block in enumerate((kept, near, far.at[0], corner.at[1])):
        out[:, lane_block(rank ^ k)] = block[...].astype(F32)


def taps_grad(act, shifted, flat):
    channels = act.shape[1]
    for i in range(channels // LANES):
        part = mm(act[:, i * LANES : (i + 1) * LANES], shifted[...], 0, 0)
        for tap in range(9):
            flat[0, tap * channels + i * LANES : tap * channels + (i + 1) * LANES, :] = part[
                :, tap * LANES : (tap + 1) * LANES
            ]


def dp_parts(dests, sources, dp_count):
    place = lax.axis_index("dp") if dp_count > 1 else 0
    for k, dest in enumerate(dests):
        at = 0
        for source in sources:
            size = source.shape[1] // dp_count
            for g in range(source.shape[0]):
                dest[at : at + size, :] = source[g, row_block(place ^ k, size), :].astype(dest.dtype)
                at += size


def second_grads_kernel(ext, third, act, attn, grads, attended, cot, *refs, cols, dp_count):
    dests = refs[0:-4]
    shifted, flat, qkv, proj = refs[-4:]
    shifted_grads(third[...].astype(F32), shifted, cols)
    act = act.get()
    taps_grad(act, shifted, flat)
    attn, grads = (attn.get(), grads.get())
    part = mm(attn[...], grads[...], 0, 0)
    for g in range(3):
        qkv[g] = part[:, g * LANES : (g + 1) * LANES]
    attended, cot = (attended.get(), cot.get())
    part = mm(attended[...], cot[...], 0, 0)
    for g in range(proj.shape[0]):
        proj[g] = part[:, g * LANES : (g + 1) * LANES]
    dp_parts(split_dests(dests), (flat, qkv, proj), dp_count)


def split_dests(dests):
    if len(dests) == 1:
        return dests
    own, two, four, six, first_pair, second_pair = dests
    return (
        own, second_pair.at[1], two, first_pair.at[0], four, first_pair.at[1], six, second_pair.at[0]
    )


def first_grads_kernel(ext, first, act, sums, ada, *refs, cols, dp_count):
    dests = refs[0:-3]
    emb_part, shifted, flat = refs[-3:]
    shifted_grads(first[...].astype(F32), shifted, cols)
    taps_grad(act.get(), shifted, flat)
    dp_parts(split_dests(dests), (flat,), dp_count)
    ada = ada.get()
    for j in range(emb_part.shape[0]):
        row = jnp.zeros((1, LANES), F32)
        for side in range(2):
            mod = jnp.broadcast_to(sums[side : side + 1, :], (16, LANES)).astype(BF16)
            row = row + mm(mod, ada[side, j * LANES : (j + 1) * LANES, :], 1, 1)[0:1]
        emb_part[j : j + 1, :] = row


def dp_add_kernel(ext, pair, *refs):
    count = len(refs) // 2
    for k in range(count):
        refs[count + k][...] = (refs[k][...].astype(F32) + pair[k].astype(F32)).astype(BF16)


def dp_pairs(parts):
    return (hop(parts[4], "dp", 1), hop(parts[5], "dp", 1))


def dp_scatter(ext, parts, pairs, early=(), late=()):
    own, two, four, six = parts[:4]
    out = sds(two.shape, BF16)
    two, four = call(dp_add_kernel, [out, out], [ext, pairs[0], two, four], us=0.7, after=early)
    (six,) = call(dp_add_kernel, [out], [ext, pairs[1], six], us=0.5, after=late)
    return (own, pairs[1], hop(two, "dp", 2), hop(four, "dp", 4), hop(six, "dp", 6))


def split_second_kernel(ext, a, b, c, d, e, kept, near, pair, proj, held, *, rows_conv, rows_qkv):
    rank = head_rank()
    held[...] = a[...] + sum(part[...].astype(F32) for part in (b.at[1], c, d, e))
    for k, dest in enumerate((kept, near, pair.at[0], pair.at[1])):
        peer = rank ^ k
        dest[0:rows_conv, :] = held[row_block(peer, rows_conv), :].astype(dest.dtype)
        for g in range(3):
            begin = 4 * rows_conv + g * 4 * rows_qkv
            dest[rows_conv + g * rows_qkv : rows_conv + (g + 1) * rows_qkv, :] = held[
                pl.ds(pl.multiple_of(begin + peer * rows_qkv, 8), rows_qkv), :
            ].astype(dest.dtype)
    proj[...] = held[4 * rows_conv + 12 * rows_qkv :, :].astype(BF16)


def split_first_kernel(ext, a, b, c, d, e, kept, near, pair, held, *, rows_conv):
    rank = head_rank()
    held[...] = a[...] + sum(part[...].astype(F32) for part in (b.at[1], c, d, e))
    for k, dest in enumerate((kept, near, pair.at[0], pair.at[1])):
        dest[...] = held[row_block(rank ^ k, rows_conv), :].astype(dest.dtype)


def join_second_kernel(ext, kept, near, far, corner, proj, conv_out, qkv_out, proj_out, *, rows_conv, rows_qkv):
    rank = head_rank()
    rows_proj = proj.shape[0] // 4
    low_half = lax.broadcasted_iota(jnp.int32, (rows_qkv, LANES), 1) < HD
    for k, block in enumerate((kept, near, far.at[0], corner.at[1])):
        peer = rank ^ k
        conv_out[pl.ds(peer, rows_conv, stride=4), :] = block[0:rows_conv, :].astype(F32)
        part = [
            block[rows_conv + g * rows_qkv : rows_conv + (g + 1) * rows_qkv, :].astype(F32)
            for g in range(3)
        ]
        keys = pltpu.roll(part[1], HD, 1)
        mixed = (
            jnp.where(low_half, part[0], keys),
            jnp.where(low_half, part[2], part[0]),
            jnp.where(low_half, keys, part[2]),
        )
        for g in range(3):
            qkv_out[pl.ds(peer * 3 + g, rows_qkv, stride=12), :] = mixed[g]
    for g in range(4):
        proj_out[pl.ds(g, rows_proj, stride=4), :] = proj[
            g * rows_proj : (g + 1) * rows_proj, :
        ].astype(F32)


def join_first_kernel(ext, kept, near, far, corner, conv_out, *, rows_conv):
    rank = head_rank()
    for k, block in enumerate((kept, near, far.at[0], corner.at[1])):
        conv_out[pl.ds(rank ^ k, rows_conv, stride=4), :] = block[...].astype(F32)


def table_kernel(ext, table, other, emb_part, out):
    rows = table.shape[0]
    out[0:rows, :] = table[...] + other[...]
    out[rows:, :] = emb_part[...]


def small_grads_kernel(ext, embs, emb, t0, t1, t2, t3, gains_out, biases_out, ada_out, emb_out, mods, table, held):
    rank = head_rank()
    images = embs.shape[0]
    for k, block in enumerate((t0, t1, t2, t3)):
        table[:, lane_block(rank ^ k)] = block[0:16, :]
        for side in range(2):
            mods[:, lane_block(side * 4 + (rank ^ k))] = block[pl.ds(16 + side, images, stride=2), :]
    gains_out[...] = table[0:2, :]
    biases_out[...] = table[2:9, :]
    value = embs[...]
    part = mm((value * jax.nn.sigmoid(value)).astype(BF16), mods[...].astype(BF16), 0, 0)
    rows = ada_out.shape[0] // 8
    if part.shape[0] != rows:
        held[...] = part
        part = held[row_block(rank, rows), :]
    for g in range(8):
        ada_out[pl.ds(g, rows, stride=8), :] = part[:, g * LANES : (g + 1) * LANES]
    value = emb.get()[...].astype(F32)
    slope = silu_grad(value)
    begin = 16 + 2 * images
    for j in range(value.shape[1] // LANES):
        lanes = slice(j * LANES, (j + 1) * LANES)
        total = sum(block[begin + j : begin + j + 1, :] for block in (t0, t1, t2, t3))
        emb_out[:, lanes] = total * slope[:, lanes]


def body(
    inputs, embedding, extent, cotangent, gains, biases,
    conv_first, conv_second, qkv_master, ada_master, proj_master,
):
    heads = lax.axis_size("head")
    dps = lax.axis_size("dp")
    batch, row_count, cols, channels = inputs.shape
    rows = row_count * cols
    pixels = rows * heads
    width = channels // GROUPS
    emb_rows = embedding.shape[1] // LANES
    ext = extent
    direct = dps == 8
    flats = [
        master.reshape(-1, LANES)
        for master in (conv_first, conv_second, qkv_master, ada_master, proj_master)
    ]
    rows_conv = flats[0].shape[0] // 4
    rows_qkv = flats[2].shape[0] // 12
    rows_ada = flats[3].shape[0] // 8
    rows_proj = flats[4].shape[0] // 4
    far_gains, far_biases, far_emb = (Far(gains), Far(biases), Far(embedding))
    spread = [(i, (i % dps) * heads + i // dps) for i in range(dps * heads)]
    inputs_own = inputs.reshape(rows, channels)
    cot_own = cotangent.reshape(rows, channels)
    if direct:
        rows_a = rows_conv + 2 * rows_ada
        rows_b = rows_conv + 3 * rows_qkv
        a0, a1, a23, b0, b1, b23, pj = call(
            weights_out_kernel,
            [
                sds(shape, BF16)
                for size in (rows_a, rows_b)
                for shape in ((size, LANES), (size, LANES), (2, size, LANES))
            ]
            + [sds((4 * rows_proj, LANES), BF16)],
            [ext] + [Far(flat, pinned=True) for flat in flats],
        )
        a_blocks = head_exchange(a1, a23)
        (first_piece,) = call(
            functools.partial(first_piece_kernel, rows_conv=rows_conv, rows_ada=rows_ada),
            [sds((4 * rows_conv + 8 * rows_ada + 16, LANES), BF16)],
            [ext, a0, *a_blocks, far_emb],
            scratch=[pltpu.VMEM((16, LANES), F32)],
        )
        first_straight = dp_straight(first_piece)
        b_blocks = head_exchange(b1, following(b23, first_straight[1]))
        inputs_sent = following(inputs_own, first_straight[1])
        pj = lax.ppermute(pj, ("dp", "head"), spread)
        rows_second = 4 * rows_conv + 12 * rows_qkv + 4 * rows_proj
        (second_piece,) = call(
            functools.partial(second_piece_kernel, rows_conv=rows_conv, rows_qkv=rows_qkv),
            [sds((rows_second, LANES), BF16)],
            [ext, b0, *b_blocks, pj],
        )
        first_pieces = dp_beside(first_straight)
        second_straight = dp_straight(second_piece)
        first_segments = ((0, 1, 4 * rows_conv), (4 * rows_conv, 2, 4 * rows_ada))
        second_segments = (
            (0, 1, 4 * rows_conv),
            (4 * rows_conv, 3, 4 * rows_qkv),
            (4 * rows_conv + 12 * rows_qkv, 4, rows_proj),
        )
    else:
        first_pieces, first_segments, second_pieces, second_segments, embs = gather_plain(
            flats, embedding, spread, channels
        )
        inputs_sent = inputs_own

    blocks = head_gather(inputs_sent)
    act_first, own, stats_first = call(
        functools.partial(norm_first_kernel, cols=cols, width=width),
        [sds((pixels, channels), BF16), Far(sds((pixels, LANES), BF16)), sds((8, LANES), F32)],
        [ext, far_gains, far_biases, *blocks],
        scratch=[pltpu.VMEM((8, channels), F32)],
        us=2.0,
    )
    cots = head_gather(following(cot_own, blocks[2]))
    wide_shape = (channels, 9 * LANES)
    taps_scratch = pltpu.VMEM((pixels + 2 * cols, 9 * LANES), F32)
    flat_scratch = pltpu.VMEM((1, 9 * channels, LANES), BF16)
    n_pieces = len(first_pieces)
    first_outs = call(
        functools.partial(
            conv_first_kernel, cols=cols, width=width, count_pieces=n_pieces,
            segments=first_segments,
            emb_at=4 * rows_conv + 8 * rows_ada if direct else None,
        ),
        [
            sds((pixels, LANES), BF16), Far(sds((pixels, LANES), F32)), sds((8, LANES), F32),
            Far(sds(wide_shape, BF16)), Far(sds((2, emb_rows * LANES, LANES), BF16)),
            Far(sds((pixels, channels), BF16), held=False),
        ]
        + ([sds((dps, LANES), F32)] if direct else []),
        [ext, far_biases, act_first, far_emb, *first_pieces],
        scratch=[flat_scratch, taps_scratch, pltpu.VMEM((pixels, LANES), F32)],
        us=4.0,
    )
    act_second_own, normed_second, aux_second, wide_first, ada_full, act_first = first_outs[:6]
    if direct:
        embs = first_outs[6]
        second_pieces = dp_beside(second_straight)
        act_second_own = following(act_second_own, second_straight[1])
    blocks = head_gather(act_second_own)
    attn_own, act_second, residual, normed_third, aux_third, wide_second, w_qkv, rows_weight = call(
        functools.partial(
            conv_second_kernel, cols=cols, width=width, count_pieces=n_pieces,
            segments=second_segments,
        ),
        [
            sds((pixels, LANES), BF16), Far(sds((pixels, channels), BF16)),
            Far(sds((pixels, LANES), F32)), Far(sds((pixels, LANES), F32)), sds((8, LANES), F32),
            Far(sds(wide_shape, BF16)), sds((channels, 3 * LANES), BF16),
            sds((LANES, channels), BF16),
        ],
        [ext, far_gains, far_biases, Far(own), *blocks, *second_pieces],
        scratch=[
            flat_scratch,
            pltpu.VMEM((3, channels, LANES), BF16),
            pltpu.VMEM((channels // LANES, LANES, LANES), BF16),
            taps_scratch,
        ],
        us=4.0,
    )
    cot_full, cot_own, cot_att, cot_att_t = call(
        cotangent_kernel,
        [
            Far(sds((pixels, channels), BF16)), Far(sds((pixels, LANES), BF16)),
            sds((pixels, LANES), BF16), sds((LANES, pixels), F32),
        ],
        [ext, *cots, rows_weight],
    )
    blocks = head_gather(attn_own, cot_att)
    whole_scratch = pltpu.VMEM((pixels, channels), F32)
    shifted_scratch = pltpu.VMEM((pixels, 9 * LANES), BF16)
    split_outs = [sds((pixels, LANES), F32)] + [sds((pixels, LANES), BF16)] * 3
    *parts, attn_full, grads_qkv, attended = call(
        functools.partial(attention_kernel, cols=cols),
        split_outs
        + [
            Far(sds((pixels, channels), BF16)), Far(sds((pixels, 3 * LANES), BF16)),
            Far(sds((pixels, LANES), BF16)),
        ],
        [ext, *blocks, w_qkv, cot_att, cot_att_t],
        scratch=[
            pltpu.VMEM((pixels, 3 * LANES), BF16),
            pltpu.VMEM((LANES, pixels), BF16),
            pltpu.VMEM((LANES, pixels), BF16),
            pltpu.VMEM((pixels, 2 * LANES), F32),
            whole_scratch,
        ],
        us=15.0,
    )
    parts = head_reduce(ext, parts)
    out_parts = call(
        out_partial_kernel,
        [sds((rows, channels), F32)] + [sds((rows, channels), BF16)] * 3,
        [ext, far_biases, Far(attended), rows_weight, Far(residual)],
        scratch=[whole_scratch],
        us=2.0,
    )
    *parts, grad_res, third, sums_third = call(
        functools.partial(norm_third_back_kernel, cols=cols, width=width),
        split_outs
        + [Far(sds((pixels, LANES), F32)), sds((pixels, LANES), BF16), sds((8, LANES), F32)],
        [
            ext, far_gains, *parts, Far(normed_third), aux_third, Far(cot_own), Far(wide_second),
        ],
        scratch=[shifted_scratch, whole_scratch],
        us=4.0,
    )
    (output,) = call(
        sum_kernel, [sds((rows, channels), BF16)], [ext, *head_reduce(ext, out_parts)]
    )
    parts = head_reduce(ext, parts)
    n_dests = dps if direct else 1

    def grad_outs(size):
        size = size // n_dests
        if not direct:
            return [sds((size, LANES), F32)]
        one = sds((size, LANES), BF16)
        return [sds((size, LANES), F32), one, one, one] + [sds((2, size, LANES), BF16)] * 2

    flat_grad = pltpu.VMEM((1, 9 * channels, LANES), F32)
    second_parts = call(
        functools.partial(second_grads_kernel, cols=cols, dp_count=n_dests),
        grad_outs(13 * channels),
        [ext, third] + [Far(x) for x in (act_second, attn_full, grads_qkv, attended, cot_full)],
        scratch=[
            shifted_scratch,
            flat_grad,
            pltpu.VMEM((3, channels, LANES), F32),
            pltpu.VMEM((channels // LANES, LANES, LANES), F32),
        ],
        us=4.0,
    )
    *parts, first, sums_second = call(
        functools.partial(norm_second_back_kernel, cols=cols, width=width),
        split_outs + [sds((pixels, LANES), BF16), sds((8, LANES), F32)],
        [ext, *parts, Far(normed_second), aux_second, Far(wide_first)],
        scratch=[shifted_scratch, whole_scratch],
        us=4.0,
        after=second_parts[:1],
    )
    if direct:
        second_pairs = dp_pairs(second_parts)
        parts[3] = following(parts[3], second_pairs[0])
    parts = head_reduce(ext, parts)
    *first_parts, emb_part = call(
        functools.partial(first_grads_kernel, cols=cols, dp_count=n_dests),
        grad_outs(9 * channels) + [sds((emb_rows, LANES), F32)],
        [ext, first, Far(act_first), sums_second, Far(ada_full)],
        scratch=[shifted_scratch, flat_grad],
        us=3.0,
    )
    if direct:
        first_pairs = dp_pairs(first_parts)
        second_left = dp_scatter(ext, second_parts, second_pairs)
    table_rows = 16 + 2 * dps
    kept, near, pair, table = call(
        functools.partial(norm_first_back_kernel, cols=cols, width=width),
        [
            sds((rows, LANES), F32), sds((rows, LANES), BF16), sds((2, rows, LANES), BF16),
            sds((table_rows, LANES), F32),
        ],
        [
            ext, far_gains, far_biases, *parts, Far(own), stats_first, Far(grad_res), sums_third,
            sums_second,
        ],
        scratch=[pltpu.VMEM((pixels, LANES), F32)],
        us=2.0,
        after=[emb_part, second_pairs[1]] if direct else (),
    )
    if direct:
        table = following(table, first_pairs[0])
    (grad_inputs,) = call(
        rows_join_kernel,
        [sds((rows, channels), F32)],
        [ext, kept, *head_exchange(near, pair)],
    )

    if direct:
        for bit in (1, 2):
            table = table + hop(table, "dp", bit)
        other = hop(table, "dp", 4)
    else:
        table = lax.psum(table, "dp")
        other = jnp.zeros_like(table)
    (table,) = call(
        table_kernel,
        [sds((table_rows + emb_rows, LANES), F32)],
        [ext, table, other, emb_part],
        us=0.5,
    )
    grad_gains, grad_biases, ada_grad, grad_embedding = call(
        small_grads_kernel,
        [
            sds(gains.shape, F32), sds(biases.shape, F32), sds(flats[3].shape, F32),
            sds(embedding.shape, F32),
        ],
        [ext, embs, far_emb, *head_gather(table)],
        scratch=[
            pltpu.VMEM((dps, 8 * LANES), F32),
            pltpu.VMEM((16, channels), F32),
            pltpu.VMEM((LANES, 8 * LANES), F32),
        ],
    )

    if direct:
        kept, near, pair, pj = call(
            functools.partial(split_second_kernel, rows_conv=rows_conv, rows_qkv=rows_qkv),
            [
                sds((rows_b, LANES), F32), sds((rows_b, LANES), BF16),
                sds((2, rows_b, LANES), BF16), sds((4 * rows_proj, LANES), BF16),
            ],
            [ext, *second_left],
            scratch=[pltpu.VMEM((rows_second, LANES), F32)],
        )
        pj = lax.ppermute(pj, ("dp", "head"), [(j, i) for i, j in spread])
        second_grad, qkv_grad, proj_grad = call(
            functools.partial(join_second_kernel, rows_conv=rows_conv, rows_qkv=rows_qkv),
            [sds(flats[i].shape, F32) for i in (1, 2, 4)],
            [ext, kept, *head_exchange(near, pair), pj],
        )
        kept, near, pair = call(
            functools.partial(split_first_kernel, rows_conv=rows_conv),
            [
                sds((rows_conv, LANES), F32), sds((rows_conv, LANES), BF16),
                sds((2, rows_conv, LANES), BF16),
            ],
            [ext, *dp_scatter(ext, first_parts, first_pairs)],
            scratch=[pltpu.VMEM((4 * rows_conv, LANES), F32)],
        )
        (first_grad,) = call(
            functools.partial(join_first_kernel, rows_conv=rows_conv),
            [sds(flats[0].shape, F32)],
            [ext, kept, *head_exchange(near, pair)],
        )
    else:
        first_grad, second_grad, qkv_grad, proj_grad = scatter_plain(
            first_parts[0], second_parts[0], spread, channels
        )
    return (
        output.reshape(inputs.shape),
        grad_inputs.reshape(inputs.shape),
        grad_embedding,
        grad_gains,
        grad_biases,
        first_grad.reshape(-1),
        second_grad.reshape(-1),
        qkv_grad.reshape(-1),
        ada_grad.reshape(-1),
        proj_grad.reshape(-1),
    )


def gather_plain(flats, embedding, spread, channels):
    heads = lax.axis_size("head")

    def columns(flat, groups):
        blocks = flat.astype(BF16).reshape(-1, groups, LANES)
        return blocks

    def own_columns(blocks):
        got = lax.all_to_all(blocks, "head", split_axis=1, concat_axis=0, tiled=True)
        return lax.all_gather(got[:, 0], "dp", axis=0, tiled=True)

    first, second = (own_columns(columns(flats[i], heads).reshape(-1, heads, 1, LANES))[:, 0] for i in (0, 1))
    qkv = columns(flats[2], 12).reshape(-1, heads, 2, 3, HD)
    qkv = jnp.swapaxes(qkv, 2, 3).reshape(-1, heads, 3, LANES)
    qkv = jnp.swapaxes(own_columns(qkv), 0, 1).reshape(-1, LANES)
    ada = columns(flats[3], 8).reshape(-1, 2, heads, LANES)
    ada = jnp.swapaxes(own_columns(jnp.swapaxes(ada, 1, 2)), 0, 1).reshape(-1, LANES)
    proj = lax.ppermute(flats[4].astype(BF16), ("dp", "head"), spread)
    proj = lax.all_gather(proj, "dp", axis=0, tiled=True).reshape(-1, channels // LANES, LANES)
    proj = jnp.swapaxes(proj, 0, 1).reshape(-1, LANES)
    embs = lax.all_gather(embedding, "dp", axis=0, tiled=True).astype(F32)
    embs = embs.reshape(embs.shape[0], -1, flats[3].shape[0] // 8)
    embs = lax.dynamic_index_in_dim(
        embs, lax.axis_index("dp") * heads + lax.axis_index("head"), 1, False
    )
    first_piece = jnp.concatenate([first, ada])
    second_piece = jnp.concatenate([second, qkv, proj])
    return (
        [first_piece],
        ((0, 1, 9 * channels), (9 * channels, 2, ada.shape[0] // 2)),
        [second_piece],
        (
            (0, 1, 9 * channels),
            (9 * channels, 3, channels),
            (12 * channels, channels // LANES, LANES),
        ),
        embs,
    )


def scatter_plain(first, second, spread, channels):
    heads = lax.axis_size("head")

    def rows_of(grad):
        part = lax.psum_scatter(grad, "dp", scatter_dimension=0, tiled=True)
        return lax.all_to_all(part[:, None], "head", split_axis=0, concat_axis=1, tiled=True)

    def conv(grad):
        return rows_of(grad[:, None])

    qkv = jnp.swapaxes(second[9 * channels : 12 * channels].reshape(3, channels, LANES), 0, 1)
    qkv = rows_of(qkv).reshape(-1, heads, 3, 2, HD)
    qkv = jnp.swapaxes(qkv, 2, 3)
    proj = jnp.swapaxes(second[12 * channels :].reshape(-1, LANES, LANES), 0, 1)
    proj = lax.psum_scatter(proj, "dp", scatter_dimension=0, tiled=True)
    proj = lax.ppermute(proj, ("dp", "head"), [(j, i) for i, j in spread])
    return (conv(first), conv(second[: 9 * channels]), qkv, proj)


def solution(mesh):
    flat = P(("dp", "head"))
    image = P("dp", "head", None, None)
    return jax.shard_map(
        body,
        mesh=mesh,
        in_specs=(image, P("dp", None), P("dp", None), image, P(), P(), flat, flat, flat, flat, flat),
        out_specs=(image, image, P("dp", None), P(), P(), flat, flat, flat, flat, flat),
        check_vma=False,
    )
```

```python
import functools
import math

import jax
import jax.numpy as jnp
from jax import lax
from jax.experimental import pallas as pl
from jax.experimental.pallas import tpu as pltpu
from jax.sharding import PartitionSpec as P

HD = 64
PROJ_PARTS = 2
MARK = 640
GROUPS = 32
EPS = 1e-05
MASKED = -1e30
LANES = 128
F32 = jnp.float32
BF16 = jnp.bfloat16
VMEM_SPEC = pl.BlockSpec(memory_space=pltpu.VMEM)
SMEM_SPEC = pl.BlockSpec(memory_space=pltpu.SMEM)


def sds(shape, dtype):
    return jax.ShapeDtypeStruct(shape, dtype)


class Far:
    def __init__(self, array, held=True, pinned=False):
        self.array = pltpu.with_memory_space_constraint(array, pltpu.HBM) if pinned else array
        self.held = held


class Fetch:
    def __init__(self, source, ref, sem):
        self.copy = pltpu.make_async_copy(source, ref, sem)
        self.ref = ref
        self.copy.start()

    def get(self):
        self.copy.wait()
        return self.ref


class Store:
    def __init__(self, dest, ref, sem):
        self.dest = dest
        self.ref = ref
        self.sem = sem
        self.copy = None

    def send(self, source=None):
        self.copy = pltpu.make_async_copy(self.ref if source is None else source, self.dest, self.sem)
        self.copy.start()


def call(kernel, outs, args, scratch=(), us=1.0, vmem=24, after=()):
    scalars = args[0] is not None
    args = list(args) if scalars else list(args[1:])
    arrays = [arg.array if isinstance(arg, Far) else arg for arg in args]
    results = [out.array if isinstance(out, Far) else out for out in outs]
    far_in = [isinstance(arg, Far) for arg in args]
    far_out = [isinstance(out, Far) for out in outs]
    held = [
        pltpu.VMEM(x.array.shape, x.array.dtype)
        for x in list(args) + list(outs)
        if isinstance(x, Far) and x.held
    ]
    copies = sum(far_in) + sum(far_out)

    def run(*refs):
        ins = refs[: len(args)]
        begin = len(args) + len(after)
        dests = refs[begin : begin + len(outs)]
        begin += len(outs)
        buffers = iter(refs[begin : begin + len(held)])
        begin += len(held)
        sems = refs[begin] if copies else None
        rest = refs[begin + (1 if copies else 0) :]
        count = 0
        given = []
        for ref, far in zip(ins, far_in):
            if far:
                ref = Fetch(ref, next(buffers), sems.at[count])
                count += 1
            given.append(ref)
        stores = []
        for ref, out in zip(dests, outs):
            if isinstance(out, Far):
                ref = Store(ref, next(buffers) if out.held else None, sems.at[count])
                stores.append(ref)
                count += 1
            given.append(ref)
        kernel(*([] if scalars else [None]), *given, *rest)
        for store in stores:
            store.copy.wait()

    hbm = pl.BlockSpec(memory_space=pltpu.HBM)
    anywhere = pl.BlockSpec(memory_space=pl.ANY)
    return pl.pallas_call(
        run,
        out_shape=tuple(results),
        in_specs=[
            hbm if far else SMEM_SPEC if scalars and i == 0 else VMEM_SPEC
            for i, far in enumerate(far_in)
        ]
        + [anywhere for _ in after],
        out_specs=tuple(hbm if far else VMEM_SPEC for far in far_out),
        scratch_shapes=held
        + ([pltpu.SemaphoreType.DMA((copies,))] if copies else [])
        + list(scratch),
        compiler_params=pltpu.CompilerParams(vmem_limit_bytes=vmem * 1024 * 1024),
        cost_estimate=pl.CostEstimate(
            flops=int(3e7 * us),
            bytes_accessed=1024,
            transcendentals=0,
        ),
    )(*arrays, *after)


def following(value, *earlier):
    return lax.optimization_barrier((value, *earlier))[0]


def hop(value, axis, bit):
    count = lax.axis_size(axis)
    return lax.ppermute(value, axis, [(i, i ^ bit) for i in range(count)])


def head_gather(block, *earlier):
    far = hop(block, "head", 2)
    near = hop(block, "head", 1)
    return (block, near, far, hop(following(far, *earlier) if earlier else far, "head", 1))


def head_exchange(near_block, far_pair, *earlier):
    far = hop(far_pair, "head", 2)
    near = hop(near_block, "head", 1)
    return (near, far, hop(following(far, *earlier) if earlier else far, "head", 1))


def add_kernel(ext, first, second, out):
    out[...] = (first[...].astype(F32) + second[...].astype(F32)).astype(out.dtype)


def head_reduce(ext, blocks, after=()):
    kept, near_block, far_block, corner = blocks
    corner = hop(corner, "head", 1)
    (far_block,) = call(
        add_kernel, [sds(far_block.shape, BF16)], [None, far_block, corner], us=0.7, after=after
    )
    return ((kept, hop(near_block, "head", 1), hop(far_block, "head", 2)), [far_block])


def mm(left, right, left_dim, right_dim):
    return lax.dot_general(
        left, right, (((left_dim,), (right_dim,)), ((), ())), preferred_element_type=F32
    )


def lane_block(index):
    return pl.ds(pl.multiple_of(index * LANES, LANES), LANES)


def row_block(index, rows):
    return pl.ds(pl.multiple_of(index * rows, rows), rows)


def pixel_place(rows, lanes, cols, start=0):
    pixel = lax.broadcasted_iota(jnp.int32, (rows, lanes), 0) + start
    shift = cols.bit_length() - 1
    return (lax.shift_right_logical(pixel, shift), lax.bitwise_and(pixel, cols - 1))


def valid_of(ext, rows, lanes, cols, start=0):
    place_row, place_col = pixel_place(rows, lanes, cols, start)
    inside = jnp.logical_and(place_row < ext[0, 0], place_col < ext[0, 1])
    return jnp.where(inside, 1.0, 0.0).astype(F32)


def group_total(first, second, width):
    lanes = first.shape[-1]
    pick = lax.broadcasted_iota(jnp.int32, (8, lanes), 0)
    both = jnp.where(pick == 0, first, jnp.where(pick == 1, second, 0.0))
    shift = width.bit_length() - 1
    left = lax.shift_right_logical(lax.broadcasted_iota(jnp.int32, (lanes, lanes), 0), shift)
    right = lax.shift_right_logical(lax.broadcasted_iota(jnp.int32, (lanes, lanes), 1), shift)
    same = jnp.where(left == right, 1.0, 0.0).astype(F32)
    total = lax.dot_general(
        both,
        same,
        (((1,), (0,)), ((), ())),
        precision=lax.Precision.HIGHEST,
        preferred_element_type=F32,
    )
    return (total[0:1], total[1:2])


def pixel_count(ext, width):
    return (ext[0, 0] * ext[0, 1] * width).astype(F32)


def col_sum(value):
    return jnp.sum(value, axis=0, keepdims=True)


def head_rank():
    return lax.axis_index("head")


def norm_stats(value, valid, count, width):
    masked = value * valid
    total, square = group_total(col_sum(masked), col_sum(masked * value), width)
    center = total / count
    return (center, lax.rsqrt(square / count - center * center + EPS))


def norm_back(grad, normed, inverse, valid, count, width):
    first, second = group_total(col_sum(grad), col_sum(grad * normed), width)
    return (grad - valid * ((first + normed * second) * (1.0 / count))) * inverse


def silu_grad(value):
    gate = jax.nn.sigmoid(value)
    return gate * (1.0 + value * (1.0 - gate))


def place_pieces(dest, pieces, start, groups, rows):
    for k, piece in enumerate(pieces):
        part = lax.axis_index("dp") ^ k if len(pieces) > 1 else 0
        for group in range(groups):
            begin = start + group * rows
            dest[group, pl.ds(pl.multiple_of(part * rows, rows), rows), :] = piece[
                begin : begin + rows, :
            ]


def taps_side_by_side(flat, wide):
    channels = wide.shape[0]
    for tap in range(9):
        wide[:, tap * LANES : (tap + 1) * LANES] = flat[0, tap * channels : (tap + 1) * channels, :]


def conv_taps(act, wide, taps, cols):
    pixels = act.shape[0]
    lanes = wide.shape[1]
    taps[0:cols, :] = jnp.zeros((cols, lanes), F32)
    taps[pixels + cols :, :] = jnp.zeros((cols, lanes), F32)
    step = 256

    def one(i, carry):
        begin = pl.multiple_of(i * step, step)
        taps[pl.ds(pl.multiple_of(begin + cols, cols), step), :] = mm(
            act[pl.ds(begin, step), :], wide[...], 1, 0
        )
        return carry

    lax.fori_loop(0, pixels // step, one, 0)


def conv_sum(taps, begin, rows, cols):
    def column(side):
        return sum(
            taps[
                pl.ds(pl.multiple_of(begin + up * cols, cols), rows),
                (up * 3 + side) * LANES : (up * 3 + side + 1) * LANES,
            ]
            for up in range(3)
        )

    place_col = pixel_place(rows, LANES, cols)[1]
    left = jnp.where(place_col > 0, pltpu.roll(column(0), 1, 0), 0.0)
    right = jnp.where(place_col < cols - 1, pltpu.roll(column(2), rows - 1, 0), 0.0)
    return column(1) + left + right


def shifted_grads(grad, dest, cols):
    pixels = grad.shape[0]
    place_col = pixel_place(pixels, LANES, cols)[1]
    sides = (
        jnp.where(place_col < cols - 1, pltpu.roll(grad, pixels - 1, 0), 0.0),
        grad,
        jnp.where(place_col > 0, pltpu.roll(grad, 1, 0), 0.0),
    )
    blank = jnp.zeros((cols, LANES), BF16)
    for side, value in enumerate(sides):
        low = value.astype(BF16)
        for up in range(3):
            lanes = slice((up * 3 + side) * LANES, (up * 3 + side + 1) * LANES)
            if up == 0:
                dest[0 : pixels - cols, lanes] = low[cols:, :]
                dest[pixels - cols :, lanes] = blank
            elif up == 1:
                dest[:, lanes] = low
            else:
                dest[cols:, lanes] = low[0 : pixels - cols, :]
                dest[0:cols, lanes] = blank


def partial_sums(left, right, whole, outs):
    pixels = left.shape[0]
    step = 256

    def one(i, carry):
        rows = pl.ds(pl.multiple_of(i * step, step), step)
        whole[rows, :] = mm(left[rows, :], right[...], 1, 1)
        return carry

    lax.fori_loop(0, pixels // step, one, 0)
    rank = head_rank()
    for k, out in enumerate(outs):
        out[...] = whole[:, lane_block(rank ^ k)].astype(out.dtype)


def weights_out_kernel(ext, *refs):
    first, second, qkv, ada, proj = refs[0:5]
    kept, near, pair, pj = refs[5:]
    rank = head_rank()
    low_half = lax.broadcasted_iota(jnp.int32, (qkv.ref.shape[0] // 12, LANES), 1) < HD
    first, second, qkv, ada, proj = (x.get() for x in (first, second, qkv, ada, proj))

    def strided(ref, begin, stride):
        return ref[pl.ds(begin, ref.shape[0] // stride, stride=stride), :]

    def put(dest, begin, value):
        rows = value.shape[0]
        dest[begin : begin + rows, :] = value.astype(BF16)
        return begin + rows

    at = 0
    for g in range(4):
        at = put(pj, at, strided(proj, g, 4))
    for k, dest in enumerate((kept, near, pair.at[0], pair.at[1])):
        peer = rank ^ k
        at = put(dest, 0, strided(first, peer, 4))
        for side in range(2):
            at = put(dest, at, strided(ada, 4 * side + peer, 8))
        at = put(dest, at, strided(second, peer, 4))
        part = [strided(qkv, peer * 3 + g, 12) for g in range(3)]
        at = put(dest, at, jnp.where(low_half, part[0], part[1]))
        at = put(dest, at, pltpu.roll(jnp.where(low_half, part[2], part[0]), HD, 1))
        put(dest, at, jnp.where(low_half, part[1], part[2]))


def join_blocks(dest, blocks, source, segments):
    rank = head_rank()
    for k, block in enumerate(blocks):
        at, begin = (source, 0)
        for rows in segments:
            place = pl.ds(pl.multiple_of(begin + (rank ^ k) * rows, 16), rows)
            dest[place, :] = block[at : at + rows, :]
            at += rows
            begin += 4 * rows
    return 4 * sum(segments)


def first_piece_kernel(ext, kept, near, far, corner, emb, proj, piece, line, *, segments):
    at = join_blocks(piece, (kept, near, far.at[0], corner.at[1]), 0, segments)
    emb = emb.get()
    line[...] = jnp.zeros(line.shape, F32)
    for j in range(emb.shape[1] // LANES):
        line[j : j + 1, :] = emb[0:1, j * LANES : (j + 1) * LANES].astype(F32)
    piece[at : at + 16, :] = line[...].astype(BF16)
    piece[at + 16 :, :] = proj[...]


def second_piece_kernel(ext, kept, near, far, corner, piece, *, source, segments):
    join_blocks(piece, (kept, near, far.at[0], corner.at[1]), source, segments)


def dp_straight(piece):
    return [piece] + [hop(piece, "dp", k) for k in (2, 4, 6)]


def dp_beside(straight, *earlier):
    own, two, four, six = straight
    near = [hop(value, "dp", 1) for value in (own, two, six)]
    near.insert(2, hop(following(four, *near, *earlier) if earlier else four, "dp", 1))
    return [value for pair in zip(straight, near) for value in pair]


def norm_first_kernel(ext, gains, biases, *refs, cols, width):
    blocks = refs[0:4]
    act, own_out, stats, held = refs[4:]
    own = own_out.ref
    rank = head_rank()
    rows, channels = blocks[0].shape
    count = pixel_count(ext, width)
    total = jnp.zeros((1, channels), F32)
    square = jnp.zeros((1, channels), F32)
    for k, block in enumerate(blocks):
        own[row_block(rank ^ k, rows), :] = block[:, lane_block(rank)]
    own_out.send()
    for k, block in enumerate(blocks):
        value = block[...].astype(F32)
        masked = value * valid_of(ext, rows, channels, cols, (rank ^ k) * rows)
        total = total + col_sum(masked)
        square = square + col_sum(masked * value)
    total, square = group_total(total, square, width)
    center = total / count
    inverse = lax.rsqrt(square / count - center * center + EPS)
    held[0:1, :] = center
    held[1:2, :] = inverse
    gain, bias = (gains.get()[0:1, :], biases.get()[0:1, :])
    for k, block in enumerate(blocks):
        peer = rank ^ k
        pre = (block[...].astype(F32) - center) * inverse * gain + bias
        valid = valid_of(ext, rows, channels, cols, peer * rows)
        act[row_block(peer, rows), :] = (pre * jax.nn.sigmoid(pre) * valid).astype(BF16)
    stats[...] = held[:, lane_block(rank)]


def conv_first_kernel(ext, biases, act, emb, *refs, cols, width, count_pieces, segments, emb_at):
    pieces = refs[0:count_pieces]
    act_out, normed_out, aux, wide_out, ada_out, act_far = refs[count_pieces : count_pieces + 6]
    w_proj = refs[count_pieces + 6 : -4 if emb_at is None else -5]
    flat, taps, hidden, proj = refs[-4:]
    rank = head_rank()
    pixels = act.shape[0]
    act_far.send(act)
    place_pieces(flat, pieces, *segments[0])
    wide = wide_out.ref
    taps_side_by_side(flat, wide)
    wide_out.send()
    ada = ada_out.ref
    place_pieces(ada, pieces, *segments[1])
    ada_out.send()
    place_pieces(proj, pieces, *segments[2])
    if len(w_proj) == 1:
        for g in range(proj.shape[0]):
            w_proj[0][:, g * LANES : (g + 1) * LANES] = proj[g]
    else:
        kept, near, pair = w_proj
        for k, dest in enumerate((kept, near, pair.at[0], pair.at[1])):
            for g in range(proj.shape[0]):
                dest[g] = proj[g, row_block(rank ^ k, dest.shape[1]), :]
    if emb_at is not None:
        table = refs[-5]
        place = lax.axis_index("dp")
        table[...] = jnp.zeros(table.shape, F32)
        for k, piece in enumerate(pieces):
            lines = piece[emb_at : emb_at + 16, :].astype(F32)
            mine = lax.broadcasted_iota(jnp.int32, lines.shape, 0) == place
            table[pl.ds(place ^ k, 1), :] = col_sum(jnp.where(mine, lines, 0.0))
    conv_taps(act, wide, taps, cols)
    biases = biases.get()
    bias = biases[1:2, lane_block(rank)]
    step = 256
    for i in range(pixels // step):
        hidden[i * step : (i + 1) * step, :] = conv_sum(taps, i * step, step, cols) + bias
    value = hidden[...]
    valid = valid_of(ext, pixels, LANES, cols)
    center, inverse = norm_stats(value, valid, pixel_count(ext, width), width)
    normed = (value - center) * inverse
    normed_out.ref[...] = normed
    normed_out.send()
    emb_value = emb.get()[...].astype(F32)
    emb_act = (emb_value * jax.nn.sigmoid(emb_value)).astype(BF16).astype(F32)
    mods = []
    for side in range(2):
        mod = biases[2 + side : 3 + side, lane_block(rank)]
        for j in range(emb_act.shape[1] // LANES):
            lanes = slice(j * LANES, (j + 1) * LANES)
            row = jnp.broadcast_to(emb_act[:, lanes], (16, LANES)).astype(BF16)
            mod = mod + mm(row, ada[side, lanes, :], 1, 0)[0:1]
        mods.append(mod)
    pre = normed * (1.0 + mods[0]) + mods[1]
    act_out[...] = (pre * jax.nn.sigmoid(pre) * valid).astype(BF16)
    aux[...] = jnp.zeros(aux.shape, F32)
    aux[0:1, :] = inverse
    aux[1:2, :] = mods[0]
    aux[2:3, :] = mods[1]


def conv_second_kernel(ext, gains, biases, own, *refs, cols, width, count_pieces, segments):
    blocks = refs[0:4]
    pieces = refs[4 : 4 + count_pieces]
    attn_in, act_out, residual_out, normed_out, aux, wide_out, w_qkv = refs[4 + count_pieces : -3]
    flat, qkv, taps = refs[-3:]
    rank = head_rank()
    act, wide, residual = (act_out.ref, wide_out.ref, residual_out.ref)
    pixels = act.shape[0]
    for k, block in enumerate(blocks):
        act[:, lane_block(rank ^ k)] = block[...]
    act_out.send()
    place_pieces(flat, pieces, *segments[0])
    taps_side_by_side(flat, wide)
    wide_out.send()
    place_pieces(qkv, pieces, *segments[1])
    for g in range(3):
        w_qkv[:, g * LANES : (g + 1) * LANES] = qkv[g]
    conv_taps(act, wide, taps, cols)
    gains, biases, own = (gains.get(), biases.get(), own.get())
    bias = biases[4:5, lane_block(rank)]
    step = 256
    for i in range(pixels // step):
        rows = slice(i * step, (i + 1) * step)
        third = conv_sum(taps, i * step, step, cols) + bias
        valid = valid_of(ext, step, LANES, cols, i * step)
        residual[rows, :] = own[rows, :].astype(F32) + valid * third
    residual_out.send()
    value = residual[...]
    valid = valid_of(ext, pixels, LANES, cols)
    center, inverse = norm_stats(value, valid, pixel_count(ext, width), width)
    normed = (value - center) * inverse
    normed_out.ref[...] = normed
    normed_out.send()
    attn_in[...] = (
        normed * gains[1:2, lane_block(rank)] + biases[5:6, lane_block(rank)]
    ).astype(BF16)
    aux[...] = jnp.broadcast_to(inverse, aux.shape)


def cotangent_kernel(ext, *refs):
    cots = refs[0:4]
    full_out, own_out, att, att_t, rows_weight = refs[-5:]
    rank = head_rank()
    rows = cots[0].shape[0]
    for k, cot in enumerate(cots):
        at = row_block(rank ^ k, rows)
        full_out.ref[at, :] = cot[...]
        own_out.ref[at, :] = cot[:, lane_block(rank)]
    full_out.send()
    own_out.send()
    weights = refs[4:-5]
    if len(weights) == 1:
        rows_weight[...] = weights[0][...]
    else:
        kept, near, far, corner = weights
        count = len(cots)
        size = LANES // (count * PROJ_PARTS)
        for k, block in enumerate((kept, near, far.at[0], corner.at[1])):
            for part in range(PROJ_PARTS):
                at = pl.ds(pl.multiple_of((part * count + (rank ^ k)) * size, 16), size)
                for g in range(block.shape[0]):
                    lanes = slice(g * LANES, (g + 1) * LANES)
                    rows_weight[at, lanes] = block[g, part * size : (part + 1) * size, :]
    for i in range(4):
        at = slice(i * rows, (i + 1) * rows)
        grad = mm(full_out.ref[at, :], rows_weight[...], 1, 1).astype(BF16)
        att[at, :] = grad
        att_t[:, at] = grad.astype(F32).T


def attention_kernel(ext, *refs, cols):
    blocks = refs[0:4]
    wide, cot_att, cot_att_t = refs[4:7]
    outs = refs[7:11]
    full_out, grads_out, attended_out = refs[11:14]
    qkv, keys_t, values_t, grad_kv, whole = refs[14:]
    attn_full, grads, attended = (full_out.ref, grads_out.ref, attended_out.ref)
    rank = head_rank()
    pixels = attn_full.shape[0]
    scale = 1.0 / math.sqrt(HD)
    for k in range(4):
        attn_full[:, lane_block(rank ^ k)] = blocks[k][...]
    full_out.send()
    step = 256

    def project(i, carry):
        at = pl.ds(pl.multiple_of(i * step, step), step)
        qkv[at, :] = mm(attn_full[at, :], wide[...], 1, 0).astype(BF16)
        return carry

    lax.fori_loop(0, pixels // step, project, 0)
    for i in range(pixels // step):
        at = slice(i * step, (i + 1) * step)
        keys_t[:, at] = qkv[at, LANES : 2 * LANES].astype(F32).T.astype(BF16)
        values_t[:, at] = qkv[at, 2 * LANES :].astype(F32).T.astype(BF16)
    grad_kv[...] = jnp.zeros(grad_kv.shape, F32)
    span = 256
    lane = lax.broadcasted_iota(jnp.int32, (span, LANES), 1)
    sublane_all = lax.broadcasted_iota(jnp.int32, (LANES, pixels), 0)

    def attend(i, carry):
        at = pl.ds(pl.multiple_of(i * span, span), span)
        queries = qkv[at, 0:LANES]
        cot_rows = cot_att[at, :]
        cot_cols = cot_att_t[:, at]
        key_row, key_col = pixel_place(pixels, span, cols)
        key_valid = jnp.logical_and(key_row < ext[0, 0], key_col < ext[0, 1])
        att_sum = jnp.zeros((LANES, span), F32)
        query_sum = jnp.zeros((LANES, span), F32)
        for h in range(LANES // HD):
            mine = lax.shift_right_logical(lane, 6) == h
            mine_all = lax.shift_right_logical(sublane_all, 6) == h
            query = jnp.where(mine, queries, jnp.zeros_like(queries))
            cot = jnp.where(mine, cot_rows, jnp.zeros_like(cot_rows))
            scores = mm(qkv[:, LANES : 2 * LANES], query, 1, 1) * scale
            scores = jnp.where(key_valid, scores, MASKED)
            top = jnp.max(scores, axis=0, keepdims=True)
            expo = jnp.exp(scores - top)
            probs = expo * (1.0 / col_sum(expo))
            probs_low = probs.astype(BF16)
            value_t = jnp.where(mine_all, values_t[...], jnp.zeros_like(values_t[...]))
            att = mm(value_t, probs_low, 1, 0)
            att_sum = att_sum + att
            row_dot = col_sum(att * cot_cols)
            grad_kv[:, LANES:] += mm(probs_low, cot, 1, 0)
            grad_probs = mm(qkv[:, 2 * LANES :], cot, 1, 1)
            grad_scores = (probs * (grad_probs - row_dot)).astype(BF16)
            grad_kv[:, 0:LANES] += mm(grad_scores, query, 1, 0)
            key_t = jnp.where(mine_all, keys_t[...], jnp.zeros_like(keys_t[...]))
            query_sum = query_sum + mm(key_t, grad_scores, 1, 0)
        attended[at, :] = att_sum.T.astype(BF16)
        grads[at, 0:LANES] = (query_sum.T * scale).astype(BF16)
        return carry

    lax.fori_loop(0, pixels // span, attend, 0)
    attended_out.send()
    grads[:, LANES : 2 * LANES] = (grad_kv[:, 0:LANES] * scale).astype(BF16)
    grads[:, 2 * LANES :] = grad_kv[:, LANES:].astype(BF16)
    grads_out.send()
    partial_sums(grads, wide, whole, outs)


def out_partial_kernel(ext, biases, attended, rows_weight, residual, cot, *refs):
    outs = refs[0:4]
    grads = refs[4:-1]
    whole = refs[-1]
    rank = head_rank()
    rows = outs[0].shape[0]
    attended = attended.get()
    for i in range(4):
        at = slice(i * rows, (i + 1) * rows)
        whole[at, :] = mm(attended[at, :], rows_weight[...], 1, 0)
    bias = biases.get()[6:7, lane_block(rank)]
    whole[:, lane_block(rank)] += residual.get()[...] + bias
    for k, out in enumerate(outs):
        out[...] = whole[row_block(rank ^ k, rows), :].astype(out.dtype)
    whole[0:LANES, :] = mm(attended[...], cot.get()[...], 0, 0)
    if len(grads) == 1:
        for g in range(grads[0].shape[0]):
            grads[0][g] = whole[0:LANES, g * LANES : (g + 1) * LANES]
    else:
        kept, near, pair = grads
        count = len(outs)
        size = LANES // (count * PROJ_PARTS)
        for k, dest in enumerate((kept, near, pair.at[0], pair.at[1])):
            for part in range(PROJ_PARTS):
                at = row_block(part * count + (rank ^ k), size)
                for g in range(dest.shape[0]):
                    dest[g, part * size : (part + 1) * size, :] = whole[
                        at, g * LANES : (g + 1) * LANES
                    ].astype(BF16)


def sum_kernel(ext, first, second, third, out):
    out[...] = (first[...] + second[...].astype(F32) + third[...].astype(F32)).astype(out.dtype)


def norm_third_back_kernel(ext, gains, kept, near, far, normed, inverse, cot, wide, *refs, cols, width):
    outs = refs[0:4]
    grad_res, third_out, sums, shifted, whole = refs[4:]
    rank = head_rank()
    pixels = kept.shape[0]
    grad = kept[...] + near[...].astype(F32) + far[...].astype(F32)
    normed, gains, cot = (normed.get()[...], gains.get(), cot.get())
    valid = valid_of(ext, pixels, LANES, cols)
    back = norm_back(
        grad * gains[1:2, lane_block(rank)], normed, inverse[0:1, :], valid,
        pixel_count(ext, width), width,
    )
    cot_value = cot[...].astype(F32)
    residual = cot_value + back
    grad_res.ref[...] = residual
    grad_res.send()
    third = (valid * residual).astype(BF16)
    third_out[...] = third
    third = third.astype(F32)
    shifted_grads(third, shifted, cols)
    sums[...] = jnp.zeros(sums.shape, F32)
    sums[0:1, :] = col_sum(grad * normed)
    sums[1:2, :] = col_sum(grad)
    sums[2:3, :] = col_sum(third)
    sums[3:4, :] = col_sum(cot_value)
    partial_sums(shifted, wide.get(), whole, outs)


def norm_second_back_kernel(ext, kept, near, far, normed, aux, wide, *refs, cols, width):
    outs = refs[0:4]
    first_out, sums, shifted, whole = refs[4:]
    pixels = kept.shape[0]
    grad_act = kept[...] + near[...].astype(F32) + far[...].astype(F32)
    normed = normed.get()[...]
    valid = valid_of(ext, pixels, LANES, cols)
    inverse, scale, shift = (aux[0:1, :], aux[1:2, :], aux[2:3, :])
    grad_pre = grad_act * valid * silu_grad(normed * (1.0 + scale) + shift)
    back = norm_back(
        grad_pre * (1.0 + scale), normed, inverse, valid, pixel_count(ext, width), width
    )
    first = back.astype(BF16)
    first_out[...] = first
    first = first.astype(F32)
    shifted_grads(first, shifted, cols)
    sums[...] = jnp.zeros(sums.shape, F32)
    sums[0:1, :] = col_sum(grad_pre * normed).astype(BF16).astype(F32)
    sums[1:2, :] = col_sum(grad_pre).astype(BF16).astype(F32)
    sums[2:3, :] = col_sum(first)
    partial_sums(shifted, wide.get(), whole, outs)


def norm_first_back_kernel(
    ext, gains, biases, kept, near, far, own, stats, grad_res, sums_third, sums_second, *refs,
    cols, width,
):
    out_kept, out_near, out_pair, table, held = refs
    rank = head_rank()
    pixels = kept.shape[0]
    rows = out_kept.shape[0]
    grad_act = kept[...] + near[...].astype(F32) + far[...].astype(F32)
    valid = valid_of(ext, pixels, LANES, cols)
    center, inverse = (stats[0:1, :], stats[1:2, :])
    normed = (own.get()[...].astype(F32) - center) * inverse
    gain = gains.get()[0:1, lane_block(rank)]
    bias = biases.get()[0:1, lane_block(rank)]
    grad_pre = grad_act * valid * silu_grad(normed * gain + bias)
    back = norm_back(grad_pre * gain, normed, inverse, valid, pixel_count(ext, width), width)
    held[...] = grad_res.get()[...] + back
    out_kept[...] = held[row_block(rank, rows), :]
    out_near[...] = held[row_block(rank ^ 1, rows), :].astype(BF16)
    for k in (2, 3):
        out_pair[k - 2] = held[row_block(rank ^ k, rows), :].astype(BF16)
    table[...] = jnp.zeros(table.shape, F32)
    table[0:1, :] = col_sum(grad_pre * normed)
    table[1:2, :] = sums_third[0:1, :]
    table[2:3, :] = col_sum(grad_pre)
    table[3:4, :] = sums_second[2:3, :]
    table[4:6, :] = sums_second[0:2, :]
    table[6:7, :] = sums_third[2:3, :]
    table[7:8, :] = sums_third[1:2, :]
    table[8:9, :] = sums_third[3:4, :]
    table[pl.ds(16 + 2 * lax.axis_index("dp"), 2), :] = sums_second[0:2, :]


def put_exact(dest, begin, value):
    rows = value.shape[0]
    high = value.astype(BF16)
    dest[begin : begin + rows, :] = high
    dest[begin + rows : begin + 2 * rows, :] = (value - high.astype(F32)).astype(BF16)


def get_exact(source, begin, rows):
    high = source[begin : begin + rows, :].astype(F32)
    return high + source[begin + rows : begin + 2 * rows, :].astype(F32)


def rows_join_kernel(ext, kept, near, far, corner, out):
    rank = head_rank()
    for k, block in enumerate((kept, near, far.at[0], corner.at[1])):
        out[:, lane_block(rank ^ k)] = block[...].astype(F32)


def taps_grad(act, shifted, flat):
    channels = act.shape[1]
    for i in range(channels // LANES):
        part = mm(act[:, i * LANES : (i + 1) * LANES], shifted[...], 0, 0)
        for tap in range(9):
            flat[0, tap * channels + i * LANES : tap * channels + (i + 1) * LANES, :] = part[
                :, tap * LANES : (tap + 1) * LANES
            ]


def dp_parts(dests, sources, dp_count):
    place = lax.axis_index("dp") if dp_count > 1 else 0
    for k, dest in enumerate(dests):
        at = 0
        for source in sources:
            size = source.shape[1] // dp_count
            for g in range(source.shape[0]):
                dest[at : at + size, :] = source[g, row_block(place ^ k, size), :].astype(dest.dtype)
                at += size


def second_grads_kernel(ext, third, act, attn, grads, *refs, cols, dp_count):
    grad_proj = refs[0 : 4 if dp_count > 1 else 1]
    dests = refs[len(grad_proj) : -4]
    shifted, flat, qkv, proj = refs[-4:]
    shifted_grads(third[...].astype(F32), shifted, cols)
    act = act.get()
    taps_grad(act, shifted, flat)
    attn, grads = (attn.get(), grads.get())
    part = mm(attn[...], grads[...], 0, 0)
    for g in range(3):
        qkv[g] = part[:, g * LANES : (g + 1) * LANES]
    if len(grad_proj) == 1:
        proj[...] = grad_proj[0][...]
    else:
        kept, near, far, corner = grad_proj
        rank = head_rank()
        for k, block in enumerate((kept, near, far.at[0], corner.at[1])):
            size = block.shape[1]
            for g in range(proj.shape[0]):
                proj[g, row_block(rank ^ k, size), :] = block[g].astype(F32)
    dp_parts(split_dests(dests), (flat, qkv, proj), dp_count)


def split_dests(dests):
    if len(dests) == 1:
        return dests
    own, two, four, six, first_pair, second_pair = dests
    return (
        own, second_pair.at[1], two, first_pair.at[0], four, second_pair.at[0], six, first_pair.at[1]
    )


def first_grads_kernel(ext, first, act, sums, ada, *refs, cols, dp_count):
    dests = refs[0:-3]
    emb_part, shifted, flat = refs[-3:]
    shifted_grads(first[...].astype(F32), shifted, cols)
    taps_grad(act.get(), shifted, flat)
    dp_parts(split_dests(dests), (flat,), dp_count)
    ada = ada.get()
    for j in range(emb_part.shape[0]):
        row = jnp.zeros((1, LANES), F32)
        for side in range(2):
            mod = jnp.broadcast_to(sums[side : side + 1, :], (16, LANES)).astype(BF16)
            row = row + mm(mod, ada[side, j * LANES : (j + 1) * LANES, :], 1, 1)[0:1]
        emb_part[j : j + 1, :] = row


def near_kernel(ext, other, two, six, out):
    size = two.shape[0]
    for k, mine in enumerate((two, six)):
        out[k, 0:size, :] = (mine[...].astype(F32) + other[k].astype(F32)).astype(BF16)


def near_table_kernel(ext, other, two, six, table, beside, out, total):
    size = two.shape[0]
    near_kernel(ext, other, two, six, out)
    total[...] = table[...] + beside[...]
    put_exact(out.at[0], size, total[...])
    out[1, size:, :] = jnp.zeros((out.shape[1] - size, LANES), BF16)


def far_kernel(ext, four, late, near, out):
    size = four.shape[0]
    value = four[...].astype(F32) + late[0].astype(F32) + near[1, 0:size, :].astype(F32)
    out[0:size, :] = value.astype(BF16)


def far_table_kernel(ext, four, late, near, table, out, total):
    size = four.shape[0]
    far_kernel(ext, four, late, near, out)
    total[...] = table[...] + get_exact(near.at[0], size, table.shape[0])
    put_exact(out, size, total[...])


def dp_pairs(parts):
    return (hop(parts[4], "dp", 1), hop(parts[5], "dp", 1))


def split_second_kernel(ext, own, late, straight, far, kept, near, pair, proj, held, *, rows_conv, rows_qkv):
    rank = head_rank()
    held[...] = own[...] + sum(
        part[...].astype(F32) for part in (late.at[1], straight.at[0], far)
    )
    for k, dest in enumerate((kept, near, pair.at[0], pair.at[1])):
        peer = rank ^ k
        dest[0:rows_conv, :] = held[row_block(peer, rows_conv), :].astype(dest.dtype)
        for g in range(3):
            begin = 4 * rows_conv + g * 4 * rows_qkv
            dest[rows_conv + g * rows_qkv : rows_conv + (g + 1) * rows_qkv, :] = held[
                pl.ds(pl.multiple_of(begin + peer * rows_qkv, 8), rows_qkv), :
            ].astype(dest.dtype)
    proj[...] = held[4 * rows_conv + 12 * rows_qkv :, :]


def split_first_kernel(
    ext, own, late, straight, far, table, emb_part, kept, near, pair, total, held, *, rows_conv
):
    rank = head_rank()
    size = held.shape[0]
    lines = table.shape[0]
    held[...] = own[...] + sum(
        part[0:size, :].astype(F32) for part in (late.at[1], straight.at[0], far)
    )
    total[0:lines, :] = table[...] + get_exact(far, size, lines)
    total[lines:, :] = emb_part[...]
    kept[...] = held[row_block(rank, rows_conv), :]
    for k, dest in enumerate((near, pair.at[0], pair.at[1])):
        dest[0:rows_conv, :] = held[row_block(rank ^ (k + 1), rows_conv), :].astype(BF16)
        put_exact(dest, rows_conv, total[...])


def join_second_kernel(ext, kept, near, far, corner, proj, conv_out, qkv_out, proj_out, *, rows_conv, rows_qkv):
    rank = head_rank()
    rows_proj = proj.shape[0] // 4
    low_half = lax.broadcasted_iota(jnp.int32, (rows_qkv, LANES), 1) < HD
    for k, block in enumerate((kept, near, far.at[0], corner.at[1])):
        peer = rank ^ k
        conv_out[pl.ds(peer, rows_conv, stride=4), :] = block[0:rows_conv, :].astype(F32)
        part = [
            block[rows_conv + g * rows_qkv : rows_conv + (g + 1) * rows_qkv, :].astype(F32)
            for g in range(3)
        ]
        keys = pltpu.roll(part[1], HD, 1)
        mixed = (
            jnp.where(low_half, part[0], keys),
            jnp.where(low_half, part[2], part[0]),
            jnp.where(low_half, keys, part[2]),
        )
        for g in range(3):
            qkv_out[pl.ds(peer * 3 + g, rows_qkv, stride=12), :] = mixed[g]
    for g in range(4):
        proj_out[pl.ds(g, rows_proj, stride=4), :] = proj[
            g * rows_proj : (g + 1) * rows_proj, :
        ].astype(F32)


def join_first_kernel(
    ext, kept, near, far, corner, total, embs, emb, conv_out, *refs, rows_conv
):
    rank = head_rank()
    outs, (mods, table, held, t1, t2, t3) = (refs[:4], refs[4:])
    blocks = (near, far.at[0], corner.at[1])
    conv_out[pl.ds(rank, rows_conv, stride=4), :] = kept[...]
    for k, (block, other) in enumerate(zip(blocks, (t1, t2, t3))):
        conv_out[pl.ds(rank ^ (k + 1), rows_conv, stride=4), :] = block[0:rows_conv, :].astype(F32)
        other[...] = get_exact(block, rows_conv, other.shape[0])
    small_grads_kernel(ext, embs, emb, total, t1, t2, t3, *outs, mods, table, held)


def small_grads_kernel(ext, embs, emb, t0, t1, t2, t3, gains_out, biases_out, ada_out, emb_out, mods, table, held):
    rank = head_rank()
    images = embs.shape[0]
    for k, block in enumerate((t0, t1, t2, t3)):
        table[:, lane_block(rank ^ k)] = block[0:16, :]
        for side in range(2):
            mods[:, lane_block(side * 4 + (rank ^ k))] = block[pl.ds(16 + side, images, stride=2), :]
    gains_out[...] = table[0:2, :]
    biases_out[...] = table[2:9, :]
    value = embs[...]
    part = mm((value * jax.nn.sigmoid(value)).astype(BF16), mods[...].astype(BF16), 0, 0)
    rows = ada_out.shape[0] // 8
    if part.shape[0] != rows:
        held[...] = part
        part = held[row_block(rank, rows), :]
    for g in range(8):
        ada_out[pl.ds(g, rows, stride=8), :] = part[:, g * LANES : (g + 1) * LANES]
    value = emb.get()[...].astype(F32)
    slope = silu_grad(value)
    begin = 16 + 2 * images
    for j in range(value.shape[1] // LANES):
        lanes = slice(j * LANES, (j + 1) * LANES)
        total = sum(block[begin + j : begin + j + 1, :] for block in (t0, t1, t2, t3))
        emb_out[:, lanes] = total * slope[:, lanes]


def body(
    inputs, embedding, extent, cotangent, gains, biases,
    conv_first, conv_second, qkv_master, ada_master, proj_master,
):
    heads = lax.axis_size("head")
    dps = lax.axis_size("dp")
    batch, row_count, cols, channels = inputs.shape
    rows = row_count * cols
    pixels = rows * heads
    width = channels // GROUPS
    emb_rows = embedding.shape[1] // LANES
    ext = extent
    direct = dps == 8
    flats = [
        master.reshape(-1, LANES)
        for master in (conv_first, conv_second, qkv_master, ada_master, proj_master)
    ]
    rows_conv = flats[0].shape[0] // 4
    rows_qkv = flats[2].shape[0] // 12
    rows_ada = flats[3].shape[0] // 8
    rows_proj = flats[4].shape[0] // 4
    far_gains, far_biases, far_emb = (Far(x, pinned=True) for x in (gains, biases, embedding))
    spread = [(i, (i % dps) * heads + i // dps) for i in range(dps * heads)]
    inputs_own = inputs.reshape(rows, channels)
    cot_own = cotangent.reshape(rows, channels)
    if direct:
        rows_a = rows_conv + 2 * rows_ada
        rows_b = rows_conv + 3 * rows_qkv
        rows_ab = rows_a + rows_b
        kept, near, pair, pj = call(
            weights_out_kernel,
            [
                sds((rows_ab, LANES), BF16), sds((rows_ab, LANES), BF16),
                sds((2, rows_ab, LANES), BF16), sds((4 * rows_proj, LANES), BF16),
            ],
            [None] + [Far(flat, pinned=True) for flat in flats],
        )
        rows_second = 4 * rows_conv + 12 * rows_qkv + 4 * rows_proj
        blocks = (kept, *head_exchange(near, pair))
        (first_piece,) = call(
            functools.partial(first_piece_kernel, segments=(rows_conv, rows_ada, rows_ada)),
            [sds((4 * rows_conv + 8 * rows_ada + 16 + 4 * rows_proj, LANES), BF16)],
            [None, *blocks, far_emb, pj],
            scratch=[pltpu.VMEM((16, LANES), F32)],
        )
        (second_piece,) = call(
            functools.partial(
                second_piece_kernel, source=rows_a, segments=(rows_conv,) + (rows_qkv,) * 3
            ),
            [sds((rows_second - 4 * rows_proj, LANES), BF16)],
            [None, *blocks],
        )
        first_straight = dp_straight(first_piece)
        inputs_sent = following(inputs_own, first_piece)
        second_straight = dp_straight(second_piece)
        proj_at = 4 * rows_conv + 8 * rows_ada + 16
        first_segments = (
            (0, 1, 4 * rows_conv),
            (4 * rows_conv, 2, 4 * rows_ada),
            (proj_at, 4, rows_proj),
        )
        second_segments = ((0, 1, 4 * rows_conv), (4 * rows_conv, 3, 4 * rows_qkv))
    else:
        first_pieces, first_segments, second_pieces, second_segments, embs = gather_plain(
            flats, embedding, spread, channels
        )
        inputs_sent = inputs_own

    blocks = head_gather(inputs_sent)
    act_first, own, stats_first = call(
        functools.partial(norm_first_kernel, cols=cols, width=width),
        [sds((pixels, channels), BF16), Far(sds((pixels, LANES), BF16)), sds((8, LANES), F32)],
        [ext, far_gains, far_biases, *blocks],
        scratch=[pltpu.VMEM((8, channels), F32)],
        us=2.0,
    )
    if direct:
        first_pieces = dp_beside(first_straight, first_piece)
    cots = head_gather(following(cot_own, blocks[2]))
    wide_shape = (channels, 9 * LANES)
    taps_scratch = pltpu.VMEM((pixels + 2 * cols, 9 * LANES), F32)
    flat_scratch = pltpu.VMEM((1, 9 * channels, LANES), BF16)
    n_pieces = len(first_pieces)
    groups = channels // LANES
    if direct:
        part = (groups, LANES // heads, LANES)
        proj_outs = [sds(part, BF16), sds(part, BF16), sds((2, *part), BF16)]
    else:
        proj_outs = [sds((LANES, channels), BF16)]
    first_outs = call(
        functools.partial(
            conv_first_kernel, cols=cols, width=width, count_pieces=n_pieces,
            segments=first_segments,
            emb_at=4 * rows_conv + 8 * rows_ada if direct else None,
        ),
        [
            sds((pixels, LANES), BF16), Far(sds((pixels, LANES), F32)), sds((8, LANES), F32),
            Far(sds(wide_shape, BF16)), Far(sds((2, emb_rows * LANES, LANES), BF16)),
            Far(sds((pixels, channels), BF16), held=False),
        ]
        + proj_outs
        + ([sds((dps, LANES), F32)] if direct else []),
        [ext, far_biases, act_first, far_emb, *first_pieces],
        scratch=[
            flat_scratch,
            taps_scratch,
            pltpu.VMEM((pixels, LANES), F32),
            pltpu.VMEM((groups, LANES, LANES), BF16),
        ],
        us=4.0,
    )
    act_second_own, normed_second, aux_second, wide_first, ada_full, act_first = first_outs[:6]
    w_proj = first_outs[6 : 6 + len(proj_outs)]
    if direct:
        embs = first_outs[-1]
        second_pieces = dp_beside(second_straight)
        w_proj = (w_proj[0], *head_exchange(*w_proj[1:]))
        mark = [hop(following(second_piece[:MARK], *second_pieces[1::2], *w_proj[1:]), "head", 1)]
        act_second_own = following(act_second_own, second_pieces[1])
    blocks = head_gather(act_second_own)
    attn_own, act_second, residual, normed_third, aux_third, wide_second, w_qkv = call(
        functools.partial(
            conv_second_kernel, cols=cols, width=width, count_pieces=n_pieces,
            segments=second_segments,
        ),
        [
            sds((pixels, LANES), BF16), Far(sds((pixels, channels), BF16)),
            Far(sds((pixels, LANES), F32)), Far(sds((pixels, LANES), F32)), sds((8, LANES), F32),
            Far(sds(wide_shape, BF16)), sds((channels, 3 * LANES), BF16),
        ],
        [ext, far_gains, far_biases, Far(own), *blocks, *second_pieces],
        scratch=[
            flat_scratch,
            pltpu.VMEM((3, channels, LANES), BF16),
            taps_scratch,
        ],
        us=4.0,
        after=mark if direct else (),
    )
    cot_full, cot_own, cot_att, cot_att_t, rows_weight = call(
        cotangent_kernel,
        [
            Far(sds((pixels, channels), BF16)), Far(sds((pixels, LANES), BF16)),
            sds((pixels, LANES), BF16), sds((LANES, pixels), F32), sds((LANES, channels), BF16),
        ],
        [None, *cots, *w_proj],
    )
    blocks = head_gather(attn_own, cot_att)
    whole_scratch = pltpu.VMEM((pixels, channels), F32)
    shifted_scratch = pltpu.VMEM((pixels, 9 * LANES), BF16)
    split_outs = [sds((pixels, LANES), F32)] + [sds((pixels, LANES), BF16)] * 3
    *parts, attn_full, grads_qkv, attended = call(
        functools.partial(attention_kernel, cols=cols),
        split_outs
        + [
            Far(sds((pixels, channels), BF16)), Far(sds((pixels, 3 * LANES), BF16)),
            Far(sds((pixels, LANES), BF16)),
        ],
        [ext, *blocks, w_qkv, cot_att, cot_att_t],
        scratch=[
            pltpu.VMEM((pixels, 3 * LANES), BF16),
            pltpu.VMEM((LANES, pixels), BF16),
            pltpu.VMEM((LANES, pixels), BF16),
            pltpu.VMEM((pixels, 2 * LANES), F32),
            whole_scratch,
        ],
        us=15.0,
    )
    parts, _ = head_reduce(ext, parts)
    grad_outs = proj_outs if direct else [sds((groups, LANES, LANES), F32)]
    out_all = call(
        out_partial_kernel,
        [sds((rows, channels), F32)] + [sds((rows, channels), BF16)] * 3 + grad_outs,
        [None, far_biases, Far(attended), rows_weight, Far(residual), Far(cot_full)],
        scratch=[whole_scratch],
        us=2.0,
    )
    out_parts, grad_proj = (out_all[:4], out_all[4:])
    if direct:
        grad_proj = (grad_proj[0], *head_exchange(*grad_proj[1:]))
    *parts, grad_res, third, sums_third = call(
        functools.partial(norm_third_back_kernel, cols=cols, width=width),
        split_outs
        + [Far(sds((pixels, LANES), F32)), sds((pixels, LANES), BF16), sds((8, LANES), F32)],
        [
            ext, far_gains, *parts, Far(normed_third), aux_third, Far(cot_own), Far(wide_second),
        ],
        scratch=[shifted_scratch, whole_scratch],
        us=150.0,
        after=out_parts[:1],
    )
    if direct:
        parts[3] = following(parts[3], *grad_proj[1:3])
    out_sums, _ = head_reduce(ext, out_parts)
    (output,) = call(sum_kernel, [sds((rows, channels), BF16)], [None, *out_sums])
    parts, sent = head_reduce(ext, parts)
    n_dests = dps if direct else 1

    def grad_outs(size):
        size = size // n_dests
        if not direct:
            return [sds((size, LANES), F32)]
        one = sds((size, LANES), BF16)
        return [sds((size, LANES), F32), one, one, one] + [sds((2, size, LANES), BF16)] * 2

    flat_grad = pltpu.VMEM((1, 9 * channels, LANES), F32)
    second_parts = call(
        functools.partial(second_grads_kernel, cols=cols, dp_count=n_dests),
        grad_outs(13 * channels),
        [None, third, Far(act_second), Far(attn_full), Far(grads_qkv), *grad_proj],
        scratch=[
            shifted_scratch,
            flat_grad,
            pltpu.VMEM((3, channels, LANES), F32),
            pltpu.VMEM((channels // LANES, LANES, LANES), F32),
        ],
        us=4.0,
        after=sent,
    )
    *parts, first, sums_second = call(
        functools.partial(norm_second_back_kernel, cols=cols, width=width),
        split_outs + [sds((pixels, LANES), BF16), sds((8, LANES), F32)],
        [ext, *parts, Far(normed_second), aux_second, Far(wide_first)],
        scratch=[shifted_scratch, whole_scratch],
        us=150.0,
        after=second_parts[:1],
    )
    if direct:
        second_pairs = dp_pairs(second_parts)
    parts, sent = head_reduce(ext, parts, second_pairs[:1] if direct else ())
    *first_parts, emb_part = call(
        functools.partial(first_grads_kernel, cols=cols, dp_count=n_dests),
        grad_outs(9 * channels) + [sds((emb_rows, LANES), F32)],
        [ext, first, Far(act_first), sums_second, Far(ada_full)],
        scratch=[shifted_scratch, flat_grad],
        us=3.0,
        after=sent,
    )
    table_rows = 16 + 2 * dps
    early = [emb_part]
    if direct:
        first_early, first_late = (hop(pair, "dp", 1) for pair in first_parts[4:6])
        (near_pair,) = call(
            near_kernel,
            [sds(second_parts[4].shape, BF16)],
            [None, second_pairs[0], second_parts[1], second_parts[3]],
            us=0.6,
            after=sent,
        )
        early += [near_pair, second_pairs[1]]
        second_near = hop(near_pair, "dp", 2)
    kept_rows, near, pair, table = call(
        functools.partial(norm_first_back_kernel, cols=cols, width=width),
        [
            sds((rows, LANES), F32), sds((rows, LANES), BF16), sds((2, rows, LANES), BF16),
            sds((table_rows, LANES), F32),
        ],
        [
            ext, far_gains, far_biases, *parts, Far(own), stats_first, Far(grad_res), sums_third,
            sums_second,
        ],
        scratch=[pltpu.VMEM((pixels, LANES), F32)],
        us=40.0,
        after=early,
    )
    small_outs = [
        sds(gains.shape, F32), sds(biases.shape, F32), sds(flats[3].shape, F32),
        sds(embedding.shape, F32),
    ]
    small_scratch = [
        pltpu.VMEM((dps, 8 * LANES), F32),
        pltpu.VMEM((16, channels), F32),
        pltpu.VMEM((LANES, 8 * LANES), F32),
    ]
    if direct:
        beside = hop(table, "dp", 1)
        (far_block,) = call(
            far_kernel,
            [sds(second_parts[2].shape, BF16)],
            [None, second_parts[2], second_pairs[1], second_near],
            us=0.6,
            after=[kept_rows],
        )
        second_left = [second_parts[0], second_pairs[1], second_near, hop(far_block, "dp", 4)]
        size = 4 * rows_conv + 2 * table_rows
        near_pair, table = call(
            near_table_kernel,
            [sds((2, size, LANES), BF16), sds(table.shape, F32)],
            [None, first_early, first_parts[1], first_parts[3], table, beside],
            us=0.6,
        )
        first_near = hop(near_pair, "dp", 2)
        far_block, table = call(
            far_table_kernel,
            [sds((size, LANES), BF16), sds(table.shape, F32)],
            [None, first_parts[2], first_late, first_near, table],
            us=0.6,
            after=[far_block],
        )
        first_left = [first_parts[0], first_late, first_near, hop(far_block, "dp", 4)]
    (grad_inputs,) = call(
        rows_join_kernel,
        [sds((rows, channels), F32)],
        [None, kept_rows, *head_exchange(near, pair)],
    )
    if direct:
        second_own, near, pair, pj = call(
            functools.partial(split_second_kernel, rows_conv=rows_conv, rows_qkv=rows_qkv),
            [
                sds((rows_b, LANES), F32), sds((rows_b, LANES), BF16),
                sds((2, rows_b, LANES), BF16), sds((4 * rows_proj, LANES), F32),
            ],
            [None, *second_left],
            scratch=[pltpu.VMEM((rows_second, LANES), F32)],
        )
        second_blocks = head_exchange(near, pair)
        second_grad, qkv_grad, proj_grad = call(
            functools.partial(join_second_kernel, rows_conv=rows_conv, rows_qkv=rows_qkv),
            [sds(flats[i].shape, F32) for i in (1, 2, 4)],
            [None, second_own, *second_blocks, pj],
        )
        lines = table_rows + emb_rows
        kept, near, pair, table = call(
            functools.partial(split_first_kernel, rows_conv=rows_conv),
            [
                sds((rows_conv, LANES), F32), sds((rows_conv + 2 * lines, LANES), BF16),
                sds((2, rows_conv + 2 * lines, LANES), BF16), sds((lines, LANES), F32),
            ],
            [None, *first_left, table, emb_part],
            scratch=[pltpu.VMEM((4 * rows_conv, LANES), F32)],
            after=second_blocks[:2],
        )
        first_blocks = head_exchange(near, pair, output, grad_inputs, second_grad)
        first_grad, grad_gains, grad_biases, ada_grad, grad_embedding = call(
            functools.partial(join_first_kernel, rows_conv=rows_conv),
            [sds(flats[0].shape, F32)] + small_outs,
            [None, kept, *first_blocks, table, embs, far_emb],
            scratch=small_scratch + [pltpu.VMEM((lines, LANES), F32)] * 3,
        )
    else:
        table = jnp.concatenate([lax.psum(table, "dp"), emb_part])
        grad_gains, grad_biases, ada_grad, grad_embedding = call(
            small_grads_kernel,
            small_outs,
            [ext, embs, far_emb, *head_gather(table)],
            scratch=small_scratch,
        )
        first_grad, second_grad, qkv_grad, proj_grad = scatter_plain(
            first_parts[0], second_parts[0], spread, channels
        )
    return (
        output.reshape(inputs.shape),
        grad_inputs.reshape(inputs.shape),
        grad_embedding,
        grad_gains,
        grad_biases,
        first_grad.reshape(-1),
        second_grad.reshape(-1),
        qkv_grad.reshape(-1),
        ada_grad.reshape(-1),
        proj_grad.reshape(-1),
    )


def gather_plain(flats, embedding, spread, channels):
    heads = lax.axis_size("head")

    def columns(flat, groups):
        blocks = flat.astype(BF16).reshape(-1, groups, LANES)
        return blocks

    def own_columns(blocks):
        got = lax.all_to_all(blocks, "head", split_axis=1, concat_axis=0, tiled=True)
        return lax.all_gather(got[:, 0], "dp", axis=0, tiled=True)

    first, second = (own_columns(columns(flats[i], heads).reshape(-1, heads, 1, LANES))[:, 0] for i in (0, 1))
    qkv = columns(flats[2], 12).reshape(-1, heads, 2, 3, HD)
    qkv = jnp.swapaxes(qkv, 2, 3).reshape(-1, heads, 3, LANES)
    qkv = jnp.swapaxes(own_columns(qkv), 0, 1).reshape(-1, LANES)
    ada = columns(flats[3], 8).reshape(-1, 2, heads, LANES)
    ada = jnp.swapaxes(own_columns(jnp.swapaxes(ada, 1, 2)), 0, 1).reshape(-1, LANES)
    proj = lax.ppermute(flats[4].astype(BF16), ("dp", "head"), spread)
    proj = lax.all_gather(proj, "dp", axis=0, tiled=True).reshape(-1, channels // LANES, LANES)
    proj = jnp.swapaxes(proj, 0, 1).reshape(-1, LANES)
    embs = lax.all_gather(embedding, "dp", axis=0, tiled=True).astype(F32)
    embs = embs.reshape(embs.shape[0], -1, flats[3].shape[0] // 8)
    embs = lax.dynamic_index_in_dim(
        embs, lax.axis_index("dp") * heads + lax.axis_index("head"), 1, False
    )
    first_piece = jnp.concatenate([first, ada, proj])
    second_piece = jnp.concatenate([second, qkv])
    proj_at = 9 * channels + ada.shape[0]
    return (
        [first_piece],
        (
            (0, 1, 9 * channels),
            (9 * channels, 2, ada.shape[0] // 2),
            (proj_at, channels // LANES, LANES),
        ),
        [second_piece],
        ((0, 1, 9 * channels), (9 * channels, 3, channels)),
        embs,
    )


def scatter_plain(first, second, spread, channels):
    heads = lax.axis_size("head")

    def rows_of(grad):
        part = lax.psum_scatter(grad, "dp", scatter_dimension=0, tiled=True)
        return lax.all_to_all(part[:, None], "head", split_axis=0, concat_axis=1, tiled=True)

    def conv(grad):
        return rows_of(grad[:, None])

    qkv = jnp.swapaxes(second[9 * channels : 12 * channels].reshape(3, channels, LANES), 0, 1)
    qkv = rows_of(qkv).reshape(-1, heads, 3, 2, HD)
    qkv = jnp.swapaxes(qkv, 2, 3)
    proj = jnp.swapaxes(second[12 * channels :].reshape(-1, LANES, LANES), 0, 1)
    proj = lax.psum_scatter(proj, "dp", scatter_dimension=0, tiled=True)
    proj = lax.ppermute(proj, ("dp", "head"), [(j, i) for i, j in spread])
    return (conv(first), conv(second[: 9 * channels]), qkv, proj)


def solution(mesh):
    flat = P(("dp", "head"))
    image = P("dp", "head", None, None)
    return jax.shard_map(
        body,
        mesh=mesh,
        in_specs=(image, P("dp", None), P("dp", None), image, P(), P(), flat, flat, flat, flat, flat),
        out_specs=(image, image, P("dp", None), P(), P(), flat, flat, flat, flat, flat),
        check_vma=False,
    )
```

```python
import functools
import math

import jax
import jax.numpy as jnp
from jax import lax
from jax.experimental import pallas as pl
from jax.experimental.pallas import tpu as pltpu
from jax.sharding import PartitionSpec as P

HD = 64
PROJ_PARTS = 2
MARK = 640
GROUPS = 32
EPS = 1e-05
MASKED = -1e30
LANES = 128
F32 = jnp.float32
BF16 = jnp.bfloat16
VMEM_SPEC = pl.BlockSpec(memory_space=pltpu.VMEM)
SMEM_SPEC = pl.BlockSpec(memory_space=pltpu.SMEM)


def sds(shape, dtype):
    return jax.ShapeDtypeStruct(shape, dtype)


class Far:
    def __init__(self, array, held=True, pinned=False):
        self.array = pltpu.with_memory_space_constraint(array, pltpu.HBM) if pinned else array
        self.held = held


class Fetch:
    def __init__(self, source, ref, sem):
        self.copy = pltpu.make_async_copy(source, ref, sem)
        self.ref = ref
        self.copy.start()

    def get(self):
        self.copy.wait()
        return self.ref


class Store:
    def __init__(self, dest, ref, sem):
        self.dest = dest
        self.ref = ref
        self.sem = sem
        self.copy = None

    def send(self, source=None):
        self.copy = pltpu.make_async_copy(self.ref if source is None else source, self.dest, self.sem)
        self.copy.start()


def call(kernel, outs, args, scratch=(), us=1.0, vmem=24, after=()):
    scalars = args[0] is not None
    args = list(args) if scalars else list(args[1:])
    arrays = [arg.array if isinstance(arg, Far) else arg for arg in args]
    results = [out.array if isinstance(out, Far) else out for out in outs]
    far_in = [isinstance(arg, Far) for arg in args]
    far_out = [isinstance(out, Far) for out in outs]
    held = [
        pltpu.VMEM(x.array.shape, x.array.dtype)
        for x in list(args) + list(outs)
        if isinstance(x, Far) and x.held
    ]
    copies = sum(far_in) + sum(far_out)

    def run(*refs):
        ins = refs[: len(args)]
        begin = len(args) + len(after)
        dests = refs[begin : begin + len(outs)]
        begin += len(outs)
        buffers = iter(refs[begin : begin + len(held)])
        begin += len(held)
        sems = refs[begin] if copies else None
        rest = refs[begin + (1 if copies else 0) :]
        count = 0
        given = []
        for ref, far in zip(ins, far_in):
            if far:
                ref = Fetch(ref, next(buffers), sems.at[count])
                count += 1
            given.append(ref)
        stores = []
        for ref, out in zip(dests, outs):
            if isinstance(out, Far):
                ref = Store(ref, next(buffers) if out.held else None, sems.at[count])
                stores.append(ref)
                count += 1
            given.append(ref)
        kernel(*([] if scalars else [None]), *given, *rest)
        for store in stores:
            store.copy.wait()

    hbm = pl.BlockSpec(memory_space=pltpu.HBM)
    anywhere = pl.BlockSpec(memory_space=pl.ANY)
    return pl.pallas_call(
        run,
        out_shape=tuple(results),
        in_specs=[
            hbm if far else SMEM_SPEC if scalars and i == 0 else VMEM_SPEC
            for i, far in enumerate(far_in)
        ]
        + [anywhere for _ in after],
        out_specs=tuple(hbm if far else VMEM_SPEC for far in far_out),
        scratch_shapes=held
        + ([pltpu.SemaphoreType.DMA((copies,))] if copies else [])
        + list(scratch),
        compiler_params=pltpu.CompilerParams(vmem_limit_bytes=vmem * 1024 * 1024),
        cost_estimate=pl.CostEstimate(
            flops=int(3e7 * us),
            bytes_accessed=1024,
            transcendentals=0,
        ),
    )(*arrays, *after)


def following(value, *earlier):
    return lax.optimization_barrier((value, *earlier))[0]


def hop(value, axis, bit):
    count = lax.axis_size(axis)
    return lax.ppermute(value, axis, [(i, i ^ bit) for i in range(count)])


def head_gather(block, *earlier):
    far = hop(block, "head", 2)
    near = hop(block, "head", 1)
    return (block, near, far, hop(following(far, *earlier) if earlier else far, "head", 1))


def head_exchange(near_block, far_pair, *earlier):
    far = hop(far_pair, "head", 2)
    near = hop(near_block, "head", 1)
    return (near, far, hop(following(far, *earlier) if earlier else far, "head", 1))


def add_kernel(ext, first, second, out):
    out[...] = (first[...].astype(F32) + second[...].astype(F32)).astype(out.dtype)


def head_reduce(ext, blocks, after=()):
    kept, near_block, far_block, corner = blocks
    corner = hop(corner, "head", 1)
    (far_block,) = call(
        add_kernel, [sds(far_block.shape, BF16)], [None, far_block, corner], us=0.7, after=after
    )
    return ((kept, hop(near_block, "head", 1), hop(far_block, "head", 2)), [far_block])


def mm(left, right, left_dim, right_dim):
    return lax.dot_general(
        left, right, (((left_dim,), (right_dim,)), ((), ())), preferred_element_type=F32
    )


def lane_block(index):
    return pl.ds(pl.multiple_of(index * LANES, LANES), LANES)


def row_block(index, rows):
    return pl.ds(pl.multiple_of(index * rows, rows), rows)


def pixel_place(rows, lanes, cols, start=0):
    pixel = lax.broadcasted_iota(jnp.int32, (rows, lanes), 0) + start
    shift = cols.bit_length() - 1
    return (lax.shift_right_logical(pixel, shift), lax.bitwise_and(pixel, cols - 1))


def valid_of(ext, rows, lanes, cols, start=0):
    place_row, place_col = pixel_place(rows, lanes, cols, start)
    inside = jnp.logical_and(place_row < ext[0, 0], place_col < ext[0, 1])
    return jnp.where(inside, 1.0, 0.0).astype(F32)


def group_total(first, second, width):
    lanes = first.shape[-1]
    pick = lax.broadcasted_iota(jnp.int32, (8, lanes), 0)
    both = jnp.where(pick == 0, first, jnp.where(pick == 1, second, 0.0))
    shift = width.bit_length() - 1
    left = lax.shift_right_logical(lax.broadcasted_iota(jnp.int32, (lanes, lanes), 0), shift)
    right = lax.shift_right_logical(lax.broadcasted_iota(jnp.int32, (lanes, lanes), 1), shift)
    same = jnp.where(left == right, 1.0, 0.0).astype(F32)
    total = lax.dot_general(
        both,
        same,
        (((1,), (0,)), ((), ())),
        precision=lax.Precision.HIGHEST,
        preferred_element_type=F32,
    )
    return (total[0:1], total[1:2])


def pixel_count(ext, width):
    return (ext[0, 0] * ext[0, 1] * width).astype(F32)


def col_sum(value):
    return jnp.sum(value, axis=0, keepdims=True)


def head_rank():
    return lax.axis_index("head")


def norm_stats(value, valid, count, width):
    masked = value * valid
    total, square = group_total(col_sum(masked), col_sum(masked * value), width)
    center = total / count
    return (center, lax.rsqrt(square / count - center * center + EPS))


def norm_back(grad, normed, inverse, valid, count, width):
    first, second = group_total(col_sum(grad), col_sum(grad * normed), width)
    return (grad - valid * ((first + normed * second) * (1.0 / count))) * inverse


def silu_grad(value):
    gate = jax.nn.sigmoid(value)
    return gate * (1.0 + value * (1.0 - gate))


def place_pieces(dest, pieces, start, groups, rows):
    for k, piece in enumerate(pieces):
        part = lax.axis_index("dp") ^ k if len(pieces) > 1 else 0
        for group in range(groups):
            begin = start + group * rows
            dest[group, pl.ds(pl.multiple_of(part * rows, rows), rows), :] = piece[
                begin : begin + rows, :
            ]


def taps_side_by_side(flat, wide):
    channels = wide.shape[0]
    for tap in range(9):
        wide[:, tap * LANES : (tap + 1) * LANES] = flat[0, tap * channels : (tap + 1) * channels, :]


def conv_taps(act, wide, taps, cols):
    pixels = act.shape[0]
    blank = jnp.zeros((cols, wide.shape[1]), F32)
    taps[0:cols, :] = blank
    taps[pixels + cols :, :] = blank
    taps[cols : pixels + cols, :] = mm(act[...], wide[...], 1, 0)


def conv_sum(taps, begin, rows, cols):
    def column(side):
        return sum(
            taps[
                pl.ds(pl.multiple_of(begin + up * cols, cols), rows),
                (up * 3 + side) * LANES : (up * 3 + side + 1) * LANES,
            ]
            for up in range(3)
        )

    place_col = pixel_place(rows, LANES, cols)[1]
    left = jnp.where(place_col > 0, pltpu.roll(column(0), 1, 0), 0.0)
    right = jnp.where(place_col < cols - 1, pltpu.roll(column(2), rows - 1, 0), 0.0)
    return column(1) + left + right


def shifted_grads(grad, dest, cols):
    pixels = grad.shape[0]
    place_col = pixel_place(pixels, LANES, cols)[1]
    sides = (
        jnp.where(place_col < cols - 1, pltpu.roll(grad, pixels - 1, 0), 0.0),
        grad,
        jnp.where(place_col > 0, pltpu.roll(grad, 1, 0), 0.0),
    )
    blank = jnp.zeros((cols, LANES), BF16)
    for side, value in enumerate(sides):
        low = value.astype(BF16)
        for up in range(3):
            lanes = slice((up * 3 + side) * LANES, (up * 3 + side + 1) * LANES)
            if up == 0:
                dest[0 : pixels - cols, lanes] = low[cols:, :]
                dest[pixels - cols :, lanes] = blank
            elif up == 1:
                dest[:, lanes] = low
            else:
                dest[cols:, lanes] = low[0 : pixels - cols, :]
                dest[0:cols, lanes] = blank


def partial_sums(left, right, whole, outs):
    whole[...] = mm(left[...], right[...], 1, 1)
    rank = head_rank()
    for k, out in enumerate(outs):
        out[...] = whole[:, lane_block(rank ^ k)].astype(out.dtype)


def weights_out_kernel(ext, *refs):
    first, second, qkv, ada, proj = refs[0:5]
    kept, near, pair, pj = refs[5:]
    rank = head_rank()
    low_half = lax.broadcasted_iota(jnp.int32, (qkv.ref.shape[0] // 12, LANES), 1) < HD
    first, second, qkv, ada, proj = (x.get() for x in (first, second, qkv, ada, proj))

    def strided(ref, begin, stride):
        return ref[pl.ds(begin, ref.shape[0] // stride, stride=stride), :]

    def put(dest, begin, value):
        rows = value.shape[0]
        dest[begin : begin + rows, :] = value.astype(BF16)
        return begin + rows

    at = 0
    for g in range(4):
        at = put(pj, at, strided(proj, g, 4))
    for k, dest in enumerate((kept, near, pair.at[0], pair.at[1])):
        peer = rank ^ k
        at = put(dest, 0, strided(first, peer, 4))
        for side in range(2):
            at = put(dest, at, strided(ada, 4 * side + peer, 8))
        at = put(dest, at, strided(second, peer, 4))
        part = [strided(qkv, peer * 3 + g, 12) for g in range(3)]
        at = put(dest, at, jnp.where(low_half, part[0], part[1]))
        at = put(dest, at, pltpu.roll(jnp.where(low_half, part[2], part[0]), HD, 1))
        put(dest, at, jnp.where(low_half, part[1], part[2]))


def join_blocks(dest, blocks, source, segments):
    rank = head_rank()
    for k, block in enumerate(blocks):
        at, begin = (source, 0)
        for rows in segments:
            place = pl.ds(pl.multiple_of(begin + (rank ^ k) * rows, 16), rows)
            dest[place, :] = block[at : at + rows, :]
            at += rows
            begin += 4 * rows
    return 4 * sum(segments)


def first_piece_kernel(ext, kept, near, far, corner, emb, proj, piece, line, *, segments):
    at = join_blocks(piece, (kept, near, far.at[0], corner.at[1]), 0, segments)
    emb = emb.get()
    line[...] = jnp.zeros(line.shape, F32)
    for j in range(emb.shape[1] // LANES):
        line[j : j + 1, :] = emb[0:1, j * LANES : (j + 1) * LANES].astype(F32)
    piece[at : at + 16, :] = line[...].astype(BF16)
    piece[at + 16 :, :] = proj[...]


def second_piece_kernel(ext, kept, near, far, corner, piece, *, source, segments):
    join_blocks(piece, (kept, near, far.at[0], corner.at[1]), source, segments)


def dp_straight(piece):
    return [piece] + [hop(piece, "dp", k) for k in (2, 4, 6)]


def dp_beside(straight, *earlier):
    own, two, four, six = straight
    near = [hop(value, "dp", 1) for value in (own, two, six)]
    near.insert(2, hop(following(four, *near, *earlier) if earlier else four, "dp", 1))
    return [value for pair in zip(straight, near) for value in pair]


def norm_first_kernel(ext, gains, biases, *refs, cols, width):
    blocks = refs[0:4]
    act, own_out, stats, held = refs[4:]
    own = own_out.ref
    rank = head_rank()
    rows, channels = blocks[0].shape
    count = pixel_count(ext, width)
    total = jnp.zeros((1, channels), F32)
    square = jnp.zeros((1, channels), F32)
    for k, block in enumerate(blocks):
        own[row_block(rank ^ k, rows), :] = block[:, lane_block(rank)]
    own_out.send()
    for k, block in enumerate(blocks):
        value = block[...].astype(F32)
        masked = value * valid_of(ext, rows, channels, cols, (rank ^ k) * rows)
        total = total + col_sum(masked)
        square = square + col_sum(masked * value)
    total, square = group_total(total, square, width)
    center = total / count
    inverse = lax.rsqrt(square / count - center * center + EPS)
    held[0:1, :] = center
    held[1:2, :] = inverse
    gain, bias = (gains.get()[0:1, :], biases.get()[0:1, :])
    for k, block in enumerate(blocks):
        peer = rank ^ k
        pre = (block[...].astype(F32) - center) * inverse * gain + bias
        valid = valid_of(ext, rows, channels, cols, peer * rows)
        act[row_block(peer, rows), :] = (pre * jax.nn.sigmoid(pre) * valid).astype(BF16)
    stats[...] = held[:, lane_block(rank)]


def conv_first_kernel(ext, biases, act, emb, *refs, cols, width, count_pieces, segments, emb_at):
    pieces = refs[0:count_pieces]
    act_out, normed_out, aux, wide_out, ada_out, act_far = refs[count_pieces : count_pieces + 6]
    w_proj = refs[count_pieces + 6 : -4 if emb_at is None else -5]
    flat, taps, hidden, proj = refs[-4:]
    rank = head_rank()
    pixels = act.shape[0]
    act_far.send(act)
    place_pieces(flat, pieces, *segments[0])
    wide = wide_out.ref
    taps_side_by_side(flat, wide)
    wide_out.send()
    ada = ada_out.ref
    place_pieces(ada, pieces, *segments[1])
    ada_out.send()
    place_pieces(proj, pieces, *segments[2])
    if len(w_proj) == 1:
        for g in range(proj.shape[0]):
            w_proj[0][:, g * LANES : (g + 1) * LANES] = proj[g]
    else:
        kept, near, pair = w_proj
        for k, dest in enumerate((kept, near, pair.at[0], pair.at[1])):
            for g in range(proj.shape[0]):
                dest[g] = proj[g, row_block(rank ^ k, dest.shape[1]), :]
    if emb_at is not None:
        table = refs[-5]
        place = lax.axis_index("dp")
        table[...] = jnp.zeros(table.shape, F32)
        for k, piece in enumerate(pieces):
            lines = piece[emb_at : emb_at + 16, :].astype(F32)
            mine = lax.broadcasted_iota(jnp.int32, lines.shape, 0) == place
            table[pl.ds(place ^ k, 1), :] = col_sum(jnp.where(mine, lines, 0.0))
    conv_taps(act, wide, taps, cols)
    biases = biases.get()
    bias = biases[1:2, lane_block(rank)]
    step = 256
    for i in range(pixels // step):
        hidden[i * step : (i + 1) * step, :] = conv_sum(taps, i * step, step, cols) + bias
    value = hidden[...]
    valid = valid_of(ext, pixels, LANES, cols)
    center, inverse = norm_stats(value, valid, pixel_count(ext, width), width)
    normed = (value - center) * inverse
    normed_out.ref[...] = normed
    normed_out.send()
    emb_value = emb.get()[...].astype(F32)
    emb_act = (emb_value * jax.nn.sigmoid(emb_value)).astype(BF16).astype(F32)
    mods = []
    for side in range(2):
        mod = biases[2 + side : 3 + side, lane_block(rank)]
        for j in range(emb_act.shape[1] // LANES):
            lanes = slice(j * LANES, (j + 1) * LANES)
            row = jnp.broadcast_to(emb_act[:, lanes], (16, LANES)).astype(BF16)
            mod = mod + mm(row, ada[side, lanes, :], 1, 0)[0:1]
        mods.append(mod)
    pre = normed * (1.0 + mods[0]) + mods[1]
    act_out[...] = (pre * jax.nn.sigmoid(pre) * valid).astype(BF16)
    aux[...] = jnp.zeros(aux.shape, F32)
    aux[0:1, :] = inverse
    aux[1:2, :] = mods[0]
    aux[2:3, :] = mods[1]


def conv_second_kernel(ext, gains, biases, own, *refs, cols, width, count_pieces, segments):
    blocks = refs[0:4]
    pieces = refs[4 : 4 + count_pieces]
    attn_in, act_out, residual_out, normed_out, aux, wide_out, w_qkv = refs[4 + count_pieces : -3]
    flat, qkv, taps = refs[-3:]
    rank = head_rank()
    act, wide, residual = (act_out.ref, wide_out.ref, residual_out.ref)
    pixels = act.shape[0]
    for k, block in enumerate(blocks):
        act[:, lane_block(rank ^ k)] = block[...]
    act_out.send()
    place_pieces(flat, pieces, *segments[0])
    taps_side_by_side(flat, wide)
    wide_out.send()
    place_pieces(qkv, pieces, *segments[1])
    for g in range(3):
        w_qkv[:, g * LANES : (g + 1) * LANES] = qkv[g]
    conv_taps(act, wide, taps, cols)
    gains, biases, own = (gains.get(), biases.get(), own.get())
    bias = biases[4:5, lane_block(rank)]
    step = 256
    for i in range(pixels // step):
        rows = slice(i * step, (i + 1) * step)
        third = conv_sum(taps, i * step, step, cols) + bias
        valid = valid_of(ext, step, LANES, cols, i * step)
        residual[rows, :] = own[rows, :].astype(F32) + valid * third
    residual_out.send()
    value = residual[...]
    valid = valid_of(ext, pixels, LANES, cols)
    center, inverse = norm_stats(value, valid, pixel_count(ext, width), width)
    normed = (value - center) * inverse
    normed_out.ref[...] = normed
    normed_out.send()
    attn_in[...] = (
        normed * gains[1:2, lane_block(rank)] + biases[5:6, lane_block(rank)]
    ).astype(BF16)
    aux[...] = jnp.broadcast_to(inverse, aux.shape)


def cotangent_kernel(ext, *refs):
    cots = refs[0:4]
    full_out, own_out, att, att_t, rows_weight = refs[-5:]
    rank = head_rank()
    rows = cots[0].shape[0]
    for k, cot in enumerate(cots):
        at = row_block(rank ^ k, rows)
        full_out.ref[at, :] = cot[...]
        own_out.ref[at, :] = cot[:, lane_block(rank)]
    full_out.send()
    own_out.send()
    weights = refs[4:-5]
    if len(weights) == 1:
        rows_weight[...] = weights[0][...]
    else:
        kept, near, far, corner = weights
        count = len(cots)
        size = LANES // (count * PROJ_PARTS)
        for k, block in enumerate((kept, near, far.at[0], corner.at[1])):
            for part in range(PROJ_PARTS):
                at = pl.ds(pl.multiple_of((part * count + (rank ^ k)) * size, 16), size)
                for g in range(block.shape[0]):
                    lanes = slice(g * LANES, (g + 1) * LANES)
                    rows_weight[at, lanes] = block[g, part * size : (part + 1) * size, :]
    for i in range(4):
        at = slice(i * rows, (i + 1) * rows)
        grad = mm(full_out.ref[at, :], rows_weight[...], 1, 1).astype(BF16)
        att[at, :] = grad
        att_t[:, at] = grad.astype(F32).T


def attention_kernel(ext, *refs, cols):
    blocks = refs[0:4]
    wide, cot_att, cot_att_t = refs[4:7]
    outs = refs[7:11]
    full_out, grads_out, attended_out = refs[11:14]
    qkv, keys_t, values_t, grad_kv, whole = refs[14:]
    attn_full, grads, attended = (full_out.ref, grads_out.ref, attended_out.ref)
    rank = head_rank()
    pixels = attn_full.shape[0]
    scale = 1.0 / math.sqrt(HD)
    for k in range(4):
        attn_full[:, lane_block(rank ^ k)] = blocks[k][...]
    full_out.send()
    step = 256
    qkv[...] = mm(attn_full[...], wide[...], 1, 0).astype(BF16)
    for i in range(pixels // step):
        at = slice(i * step, (i + 1) * step)
        keys_t[:, at] = qkv[at, LANES : 2 * LANES].astype(F32).T.astype(BF16)
        values_t[:, at] = qkv[at, 2 * LANES :].astype(F32).T.astype(BF16)
    lane = lax.broadcasted_iota(jnp.int32, (pixels, LANES), 1)
    sublane = lax.broadcasted_iota(jnp.int32, (LANES, pixels), 0)
    key_row, key_col = pixel_place(pixels, pixels, cols)
    key_valid = jnp.logical_and(key_row < ext[0, 0], key_col < ext[0, 1])
    att_sum = jnp.zeros((LANES, pixels), F32)
    query_sum = jnp.zeros((LANES, pixels), F32)
    for h in range(LANES // HD):
        mine = lax.shift_right_logical(lane, 6) == h
        mine_t = lax.shift_right_logical(sublane, 6) == h
        query = jnp.where(mine, qkv[:, 0:LANES], jnp.zeros((pixels, LANES), BF16))
        cot = jnp.where(mine, cot_att[...], jnp.zeros((pixels, LANES), BF16))
        scores = mm(qkv[:, LANES : 2 * LANES], query, 1, 1) * scale
        scores = jnp.where(key_valid, scores, MASKED)
        top = jnp.max(scores, axis=0, keepdims=True)
        expo = jnp.exp(scores - top)
        probs = expo * (1.0 / col_sum(expo))
        probs_low = probs.astype(BF16)
        att = mm(jnp.where(mine_t, values_t[...], jnp.zeros((LANES, pixels), BF16)), probs_low, 1, 0)
        att_sum = att_sum + att
        row_dot = col_sum(att * cot_att_t[...])
        grad_probs = mm(qkv[:, 2 * LANES :], cot, 1, 1)
        grad_scores = (probs * (grad_probs - row_dot)).astype(BF16)
        grad_values = mm(probs_low, cot, 1, 0)
        grad_keys = mm(grad_scores, query, 1, 0)
        if h == 0:
            grad_kv[:, LANES:] = grad_values
            grad_kv[:, 0:LANES] = grad_keys
        else:
            grad_kv[:, LANES:] += grad_values
            grad_kv[:, 0:LANES] += grad_keys
        query_sum = query_sum + mm(
            jnp.where(mine_t, keys_t[...], jnp.zeros((LANES, pixels), BF16)), grad_scores, 1, 0
        )
    attended[...] = att_sum.T.astype(BF16)
    grads[:, 0:LANES] = (query_sum.T * scale).astype(BF16)
    attended_out.send()
    grads[:, LANES : 2 * LANES] = (grad_kv[:, 0:LANES] * scale).astype(BF16)
    grads[:, 2 * LANES :] = grad_kv[:, LANES:].astype(BF16)
    grads_out.send()
    partial_sums(grads, wide, whole, outs)


def out_partial_kernel(ext, biases, attended, rows_weight, residual, cot, *refs):
    outs = refs[0:4]
    grads = refs[4:-1]
    whole = refs[-1]
    rank = head_rank()
    rows = outs[0].shape[0]
    attended = attended.get()
    for i in range(4):
        at = slice(i * rows, (i + 1) * rows)
        whole[at, :] = mm(attended[at, :], rows_weight[...], 1, 0)
    bias = biases.get()[6:7, lane_block(rank)]
    whole[:, lane_block(rank)] += residual.get()[...] + bias
    for k, out in enumerate(outs):
        out[...] = whole[row_block(rank ^ k, rows), :].astype(out.dtype)
    whole[0:LANES, :] = mm(attended[...], cot.get()[...], 0, 0)
    if len(grads) == 1:
        for g in range(grads[0].shape[0]):
            grads[0][g] = whole[0:LANES, g * LANES : (g + 1) * LANES]
    else:
        kept, near, pair = grads
        count = len(outs)
        size = LANES // (count * PROJ_PARTS)
        for k, dest in enumerate((kept, near, pair.at[0], pair.at[1])):
            for part in range(PROJ_PARTS):
                at = row_block(part * count + (rank ^ k), size)
                for g in range(dest.shape[0]):
                    dest[g, part * size : (part + 1) * size, :] = whole[
                        at, g * LANES : (g + 1) * LANES
                    ].astype(BF16)


def sum_kernel(ext, first, second, third, out):
    out[...] = (first[...] + second[...].astype(F32) + third[...].astype(F32)).astype(out.dtype)


def norm_third_back_kernel(ext, gains, kept, near, far, normed, inverse, cot, wide, *refs, cols, width):
    outs = refs[0:4]
    grad_res, third_out, sums, shifted, whole = refs[4:]
    rank = head_rank()
    pixels = kept.shape[0]
    grad = kept[...] + near[...].astype(F32) + far[...].astype(F32)
    normed, gains, cot = (normed.get()[...], gains.get(), cot.get())
    valid = valid_of(ext, pixels, LANES, cols)
    back = norm_back(
        grad * gains[1:2, lane_block(rank)], normed, inverse[0:1, :], valid,
        pixel_count(ext, width), width,
    )
    cot_value = cot[...].astype(F32)
    residual = cot_value + back
    grad_res.ref[...] = residual
    grad_res.send()
    third = (valid * residual).astype(BF16)
    third_out[...] = third
    third = third.astype(F32)
    shifted_grads(third, shifted, cols)
    sums[...] = jnp.zeros(sums.shape, F32)
    sums[0:1, :] = col_sum(grad * normed)
    sums[1:2, :] = col_sum(grad)
    sums[2:3, :] = col_sum(third)
    sums[3:4, :] = col_sum(cot_value)
    partial_sums(shifted, wide.get(), whole, outs)


def norm_second_back_kernel(ext, kept, near, far, normed, aux, wide, *refs, cols, width):
    outs = refs[0:4]
    first_out, sums, shifted, whole = refs[4:]
    pixels = kept.shape[0]
    grad_act = kept[...] + near[...].astype(F32) + far[...].astype(F32)
    normed = normed.get()[...]
    valid = valid_of(ext, pixels, LANES, cols)
    inverse, scale, shift = (aux[0:1, :], aux[1:2, :], aux[2:3, :])
    grad_pre = grad_act * valid * silu_grad(normed * (1.0 + scale) + shift)
    back = norm_back(
        grad_pre * (1.0 + scale), normed, inverse, valid, pixel_count(ext, width), width
    )
    first = back.astype(BF16)
    first_out[...] = first
    first = first.astype(F32)
    shifted_grads(first, shifted, cols)
    sums[...] = jnp.zeros(sums.shape, F32)
    sums[0:1, :] = col_sum(grad_pre * normed).astype(BF16).astype(F32)
    sums[1:2, :] = col_sum(grad_pre).astype(BF16).astype(F32)
    sums[2:3, :] = col_sum(first)
    partial_sums(shifted, wide.get(), whole, outs)


def norm_first_back_kernel(
    ext, gains, biases, kept, near, far, own, stats, grad_res, sums_third, sums_second, *refs,
    cols, width,
):
    out_kept, out_near, out_pair, table, held = refs
    rank = head_rank()
    pixels = kept.shape[0]
    rows = out_kept.shape[0]
    grad_act = kept[...] + near[...].astype(F32) + far[...].astype(F32)
    valid = valid_of(ext, pixels, LANES, cols)
    center, inverse = (stats[0:1, :], stats[1:2, :])
    normed = (own.get()[...].astype(F32) - center) * inverse
    gain = gains.get()[0:1, lane_block(rank)]
    bias = biases.get()[0:1, lane_block(rank)]
    grad_pre = grad_act * valid * silu_grad(normed * gain + bias)
    back = norm_back(grad_pre * gain, normed, inverse, valid, pixel_count(ext, width), width)
    held[...] = grad_res.get()[...] + back
    out_kept[...] = held[row_block(rank, rows), :]
    out_near[...] = held[row_block(rank ^ 1, rows), :].astype(BF16)
    for k in (2, 3):
        out_pair[k - 2] = held[row_block(rank ^ k, rows), :].astype(BF16)
    table[...] = jnp.zeros(table.shape, F32)
    table[0:1, :] = col_sum(grad_pre * normed)
    table[1:2, :] = sums_third[0:1, :]
    table[2:3, :] = col_sum(grad_pre)
    table[3:4, :] = sums_second[2:3, :]
    table[4:6, :] = sums_second[0:2, :]
    table[6:7, :] = sums_third[2:3, :]
    table[7:8, :] = sums_third[1:2, :]
    table[8:9, :] = sums_third[3:4, :]
    table[pl.ds(16 + 2 * lax.axis_index("dp"), 2), :] = sums_second[0:2, :]


def put_exact(dest, begin, value):
    rows = value.shape[0]
    high = value.astype(BF16)
    dest[begin : begin + rows, :] = high
    dest[begin + rows : begin + 2 * rows, :] = (value - high.astype(F32)).astype(BF16)


def get_exact(source, begin, rows):
    high = source[begin : begin + rows, :].astype(F32)
    return high + source[begin + rows : begin + 2 * rows, :].astype(F32)


def rows_join_kernel(ext, kept, near, far, corner, out):
    rank = head_rank()
    for k, block in enumerate((kept, near, far.at[0], corner.at[1])):
        out[:, lane_block(rank ^ k)] = block[...].astype(F32)


def taps_grad(act, shifted, flat):
    channels = act.shape[1]
    for i in range(channels // LANES):
        part = mm(act[:, i * LANES : (i + 1) * LANES], shifted[...], 0, 0)
        for tap in range(9):
            flat[0, tap * channels + i * LANES : tap * channels + (i + 1) * LANES, :] = part[
                :, tap * LANES : (tap + 1) * LANES
            ]


def dp_parts(dests, sources, dp_count):
    place = lax.axis_index("dp") if dp_count > 1 else 0
    for k, dest in enumerate(dests):
        at = 0
        for source in sources:
            size = source.shape[1] // dp_count
            for g in range(source.shape[0]):
                dest[at : at + size, :] = source[g, row_block(place ^ k, size), :].astype(dest.dtype)
                at += size


def qkv_grads_kernel(ext, attn, grads, *refs, dp_count):
    dests = refs[0:-1]
    qkv = refs[-1]
    part = mm(attn.get()[...], grads.get()[...], 0, 0)
    for g in range(3):
        qkv[g] = part[:, g * LANES : (g + 1) * LANES]
    if dp_count > 1:
        own, two, four, six, pairs = dests
        dests = (own, pairs.at[3], two, pairs.at[0], four, pairs.at[2], six, pairs.at[1])
    dp_parts(dests, (qkv,), dp_count)


def second_grads_kernel(ext, third, act, *refs, cols, dp_count):
    grad_proj = refs[0 : 4 if dp_count > 1 else 1]
    dests = refs[len(grad_proj) : -3]
    shifted, flat, proj = refs[-3:]
    shifted_grads(third[...].astype(F32), shifted, cols)
    act = act.get()
    taps_grad(act, shifted, flat)
    if len(grad_proj) == 1:
        proj[...] = grad_proj[0][...]
    else:
        kept, near, far, corner = grad_proj
        rank = head_rank()
        for k, block in enumerate((kept, near, far.at[0], corner.at[1])):
            size = block.shape[1]
            for g in range(proj.shape[0]):
                proj[g, row_block(rank ^ k, size), :] = block[g].astype(F32)
    dp_parts(split_dests(dests), (flat, proj), dp_count)


def split_dests(dests):
    if len(dests) == 1:
        return dests
    own, two, four, six, first_pair, second_pair = dests
    return (
        own, second_pair.at[1], two, first_pair.at[0], four, second_pair.at[0], six, first_pair.at[1]
    )


def first_grads_kernel(ext, first, act, sums, ada, *refs, cols, dp_count):
    dests = refs[0:-3]
    emb_part, shifted, flat = refs[-3:]
    shifted_grads(first[...].astype(F32), shifted, cols)
    taps_grad(act.get(), shifted, flat)
    dp_parts(split_dests(dests), (flat,), dp_count)
    ada = ada.get()
    for j in range(emb_part.shape[0]):
        row = jnp.zeros((1, LANES), F32)
        for side in range(2):
            mod = jnp.broadcast_to(sums[side : side + 1, :], (16, LANES)).astype(BF16)
            row = row + mm(mod, ada[side, j * LANES : (j + 1) * LANES, :], 1, 1)[0:1]
        emb_part[j : j + 1, :] = row


def near_kernel(ext, other, two, six, out):
    size = two.shape[0]
    for k, mine in enumerate((two, six)):
        out[k, 0:size, :] = (mine[...].astype(F32) + other[k].astype(F32)).astype(BF16)


def near_both_kernel(ext, other, two, six, ahead, ahead_two, ahead_six, out):
    size = two.shape[0]
    near_kernel(ext, other, two, six, out.at[:, pl.ds(0, size)])
    near_kernel(ext, ahead, ahead_two, ahead_six, out.at[:, pl.ds(size, ahead_two.shape[0])])


def near_table_kernel(ext, other, two, six, table, beside, out, total):
    size = two.shape[0]
    near_kernel(ext, other, two, six, out)
    total[...] = table[...] + beside[...]
    put_exact(out.at[0], size, total[...])
    out[1, size:, :] = jnp.zeros((out.shape[1] - size, LANES), BF16)


def far_kernel(ext, four, late, near, out):
    size = four.shape[0]
    value = four[...].astype(F32) + late[0].astype(F32) + near[1, 0:size, :].astype(F32)
    out[0:size, :] = value.astype(BF16)


def far_both_kernel(ext, four, late, ahead_four, ahead, near, out):
    size = four.shape[0]
    far_kernel(ext, four, late, near, out)
    rows = pl.ds(size, ahead_four.shape[0])
    far_kernel(ext, ahead_four, ahead.at[pl.ds(2, 2)], near.at[:, rows], out.at[rows])


def far_table_kernel(ext, four, late, near, table, out, total):
    size = four.shape[0]
    far_kernel(ext, four, late, near, out)
    total[...] = table[...] + get_exact(near.at[0], size, table.shape[0])
    put_exact(out, size, total[...])


def dp_pairs(parts):
    early = hop(parts[4], "dp", 1)
    return (early, hop(following(parts[5], early), "dp", 1))


def split_second_kernel(
    ext, own, late, ahead_own, ahead, straight, far, kept, near, pair, proj, held, *,
    rows_conv, rows_qkv,
):
    rank = head_rank()
    size = own.shape[0]
    held[...] = straight[0].astype(F32) + far[...].astype(F32)
    held[0:size, :] += own[...] + late[1].astype(F32)
    held[size:, :] += ahead_own[...] + ahead[3].astype(F32)
    for k, dest in enumerate((kept, near, pair.at[0], pair.at[1])):
        peer = rank ^ k
        dest[0:rows_conv, :] = held[row_block(peer, rows_conv), :].astype(dest.dtype)
        for g in range(3):
            begin = size + g * 4 * rows_qkv
            dest[rows_conv + g * rows_qkv : rows_conv + (g + 1) * rows_qkv, :] = held[
                pl.ds(pl.multiple_of(begin + peer * rows_qkv, 8), rows_qkv), :
            ].astype(dest.dtype)
    proj[...] = held[4 * rows_conv : size, :]


def split_first_kernel(
    ext, own, late, straight, far, table, emb_part, kept, near, pair, total, held, *, rows_conv
):
    rank = head_rank()
    size = held.shape[0]
    lines = table.shape[0]
    held[...] = own[...] + sum(
        part[0:size, :].astype(F32) for part in (late.at[1], straight.at[0], far)
    )
    total[0:lines, :] = table[...] + get_exact(far, size, lines)
    total[lines:, :] = emb_part[...]
    kept[...] = held[row_block(rank, rows_conv), :]
    for k, dest in enumerate((near, pair.at[0], pair.at[1])):
        dest[0:rows_conv, :] = held[row_block(rank ^ (k + 1), rows_conv), :].astype(BF16)
        put_exact(dest, rows_conv, total[...])


def join_second_kernel(ext, kept, near, far, corner, proj, conv_out, qkv_out, proj_out, *, rows_conv, rows_qkv):
    rank = head_rank()
    rows_proj = proj.shape[0] // 4
    low_half = lax.broadcasted_iota(jnp.int32, (rows_qkv, LANES), 1) < HD
    for k, block in enumerate((kept, near, far.at[0], corner.at[1])):
        peer = rank ^ k
        conv_out[pl.ds(peer, rows_conv, stride=4), :] = block[0:rows_conv, :].astype(F32)
        part = [
            block[rows_conv + g * rows_qkv : rows_conv + (g + 1) * rows_qkv, :].astype(F32)
            for g in range(3)
        ]
        keys = pltpu.roll(part[1], HD, 1)
        mixed = (
            jnp.where(low_half, part[0], keys),
            jnp.where(low_half, part[2], part[0]),
            jnp.where(low_half, keys, part[2]),
        )
        for g in range(3):
            qkv_out[pl.ds(peer * 3 + g, rows_qkv, stride=12), :] = mixed[g]
    for g in range(4):
        proj_out[pl.ds(g, rows_proj, stride=4), :] = proj[
            g * rows_proj : (g + 1) * rows_proj, :
        ].astype(F32)


def join_first_kernel(
    ext, kept, near, far, corner, total, embs, emb, conv_out, *refs, rows_conv
):
    rank = head_rank()
    outs, (mods, table, held, t1, t2, t3) = (refs[:4], refs[4:])
    blocks = (near, far.at[0], corner.at[1])
    conv_out[pl.ds(rank, rows_conv, stride=4), :] = kept[...]
    for k, (block, other) in enumerate(zip(blocks, (t1, t2, t3))):
        conv_out[pl.ds(rank ^ (k + 1), rows_conv, stride=4), :] = block[0:rows_conv, :].astype(F32)
        other[...] = get_exact(block, rows_conv, other.shape[0])
    small_grads_kernel(ext, embs, emb, total, t1, t2, t3, *outs, mods, table, held)


def small_grads_kernel(ext, embs, emb, t0, t1, t2, t3, gains_out, biases_out, ada_out, emb_out, mods, table, held):
    rank = head_rank()
    images = embs.shape[0]
    for k, block in enumerate((t0, t1, t2, t3)):
        table[:, lane_block(rank ^ k)] = block[0:16, :]
        for side in range(2):
            mods[:, lane_block(side * 4 + (rank ^ k))] = block[pl.ds(16 + side, images, stride=2), :]
    gains_out[...] = table[0:2, :]
    biases_out[...] = table[2:9, :]
    value = embs[...]
    part = mm((value * jax.nn.sigmoid(value)).astype(BF16), mods[...].astype(BF16), 0, 0)
    rows = ada_out.shape[0] // 8
    if part.shape[0] != rows:
        held[...] = part
        part = held[row_block(rank, rows), :]
    for g in range(8):
        ada_out[pl.ds(g, rows, stride=8), :] = part[:, g * LANES : (g + 1) * LANES]
    value = emb.get()[...].astype(F32)
    slope = silu_grad(value)
    begin = 16 + 2 * images
    for j in range(value.shape[1] // LANES):
        lanes = slice(j * LANES, (j + 1) * LANES)
        total = sum(block[begin + j : begin + j + 1, :] for block in (t0, t1, t2, t3))
        emb_out[:, lanes] = total * slope[:, lanes]


def body(
    inputs, embedding, extent, cotangent, gains, biases,
    conv_first, conv_second, qkv_master, ada_master, proj_master,
):
    heads = lax.axis_size("head")
    dps = lax.axis_size("dp")
    batch, row_count, cols, channels = inputs.shape
    rows = row_count * cols
    pixels = rows * heads
    width = channels // GROUPS
    emb_rows = embedding.shape[1] // LANES
    ext = extent
    direct = dps == 8
    flats = [
        master.reshape(-1, LANES)
        for master in (conv_first, conv_second, qkv_master, ada_master, proj_master)
    ]
    rows_conv = flats[0].shape[0] // 4
    rows_qkv = flats[2].shape[0] // 12
    rows_ada = flats[3].shape[0] // 8
    rows_proj = flats[4].shape[0] // 4
    far_gains, far_biases, far_emb = (Far(x, pinned=True) for x in (gains, biases, embedding))
    spread = [(i, (i % dps) * heads + i // dps) for i in range(dps * heads)]
    inputs_own = inputs.reshape(rows, channels)
    cot_own = cotangent.reshape(rows, channels)
    if direct:
        rows_a = rows_conv + 2 * rows_ada
        rows_b = rows_conv + 3 * rows_qkv
        rows_ab = rows_a + rows_b
        kept, near, pair, pj = call(
            weights_out_kernel,
            [
                sds((rows_ab, LANES), BF16), sds((rows_ab, LANES), BF16),
                sds((2, rows_ab, LANES), BF16), sds((4 * rows_proj, LANES), BF16),
            ],
            [None] + [Far(flat, pinned=True) for flat in flats],
        )
        rows_second = 4 * rows_conv + 12 * rows_qkv + 4 * rows_proj
        blocks = (kept, *head_exchange(near, pair))
        (first_piece,) = call(
            functools.partial(first_piece_kernel, segments=(rows_conv, rows_ada, rows_ada)),
            [sds((4 * rows_conv + 8 * rows_ada + 16 + 4 * rows_proj, LANES), BF16)],
            [None, *blocks, far_emb, pj],
            scratch=[pltpu.VMEM((16, LANES), F32)],
        )
        (second_piece,) = call(
            functools.partial(
                second_piece_kernel, source=rows_a, segments=(rows_conv,) + (rows_qkv,) * 3
            ),
            [sds((rows_second - 4 * rows_proj, LANES), BF16)],
            [None, *blocks],
        )
        first_straight = dp_straight(first_piece)
        inputs_sent = following(inputs_own, first_piece)
        second_straight = dp_straight(second_piece)
        proj_at = 4 * rows_conv + 8 * rows_ada + 16
        first_segments = (
            (0, 1, 4 * rows_conv),
            (4 * rows_conv, 2, 4 * rows_ada),
            (proj_at, 4, rows_proj),
        )
        second_segments = ((0, 1, 4 * rows_conv), (4 * rows_conv, 3, 4 * rows_qkv))
    else:
        first_pieces, first_segments, second_pieces, second_segments, embs = gather_plain(
            flats, embedding, spread, channels
        )
        inputs_sent = inputs_own

    blocks = head_gather(inputs_sent)
    act_first, own, stats_first = call(
        functools.partial(norm_first_kernel, cols=cols, width=width),
        [sds((pixels, channels), BF16), Far(sds((pixels, LANES), BF16)), sds((8, LANES), F32)],
        [ext, far_gains, far_biases, *blocks],
        scratch=[pltpu.VMEM((8, channels), F32)],
        us=2.0,
    )
    if direct:
        first_pieces = dp_beside(first_straight, first_piece)
    cots = head_gather(following(cot_own, blocks[2]))
    wide_shape = (channels, 9 * LANES)
    taps_scratch = pltpu.VMEM((pixels + 2 * cols, 9 * LANES), F32)
    flat_scratch = pltpu.VMEM((1, 9 * channels, LANES), BF16)
    n_pieces = len(first_pieces)
    groups = channels // LANES
    if direct:
        part = (groups, LANES // heads, LANES)
        proj_outs = [sds(part, BF16), sds(part, BF16), sds((2, *part), BF16)]
    else:
        proj_outs = [sds((LANES, channels), BF16)]
    first_outs = call(
        functools.partial(
            conv_first_kernel, cols=cols, width=width, count_pieces=n_pieces,
            segments=first_segments,
            emb_at=4 * rows_conv + 8 * rows_ada if direct else None,
        ),
        [
            sds((pixels, LANES), BF16), Far(sds((pixels, LANES), F32)), sds((8, LANES), F32),
            Far(sds(wide_shape, BF16)), Far(sds((2, emb_rows * LANES, LANES), BF16)),
            Far(sds((pixels, channels), BF16), held=False),
        ]
        + proj_outs
        + ([sds((dps, LANES), F32)] if direct else []),
        [ext, far_biases, act_first, far_emb, *first_pieces],
        scratch=[
            flat_scratch,
            taps_scratch,
            pltpu.VMEM((pixels, LANES), F32),
            pltpu.VMEM((groups, LANES, LANES), BF16),
        ],
        us=4.0,
    )
    act_second_own, normed_second, aux_second, wide_first, ada_full, act_first = first_outs[:6]
    w_proj = first_outs[6 : 6 + len(proj_outs)]
    if direct:
        embs = first_outs[-1]
        second_pieces = dp_beside(second_straight)
        w_proj = (w_proj[0], *head_exchange(*w_proj[1:]))
        mark = [hop(following(second_piece[:MARK], *second_pieces[1::2], *w_proj[1:]), "head", 1)]
        act_second_own = following(act_second_own, second_pieces[1])
    blocks = head_gather(act_second_own)
    attn_own, act_second, residual, normed_third, aux_third, wide_second, w_qkv = call(
        functools.partial(
            conv_second_kernel, cols=cols, width=width, count_pieces=n_pieces,
            segments=second_segments,
        ),
        [
            sds((pixels, LANES), BF16), Far(sds((pixels, channels), BF16)),
            Far(sds((pixels, LANES), F32)), Far(sds((pixels, LANES), F32)), sds((8, LANES), F32),
            Far(sds(wide_shape, BF16)), sds((channels, 3 * LANES), BF16),
        ],
        [ext, far_gains, far_biases, Far(own), *blocks, *second_pieces],
        scratch=[
            flat_scratch,
            pltpu.VMEM((3, channels, LANES), BF16),
            taps_scratch,
        ],
        us=4.0,
        after=mark if direct else (),
    )
    cot_full, cot_own, cot_att, cot_att_t, rows_weight = call(
        cotangent_kernel,
        [
            Far(sds((pixels, channels), BF16)), Far(sds((pixels, LANES), BF16)),
            sds((pixels, LANES), BF16), sds((LANES, pixels), F32), sds((LANES, channels), BF16),
        ],
        [None, *cots, *w_proj],
    )
    blocks = head_gather(attn_own, cot_att)
    whole_scratch = pltpu.VMEM((pixels, channels), F32)
    shifted_scratch = pltpu.VMEM((pixels, 9 * LANES), BF16)
    split_outs = [sds((pixels, LANES), F32)] + [sds((pixels, LANES), BF16)] * 3
    *parts, attn_full, grads_qkv, attended = call(
        functools.partial(attention_kernel, cols=cols),
        split_outs
        + [
            Far(sds((pixels, channels), BF16)), Far(sds((pixels, 3 * LANES), BF16)),
            Far(sds((pixels, LANES), BF16)),
        ],
        [ext, *blocks, w_qkv, cot_att, cot_att_t],
        scratch=[
            pltpu.VMEM((pixels, 3 * LANES), BF16),
            pltpu.VMEM((LANES, pixels), BF16),
            pltpu.VMEM((LANES, pixels), BF16),
            pltpu.VMEM((pixels, 2 * LANES), F32),
            whole_scratch,
        ],
        us=15.0,
    )
    parts, _ = head_reduce(ext, parts)
    grad_outs = proj_outs if direct else [sds((groups, LANES, LANES), F32)]
    out_all = call(
        out_partial_kernel,
        [sds((rows, channels), F32)] + [sds((rows, channels), BF16)] * 3 + grad_outs,
        [None, far_biases, Far(attended), rows_weight, Far(residual), Far(cot_full)],
        scratch=[whole_scratch],
        us=2.0,
    )
    out_parts, grad_proj = (out_all[:4], out_all[4:])
    if direct:
        grad_proj = (grad_proj[0], *head_exchange(*grad_proj[1:]))
    n_dests = dps if direct else 1

    def grad_outs(size):
        size = size // n_dests
        if not direct:
            return [sds((size, LANES), F32)]
        one = sds((size, LANES), BF16)
        return [sds((size, LANES), F32), one, one, one] + [sds((2, size, LANES), BF16)] * 2

    ahead_outs = grad_outs(3 * channels)
    if direct:
        ahead_outs = ahead_outs[:4] + [sds((4, *ahead_outs[1].shape), BF16)]
    ahead_parts = call(
        functools.partial(qkv_grads_kernel, dp_count=n_dests),
        ahead_outs,
        [None, Far(attn_full), Far(grads_qkv)],
        scratch=[pltpu.VMEM((3, channels, LANES), F32)],
        after=out_parts[:1],
    )
    if direct:
        ahead = hop(ahead_parts[4], "dp", 1)
    *parts, grad_res, third, sums_third = call(
        functools.partial(norm_third_back_kernel, cols=cols, width=width),
        split_outs
        + [Far(sds((pixels, LANES), F32)), sds((pixels, LANES), BF16), sds((8, LANES), F32)],
        [
            ext, far_gains, *parts, Far(normed_third), aux_third, Far(cot_own), Far(wide_second),
        ],
        scratch=[shifted_scratch, whole_scratch],
        us=150.0,
        after=ahead_parts[:1],
    )
    if direct:
        parts[3] = following(parts[3], *grad_proj[1:3], ahead)
    out_sums, _ = head_reduce(ext, out_parts)
    (output,) = call(sum_kernel, [sds((rows, channels), BF16)], [None, *out_sums])
    parts, sent = head_reduce(ext, parts)
    flat_grad = pltpu.VMEM((1, 9 * channels, LANES), F32)
    second_parts = call(
        functools.partial(second_grads_kernel, cols=cols, dp_count=n_dests),
        grad_outs(10 * channels),
        [None, third, Far(act_second), *grad_proj],
        scratch=[
            shifted_scratch,
            flat_grad,
            pltpu.VMEM((channels // LANES, LANES, LANES), F32),
        ],
        us=4.0,
        after=sent,
    )
    *parts, first, sums_second = call(
        functools.partial(norm_second_back_kernel, cols=cols, width=width),
        split_outs + [sds((pixels, LANES), BF16), sds((8, LANES), F32)],
        [ext, *parts, Far(normed_second), aux_second, Far(wide_first)],
        scratch=[shifted_scratch, whole_scratch],
        us=150.0,
        after=second_parts[:1],
    )
    if direct:
        second_pairs = dp_pairs(second_parts)
    parts, sent = head_reduce(ext, parts, second_pairs[:1] if direct else ())
    *first_parts, emb_part = call(
        functools.partial(first_grads_kernel, cols=cols, dp_count=n_dests),
        grad_outs(9 * channels) + [sds((emb_rows, LANES), F32)],
        [ext, first, Far(act_first), sums_second, Far(ada_full)],
        scratch=[shifted_scratch, flat_grad],
        us=3.0,
        after=sent,
    )
    table_rows = 16 + 2 * dps
    early = [emb_part]
    if direct:
        first_early, first_late = (hop(pair, "dp", 1) for pair in first_parts[4:6])
        (near_pair,) = call(
            near_both_kernel,
            [sds((2, rows_second, LANES), BF16)],
            [
                None, second_pairs[0], second_parts[1], second_parts[3], ahead, ahead_parts[1],
                ahead_parts[3],
            ],
            us=0.6,
            after=sent,
        )
        early += [near_pair, second_pairs[1]]
        second_near = hop(near_pair, "dp", 2)
    kept_rows, near, pair, table = call(
        functools.partial(norm_first_back_kernel, cols=cols, width=width),
        [
            sds((rows, LANES), F32), sds((rows, LANES), BF16), sds((2, rows, LANES), BF16),
            sds((table_rows, LANES), F32),
        ],
        [
            ext, far_gains, far_biases, *parts, Far(own), stats_first, Far(grad_res), sums_third,
            sums_second,
        ],
        scratch=[pltpu.VMEM((pixels, LANES), F32)],
        us=40.0,
        after=early,
    )
    small_outs = [
        sds(gains.shape, F32), sds(biases.shape, F32), sds(flats[3].shape, F32),
        sds(embedding.shape, F32),
    ]
    small_scratch = [
        pltpu.VMEM((dps, 8 * LANES), F32),
        pltpu.VMEM((16, channels), F32),
        pltpu.VMEM((LANES, 8 * LANES), F32),
    ]
    if direct:
        beside = hop(table, "dp", 1)
        (far_block,) = call(
            far_both_kernel,
            [sds((rows_second, LANES), BF16)],
            [None, second_parts[2], second_pairs[1], ahead_parts[2], ahead, second_near],
            us=0.6,
            after=[kept_rows],
        )
        second_left = [
            second_parts[0], second_pairs[1], ahead_parts[0], ahead, second_near,
            hop(far_block, "dp", 4),
        ]
        size = 4 * rows_conv + 2 * table_rows
        near_pair, table = call(
            near_table_kernel,
            [sds((2, size, LANES), BF16), sds(table.shape, F32)],
            [None, first_early, first_parts[1], first_parts[3], table, beside],
            us=0.6,
        )
        first_near = hop(near_pair, "dp", 2)
        far_block, table = call(
            far_table_kernel,
            [sds((size, LANES), BF16), sds(table.shape, F32)],
            [None, first_parts[2], first_late, first_near, table],
            us=0.6,
            after=[far_block],
        )
        first_left = [first_parts[0], first_late, first_near, hop(far_block, "dp", 4)]
    (grad_inputs,) = call(
        rows_join_kernel,
        [sds((rows, channels), F32)],
        [None, kept_rows, *head_exchange(near, pair)],
    )
    if direct:
        second_own, near, pair, pj = call(
            functools.partial(split_second_kernel, rows_conv=rows_conv, rows_qkv=rows_qkv),
            [
                sds((rows_b, LANES), F32), sds((rows_b, LANES), BF16),
                sds((2, rows_b, LANES), BF16), sds((4 * rows_proj, LANES), F32),
            ],
            [None, *second_left],
            scratch=[pltpu.VMEM((rows_second, LANES), F32)],
        )
        second_blocks = head_exchange(near, pair)
        second_grad, qkv_grad, proj_grad = call(
            functools.partial(join_second_kernel, rows_conv=rows_conv, rows_qkv=rows_qkv),
            [sds(flats[i].shape, F32) for i in (1, 2, 4)],
            [None, second_own, *second_blocks, pj],
        )
        lines = table_rows + emb_rows
        kept, near, pair, table = call(
            functools.partial(split_first_kernel, rows_conv=rows_conv),
            [
                sds((rows_conv, LANES), F32), sds((rows_conv + 2 * lines, LANES), BF16),
                sds((2, rows_conv + 2 * lines, LANES), BF16), sds((lines, LANES), F32),
            ],
            [None, *first_left, table, emb_part],
            scratch=[pltpu.VMEM((4 * rows_conv, LANES), F32)],
            after=second_blocks[:2],
        )
        first_blocks = head_exchange(near, pair, output, grad_inputs, second_grad)
        first_grad, grad_gains, grad_biases, ada_grad, grad_embedding = call(
            functools.partial(join_first_kernel, rows_conv=rows_conv),
            [sds(flats[0].shape, F32)] + small_outs,
            [None, kept, *first_blocks, table, embs, far_emb],
            scratch=small_scratch + [pltpu.VMEM((lines, LANES), F32)] * 3,
        )
    else:
        table = jnp.concatenate([lax.psum(table, "dp"), emb_part])
        grad_gains, grad_biases, ada_grad, grad_embedding = call(
            small_grads_kernel,
            small_outs,
            [ext, embs, far_emb, *head_gather(table)],
            scratch=small_scratch,
        )
        first_grad, second_grad, qkv_grad, proj_grad = scatter_plain(
            first_parts[0], second_parts[0], ahead_parts[0], spread, channels
        )
    return (
        output.reshape(inputs.shape),
        grad_inputs.reshape(inputs.shape),
        grad_embedding,
        grad_gains,
        grad_biases,
        first_grad.reshape(-1),
        second_grad.reshape(-1),
        qkv_grad.reshape(-1),
        ada_grad.reshape(-1),
        proj_grad.reshape(-1),
    )


def gather_plain(flats, embedding, spread, channels):
    heads = lax.axis_size("head")

    def columns(flat, groups):
        blocks = flat.astype(BF16).reshape(-1, groups, LANES)
        return blocks

    def own_columns(blocks):
        got = lax.all_to_all(blocks, "head", split_axis=1, concat_axis=0, tiled=True)
        return lax.all_gather(got[:, 0], "dp", axis=0, tiled=True)

    first, second = (own_columns(columns(flats[i], heads).reshape(-1, heads, 1, LANES))[:, 0] for i in (0, 1))
    qkv = columns(flats[2], 12).reshape(-1, heads, 2, 3, HD)
    qkv = jnp.swapaxes(qkv, 2, 3).reshape(-1, heads, 3, LANES)
    qkv = jnp.swapaxes(own_columns(qkv), 0, 1).reshape(-1, LANES)
    ada = columns(flats[3], 8).reshape(-1, 2, heads, LANES)
    ada = jnp.swapaxes(own_columns(jnp.swapaxes(ada, 1, 2)), 0, 1).reshape(-1, LANES)
    proj = lax.ppermute(flats[4].astype(BF16), ("dp", "head"), spread)
    proj = lax.all_gather(proj, "dp", axis=0, tiled=True).reshape(-1, channels // LANES, LANES)
    proj = jnp.swapaxes(proj, 0, 1).reshape(-1, LANES)
    embs = lax.all_gather(embedding, "dp", axis=0, tiled=True).astype(F32)
    embs = embs.reshape(embs.shape[0], -1, flats[3].shape[0] // 8)
    embs = lax.dynamic_index_in_dim(
        embs, lax.axis_index("dp") * heads + lax.axis_index("head"), 1, False
    )
    first_piece = jnp.concatenate([first, ada, proj])
    second_piece = jnp.concatenate([second, qkv])
    proj_at = 9 * channels + ada.shape[0]
    return (
        [first_piece],
        (
            (0, 1, 9 * channels),
            (9 * channels, 2, ada.shape[0] // 2),
            (proj_at, channels // LANES, LANES),
        ),
        [second_piece],
        ((0, 1, 9 * channels), (9 * channels, 3, channels)),
        embs,
    )


def scatter_plain(first, second, qkv, spread, channels):
    heads = lax.axis_size("head")

    def rows_of(grad):
        part = lax.psum_scatter(grad, "dp", scatter_dimension=0, tiled=True)
        return lax.all_to_all(part[:, None], "head", split_axis=0, concat_axis=1, tiled=True)

    def conv(grad):
        return rows_of(grad[:, None])

    qkv = jnp.swapaxes(qkv.reshape(3, channels, LANES), 0, 1)
    qkv = rows_of(qkv).reshape(-1, heads, 3, 2, HD)
    qkv = jnp.swapaxes(qkv, 2, 3)
    proj = jnp.swapaxes(second[9 * channels :].reshape(-1, LANES, LANES), 0, 1)
    proj = lax.psum_scatter(proj, "dp", scatter_dimension=0, tiled=True)
    proj = lax.ppermute(proj, ("dp", "head"), [(j, i) for i, j in spread])
    return (conv(first), conv(second[: 9 * channels]), qkv, proj)


def solution(mesh):
    flat = P(("dp", "head"))
    image = P("dp", "head", None, None)
    return jax.shard_map(
        body,
        mesh=mesh,
        in_specs=(image, P("dp", None), P("dp", None), image, P(), P(), flat, flat, flat, flat, flat),
        out_specs=(image, image, P("dp", None), P(), P(), flat, flat, flat, flat, flat),
        check_vma=False,
    )
```

```python
import functools
import math

import jax
import jax.numpy as jnp
from jax import lax
from jax.experimental import pallas as pl
from jax.experimental.pallas import tpu as pltpu
from jax.sharding import PartitionSpec as P

HD = 64
STEP = 512
PROJ_PARTS = 2
MARK = 64
GROUPS = 32
EPS = 1e-05
MASKED = -1e30
LANES = 128
F32 = jnp.float32
BF16 = jnp.bfloat16
VMEM_SPEC = pl.BlockSpec(memory_space=pltpu.VMEM)
SMEM_SPEC = pl.BlockSpec(memory_space=pltpu.SMEM)


def sds(shape, dtype):
    return jax.ShapeDtypeStruct(shape, dtype)


class Far:
    def __init__(self, array, held=True, pinned=False):
        self.array = pltpu.with_memory_space_constraint(array, pltpu.HBM) if pinned else array
        self.held = held


class Fetch:
    def __init__(self, source, ref, sem):
        self.copy = pltpu.make_async_copy(source, ref, sem)
        self.ref = ref
        self.copy.start()

    def get(self):
        self.copy.wait()
        return self.ref


class Store:
    def __init__(self, dest, ref, sem):
        self.dest = dest
        self.ref = ref
        self.sem = sem
        self.copy = None

    def send(self, source=None):
        self.copy = pltpu.make_async_copy(self.ref if source is None else source, self.dest, self.sem)
        self.copy.start()


def call(kernel, outs, args, scratch=(), us=1.0, vmem=24, after=()):
    scalars = args[0] is not None
    args = list(args) if scalars else list(args[1:])
    arrays = [arg.array if isinstance(arg, Far) else arg for arg in args]
    results = [out.array if isinstance(out, Far) else out for out in outs]
    far_in = [isinstance(arg, Far) for arg in args]
    far_out = [isinstance(out, Far) for out in outs]
    held = [
        pltpu.VMEM(x.array.shape, x.array.dtype)
        for x in list(args) + list(outs)
        if isinstance(x, Far) and x.held
    ]
    copies = sum(far_in) + sum(far_out)

    def run(*refs):
        ins = refs[: len(args)]
        begin = len(args) + len(after)
        dests = refs[begin : begin + len(outs)]
        begin += len(outs)
        buffers = iter(refs[begin : begin + len(held)])
        begin += len(held)
        sems = refs[begin] if copies else None
        rest = refs[begin + (1 if copies else 0) :]
        count = 0
        given = []
        for ref, far in zip(ins, far_in):
            if far:
                ref = Fetch(ref, next(buffers), sems.at[count])
                count += 1
            given.append(ref)
        stores = []
        for ref, out in zip(dests, outs):
            if isinstance(out, Far):
                ref = Store(ref, next(buffers) if out.held else None, sems.at[count])
                stores.append(ref)
                count += 1
            given.append(ref)
        kernel(*([] if scalars else [None]), *given, *rest)
        for store in stores:
            store.copy.wait()

    hbm = pl.BlockSpec(memory_space=pltpu.HBM)
    anywhere = pl.BlockSpec(memory_space=pl.ANY)
    return pl.pallas_call(
        run,
        out_shape=tuple(results),
        in_specs=[
            hbm if far else SMEM_SPEC if scalars and i == 0 else VMEM_SPEC
            for i, far in enumerate(far_in)
        ]
        + [anywhere for _ in after],
        out_specs=tuple(hbm if far else VMEM_SPEC for far in far_out),
        scratch_shapes=held
        + ([pltpu.SemaphoreType.DMA((copies,))] if copies else [])
        + list(scratch),
        compiler_params=pltpu.CompilerParams(vmem_limit_bytes=vmem * 1024 * 1024),
        cost_estimate=pl.CostEstimate(
            flops=int(3e7 * us),
            bytes_accessed=1024,
            transcendentals=0,
        ),
    )(*arrays, *after)


def following(value, *earlier):
    return lax.optimization_barrier((value, *earlier))[0]


def hop(value, axis, bit):
    count = lax.axis_size(axis)
    return lax.ppermute(value, axis, [(i, i ^ bit) for i in range(count)])


def head_gather(block, *earlier):
    far = hop(block, "head", 2)
    near = hop(block, "head", 1)
    return (block, near, far, hop(following(far, *earlier) if earlier else far, "head", 1))


def head_exchange(near_block, far_pair, *earlier):
    far = hop(far_pair, "head", 2)
    near = hop(near_block, "head", 1)
    return (near, far, hop(following(far, *earlier) if earlier else far, "head", 1))


def add_kernel(ext, first, second, out):
    out[...] = (first[...].astype(F32) + second[...].astype(F32)).astype(out.dtype)


def head_reduce(ext, blocks, after=()):
    kept, near_block, far_block, corner = blocks
    corner = hop(corner, "head", 1)
    (far_block,) = call(
        add_kernel, [sds(far_block.shape, BF16)], [None, far_block, corner], us=0.7, after=after
    )
    return ((kept, hop(near_block, "head", 1), hop(far_block, "head", 2)), [far_block])


def mm(left, right, left_dim, right_dim):
    return lax.dot_general(
        left, right, (((left_dim,), (right_dim,)), ((), ())), preferred_element_type=F32
    )


def lane_block(index):
    return pl.ds(pl.multiple_of(index * LANES, LANES), LANES)


def row_block(index, rows):
    return pl.ds(pl.multiple_of(index * rows, rows), rows)


def pixel_place(rows, lanes, cols, start=0):
    pixel = lax.broadcasted_iota(jnp.int32, (rows, lanes), 0) + start
    shift = cols.bit_length() - 1
    return (lax.shift_right_logical(pixel, shift), lax.bitwise_and(pixel, cols - 1))


def valid_of(ext, rows, lanes, cols, start=0):
    place_row, place_col = pixel_place(rows, lanes, cols, start)
    inside = jnp.logical_and(place_row < ext[0, 0], place_col < ext[0, 1])
    return jnp.where(inside, 1.0, 0.0).astype(F32)


def group_total(first, second, width):
    lanes = first.shape[-1]
    pick = lax.broadcasted_iota(jnp.int32, (8, lanes), 0)
    both = jnp.where(pick == 0, first, jnp.where(pick == 1, second, 0.0))
    shift = width.bit_length() - 1
    left = lax.shift_right_logical(lax.broadcasted_iota(jnp.int32, (lanes, lanes), 0), shift)
    right = lax.shift_right_logical(lax.broadcasted_iota(jnp.int32, (lanes, lanes), 1), shift)
    same = jnp.where(left == right, 1.0, 0.0).astype(F32)
    total = lax.dot_general(
        both,
        same,
        (((1,), (0,)), ((), ())),
        precision=lax.Precision.HIGHEST,
        preferred_element_type=F32,
    )
    return (total[0:1], total[1:2])


def pixel_count(ext, width):
    return (ext[0, 0] * ext[0, 1] * width).astype(F32)


def col_sum(value):
    return jnp.sum(value, axis=0, keepdims=True)


def head_rank():
    return lax.axis_index("head")


def norm_stats(value, valid, count, width):
    masked = value * valid
    total, square = group_total(col_sum(masked), col_sum(masked * value), width)
    center = total / count
    return (center, lax.rsqrt(square / count - center * center + EPS))


def norm_back(grad, normed, inverse, valid, count, width):
    first, second = group_total(col_sum(grad), col_sum(grad * normed), width)
    return (grad - valid * ((first + normed * second) * (1.0 / count))) * inverse


def silu_grad(value):
    gate = jax.nn.sigmoid(value)
    return gate * (1.0 + value * (1.0 - gate))


def place_pieces(dest, pieces, start, groups, rows):
    for k, piece in enumerate(pieces):
        part = lax.axis_index("dp") ^ k if len(pieces) > 1 else 0
        for group in range(groups):
            begin = start + group * rows
            dest[group, pl.ds(pl.multiple_of(part * rows, rows), rows), :] = piece[
                begin : begin + rows, :
            ]


def taps_side_by_side(flat, wide):
    channels = wide.shape[0]
    for tap in range(9):
        wide[:, tap * LANES : (tap + 1) * LANES] = flat[0, tap * channels : (tap + 1) * channels, :]


def conv_taps(act, wide, taps, cols):
    pixels = act.shape[0]
    lanes = wide.shape[1]
    taps[0:cols, :] = jnp.zeros((cols, lanes), F32)
    taps[pixels + cols :, :] = jnp.zeros((cols, lanes), F32)
    step = STEP

    def one(i, carry):
        begin = pl.multiple_of(i * step, step)
        taps[pl.ds(pl.multiple_of(begin + cols, cols), step), :] = mm(
            act[pl.ds(begin, step), :], wide[...], 1, 0
        )
        return carry

    lax.fori_loop(0, pixels // step, one, 0)


def conv_sum(taps, begin, rows, cols):
    def column(side):
        return sum(
            taps[
                pl.ds(pl.multiple_of(begin + up * cols, cols), rows),
                (up * 3 + side) * LANES : (up * 3 + side + 1) * LANES,
            ]
            for up in range(3)
        )

    place_col = pixel_place(rows, LANES, cols)[1]
    left = jnp.where(place_col > 0, pltpu.roll(column(0), 1, 0), 0.0)
    right = jnp.where(place_col < cols - 1, pltpu.roll(column(2), rows - 1, 0), 0.0)
    return column(1) + left + right


def shifted_grads(grad, dest, cols):
    pixels = grad.shape[0]
    place_col = pixel_place(pixels, LANES, cols)[1]
    sides = (
        jnp.where(place_col < cols - 1, pltpu.roll(grad, pixels - 1, 0), 0.0),
        grad,
        jnp.where(place_col > 0, pltpu.roll(grad, 1, 0), 0.0),
    )
    blank = jnp.zeros((cols, LANES), BF16)
    for side, value in enumerate(sides):
        low = value.astype(BF16)
        for up in range(3):
            lanes = slice((up * 3 + side) * LANES, (up * 3 + side + 1) * LANES)
            if up == 0:
                dest[0 : pixels - cols, lanes] = low[cols:, :]
                dest[pixels - cols :, lanes] = blank
            elif up == 1:
                dest[:, lanes] = low
            else:
                dest[cols:, lanes] = low[0 : pixels - cols, :]
                dest[0:cols, lanes] = blank


def partial_sums(left, right, whole, outs):
    step = STEP

    def one(i, carry):
        rows = pl.ds(pl.multiple_of(i * step, step), step)
        whole[rows, :] = mm(left[rows, :], right[...], 1, 1)
        return carry

    lax.fori_loop(0, left.shape[0] // step, one, 0)
    rank = head_rank()
    for k, out in enumerate(outs):
        out[...] = whole[:, lane_block(rank ^ k)].astype(out.dtype)


def weights_out_kernel(ext, *refs):
    first, second, qkv, ada, proj = refs[0:5]
    kept, near, pair, pj = refs[5:]
    rank = head_rank()
    low_half = lax.broadcasted_iota(jnp.int32, (qkv.ref.shape[0] // 12, LANES), 1) < HD
    first, second, qkv, ada, proj = (x.get() for x in (first, second, qkv, ada, proj))

    def strided(ref, begin, stride):
        return ref[pl.ds(begin, ref.shape[0] // stride, stride=stride), :]

    def put(dest, begin, value):
        rows = value.shape[0]
        dest[begin : begin + rows, :] = value.astype(BF16)
        return begin + rows

    at = 0
    for g in range(4):
        at = put(pj, at, strided(proj, g, 4))
    for k, dest in enumerate((kept, near, pair.at[0], pair.at[1])):
        peer = rank ^ k
        at = put(dest, 0, strided(first, peer, 4))
        for side in range(2):
            at = put(dest, at, strided(ada, 4 * side + peer, 8))
        at = put(dest, at, strided(second, peer, 4))
        part = [strided(qkv, peer * 3 + g, 12) for g in range(3)]
        at = put(dest, at, jnp.where(low_half, part[0], part[1]))
        at = put(dest, at, pltpu.roll(jnp.where(low_half, part[2], part[0]), HD, 1))
        put(dest, at, jnp.where(low_half, part[1], part[2]))


def join_blocks(dest, blocks, source, segments):
    rank = head_rank()
    for k, block in enumerate(blocks):
        at, begin = (source, 0)
        for rows in segments:
            place = pl.ds(pl.multiple_of(begin + (rank ^ k) * rows, 16), rows)
            dest[place, :] = block[at : at + rows, :]
            at += rows
            begin += 4 * rows
    return 4 * sum(segments)


def first_piece_kernel(ext, kept, near, far, corner, emb, proj, piece, line, *, segments):
    at = join_blocks(piece, (kept, near, far.at[0], corner.at[1]), 0, segments)
    emb = emb.get()
    line[...] = jnp.zeros(line.shape, F32)
    for j in range(emb.shape[1] // LANES):
        line[j : j + 1, :] = emb[0:1, j * LANES : (j + 1) * LANES].astype(F32)
    piece[at : at + 16, :] = line[...].astype(BF16)
    piece[at + 16 :, :] = proj[...]


def second_piece_kernel(ext, kept, near, far, corner, piece, *, source, segments):
    join_blocks(piece, (kept, near, far.at[0], corner.at[1]), source, segments)


def dp_straight(piece):
    return [piece] + [hop(piece, "dp", k) for k in (2, 4, 6)]


def dp_stepwise(piece):
    far = hop(piece, "dp", 4)
    return [piece, hop(piece, "dp", 2), far, hop(far, "dp", 2)]


def dp_beside(straight, chained=(), last_four=False):
    own, two, four, six = straight
    near = [hop(value, "dp", 1) for value in (own, two)]
    if chained:
        other = hop(six if last_four else four, "dp", 1)
        waits = [*near, other] if last_four else []
        final = hop(following(four if last_four else six, *waits, *chained), "dp", 1)
        near += [final, other] if last_four else [other, final]
    else:
        near += [hop(four, "dp", 1), hop(six, "dp", 1)]
    return [value for pair in zip(straight, near) for value in pair]


def norm_first_kernel(ext, gains, biases, *refs, cols, width):
    blocks = refs[0:4]
    act, own_out, stats, held = refs[4:]
    own = own_out.ref
    rank = head_rank()
    rows, channels = blocks[0].shape
    count = pixel_count(ext, width)
    total = jnp.zeros((1, channels), F32)
    square = jnp.zeros((1, channels), F32)
    for k, block in enumerate(blocks):
        own[row_block(rank ^ k, rows), :] = block[:, lane_block(rank)]
    own_out.send()
    for k, block in enumerate(blocks):
        value = block[...].astype(F32)
        masked = value * valid_of(ext, rows, channels, cols, (rank ^ k) * rows)
        total = total + col_sum(masked)
        square = square + col_sum(masked * value)
    total, square = group_total(total, square, width)
    center = total / count
    inverse = lax.rsqrt(square / count - center * center + EPS)
    held[0:1, :] = center
    held[1:2, :] = inverse
    gain, bias = (gains.get()[0:1, :], biases.get()[0:1, :])
    for k, block in enumerate(blocks):
        peer = rank ^ k
        pre = (block[...].astype(F32) - center) * inverse * gain + bias
        valid = valid_of(ext, rows, channels, cols, peer * rows)
        act[row_block(peer, rows), :] = (pre * jax.nn.sigmoid(pre) * valid).astype(BF16)
    stats[...] = held[:, lane_block(rank)]


def conv_first_kernel(ext, biases, act, emb, *refs, cols, width, count_pieces, segments, emb_at):
    pieces = refs[0:count_pieces]
    act_out, normed_out, aux, wide_out, ada_out, act_far = refs[count_pieces : count_pieces + 6]
    w_proj = refs[count_pieces + 6 : -4 if emb_at is None else -5]
    flat, taps, hidden, proj = refs[-4:]
    rank = head_rank()
    pixels = act.shape[0]
    act_far.send(act)
    place_pieces(flat, pieces, *segments[0])
    wide = wide_out.ref
    taps_side_by_side(flat, wide)
    wide_out.send()
    ada = ada_out.ref
    place_pieces(ada, pieces, *segments[1])
    ada_out.send()
    place_pieces(proj, pieces, *segments[2])
    if len(w_proj) == 1:
        for g in range(proj.shape[0]):
            w_proj[0][:, g * LANES : (g + 1) * LANES] = proj[g]
    else:
        kept, near, pair = w_proj
        for k, dest in enumerate((kept, near, pair.at[0], pair.at[1])):
            for g in range(proj.shape[0]):
                dest[g] = proj[g, row_block(rank ^ k, dest.shape[1]), :]
    if emb_at is not None:
        table = refs[-5]
        place = lax.axis_index("dp")
        table[...] = jnp.zeros(table.shape, F32)
        for k, piece in enumerate(pieces):
            lines = piece[emb_at : emb_at + 16, :].astype(F32)
            mine = lax.broadcasted_iota(jnp.int32, lines.shape, 0) == place
            table[pl.ds(place ^ k, 1), :] = col_sum(jnp.where(mine, lines, 0.0))
    conv_taps(act, wide, taps, cols)
    biases = biases.get()
    bias = biases[1:2, lane_block(rank)]
    step = 256
    for i in range(pixels // step):
        hidden[i * step : (i + 1) * step, :] = conv_sum(taps, i * step, step, cols) + bias
    value = hidden[...]
    valid = valid_of(ext, pixels, LANES, cols)
    center, inverse = norm_stats(value, valid, pixel_count(ext, width), width)
    normed = (value - center) * inverse
    normed_out.ref[...] = normed
    normed_out.send()
    emb_value = emb.get()[...].astype(F32)
    emb_act = (emb_value * jax.nn.sigmoid(emb_value)).astype(BF16).astype(F32)
    mods = []
    for side in range(2):
        mod = biases[2 + side : 3 + side, lane_block(rank)]
        for j in range(emb_act.shape[1] // LANES):
            lanes = slice(j * LANES, (j + 1) * LANES)
            row = jnp.broadcast_to(emb_act[:, lanes], (16, LANES)).astype(BF16)
            mod = mod + mm(row, ada[side, lanes, :], 1, 0)[0:1]
        mods.append(mod)
    pre = normed * (1.0 + mods[0]) + mods[1]
    act_out[...] = (pre * jax.nn.sigmoid(pre) * valid).astype(BF16)
    aux[...] = jnp.zeros(aux.shape, F32)
    aux[0:1, :] = inverse
    aux[1:2, :] = mods[0]
    aux[2:3, :] = mods[1]


def conv_second_kernel(ext, gains, biases, own, *refs, cols, width, count_pieces, segments):
    blocks = refs[0:4]
    pieces = refs[4 : 4 + count_pieces]
    attn_in, act_out, residual_out, normed_out, aux, wide_out, w_qkv = refs[4 + count_pieces : -3]
    flat, qkv, taps = refs[-3:]
    rank = head_rank()
    act, wide, residual = (act_out.ref, wide_out.ref, residual_out.ref)
    pixels = act.shape[0]
    for k, block in enumerate(blocks):
        act[:, lane_block(rank ^ k)] = block[...]
    act_out.send()
    place_pieces(flat, pieces, *segments[0])
    taps_side_by_side(flat, wide)
    wide_out.send()
    place_pieces(qkv, pieces, *segments[1])
    for g in range(3):
        w_qkv[:, g * LANES : (g + 1) * LANES] = qkv[g]
    conv_taps(act, wide, taps, cols)
    gains, biases, own = (gains.get(), biases.get(), own.get())
    bias = biases[4:5, lane_block(rank)]
    step = 256
    for i in range(pixels // step):
        rows = slice(i * step, (i + 1) * step)
        third = conv_sum(taps, i * step, step, cols) + bias
        valid = valid_of(ext, step, LANES, cols, i * step)
        residual[rows, :] = own[rows, :].astype(F32) + valid * third
    residual_out.send()
    value = residual[...]
    valid = valid_of(ext, pixels, LANES, cols)
    center, inverse = norm_stats(value, valid, pixel_count(ext, width), width)
    normed = (value - center) * inverse
    normed_out.ref[...] = normed
    normed_out.send()
    attn_in[...] = (
        normed * gains[1:2, lane_block(rank)] + biases[5:6, lane_block(rank)]
    ).astype(BF16)
    aux[...] = jnp.broadcast_to(inverse, aux.shape)


def cotangent_kernel(ext, *refs):
    cots = refs[0:4]
    full_out, own_out, att, att_t, rows_weight = refs[-5:]
    rank = head_rank()
    rows = cots[0].shape[0]
    for k, cot in enumerate(cots):
        at = row_block(rank ^ k, rows)
        full_out.ref[at, :] = cot[...]
        own_out.ref[at, :] = cot[:, lane_block(rank)]
    full_out.send()
    own_out.send()
    weights = refs[4:-5]
    if len(weights) == 1:
        rows_weight[...] = weights[0][...]
    else:
        kept, near, far, corner = weights
        count = len(cots)
        size = LANES // (count * PROJ_PARTS)
        for k, block in enumerate((kept, near, far.at[0], corner.at[1])):
            for part in range(PROJ_PARTS):
                at = pl.ds(pl.multiple_of((part * count + (rank ^ k)) * size, 16), size)
                for g in range(block.shape[0]):
                    lanes = slice(g * LANES, (g + 1) * LANES)
                    rows_weight[at, lanes] = block[g, part * size : (part + 1) * size, :]
    for i in range(4):
        at = slice(i * rows, (i + 1) * rows)
        grad = mm(full_out.ref[at, :], rows_weight[...], 1, 1).astype(BF16)
        att[at, :] = grad
        att_t[:, at] = grad.astype(F32).T


def attention_kernel(ext, *refs, cols):
    blocks = refs[0:4]
    wide, cot_att, cot_att_t = refs[4:7]
    outs = refs[7:11]
    full_out, grads_out, attended_out = refs[11:14]
    qkv, keys_t, values_t, grad_kv, whole = refs[14:]
    attn_full, grads, attended = (full_out.ref, grads_out.ref, attended_out.ref)
    rank = head_rank()
    pixels = attn_full.shape[0]
    scale = 1.0 / math.sqrt(HD)
    for k in range(4):
        attn_full[:, lane_block(rank ^ k)] = blocks[k][...]
    full_out.send()
    step = 256
    qkv[...] = mm(attn_full[...], wide[...], 1, 0).astype(BF16)
    for i in range(pixels // step):
        at = slice(i * step, (i + 1) * step)
        keys_t[:, at] = qkv[at, LANES : 2 * LANES].astype(F32).T.astype(BF16)
        values_t[:, at] = qkv[at, 2 * LANES :].astype(F32).T.astype(BF16)
    lane = lax.broadcasted_iota(jnp.int32, (pixels, LANES), 1)
    sublane = lax.broadcasted_iota(jnp.int32, (LANES, pixels), 0)
    key_row, key_col = pixel_place(pixels, pixels, cols)
    key_valid = jnp.logical_and(key_row < ext[0, 0], key_col < ext[0, 1])
    att_sum = jnp.zeros((LANES, pixels), F32)
    query_sum = jnp.zeros((LANES, pixels), F32)
    for h in range(LANES // HD):
        mine = lax.shift_right_logical(lane, 6) == h
        mine_t = lax.shift_right_logical(sublane, 6) == h
        query = jnp.where(mine, qkv[:, 0:LANES], jnp.zeros((pixels, LANES), BF16))
        cot = jnp.where(mine, cot_att[...], jnp.zeros((pixels, LANES), BF16))
        scores = mm(qkv[:, LANES : 2 * LANES], query, 1, 1) * scale
        scores = jnp.where(key_valid, scores, MASKED)
        top = jnp.max(scores, axis=0, keepdims=True)
        expo = jnp.exp(scores - top)
        probs = expo * (1.0 / col_sum(expo))
        probs_low = probs.astype(BF16)
        att = mm(jnp.where(mine_t, values_t[...], jnp.zeros((LANES, pixels), BF16)), probs_low, 1, 0)
        att_sum = att_sum + att
        row_dot = col_sum(att * cot_att_t[...])
        grad_probs = mm(qkv[:, 2 * LANES :], cot, 1, 1)
        grad_scores = (probs * (grad_probs - row_dot)).astype(BF16)
        grad_values = mm(probs_low, cot, 1, 0)
        grad_keys = mm(grad_scores, query, 1, 0)
        if h == 0:
            grad_kv[:, LANES:] = grad_values
            grad_kv[:, 0:LANES] = grad_keys
        else:
            grad_kv[:, LANES:] += grad_values
            grad_kv[:, 0:LANES] += grad_keys
        query_sum = query_sum + mm(
            jnp.where(mine_t, keys_t[...], jnp.zeros((LANES, pixels), BF16)), grad_scores, 1, 0
        )
    attended[...] = att_sum.T.astype(BF16)
    grads[:, 0:LANES] = (query_sum.T * scale).astype(BF16)
    attended_out.send()
    grads[:, LANES : 2 * LANES] = (grad_kv[:, 0:LANES] * scale).astype(BF16)
    grads[:, 2 * LANES :] = grad_kv[:, LANES:].astype(BF16)
    grads_out.send()
    partial_sums(grads, wide, whole, outs)


def out_partial_kernel(ext, biases, attended, rows_weight, residual, cot, *refs):
    outs = refs[0:4]
    grads = refs[4:-1]
    whole = refs[-1]
    rank = head_rank()
    rows = outs[0].shape[0]
    attended = attended.get()
    for i in range(4):
        at = slice(i * rows, (i + 1) * rows)
        whole[at, :] = mm(attended[at, :], rows_weight[...], 1, 0)
    bias = biases.get()[6:7, lane_block(rank)]
    whole[:, lane_block(rank)] += residual.get()[...] + bias
    for k, out in enumerate(outs):
        out[...] = whole[row_block(rank ^ k, rows), :].astype(out.dtype)
    whole[0:LANES, :] = mm(attended[...], cot.get()[...], 0, 0)
    if len(grads) == 1:
        for g in range(grads[0].shape[0]):
            grads[0][g] = whole[0:LANES, g * LANES : (g + 1) * LANES]
    else:
        kept, near, pair = grads
        count = len(outs)
        size = LANES // (count * PROJ_PARTS)
        for k, dest in enumerate((kept, near, pair.at[0], pair.at[1])):
            for part in range(PROJ_PARTS):
                at = row_block(part * count + (rank ^ k), size)
                for g in range(dest.shape[0]):
                    dest[g, part * size : (part + 1) * size, :] = whole[
                        at, g * LANES : (g + 1) * LANES
                    ].astype(BF16)


def sum_kernel(ext, first, second, third, out):
    out[...] = (first[...] + second[...].astype(F32) + third[...].astype(F32)).astype(out.dtype)


def norm_third_back_kernel(ext, gains, kept, near, far, normed, inverse, cot, wide, *refs, cols, width):
    outs = refs[0:4]
    grad_res, third_out, sums, shifted, whole = refs[4:]
    rank = head_rank()
    pixels = kept.shape[0]
    grad = kept[...] + near[...].astype(F32) + far[...].astype(F32)
    normed, gains, cot = (normed.get()[...], gains.get(), cot.get())
    valid = valid_of(ext, pixels, LANES, cols)
    back = norm_back(
        grad * gains[1:2, lane_block(rank)], normed, inverse[0:1, :], valid,
        pixel_count(ext, width), width,
    )
    cot_value = cot[...].astype(F32)
    residual = cot_value + back
    grad_res.ref[...] = residual
    grad_res.send()
    third = (valid * residual).astype(BF16)
    third_out[...] = third
    third = third.astype(F32)
    shifted_grads(third, shifted, cols)
    sums[...] = jnp.zeros(sums.shape, F32)
    sums[0:1, :] = col_sum(grad * normed)
    sums[1:2, :] = col_sum(grad)
    sums[2:3, :] = col_sum(third)
    sums[3:4, :] = col_sum(cot_value)
    partial_sums(shifted, wide.get(), whole, outs)


def norm_second_back_kernel(ext, kept, near, far, normed, aux, wide, *refs, cols, width):
    outs = refs[0:4]
    first_out, sums, shifted, whole = refs[4:]
    pixels = kept.shape[0]
    grad_act = kept[...] + near[...].astype(F32) + far[...].astype(F32)
    normed = normed.get()[...]
    valid = valid_of(ext, pixels, LANES, cols)
    inverse, scale, shift = (aux[0:1, :], aux[1:2, :], aux[2:3, :])
    grad_pre = grad_act * valid * silu_grad(normed * (1.0 + scale) + shift)
    back = norm_back(
        grad_pre * (1.0 + scale), normed, inverse, valid, pixel_count(ext, width), width
    )
    first = back.astype(BF16)
    first_out[...] = first
    first = first.astype(F32)
    shifted_grads(first, shifted, cols)
    sums[...] = jnp.zeros(sums.shape, F32)
    sums[0:1, :] = col_sum(grad_pre * normed).astype(BF16).astype(F32)
    sums[1:2, :] = col_sum(grad_pre).astype(BF16).astype(F32)
    sums[2:3, :] = col_sum(first)
    partial_sums(shifted, wide.get(), whole, outs)


def norm_first_back_kernel(
    ext, gains, biases, kept, near, far, own, stats, grad_res, sums_third, sums_second, *refs,
    cols, width,
):
    out_kept, out_near, out_pair, table, held = refs
    rank = head_rank()
    pixels = kept.shape[0]
    rows = out_kept.shape[0]
    grad_act = kept[...] + near[...].astype(F32) + far[...].astype(F32)
    valid = valid_of(ext, pixels, LANES, cols)
    center, inverse = (stats[0:1, :], stats[1:2, :])
    normed = (own.get()[...].astype(F32) - center) * inverse
    gain = gains.get()[0:1, lane_block(rank)]
    bias = biases.get()[0:1, lane_block(rank)]
    grad_pre = grad_act * valid * silu_grad(normed * gain + bias)
    back = norm_back(grad_pre * gain, normed, inverse, valid, pixel_count(ext, width), width)
    held[...] = grad_res.get()[...] + back
    out_kept[...] = held[row_block(rank, rows), :]
    out_near[...] = held[row_block(rank ^ 1, rows), :].astype(BF16)
    for k in (2, 3):
        out_pair[k - 2] = held[row_block(rank ^ k, rows), :].astype(BF16)
    table[...] = jnp.zeros(table.shape, F32)
    table[0:1, :] = col_sum(grad_pre * normed)
    table[1:2, :] = sums_third[0:1, :]
    table[2:3, :] = col_sum(grad_pre)
    table[3:4, :] = sums_second[2:3, :]
    table[4:6, :] = sums_second[0:2, :]
    table[6:7, :] = sums_third[2:3, :]
    table[7:8, :] = sums_third[1:2, :]
    table[8:9, :] = sums_third[3:4, :]
    table[pl.ds(16 + 2 * lax.axis_index("dp"), 2), :] = sums_second[0:2, :]


def put_exact(dest, begin, value):
    rows = value.shape[0]
    high = value.astype(BF16)
    dest[begin : begin + rows, :] = high
    dest[begin + rows : begin + 2 * rows, :] = (value - high.astype(F32)).astype(BF16)


def get_exact(source, begin, rows):
    high = source[begin : begin + rows, :].astype(F32)
    return high + source[begin + rows : begin + 2 * rows, :].astype(F32)


def rows_join_kernel(ext, kept, near, far, corner, out):
    rank = head_rank()
    for k, block in enumerate((kept, near, far.at[0], corner.at[1])):
        out[:, lane_block(rank ^ k)] = block[...].astype(F32)


def taps_grad(act, shifted, flat):
    channels = act.shape[1]
    for i in range(channels // LANES):
        part = mm(act[:, i * LANES : (i + 1) * LANES], shifted[...], 0, 0)
        for tap in range(9):
            flat[0, tap * channels + i * LANES : tap * channels + (i + 1) * LANES, :] = part[
                :, tap * LANES : (tap + 1) * LANES
            ]


def dp_parts(dests, sources, dp_count):
    place = lax.axis_index("dp") if dp_count > 1 else 0
    for k, dest in enumerate(dests):
        at = 0
        for source in sources:
            size = source.shape[1] // dp_count
            for g in range(source.shape[0]):
                dest[at : at + size, :] = source[g, row_block(place ^ k, size), :].astype(dest.dtype)
                at += size


def qkv_grads_kernel(ext, attn, grads, *refs, dp_count):
    dests = refs[0:-1]
    qkv = refs[-1]
    part = mm(attn.get()[...], grads.get()[...], 0, 0)
    for g in range(3):
        qkv[g] = part[:, g * LANES : (g + 1) * LANES]
    if dp_count > 1:
        own, two, four, six, pairs = dests
        dests = (own, pairs.at[3], two, pairs.at[0], four, pairs.at[2], six, pairs.at[1])
    dp_parts(dests, (qkv,), dp_count)


def second_grads_kernel(ext, third, act, *refs, cols, dp_count):
    grad_proj = refs[0 : 4 if dp_count > 1 else 1]
    dests = refs[len(grad_proj) : -3]
    shifted, flat, proj = refs[-3:]
    shifted_grads(third[...].astype(F32), shifted, cols)
    act = act.get()
    taps_grad(act, shifted, flat)
    if len(grad_proj) == 1:
        proj[...] = grad_proj[0][...]
    else:
        kept, near, far, corner = grad_proj
        rank = head_rank()
        for k, block in enumerate((kept, near, far.at[0], corner.at[1])):
            size = block.shape[1]
            for g in range(proj.shape[0]):
                proj[g, row_block(rank ^ k, size), :] = block[g].astype(F32)
    dp_parts(split_dests(dests), (flat, proj), dp_count)


def split_dests(dests):
    if len(dests) == 1:
        return dests
    own, two, four, six, first_pair, second_pair = dests
    return (
        own, second_pair.at[1], two, first_pair.at[0], four, second_pair.at[0], six, first_pair.at[1]
    )


def first_grads_kernel(ext, first, act, sums, ada, *refs, cols, dp_count):
    dests = refs[0:-3]
    emb_part, shifted, flat = refs[-3:]
    shifted_grads(first[...].astype(F32), shifted, cols)
    taps_grad(act.get(), shifted, flat)
    dp_parts(split_dests(dests), (flat,), dp_count)
    ada = ada.get()
    for j in range(emb_part.shape[0]):
        row = jnp.zeros((1, LANES), F32)
        for side in range(2):
            mod = jnp.broadcast_to(sums[side : side + 1, :], (16, LANES)).astype(BF16)
            row = row + mm(mod, ada[side, j * LANES : (j + 1) * LANES, :], 1, 1)[0:1]
        emb_part[j : j + 1, :] = row


def near_kernel(ext, other, two, six, out):
    size = two.shape[0]
    for k, mine in enumerate((two, six)):
        out[k, 0:size, :] = (mine[...].astype(F32) + other[k].astype(F32)).astype(BF16)


def near_both_kernel(ext, other, two, six, ahead, ahead_two, ahead_six, out):
    size = two.shape[0]
    near_kernel(ext, other, two, six, out.at[:, pl.ds(0, size)])
    near_kernel(ext, ahead, ahead_two, ahead_six, out.at[:, pl.ds(size, ahead_two.shape[0])])


def near_table_kernel(ext, other, two, six, table, beside, out, total):
    size = two.shape[0]
    near_kernel(ext, other, two, six, out)
    total[...] = table[...] + beside[...]
    put_exact(out.at[0], size, total[...])
    out[1, size:, :] = jnp.zeros((out.shape[1] - size, LANES), BF16)


def far_kernel(ext, four, late, near, out):
    size = four.shape[0]
    value = four[...].astype(F32) + late[0].astype(F32) + near[1, 0:size, :].astype(F32)
    out[0:size, :] = value.astype(BF16)


def far_both_kernel(ext, four, late, ahead_four, ahead, near, out):
    size = four.shape[0]
    far_kernel(ext, four, late, near, out)
    rows = pl.ds(size, ahead_four.shape[0])
    far_kernel(ext, ahead_four, ahead.at[pl.ds(2, 2)], near.at[:, rows], out.at[rows])


def far_table_kernel(ext, four, late, near, table, out, total):
    size = four.shape[0]
    far_kernel(ext, four, late, near, out)
    total[...] = table[...] + get_exact(near.at[0], size, table.shape[0])
    put_exact(out, size, total[...])


def dp_pairs(parts):
    early = hop(parts[4], "dp", 1)
    return (early, hop(following(parts[5], early), "dp", 1))


def split_second_kernel(
    ext, own, late, ahead_own, ahead, straight, far, kept, near, pair, proj, held, *,
    rows_conv, rows_qkv,
):
    rank = head_rank()
    size = own.shape[0]
    held[...] = straight[0].astype(F32) + far[...].astype(F32)
    held[0:size, :] += own[...] + late[1].astype(F32)
    held[size:, :] += ahead_own[...] + ahead[3].astype(F32)
    for k, dest in enumerate((kept, near, pair.at[0], pair.at[1])):
        peer = rank ^ k
        dest[0:rows_conv, :] = held[row_block(peer, rows_conv), :].astype(dest.dtype)
        for g in range(3):
            begin = size + g * 4 * rows_qkv
            dest[rows_conv + g * rows_qkv : rows_conv + (g + 1) * rows_qkv, :] = held[
                pl.ds(pl.multiple_of(begin + peer * rows_qkv, 8), rows_qkv), :
            ].astype(dest.dtype)
    proj[...] = held[4 * rows_conv : size, :]


def split_first_kernel(
    ext, own, late, straight, far, table, emb_part, kept, near, pair, total, held, *, rows_conv
):
    rank = head_rank()
    size = held.shape[0]
    lines = table.shape[0]
    held[...] = own[...] + sum(
        part[0:size, :].astype(F32) for part in (late.at[1], straight.at[0], far)
    )
    total[0:lines, :] = table[...] + get_exact(far, size, lines)
    total[lines:, :] = emb_part[...]
    kept[...] = held[row_block(rank, rows_conv), :]
    for k, dest in enumerate((near, pair.at[0], pair.at[1])):
        dest[0:rows_conv, :] = held[row_block(rank ^ (k + 1), rows_conv), :].astype(BF16)
        put_exact(dest, rows_conv, total[...])


def join_second_kernel(ext, kept, near, far, corner, proj, conv_out, qkv_out, proj_out, *, rows_conv, rows_qkv):
    rank = head_rank()
    rows_proj = proj.shape[0] // 4
    low_half = lax.broadcasted_iota(jnp.int32, (rows_qkv, LANES), 1) < HD
    for k, block in enumerate((kept, near, far.at[0], corner.at[1])):
        peer = rank ^ k
        conv_out[pl.ds(peer, rows_conv, stride=4), :] = block[0:rows_conv, :].astype(F32)
        part = [
            block[rows_conv + g * rows_qkv : rows_conv + (g + 1) * rows_qkv, :].astype(F32)
            for g in range(3)
        ]
        keys = pltpu.roll(part[1], HD, 1)
        mixed = (
            jnp.where(low_half, part[0], keys),
            jnp.where(low_half, part[2], part[0]),
            jnp.where(low_half, keys, part[2]),
        )
        for g in range(3):
            qkv_out[pl.ds(peer * 3 + g, rows_qkv, stride=12), :] = mixed[g]
    for g in range(4):
        proj_out[pl.ds(g, rows_proj, stride=4), :] = proj[
            g * rows_proj : (g + 1) * rows_proj, :
        ].astype(F32)


def join_first_kernel(
    ext, kept, near, far, corner, total, embs, emb, conv_out, *refs, rows_conv
):
    rank = head_rank()
    outs, (mods, table, held, t1, t2, t3) = (refs[:4], refs[4:])
    blocks = (near, far.at[0], corner.at[1])
    conv_out[pl.ds(rank, rows_conv, stride=4), :] = kept[...]
    for k, (block, other) in enumerate(zip(blocks, (t1, t2, t3))):
        conv_out[pl.ds(rank ^ (k + 1), rows_conv, stride=4), :] = block[0:rows_conv, :].astype(F32)
        other[...] = get_exact(block, rows_conv, other.shape[0])
    small_grads_kernel(ext, embs, emb, total, t1, t2, t3, *outs, mods, table, held)


def small_grads_kernel(ext, embs, emb, t0, t1, t2, t3, gains_out, biases_out, ada_out, emb_out, mods, table, held):
    rank = head_rank()
    images = embs.shape[0]
    for k, block in enumerate((t0, t1, t2, t3)):
        table[:, lane_block(rank ^ k)] = block[0:16, :]
        for side in range(2):
            mods[:, lane_block(side * 4 + (rank ^ k))] = block[pl.ds(16 + side, images, stride=2), :]
    gains_out[...] = table[0:2, :]
    biases_out[...] = table[2:9, :]
    value = embs[...]
    part = mm((value * jax.nn.sigmoid(value)).astype(BF16), mods[...].astype(BF16), 0, 0)
    rows = ada_out.shape[0] // 8
    if part.shape[0] != rows:
        held[...] = part
        part = held[row_block(rank, rows), :]
    for g in range(8):
        ada_out[pl.ds(g, rows, stride=8), :] = part[:, g * LANES : (g + 1) * LANES]
    value = emb.get()[...].astype(F32)
    slope = silu_grad(value)
    begin = 16 + 2 * images
    for j in range(value.shape[1] // LANES):
        lanes = slice(j * LANES, (j + 1) * LANES)
        total = sum(block[begin + j : begin + j + 1, :] for block in (t0, t1, t2, t3))
        emb_out[:, lanes] = total * slope[:, lanes]


def body(
    inputs, embedding, extent, cotangent, gains, biases,
    conv_first, conv_second, qkv_master, ada_master, proj_master,
):
    heads = lax.axis_size("head")
    dps = lax.axis_size("dp")
    batch, row_count, cols, channels = inputs.shape
    rows = row_count * cols
    pixels = rows * heads
    width = channels // GROUPS
    emb_rows = embedding.shape[1] // LANES
    ext = extent
    direct = dps == 8
    flats = [
        master.reshape(-1, LANES)
        for master in (conv_first, conv_second, qkv_master, ada_master, proj_master)
    ]
    rows_conv = flats[0].shape[0] // 4
    rows_qkv = flats[2].shape[0] // 12
    rows_ada = flats[3].shape[0] // 8
    rows_proj = flats[4].shape[0] // 4
    far_gains, far_biases, far_emb = (Far(x, pinned=True) for x in (gains, biases, embedding))
    spread = [(i, (i % dps) * heads + i // dps) for i in range(dps * heads)]
    inputs_own = inputs.reshape(rows, channels)
    cot_own = cotangent.reshape(rows, channels)
    if direct:
        rows_a = rows_conv + 2 * rows_ada
        rows_b = rows_conv + 3 * rows_qkv
        rows_ab = rows_a + rows_b
        kept, near, pair, pj = call(
            weights_out_kernel,
            [
                sds((rows_ab, LANES), BF16), sds((rows_ab, LANES), BF16),
                sds((2, rows_ab, LANES), BF16), sds((4 * rows_proj, LANES), BF16),
            ],
            [None] + [Far(flat, pinned=True) for flat in flats],
        )
        rows_second = 4 * rows_conv + 12 * rows_qkv + 4 * rows_proj
        blocks = (kept, *head_exchange(near, pair))
        (first_piece,) = call(
            functools.partial(first_piece_kernel, segments=(rows_conv, rows_ada, rows_ada)),
            [sds((4 * rows_conv + 8 * rows_ada + 16 + 4 * rows_proj, LANES), BF16)],
            [None, *blocks, far_emb, pj],
            scratch=[pltpu.VMEM((16, LANES), F32)],
        )
        (second_piece,) = call(
            functools.partial(
                second_piece_kernel, source=rows_a, segments=(rows_conv,) + (rows_qkv,) * 3
            ),
            [sds((rows_second - 4 * rows_proj, LANES), BF16)],
            [None, *blocks],
        )
        first_straight = dp_straight(first_piece)
        inputs_sent = following(inputs_own, first_piece)
        second_straight = dp_stepwise(second_piece)
        proj_at = 4 * rows_conv + 8 * rows_ada + 16
        first_segments = (
            (0, 1, 4 * rows_conv),
            (4 * rows_conv, 2, 4 * rows_ada),
            (proj_at, 4, rows_proj),
        )
        second_segments = ((0, 1, 4 * rows_conv), (4 * rows_conv, 3, 4 * rows_qkv))
    else:
        first_pieces, first_segments, second_pieces, second_segments, embs = gather_plain(
            flats, embedding, spread, channels
        )
        inputs_sent = inputs_own

    blocks = head_gather(inputs_sent)
    act_first, own, stats_first = call(
        functools.partial(norm_first_kernel, cols=cols, width=width),
        [sds((pixels, channels), BF16), Far(sds((pixels, LANES), BF16)), sds((8, LANES), F32)],
        [ext, far_gains, far_biases, *blocks],
        scratch=[pltpu.VMEM((8, channels), F32)],
        us=2.0,
    )
    if direct:
        first_pieces = dp_beside(first_straight, [first_piece], True)
    cots = head_gather(following(cot_own, blocks[2]))
    wide_shape = (channels, 9 * LANES)
    taps_scratch = pltpu.VMEM((pixels + 2 * cols, 9 * LANES), F32)
    flat_scratch = pltpu.VMEM((1, 9 * channels, LANES), BF16)
    n_pieces = len(first_pieces)
    groups = channels // LANES
    if direct:
        part = (groups, LANES // heads, LANES)
        proj_outs = [sds(part, BF16), sds(part, BF16), sds((2, *part), BF16)]
    else:
        proj_outs = [sds((LANES, channels), BF16)]
    first_outs = call(
        functools.partial(
            conv_first_kernel, cols=cols, width=width, count_pieces=n_pieces,
            segments=first_segments,
            emb_at=4 * rows_conv + 8 * rows_ada if direct else None,
        ),
        [
            sds((pixels, LANES), BF16), Far(sds((pixels, LANES), F32)), sds((8, LANES), F32),
            Far(sds(wide_shape, BF16)), Far(sds((2, emb_rows * LANES, LANES), BF16)),
            Far(sds((pixels, channels), BF16), held=False),
        ]
        + proj_outs
        + ([sds((dps, LANES), F32)] if direct else []),
        [ext, far_biases, act_first, far_emb, *first_pieces],
        scratch=[
            flat_scratch,
            taps_scratch,
            pltpu.VMEM((pixels, LANES), F32),
            pltpu.VMEM((groups, LANES, LANES), BF16),
        ],
        us=4.0,
    )
    act_second_own, normed_second, aux_second, wide_first, ada_full, act_first = first_outs[:6]
    w_proj = first_outs[6 : 6 + len(proj_outs)]
    if direct:
        embs = first_outs[-1]
        w_proj = (w_proj[0], *head_exchange(*w_proj[1:]))
        second_pieces = dp_beside(second_straight)
        mark = []
        act_second_own = following(act_second_own, second_pieces[1], second_straight[1])
    blocks = head_gather(act_second_own, *([second_pieces[3], second_pieces[5]] if direct else []))
    attn_own, act_second, residual, normed_third, aux_third, wide_second, w_qkv = call(
        functools.partial(
            conv_second_kernel, cols=cols, width=width, count_pieces=n_pieces,
            segments=second_segments,
        ),
        [
            sds((pixels, LANES), BF16), Far(sds((pixels, channels), BF16)),
            Far(sds((pixels, LANES), F32)), Far(sds((pixels, LANES), F32)), sds((8, LANES), F32),
            Far(sds(wide_shape, BF16)), sds((channels, 3 * LANES), BF16),
        ],
        [ext, far_gains, far_biases, Far(own), *blocks, *second_pieces],
        scratch=[
            flat_scratch,
            pltpu.VMEM((3, channels, LANES), BF16),
            taps_scratch,
        ],
        us=4.0,
        after=w_proj[1:] if direct else (),
    )
    cot_full, cot_own, cot_att, cot_att_t, rows_weight = call(
        cotangent_kernel,
        [
            Far(sds((pixels, channels), BF16)), Far(sds((pixels, LANES), BF16)),
            sds((pixels, LANES), BF16), sds((LANES, pixels), F32), sds((LANES, channels), BF16),
        ],
        [None, *cots, *w_proj],
    )
    blocks = head_gather(attn_own, cot_att)
    whole_scratch = pltpu.VMEM((pixels, channels), F32)
    shifted_scratch = pltpu.VMEM((pixels, 9 * LANES), BF16)
    split_outs = [sds((pixels, LANES), F32)] + [sds((pixels, LANES), BF16)] * 3
    *parts, attn_full, grads_qkv, attended = call(
        functools.partial(attention_kernel, cols=cols),
        split_outs
        + [
            Far(sds((pixels, channels), BF16)), Far(sds((pixels, 3 * LANES), BF16)),
            Far(sds((pixels, LANES), BF16)),
        ],
        [ext, *blocks, w_qkv, cot_att, cot_att_t],
        scratch=[
            pltpu.VMEM((pixels, 3 * LANES), BF16),
            pltpu.VMEM((LANES, pixels), BF16),
            pltpu.VMEM((LANES, pixels), BF16),
            pltpu.VMEM((pixels, 2 * LANES), F32),
            whole_scratch,
        ],
        us=15.0,
    )
    parts, _ = head_reduce(ext, parts)
    grad_outs = proj_outs if direct else [sds((groups, LANES, LANES), F32)]
    out_all = call(
        out_partial_kernel,
        [sds((rows, channels), F32)] + [sds((rows, channels), BF16)] * 3 + grad_outs,
        [None, far_biases, Far(attended), rows_weight, Far(residual), Far(cot_full)],
        scratch=[whole_scratch],
        us=2.0,
    )
    out_parts, grad_proj = (out_all[:4], out_all[4:])
    if direct:
        grad_proj = (grad_proj[0], *head_exchange(*grad_proj[1:]))
    n_dests = dps if direct else 1

    def grad_outs(size):
        size = size // n_dests
        if not direct:
            return [sds((size, LANES), F32)]
        one = sds((size, LANES), BF16)
        return [sds((size, LANES), F32), one, one, one] + [sds((2, size, LANES), BF16)] * 2

    ahead_outs = grad_outs(3 * channels)
    if direct:
        ahead_outs = ahead_outs[:4] + [sds((4, *ahead_outs[1].shape), BF16)]
    ahead_parts = call(
        functools.partial(qkv_grads_kernel, dp_count=n_dests),
        ahead_outs,
        [None, Far(attn_full), Far(grads_qkv)],
        scratch=[pltpu.VMEM((3, channels, LANES), F32)],
        after=out_parts[:1],
    )
    if direct:
        ahead = hop(ahead_parts[4], "dp", 1)
    *parts, grad_res, third, sums_third = call(
        functools.partial(norm_third_back_kernel, cols=cols, width=width),
        split_outs
        + [Far(sds((pixels, LANES), F32)), sds((pixels, LANES), BF16), sds((8, LANES), F32)],
        [
            ext, far_gains, *parts, Far(normed_third), aux_third, Far(cot_own), Far(wide_second),
        ],
        scratch=[shifted_scratch, whole_scratch],
        us=150.0,
        after=ahead_parts[:1],
    )
    if direct:
        parts[3] = following(parts[3], *grad_proj[1:3], ahead)
    out_sums, _ = head_reduce(ext, out_parts)
    (output,) = call(sum_kernel, [sds((rows, channels), BF16)], [None, *out_sums])
    parts, sent = head_reduce(ext, parts)
    flat_grad = pltpu.VMEM((1, 9 * channels, LANES), F32)
    second_parts = call(
        functools.partial(second_grads_kernel, cols=cols, dp_count=n_dests),
        grad_outs(10 * channels),
        [None, third, Far(act_second), *grad_proj],
        scratch=[
            shifted_scratch,
            flat_grad,
            pltpu.VMEM((channels // LANES, LANES, LANES), F32),
        ],
        us=4.0,
        after=sent,
    )
    *parts, first, sums_second = call(
        functools.partial(norm_second_back_kernel, cols=cols, width=width),
        split_outs + [sds((pixels, LANES), BF16), sds((8, LANES), F32)],
        [ext, *parts, Far(normed_second), aux_second, Far(wide_first)],
        scratch=[shifted_scratch, whole_scratch],
        us=150.0,
        after=second_parts[:1],
    )
    if direct:
        second_pairs = dp_pairs(second_parts)
    parts, sent = head_reduce(ext, parts, second_pairs[:1] if direct else ())
    *first_parts, emb_part = call(
        functools.partial(first_grads_kernel, cols=cols, dp_count=n_dests),
        grad_outs(9 * channels) + [sds((emb_rows, LANES), F32)],
        [ext, first, Far(act_first), sums_second, Far(ada_full)],
        scratch=[shifted_scratch, flat_grad],
        us=3.0,
        after=sent,
    )
    table_rows = 16 + 2 * dps
    early = [emb_part]
    if direct:
        first_early, first_late = (hop(pair, "dp", 1) for pair in first_parts[4:6])
        (near_pair,) = call(
            near_both_kernel,
            [sds((2, rows_second, LANES), BF16)],
            [
                None, second_pairs[0], second_parts[1], second_parts[3], ahead, ahead_parts[1],
                ahead_parts[3],
            ],
            us=0.6,
            after=sent,
        )
        early += [near_pair, second_pairs[1]]
        second_near = hop(near_pair, "dp", 2)
    kept_rows, near, pair, table = call(
        functools.partial(norm_first_back_kernel, cols=cols, width=width),
        [
            sds((rows, LANES), F32), sds((rows, LANES), BF16), sds((2, rows, LANES), BF16),
            sds((table_rows, LANES), F32),
        ],
        [
            ext, far_gains, far_biases, *parts, Far(own), stats_first, Far(grad_res), sums_third,
            sums_second,
        ],
        scratch=[pltpu.VMEM((pixels, LANES), F32)],
        us=40.0,
        after=early,
    )
    small_outs = [
        sds(gains.shape, F32), sds(biases.shape, F32), sds(flats[3].shape, F32),
        sds(embedding.shape, F32),
    ]
    small_scratch = [
        pltpu.VMEM((dps, 8 * LANES), F32),
        pltpu.VMEM((16, channels), F32),
        pltpu.VMEM((LANES, 8 * LANES), F32),
    ]
    if direct:
        beside = hop(table, "dp", 1)
        (far_block,) = call(
            far_both_kernel,
            [sds((rows_second, LANES), BF16)],
            [None, second_parts[2], second_pairs[1], ahead_parts[2], ahead, second_near],
            us=0.6,
            after=[kept_rows],
        )
        second_left = [
            second_parts[0], second_pairs[1], ahead_parts[0], ahead, second_near,
            hop(far_block, "dp", 4),
        ]
        size = 4 * rows_conv + 2 * table_rows
        near_pair, table = call(
            near_table_kernel,
            [sds((2, size, LANES), BF16), sds(table.shape, F32)],
            [None, first_early, first_parts[1], first_parts[3], table, beside],
            us=0.6,
        )
        first_near = hop(near_pair, "dp", 2)
        far_block, table = call(
            far_table_kernel,
            [sds((size, LANES), BF16), sds(table.shape, F32)],
            [None, first_parts[2], first_late, first_near, table],
            us=0.6,
            after=[far_block],
        )
        first_left = [first_parts[0], first_late, first_near, hop(far_block, "dp", 4)]
    (grad_inputs,) = call(
        rows_join_kernel,
        [sds((rows, channels), F32)],
        [None, kept_rows, *head_exchange(near, pair)],
    )
    if direct:
        second_own, near, pair, pj = call(
            functools.partial(split_second_kernel, rows_conv=rows_conv, rows_qkv=rows_qkv),
            [
                sds((rows_b, LANES), F32), sds((rows_b, LANES), BF16),
                sds((2, rows_b, LANES), BF16), sds((4 * rows_proj, LANES), F32),
            ],
            [None, *second_left],
            scratch=[pltpu.VMEM((rows_second, LANES), F32)],
        )
        second_blocks = head_exchange(near, pair)
        second_grad, qkv_grad, proj_grad = call(
            functools.partial(join_second_kernel, rows_conv=rows_conv, rows_qkv=rows_qkv),
            [sds(flats[i].shape, F32) for i in (1, 2, 4)],
            [None, second_own, *second_blocks, pj],
        )
        lines = table_rows + emb_rows
        kept, near, pair, table = call(
            functools.partial(split_first_kernel, rows_conv=rows_conv),
            [
                sds((rows_conv, LANES), F32), sds((rows_conv + 2 * lines, LANES), BF16),
                sds((2, rows_conv + 2 * lines, LANES), BF16), sds((lines, LANES), F32),
            ],
            [None, *first_left, table, emb_part],
            scratch=[pltpu.VMEM((4 * rows_conv, LANES), F32)],
            after=second_blocks[:2],
        )
        first_blocks = head_exchange(near, pair, output, grad_inputs, second_grad)
        first_grad, grad_gains, grad_biases, ada_grad, grad_embedding = call(
            functools.partial(join_first_kernel, rows_conv=rows_conv),
            [sds(flats[0].shape, F32)] + small_outs,
            [None, kept, *first_blocks, table, embs, far_emb],
            scratch=small_scratch + [pltpu.VMEM((lines, LANES), F32)] * 3,
        )
    else:
        table = jnp.concatenate([lax.psum(table, "dp"), emb_part])
        grad_gains, grad_biases, ada_grad, grad_embedding = call(
            small_grads_kernel,
            small_outs,
            [ext, embs, far_emb, *head_gather(table)],
            scratch=small_scratch,
        )
        first_grad, second_grad, qkv_grad, proj_grad = scatter_plain(
            first_parts[0], second_parts[0], ahead_parts[0], spread, channels
        )
    return (
        output.reshape(inputs.shape),
        grad_inputs.reshape(inputs.shape),
        grad_embedding,
        grad_gains,
        grad_biases,
        first_grad.reshape(-1),
        second_grad.reshape(-1),
        qkv_grad.reshape(-1),
        ada_grad.reshape(-1),
        proj_grad.reshape(-1),
    )


def gather_plain(flats, embedding, spread, channels):
    heads = lax.axis_size("head")

    def columns(flat, groups):
        blocks = flat.astype(BF16).reshape(-1, groups, LANES)
        return blocks

    def own_columns(blocks):
        got = lax.all_to_all(blocks, "head", split_axis=1, concat_axis=0, tiled=True)
        return lax.all_gather(got[:, 0], "dp", axis=0, tiled=True)

    first, second = (own_columns(columns(flats[i], heads).reshape(-1, heads, 1, LANES))[:, 0] for i in (0, 1))
    qkv = columns(flats[2], 12).reshape(-1, heads, 2, 3, HD)
    qkv = jnp.swapaxes(qkv, 2, 3).reshape(-1, heads, 3, LANES)
    qkv = jnp.swapaxes(own_columns(qkv), 0, 1).reshape(-1, LANES)
    ada = columns(flats[3], 8).reshape(-1, 2, heads, LANES)
    ada = jnp.swapaxes(own_columns(jnp.swapaxes(ada, 1, 2)), 0, 1).reshape(-1, LANES)
    proj = lax.ppermute(flats[4].astype(BF16), ("dp", "head"), spread)
    proj = lax.all_gather(proj, "dp", axis=0, tiled=True).reshape(-1, channels // LANES, LANES)
    proj = jnp.swapaxes(proj, 0, 1).reshape(-1, LANES)
    embs = lax.all_gather(embedding, "dp", axis=0, tiled=True).astype(F32)
    embs = embs.reshape(embs.shape[0], -1, flats[3].shape[0] // 8)
    embs = lax.dynamic_index_in_dim(
        embs, lax.axis_index("dp") * heads + lax.axis_index("head"), 1, False
    )
    first_piece = jnp.concatenate([first, ada, proj])
    second_piece = jnp.concatenate([second, qkv])
    proj_at = 9 * channels + ada.shape[0]
    return (
        [first_piece],
        (
            (0, 1, 9 * channels),
            (9 * channels, 2, ada.shape[0] // 2),
            (proj_at, channels // LANES, LANES),
        ),
        [second_piece],
        ((0, 1, 9 * channels), (9 * channels, 3, channels)),
        embs,
    )


def scatter_plain(first, second, qkv, spread, channels):
    heads = lax.axis_size("head")

    def rows_of(grad):
        part = lax.psum_scatter(grad, "dp", scatter_dimension=0, tiled=True)
        return lax.all_to_all(part[:, None], "head", split_axis=0, concat_axis=1, tiled=True)

    def conv(grad):
        return rows_of(grad[:, None])

    qkv = jnp.swapaxes(qkv.reshape(3, channels, LANES), 0, 1)
    qkv = rows_of(qkv).reshape(-1, heads, 3, 2, HD)
    qkv = jnp.swapaxes(qkv, 2, 3)
    proj = jnp.swapaxes(second[9 * channels :].reshape(-1, LANES, LANES), 0, 1)
    proj = lax.psum_scatter(proj, "dp", scatter_dimension=0, tiled=True)
    proj = lax.ppermute(proj, ("dp", "head"), [(j, i) for i, j in spread])
    return (conv(first), conv(second[: 9 * channels]), qkv, proj)


def solution(mesh):
    flat = P(("dp", "head"))
    image = P("dp", "head", None, None)
    return jax.shard_map(
        body,
        mesh=mesh,
        in_specs=(image, P("dp", None), P("dp", None), image, P(), P(), flat, flat, flat, flat, flat),
        out_specs=(image, image, P("dp", None), P(), P(), flat, flat, flat, flat, flat),
        check_vma=False,
    )
```

```python
import functools
import math

import jax
import jax.numpy as jnp
from jax import lax
from jax.experimental import pallas as pl
from jax.experimental.pallas import tpu as pltpu
from jax.sharding import PartitionSpec as P

HD = 64
TOKEN = 96
STEP = 512
PROJ_PARTS = 2
MARK = 64
GROUPS = 32
EPS = 1e-05
MASKED = -1e30
LANES = 128
F32 = jnp.float32
BF16 = jnp.bfloat16
VMEM_SPEC = pl.BlockSpec(memory_space=pltpu.VMEM)
SMEM_SPEC = pl.BlockSpec(memory_space=pltpu.SMEM)


def sds(shape, dtype):
    return jax.ShapeDtypeStruct(shape, dtype)


class Far:
    def __init__(self, array, held=True, pinned=False):
        self.array = pltpu.with_memory_space_constraint(array, pltpu.HBM) if pinned else array
        self.held = held


class Fetch:
    def __init__(self, source, ref, sem):
        self.copy = pltpu.make_async_copy(source, ref, sem)
        self.ref = ref
        self.copy.start()

    def get(self):
        self.copy.wait()
        return self.ref


class Store:
    def __init__(self, dest, ref, sem):
        self.dest = dest
        self.ref = ref
        self.sem = sem
        self.copy = None

    def send(self, source=None):
        self.copy = pltpu.make_async_copy(self.ref if source is None else source, self.dest, self.sem)
        self.copy.start()


def call(kernel, outs, args, scratch=(), us=1.0, vmem=24, after=()):
    scalars = args[0] is not None
    args = list(args) if scalars else list(args[1:])
    arrays = [arg.array if isinstance(arg, Far) else arg for arg in args]
    results = [out.array if isinstance(out, Far) else out for out in outs]
    far_in = [isinstance(arg, Far) for arg in args]
    far_out = [isinstance(out, Far) for out in outs]
    held = [
        pltpu.VMEM(x.array.shape, x.array.dtype)
        for x in list(args) + list(outs)
        if isinstance(x, Far) and x.held
    ]
    copies = sum(far_in) + sum(far_out)

    def run(*refs):
        ins = refs[: len(args)]
        begin = len(args) + len(after)
        dests = refs[begin : begin + len(outs)]
        begin += len(outs)
        buffers = iter(refs[begin : begin + len(held)])
        begin += len(held)
        sems = refs[begin] if copies else None
        rest = refs[begin + (1 if copies else 0) :]
        count = 0
        given = []
        for ref, far in zip(ins, far_in):
            if far:
                ref = Fetch(ref, next(buffers), sems.at[count])
                count += 1
            given.append(ref)
        stores = []
        for ref, out in zip(dests, outs):
            if isinstance(out, Far):
                ref = Store(ref, next(buffers) if out.held else None, sems.at[count])
                stores.append(ref)
                count += 1
            given.append(ref)
        kernel(*([] if scalars else [None]), *given, *rest)
        for store in stores:
            store.copy.wait()

    hbm = pl.BlockSpec(memory_space=pltpu.HBM)
    anywhere = pl.BlockSpec(memory_space=pl.ANY)
    return pl.pallas_call(
        run,
        out_shape=tuple(results),
        in_specs=[
            hbm if far else SMEM_SPEC if scalars and i == 0 else VMEM_SPEC
            for i, far in enumerate(far_in)
        ]
        + [anywhere for _ in after],
        out_specs=tuple(hbm if far else VMEM_SPEC for far in far_out),
        scratch_shapes=held
        + ([pltpu.SemaphoreType.DMA((copies,))] if copies else [])
        + list(scratch),
        compiler_params=pltpu.CompilerParams(vmem_limit_bytes=vmem * 1024 * 1024),
        cost_estimate=pl.CostEstimate(
            flops=int(3e7 * us),
            bytes_accessed=1024,
            transcendentals=0,
        ),
    )(*arrays, *after)


def following(value, *earlier):
    return lax.optimization_barrier((value, *earlier))[0]


def hop(value, axis, bit):
    count = lax.axis_size(axis)
    return lax.ppermute(value, axis, [(i, i ^ bit) for i in range(count)])


def head_gather(block, *earlier):
    far = hop(block, "head", 2)
    near = hop(block, "head", 1)
    return (block, near, far, hop(following(far, *earlier) if earlier else far, "head", 1))


def head_exchange(near_block, far_pair, *earlier):
    far = hop(far_pair, "head", 2)
    near = hop(near_block, "head", 1)
    return (near, far, hop(following(far, *earlier) if earlier else far, "head", 1))


def add_kernel(ext, first, second, out):
    out[...] = (first[...].astype(F32) + second[...].astype(F32)).astype(out.dtype)


def head_reduce(ext, blocks, after=()):
    kept, near_block, far_block, corner = blocks
    corner = hop(corner, "head", 1)
    (far_block,) = call(
        add_kernel, [sds(far_block.shape, BF16)], [None, far_block, corner], us=0.7, after=after
    )
    return ((kept, hop(near_block, "head", 1), hop(far_block, "head", 2)), [far_block])


def mm(left, right, left_dim, right_dim):
    return lax.dot_general(
        left, right, (((left_dim,), (right_dim,)), ((), ())), preferred_element_type=F32
    )


def lane_block(index):
    return pl.ds(pl.multiple_of(index * LANES, LANES), LANES)


def row_block(index, rows):
    return pl.ds(pl.multiple_of(index * rows, rows), rows)


def pixel_place(rows, lanes, cols, start=0):
    pixel = lax.broadcasted_iota(jnp.int32, (rows, lanes), 0) + start
    shift = cols.bit_length() - 1
    return (lax.shift_right_logical(pixel, shift), lax.bitwise_and(pixel, cols - 1))


def valid_of(ext, rows, lanes, cols, start=0):
    place_row, place_col = pixel_place(rows, lanes, cols, start)
    inside = jnp.logical_and(place_row < ext[0, 0], place_col < ext[0, 1])
    return jnp.where(inside, 1.0, 0.0).astype(F32)


def group_total(first, second, width):
    lanes = first.shape[-1]
    pick = lax.broadcasted_iota(jnp.int32, (8, lanes), 0)
    both = jnp.where(pick == 0, first, jnp.where(pick == 1, second, 0.0))
    shift = width.bit_length() - 1
    left = lax.shift_right_logical(lax.broadcasted_iota(jnp.int32, (lanes, lanes), 0), shift)
    right = lax.shift_right_logical(lax.broadcasted_iota(jnp.int32, (lanes, lanes), 1), shift)
    same = jnp.where(left == right, 1.0, 0.0).astype(F32)
    total = lax.dot_general(
        both,
        same,
        (((1,), (0,)), ((), ())),
        precision=lax.Precision.HIGHEST,
        preferred_element_type=F32,
    )
    return (total[0:1], total[1:2])


def pixel_count(ext, width):
    return (ext[0, 0] * ext[0, 1] * width).astype(F32)


def col_sum(value):
    return jnp.sum(value, axis=0, keepdims=True)


def head_rank():
    return lax.axis_index("head")


def norm_stats(value, valid, count, width):
    masked = value * valid
    total, square = group_total(col_sum(masked), col_sum(masked * value), width)
    center = total / count
    return (center, lax.rsqrt(square / count - center * center + EPS))


def norm_back(grad, normed, inverse, valid, count, width):
    first, second = group_total(col_sum(grad), col_sum(grad * normed), width)
    return (grad - valid * ((first + normed * second) * (1.0 / count))) * inverse


def silu_grad(value):
    gate = jax.nn.sigmoid(value)
    return gate * (1.0 + value * (1.0 - gate))


def place_pieces(dest, pieces, start, groups, rows):
    for k, piece in enumerate(pieces):
        part = lax.axis_index("dp") ^ k if len(pieces) > 1 else 0
        for group in range(groups):
            begin = start + group * rows
            dest[group, pl.ds(pl.multiple_of(part * rows, rows), rows), :] = piece[
                begin : begin + rows, :
            ]


def taps_side_by_side(flat, wide):
    channels = wide.shape[0]
    for tap in range(9):
        wide[:, tap * LANES : (tap + 1) * LANES] = flat[0, tap * channels : (tap + 1) * channels, :]


def conv_taps(act, wide, taps, cols):
    pixels = act.shape[0]
    lanes = wide.shape[1]
    taps[0:cols, :] = jnp.zeros((cols, lanes), F32)
    taps[pixels + cols :, :] = jnp.zeros((cols, lanes), F32)
    step = STEP

    def one(i, carry):
        begin = pl.multiple_of(i * step, step)
        taps[pl.ds(pl.multiple_of(begin + cols, cols), step), :] = mm(
            act[pl.ds(begin, step), :], wide[...], 1, 0
        )
        return carry

    lax.fori_loop(0, pixels // step, one, 0)


def conv_sum(taps, begin, rows, cols):
    def column(side):
        return sum(
            taps[
                pl.ds(pl.multiple_of(begin + up * cols, cols), rows),
                (up * 3 + side) * LANES : (up * 3 + side + 1) * LANES,
            ]
            for up in range(3)
        )

    place_col = pixel_place(rows, LANES, cols)[1]
    left = jnp.where(place_col > 0, pltpu.roll(column(0), 1, 0), 0.0)
    right = jnp.where(place_col < cols - 1, pltpu.roll(column(2), rows - 1, 0), 0.0)
    return column(1) + left + right


def shifted_grads(grad, dest, cols):
    pixels = grad.shape[0]
    place_col = pixel_place(pixels, LANES, cols)[1]
    sides = (
        jnp.where(place_col < cols - 1, pltpu.roll(grad, pixels - 1, 0), 0.0),
        grad,
        jnp.where(place_col > 0, pltpu.roll(grad, 1, 0), 0.0),
    )
    blank = jnp.zeros((cols, LANES), BF16)
    for side, value in enumerate(sides):
        low = value.astype(BF16)
        for up in range(3):
            lanes = slice((up * 3 + side) * LANES, (up * 3 + side + 1) * LANES)
            if up == 0:
                dest[0 : pixels - cols, lanes] = low[cols:, :]
                dest[pixels - cols :, lanes] = blank
            elif up == 1:
                dest[:, lanes] = low
            else:
                dest[cols:, lanes] = low[0 : pixels - cols, :]
                dest[0:cols, lanes] = blank


def partial_sums(left, right, whole, outs):
    step = STEP

    def one(i, carry):
        rows = pl.ds(pl.multiple_of(i * step, step), step)
        whole[rows, :] = mm(left[rows, :], right[...], 1, 1)
        return carry

    lax.fori_loop(0, left.shape[0] // step, one, 0)
    rank = head_rank()
    for k, out in enumerate(outs):
        out[...] = whole[:, lane_block(rank ^ k)].astype(out.dtype)


def strided(ref, begin, stride):
    return ref[pl.ds(begin, ref.shape[0] // stride, stride=stride), :]


def put_rows(dest, begin, value):
    rows = value.shape[0]
    dest[begin : begin + rows, :] = value.astype(BF16)
    return begin + rows


def first_out_kernel(ext, first, ada, proj, kept, near, pair, parts):
    rank = head_rank()
    first, ada = (first.get(), ada.get())
    for k, dest in enumerate((kept, near, pair.at[0], pair.at[1])):
        at = put_rows(dest, 0, strided(first, rank ^ k, 4))
        for side in range(2):
            at = put_rows(dest, at, strided(ada, 4 * side + (rank ^ k), 8))
    proj = proj.get()
    at = 0
    for g in range(4):
        at = put_rows(parts, at, strided(proj, g, 4))


def second_out_kernel(ext, second, qkv, image, kept, near, far):
    rank = head_rank()
    second, qkv, image = (second.get(), qkv.get(), image.get())
    low_half = lax.broadcasted_iota(jnp.int32, (qkv.shape[0] // 12, LANES), 1) < HD
    rows = image.shape[0]
    groups = image.shape[1] // LANES
    for g in range(groups):
        far[g * rows : (g + 1) * rows, :] = image[:, g * LANES : (g + 1) * LANES]
    begin = groups * rows
    size = kept.shape[0]
    blocks = (kept, near, far.at[pl.ds(begin, size)], far.at[pl.ds(begin + size, size)])
    for k, dest in enumerate(blocks):
        at = put_rows(dest, 0, strided(second, rank ^ k, 4))
        part = [strided(qkv, (rank ^ k) * 3 + g, 12) for g in range(3)]
        at = put_rows(dest, at, jnp.where(low_half, part[0], part[1]))
        at = put_rows(dest, at, pltpu.roll(jnp.where(low_half, part[2], part[0]), HD, 1))
        put_rows(dest, at, jnp.where(low_half, part[1], part[2]))


def join_blocks(dest, blocks, segments):
    rank = head_rank()
    for k, block in enumerate(blocks):
        at, begin = (0, 0)
        for rows in segments:
            place = pl.ds(pl.multiple_of(begin + (rank ^ k) * rows, 16), rows)
            dest[place, :] = block[at : at + rows, :]
            at += rows
            begin += 4 * rows
    return 4 * sum(segments)


def first_piece_kernel(ext, kept, near, far, corner, emb, proj, piece, line, *, segments):
    at = join_blocks(piece, (kept, near, far.at[0], corner.at[1]), segments)
    emb = emb.get()
    line[...] = jnp.zeros(line.shape, F32)
    for j in range(emb.shape[1] // LANES):
        line[j : j + 1, :] = emb[0:1, j * LANES : (j + 1) * LANES].astype(F32)
    piece[at : at + 16, :] = line[...].astype(BF16)
    piece[at + 16 :, :] = proj[...]


def second_piece_kernel(ext, kept, near, far, corner, piece, *, segments):
    size = kept.shape[0]
    begin = far.shape[0] - 2 * size
    blocks = (kept, near, far.at[pl.ds(begin, size)], corner.at[pl.ds(begin + size, size)])
    join_blocks(piece, blocks, segments)


def dp_stepwise(piece):
    far = hop(piece, "dp", 4)
    return [piece, hop(piece, "dp", 2), far, hop(far, "dp", 2)]


def dp_beside(straight):
    near = [hop(value, "dp", 1) for value in straight]
    return [value for pair in zip(straight, near) for value in pair]


def dp_beside_in_turn(straight, token):
    own, two, four, six = straight
    own = hop(own, "dp", 1)
    two_near = hop(following(two, own), "dp", 1)
    token = hop(following(token, two_near), "head", 1)
    four_near = hop(four, "dp", 1)
    six_near = hop(following(six, token, four_near), "dp", 1)
    near = (own, two_near, four_near, six_near)
    return ([value for pair in zip(straight, near) for value in pair], token)


def norm_first_kernel(ext, gains, biases, *refs, cols, width):
    blocks = refs[0:4]
    act, own_out, stats, held = refs[4:]
    own = own_out.ref
    rank = head_rank()
    rows, channels = blocks[0].shape
    count = pixel_count(ext, width)
    total = jnp.zeros((1, channels), F32)
    square = jnp.zeros((1, channels), F32)
    def whole(block):
        if block.shape[1] == channels:
            return block[...].astype(F32)
        parts = [block[g * rows : (g + 1) * rows, :] for g in range(channels // LANES)]
        return jnp.concatenate(parts, axis=1).astype(F32)

    for k, block in enumerate(blocks):
        if block.shape[1] == channels:
            own[row_block(rank ^ k, rows), :] = block[:, lane_block(rank)]
        else:
            own[row_block(rank ^ k, rows), :] = block[row_block(rank, rows), :]
    own_out.send()
    for k, block in enumerate(blocks):
        value = whole(block)
        masked = value * valid_of(ext, rows, channels, cols, (rank ^ k) * rows)
        total = total + col_sum(masked)
        square = square + col_sum(masked * value)
    total, square = group_total(total, square, width)
    center = total / count
    inverse = lax.rsqrt(square / count - center * center + EPS)
    held[0:1, :] = center
    held[1:2, :] = inverse
    gain, bias = (gains.get()[0:1, :], biases.get()[0:1, :])
    for k, block in enumerate(blocks):
        peer = rank ^ k
        pre = (whole(block) - center) * inverse * gain + bias
        valid = valid_of(ext, rows, channels, cols, peer * rows)
        act[row_block(peer, rows), :] = (pre * jax.nn.sigmoid(pre) * valid).astype(BF16)
    stats[...] = held[:, lane_block(rank)]


def conv_first_kernel(ext, biases, act, emb, *refs, cols, width, count_pieces, segments, emb_at):
    pieces = refs[0:count_pieces]
    act_out, normed_out, aux, wide_out, ada_out, act_far = refs[count_pieces : count_pieces + 6]
    w_proj = refs[count_pieces + 6 : -4 if emb_at is None else -5]
    flat, taps, hidden, proj = refs[-4:]
    rank = head_rank()
    pixels = act.shape[0]
    act_far.send(act)
    place_pieces(flat, pieces, *segments[0])
    wide = wide_out.ref
    taps_side_by_side(flat, wide)
    wide_out.send()
    ada = ada_out.ref
    place_pieces(ada, pieces, *segments[1])
    ada_out.send()
    place_pieces(proj, pieces, *segments[2])
    if len(w_proj) == 1:
        for g in range(proj.shape[0]):
            w_proj[0][:, g * LANES : (g + 1) * LANES] = proj[g]
    else:
        kept, near, pair = w_proj
        for k, dest in enumerate((kept, near, pair.at[0], pair.at[1])):
            for g in range(proj.shape[0]):
                dest[g] = proj[g, row_block(rank ^ k, dest.shape[1]), :]
    if emb_at is not None:
        table = refs[-5]
        place = lax.axis_index("dp")
        table[...] = jnp.zeros(table.shape, F32)
        for k, piece in enumerate(pieces):
            lines = piece[emb_at : emb_at + 16, :].astype(F32)
            mine = lax.broadcasted_iota(jnp.int32, lines.shape, 0) == place
            table[pl.ds(place ^ k, 1), :] = col_sum(jnp.where(mine, lines, 0.0))
    conv_taps(act, wide, taps, cols)
    biases = biases.get()
    bias = biases[1:2, lane_block(rank)]
    step = 256
    for i in range(pixels // step):
        hidden[i * step : (i + 1) * step, :] = conv_sum(taps, i * step, step, cols) + bias
    value = hidden[...]
    valid = valid_of(ext, pixels, LANES, cols)
    center, inverse = norm_stats(value, valid, pixel_count(ext, width), width)
    normed = (value - center) * inverse
    normed_out.ref[...] = normed
    normed_out.send()
    emb_value = emb.get()[...].astype(F32)
    emb_act = (emb_value * jax.nn.sigmoid(emb_value)).astype(BF16).astype(F32)
    mods = []
    for side in range(2):
        mod = biases[2 + side : 3 + side, lane_block(rank)]
        for j in range(emb_act.shape[1] // LANES):
            lanes = slice(j * LANES, (j + 1) * LANES)
            row = jnp.broadcast_to(emb_act[:, lanes], (16, LANES)).astype(BF16)
            mod = mod + mm(row, ada[side, lanes, :], 1, 0)[0:1]
        mods.append(mod)
    pre = normed * (1.0 + mods[0]) + mods[1]
    act_out[...] = (pre * jax.nn.sigmoid(pre) * valid).astype(BF16)
    aux[...] = jnp.zeros(aux.shape, F32)
    aux[0:1, :] = inverse
    aux[1:2, :] = mods[0]
    aux[2:3, :] = mods[1]


def conv_second_kernel(ext, gains, biases, own, *refs, cols, width, count_pieces, segments):
    blocks = refs[0:4]
    pieces = refs[4 : 4 + count_pieces]
    attn_in, act_out, residual_out, normed_out, aux, wide_out, w_qkv = refs[4 + count_pieces : -3]
    flat, qkv, taps = refs[-3:]
    rank = head_rank()
    act, wide, residual = (act_out.ref, wide_out.ref, residual_out.ref)
    pixels = act.shape[0]
    for k, block in enumerate(blocks):
        act[:, lane_block(rank ^ k)] = block[...]
    act_out.send()
    place_pieces(flat, pieces, *segments[0])
    taps_side_by_side(flat, wide)
    wide_out.send()
    place_pieces(qkv, pieces, *segments[1])
    for g in range(3):
        w_qkv[:, g * LANES : (g + 1) * LANES] = qkv[g]
    conv_taps(act, wide, taps, cols)
    gains, biases, own = (gains.get(), biases.get(), own.get())
    bias = biases[4:5, lane_block(rank)]
    step = 256
    for i in range(pixels // step):
        rows = slice(i * step, (i + 1) * step)
        third = conv_sum(taps, i * step, step, cols) + bias
        valid = valid_of(ext, step, LANES, cols, i * step)
        residual[rows, :] = own[rows, :].astype(F32) + valid * third
    residual_out.send()
    value = residual[...]
    valid = valid_of(ext, pixels, LANES, cols)
    center, inverse = norm_stats(value, valid, pixel_count(ext, width), width)
    normed = (value - center) * inverse
    normed_out.ref[...] = normed
    normed_out.send()
    attn_in[...] = (
        normed * gains[1:2, lane_block(rank)] + biases[5:6, lane_block(rank)]
    ).astype(BF16)
    aux[...] = jnp.broadcast_to(inverse, aux.shape)


def cotangent_kernel(ext, *refs):
    cots = refs[0:4]
    full_out, own_out, att, att_t, rows_weight = refs[-5:]
    rank = head_rank()
    rows = cots[0].shape[0]
    for k, cot in enumerate(cots):
        at = row_block(rank ^ k, rows)
        full_out.ref[at, :] = cot[...]
        own_out.ref[at, :] = cot[:, lane_block(rank)]
    full_out.send()
    own_out.send()
    weights = refs[4:-5]
    if len(weights) == 1:
        rows_weight[...] = weights[0][...]
    else:
        kept, near, far, corner = weights
        count = len(cots)
        size = LANES // (count * PROJ_PARTS)
        for k, block in enumerate((kept, near, far.at[0], corner.at[1])):
            for part in range(PROJ_PARTS):
                at = pl.ds(pl.multiple_of((part * count + (rank ^ k)) * size, 16), size)
                for g in range(block.shape[0]):
                    lanes = slice(g * LANES, (g + 1) * LANES)
                    rows_weight[at, lanes] = block[g, part * size : (part + 1) * size, :]
    for i in range(4):
        at = slice(i * rows, (i + 1) * rows)
        grad = mm(full_out.ref[at, :], rows_weight[...], 1, 1).astype(BF16)
        att[at, :] = grad
        att_t[:, at] = grad.astype(F32).T


def attention_kernel(ext, *refs, cols):
    blocks = refs[0:4]
    wide, cot_att, cot_att_t = refs[4:7]
    outs = refs[7:11]
    full_out, grads_out, attended_out = refs[11:14]
    qkv, keys_t, values_t, grad_kv, whole = refs[14:]
    attn_full, grads, attended = (full_out.ref, grads_out.ref, attended_out.ref)
    rank = head_rank()
    pixels = attn_full.shape[0]
    scale = 1.0 / math.sqrt(HD)
    for k in range(4):
        attn_full[:, lane_block(rank ^ k)] = blocks[k][...]
    full_out.send()
    step = 256
    qkv[...] = mm(attn_full[...], wide[...], 1, 0).astype(BF16)
    for i in range(pixels // step):
        at = slice(i * step, (i + 1) * step)
        keys_t[:, at] = qkv[at, LANES : 2 * LANES].astype(F32).T.astype(BF16)
        values_t[:, at] = qkv[at, 2 * LANES :].astype(F32).T.astype(BF16)
    lane = lax.broadcasted_iota(jnp.int32, (pixels, LANES), 1)
    sublane = lax.broadcasted_iota(jnp.int32, (LANES, pixels), 0)
    key_row, key_col = pixel_place(pixels, pixels, cols)
    key_valid = jnp.logical_and(key_row < ext[0, 0], key_col < ext[0, 1])
    att_sum = jnp.zeros((LANES, pixels), F32)
    query_sum = jnp.zeros((LANES, pixels), F32)
    for h in range(LANES // HD):
        mine = lax.shift_right_logical(lane, 6) == h
        mine_t = lax.shift_right_logical(sublane, 6) == h
        query = jnp.where(mine, qkv[:, 0:LANES], jnp.zeros((pixels, LANES), BF16))
        cot = jnp.where(mine, cot_att[...], jnp.zeros((pixels, LANES), BF16))
        scores = mm(qkv[:, LANES : 2 * LANES], query, 1, 1) * scale
        scores = jnp.where(key_valid, scores, MASKED)
        top = jnp.max(scores, axis=0, keepdims=True)
        expo = jnp.exp(scores - top)
        probs = expo * (1.0 / col_sum(expo))
        probs_low = probs.astype(BF16)
        att = mm(jnp.where(mine_t, values_t[...], jnp.zeros((LANES, pixels), BF16)), probs_low, 1, 0)
        att_sum = att_sum + att
        row_dot = col_sum(att * cot_att_t[...])
        grad_probs = mm(qkv[:, 2 * LANES :], cot, 1, 1)
        grad_scores = (probs * (grad_probs - row_dot)).astype(BF16)
        grad_values = mm(probs_low, cot, 1, 0)
        grad_keys = mm(grad_scores, query, 1, 0)
        if h == 0:
            grad_kv[:, LANES:] = grad_values
            grad_kv[:, 0:LANES] = grad_keys
        else:
            grad_kv[:, LANES:] += grad_values
            grad_kv[:, 0:LANES] += grad_keys
        query_sum = query_sum + mm(
            jnp.where(mine_t, keys_t[...], jnp.zeros((LANES, pixels), BF16)), grad_scores, 1, 0
        )
    attended[...] = att_sum.T.astype(BF16)
    grads[:, 0:LANES] = (query_sum.T * scale).astype(BF16)
    attended_out.send()
    grads[:, LANES : 2 * LANES] = (grad_kv[:, 0:LANES] * scale).astype(BF16)
    grads[:, 2 * LANES :] = grad_kv[:, LANES:].astype(BF16)
    grads_out.send()
    partial_sums(grads, wide, whole, outs)


def out_partial_kernel(ext, biases, attended, rows_weight, residual, cot, *refs):
    outs = refs[0:4]
    grads = refs[4:-1]
    whole = refs[-1]
    rank = head_rank()
    rows = outs[0].shape[0]
    attended = attended.get()
    for i in range(4):
        at = slice(i * rows, (i + 1) * rows)
        whole[at, :] = mm(attended[at, :], rows_weight[...], 1, 0)
    bias = biases.get()[6:7, lane_block(rank)]
    whole[:, lane_block(rank)] += residual.get()[...] + bias
    for k, out in enumerate(outs):
        out[...] = whole[row_block(rank ^ k, rows), :].astype(out.dtype)
    whole[0:LANES, :] = mm(attended[...], cot.get()[...], 0, 0)
    if len(grads) == 1:
        for g in range(grads[0].shape[0]):
            grads[0][g] = whole[0:LANES, g * LANES : (g + 1) * LANES]
    else:
        kept, near, pair = grads
        count = len(outs)
        size = LANES // (count * PROJ_PARTS)
        for k, dest in enumerate((kept, near, pair.at[0], pair.at[1])):
            for part in range(PROJ_PARTS):
                at = row_block(part * count + (rank ^ k), size)
                for g in range(dest.shape[0]):
                    dest[g, part * size : (part + 1) * size, :] = whole[
                        at, g * LANES : (g + 1) * LANES
                    ].astype(BF16)


def sum_kernel(ext, first, second, third, out):
    out[...] = (first[...] + second[...].astype(F32) + third[...].astype(F32)).astype(out.dtype)


def norm_third_back_kernel(ext, gains, kept, near, far, normed, inverse, cot, wide, *refs, cols, width):
    outs = refs[0:4]
    grad_res, third_out, sums, shifted, whole = refs[4:]
    rank = head_rank()
    pixels = kept.shape[0]
    grad = kept[...] + near[...].astype(F32) + far[...].astype(F32)
    normed, gains, cot = (normed.get()[...], gains.get(), cot.get())
    valid = valid_of(ext, pixels, LANES, cols)
    back = norm_back(
        grad * gains[1:2, lane_block(rank)], normed, inverse[0:1, :], valid,
        pixel_count(ext, width), width,
    )
    cot_value = cot[...].astype(F32)
    residual = cot_value + back
    grad_res.ref[...] = residual
    grad_res.send()
    third = (valid * residual).astype(BF16)
    third_out[...] = third
    third = third.astype(F32)
    shifted_grads(third, shifted, cols)
    sums[...] = jnp.zeros(sums.shape, F32)
    sums[0:1, :] = col_sum(grad * normed)
    sums[1:2, :] = col_sum(grad)
    sums[2:3, :] = col_sum(third)
    sums[3:4, :] = col_sum(cot_value)
    partial_sums(shifted, wide.get(), whole, outs)


def norm_second_back_kernel(ext, kept, near, far, normed, aux, wide, *refs, cols, width):
    outs = refs[0:4]
    first_out, sums, shifted, whole = refs[4:]
    pixels = kept.shape[0]
    grad_act = kept[...] + near[...].astype(F32) + far[...].astype(F32)
    normed = normed.get()[...]
    valid = valid_of(ext, pixels, LANES, cols)
    inverse, scale, shift = (aux[0:1, :], aux[1:2, :], aux[2:3, :])
    grad_pre = grad_act * valid * silu_grad(normed * (1.0 + scale) + shift)
    back = norm_back(
        grad_pre * (1.0 + scale), normed, inverse, valid, pixel_count(ext, width), width
    )
    first = back.astype(BF16)
    first_out[...] = first
    first = first.astype(F32)
    shifted_grads(first, shifted, cols)
    sums[...] = jnp.zeros(sums.shape, F32)
    sums[0:1, :] = col_sum(grad_pre * normed).astype(BF16).astype(F32)
    sums[1:2, :] = col_sum(grad_pre).astype(BF16).astype(F32)
    sums[2:3, :] = col_sum(first)
    partial_sums(shifted, wide.get(), whole, outs)


def norm_first_back_kernel(
    ext, gains, biases, kept, near, far, own, stats, grad_res, sums_third, sums_second, *refs,
    cols, width,
):
    out_kept, out_near, out_pair, table, held = refs
    rank = head_rank()
    pixels = kept.shape[0]
    rows = out_kept.shape[0]
    grad_act = kept[...] + near[...].astype(F32) + far[...].astype(F32)
    valid = valid_of(ext, pixels, LANES, cols)
    center, inverse = (stats[0:1, :], stats[1:2, :])
    normed = (own.get()[...].astype(F32) - center) * inverse
    gain = gains.get()[0:1, lane_block(rank)]
    bias = biases.get()[0:1, lane_block(rank)]
    grad_pre = grad_act * valid * silu_grad(normed * gain + bias)
    back = norm_back(grad_pre * gain, normed, inverse, valid, pixel_count(ext, width), width)
    held[...] = grad_res.get()[...] + back
    out_kept[...] = held[row_block(rank, rows), :]
    out_near[...] = held[row_block(rank ^ 1, rows), :].astype(BF16)
    for k in (2, 3):
        out_pair[k - 2] = held[row_block(rank ^ k, rows), :].astype(BF16)
    table[...] = jnp.zeros(table.shape, F32)
    table[0:1, :] = col_sum(grad_pre * normed)
    table[1:2, :] = sums_third[0:1, :]
    table[2:3, :] = col_sum(grad_pre)
    table[3:4, :] = sums_second[2:3, :]
    table[4:6, :] = sums_second[0:2, :]
    table[6:7, :] = sums_third[2:3, :]
    table[7:8, :] = sums_third[1:2, :]
    table[8:9, :] = sums_third[3:4, :]
    table[pl.ds(16 + 2 * lax.axis_index("dp"), 2), :] = sums_second[0:2, :]


def put_exact(dest, begin, value):
    rows = value.shape[0]
    high = value.astype(BF16)
    dest[begin : begin + rows, :] = high
    dest[begin + rows : begin + 2 * rows, :] = (value - high.astype(F32)).astype(BF16)


def get_exact(source, begin, rows):
    high = source[begin : begin + rows, :].astype(F32)
    return high + source[begin + rows : begin + 2 * rows, :].astype(F32)


def rows_join_kernel(ext, kept, near, far, corner, out):
    rank = head_rank()
    for k, block in enumerate((kept, near, far.at[0], corner.at[1])):
        out[:, lane_block(rank ^ k)] = block[...].astype(F32)


def taps_grad(act, shifted, flat):
    channels = act.shape[1]
    for i in range(channels // LANES):
        part = mm(act[:, i * LANES : (i + 1) * LANES], shifted[...], 0, 0)
        for tap in range(9):
            flat[0, tap * channels + i * LANES : tap * channels + (i + 1) * LANES, :] = part[
                :, tap * LANES : (tap + 1) * LANES
            ]


def dp_parts(dests, sources, dp_count):
    place = lax.axis_index("dp") if dp_count > 1 else 0
    for k, dest in enumerate(dests):
        at = 0
        for source in sources:
            size = source.shape[1] // dp_count
            for g in range(source.shape[0]):
                dest[at : at + size, :] = source[g, row_block(place ^ k, size), :].astype(dest.dtype)
                at += size


def qkv_grads_kernel(ext, attn, grads, *refs, dp_count):
    dests = refs[0:-1]
    qkv = refs[-1]
    part = mm(attn.get()[...], grads.get()[...], 0, 0)
    for g in range(3):
        qkv[g] = part[:, g * LANES : (g + 1) * LANES]
    if dp_count > 1:
        own, two, four, six, pairs = dests
        dests = (own, pairs.at[3], two, pairs.at[0], four, pairs.at[2], six, pairs.at[1])
    dp_parts(dests, (qkv,), dp_count)


def second_grads_kernel(ext, third, act, *refs, cols, dp_count):
    grad_proj = refs[0 : 4 if dp_count > 1 else 1]
    dests = refs[len(grad_proj) : -3]
    shifted, flat, proj = refs[-3:]
    shifted_grads(third[...].astype(F32), shifted, cols)
    act = act.get()
    taps_grad(act, shifted, flat)
    if len(grad_proj) == 1:
        proj[...] = grad_proj[0][...]
    else:
        kept, near, far, corner = grad_proj
        rank = head_rank()
        for k, block in enumerate((kept, near, far.at[0], corner.at[1])):
            size = block.shape[1]
            for g in range(proj.shape[0]):
                proj[g, row_block(rank ^ k, size), :] = block[g].astype(F32)
    dp_parts(split_dests(dests), (flat, proj), dp_count)


def split_dests(dests):
    if len(dests) == 1:
        return dests
    own, two, four, six, first_pair, second_pair = dests
    return (
        own, second_pair.at[1], two, first_pair.at[0], four, second_pair.at[0], six, first_pair.at[1]
    )


def first_grads_kernel(ext, first, act, sums, ada, *refs, cols, dp_count):
    dests = refs[0:-3]
    emb_part, shifted, flat = refs[-3:]
    shifted_grads(first[...].astype(F32), shifted, cols)
    taps_grad(act.get(), shifted, flat)
    dp_parts(split_dests(dests), (flat,), dp_count)
    ada = ada.get()
    for j in range(emb_part.shape[0]):
        row = jnp.zeros((1, LANES), F32)
        for side in range(2):
            mod = jnp.broadcast_to(sums[side : side + 1, :], (16, LANES)).astype(BF16)
            row = row + mm(mod, ada[side, j * LANES : (j + 1) * LANES, :], 1, 1)[0:1]
        emb_part[j : j + 1, :] = row


def near_kernel(ext, other, two, six, out):
    size = two.shape[0]
    for k, mine in enumerate((two, six)):
        out[k, 0:size, :] = (mine[...].astype(F32) + other[k].astype(F32)).astype(BF16)


def near_both_kernel(ext, other, two, six, ahead, ahead_two, ahead_six, out):
    size = two.shape[0]
    near_kernel(ext, other, two, six, out.at[:, pl.ds(0, size)])
    near_kernel(ext, ahead, ahead_two, ahead_six, out.at[:, pl.ds(size, ahead_two.shape[0])])


def near_table_kernel(ext, other, two, six, table, beside, out, total):
    size = two.shape[0]
    near_kernel(ext, other, two, six, out)
    total[...] = table[...] + beside[...]
    put_exact(out.at[0], size, total[...])
    out[1, size:, :] = jnp.zeros((out.shape[1] - size, LANES), BF16)


def far_kernel(ext, four, late, near, out):
    size = four.shape[0]
    value = four[...].astype(F32) + late[0].astype(F32) + near[1, 0:size, :].astype(F32)
    out[0:size, :] = value.astype(BF16)


def far_both_kernel(ext, four, late, ahead_four, ahead, near, out):
    size = four.shape[0]
    far_kernel(ext, four, late, near, out)
    rows = pl.ds(size, ahead_four.shape[0])
    far_kernel(ext, ahead_four, ahead.at[pl.ds(2, 2)], near.at[:, rows], out.at[rows])


def far_table_kernel(ext, four, late, near, table, out, total):
    size = four.shape[0]
    far_kernel(ext, four, late, near, out)
    total[...] = table[...] + get_exact(near.at[0], size, table.shape[0])
    put_exact(out, size, total[...])


def dp_pairs(parts):
    early = hop(parts[4], "dp", 1)
    return (early, hop(following(parts[5], early), "dp", 1))


def split_second_kernel(
    ext, own, late, ahead_own, ahead, straight, far, kept, near, pair, proj, held, *,
    rows_conv, rows_qkv,
):
    rank = head_rank()
    size = own.shape[0]
    held[...] = straight[0].astype(F32) + far[...].astype(F32)
    held[0:size, :] += own[...] + late[1].astype(F32)
    held[size:, :] += ahead_own[...] + ahead[3].astype(F32)
    for k, dest in enumerate((kept, near, pair.at[0], pair.at[1])):
        peer = rank ^ k
        dest[0:rows_conv, :] = held[row_block(peer, rows_conv), :].astype(dest.dtype)
        for g in range(3):
            begin = size + g * 4 * rows_qkv
            dest[rows_conv + g * rows_qkv : rows_conv + (g + 1) * rows_qkv, :] = held[
                pl.ds(pl.multiple_of(begin + peer * rows_qkv, 8), rows_qkv), :
            ].astype(dest.dtype)
    proj[...] = held[4 * rows_conv : size, :]


def split_first_kernel(
    ext, own, late, straight, far, table, emb_part, kept, near, pair, total, held, *, rows_conv
):
    rank = head_rank()
    size = held.shape[0]
    lines = table.shape[0]
    held[...] = own[...] + sum(
        part[0:size, :].astype(F32) for part in (late.at[1], straight.at[0], far)
    )
    total[0:lines, :] = table[...] + get_exact(far, size, lines)
    total[lines:, :] = emb_part[...]
    kept[...] = held[row_block(rank, rows_conv), :]
    for k, dest in enumerate((near, pair.at[0], pair.at[1])):
        dest[0:rows_conv, :] = held[row_block(rank ^ (k + 1), rows_conv), :].astype(BF16)
        put_exact(dest, rows_conv, total[...])


def join_second_kernel(ext, kept, near, far, corner, proj, conv_out, qkv_out, proj_out, *, rows_conv, rows_qkv):
    rank = head_rank()
    rows_proj = proj.shape[0] // 4
    low_half = lax.broadcasted_iota(jnp.int32, (rows_qkv, LANES), 1) < HD
    for k, block in enumerate((kept, near, far.at[0], corner.at[1])):
        peer = rank ^ k
        conv_out[pl.ds(peer, rows_conv, stride=4), :] = block[0:rows_conv, :].astype(F32)
        part = [
            block[rows_conv + g * rows_qkv : rows_conv + (g + 1) * rows_qkv, :].astype(F32)
            for g in range(3)
        ]
        keys = pltpu.roll(part[1], HD, 1)
        mixed = (
            jnp.where(low_half, part[0], keys),
            jnp.where(low_half, part[2], part[0]),
            jnp.where(low_half, keys, part[2]),
        )
        for g in range(3):
            qkv_out[pl.ds(peer * 3 + g, rows_qkv, stride=12), :] = mixed[g]
    for g in range(4):
        proj_out[pl.ds(g, rows_proj, stride=4), :] = proj[
            g * rows_proj : (g + 1) * rows_proj, :
        ].astype(F32)


def join_first_kernel(
    ext, kept, near, far, corner, total, embs, emb, conv_out, *refs, rows_conv
):
    rank = head_rank()
    outs, (mods, table, held, t1, t2, t3) = (refs[:4], refs[4:])
    blocks = (near, far.at[0], corner.at[1])
    conv_out[pl.ds(rank, rows_conv, stride=4), :] = kept[...]
    for k, (block, other) in enumerate(zip(blocks, (t1, t2, t3))):
        conv_out[pl.ds(rank ^ (k + 1), rows_conv, stride=4), :] = block[0:rows_conv, :].astype(F32)
        other[...] = get_exact(block, rows_conv, other.shape[0])
    small_grads_kernel(ext, embs, emb, total, t1, t2, t3, *outs, mods, table, held)


def small_grads_kernel(ext, embs, emb, t0, t1, t2, t3, gains_out, biases_out, ada_out, emb_out, mods, table, held):
    rank = head_rank()
    images = embs.shape[0]
    for k, block in enumerate((t0, t1, t2, t3)):
        table[:, lane_block(rank ^ k)] = block[0:16, :]
        for side in range(2):
            mods[:, lane_block(side * 4 + (rank ^ k))] = block[pl.ds(16 + side, images, stride=2), :]
    gains_out[...] = table[0:2, :]
    biases_out[...] = table[2:9, :]
    value = embs[...]
    part = mm((value * jax.nn.sigmoid(value)).astype(BF16), mods[...].astype(BF16), 0, 0)
    rows = ada_out.shape[0] // 8
    if part.shape[0] != rows:
        held[...] = part
        part = held[row_block(rank, rows), :]
    for g in range(8):
        ada_out[pl.ds(g, rows, stride=8), :] = part[:, g * LANES : (g + 1) * LANES]
    value = emb.get()[...].astype(F32)
    slope = silu_grad(value)
    begin = 16 + 2 * images
    for j in range(value.shape[1] // LANES):
        lanes = slice(j * LANES, (j + 1) * LANES)
        total = sum(block[begin + j : begin + j + 1, :] for block in (t0, t1, t2, t3))
        emb_out[:, lanes] = total * slope[:, lanes]


def body(
    inputs, embedding, extent, cotangent, gains, biases,
    conv_first, conv_second, qkv_master, ada_master, proj_master,
):
    heads = lax.axis_size("head")
    dps = lax.axis_size("dp")
    batch, row_count, cols, channels = inputs.shape
    rows = row_count * cols
    pixels = rows * heads
    width = channels // GROUPS
    emb_rows = embedding.shape[1] // LANES
    ext = extent
    direct = dps == 8
    flats = [
        master.reshape(-1, LANES)
        for master in (conv_first, conv_second, qkv_master, ada_master, proj_master)
    ]
    rows_conv = flats[0].shape[0] // 4
    rows_qkv = flats[2].shape[0] // 12
    rows_ada = flats[3].shape[0] // 8
    rows_proj = flats[4].shape[0] // 4
    far_gains, far_biases, far_emb = (Far(x, pinned=True) for x in (gains, biases, embedding))
    spread = [(i, (i % dps) * heads + i // dps) for i in range(dps * heads)]
    inputs_own = inputs.reshape(rows, channels)
    cot_own = cotangent.reshape(rows, channels)
    if direct:
        rows_a = rows_conv + 2 * rows_ada
        rows_b = rows_conv + 3 * rows_qkv
        far_flats = [Far(flat, pinned=True) for flat in flats]
        kept, near, pair, pj = call(
            first_out_kernel,
            [
                sds((rows_a, LANES), BF16), sds((rows_a, LANES), BF16),
                sds((2, rows_a, LANES), BF16), sds((4 * rows_proj, LANES), BF16),
            ],
            [None, far_flats[0], far_flats[3], far_flats[4]],
        )
        (first_piece,) = call(
            functools.partial(first_piece_kernel, segments=(rows_conv, rows_ada, rows_ada)),
            [sds((4 * rows_conv + 8 * rows_ada + 16 + 4 * rows_proj, LANES), BF16)],
            [None, kept, *head_exchange(near, pair), far_emb, pj],
            scratch=[pltpu.VMEM((16, LANES), F32)],
        )
        second_kept, near, far = call(
            second_out_kernel,
            [
                sds((rows_b, LANES), BF16), sds((rows_b, LANES), BF16),
                sds((channels // LANES * rows + 2 * rows_b, LANES), BF16),
            ],
            [None, far_flats[1], far_flats[2], Far(inputs_own, pinned=True)],
        )
        far = hop(far, "head", 2)
        corner = hop(far, "head", 1)
        blocks = (inputs_own, hop(inputs_own, "head", 1), far, corner)
        rows_second = 4 * rows_conv + 12 * rows_qkv + 4 * rows_proj
        (second_piece,) = call(
            functools.partial(second_piece_kernel, segments=(rows_conv,) + (rows_qkv,) * 3),
            [sds((rows_second - 4 * rows_proj, LANES), BF16)],
            [None, second_kept, hop(near, "head", 1), far, corner],
        )
        first_straight = dp_stepwise(first_piece)
        second_straight = dp_stepwise(second_piece)
        proj_at = 4 * rows_conv + 8 * rows_ada + 16
        first_segments = (
            (0, 1, 4 * rows_conv),
            (4 * rows_conv, 2, 4 * rows_ada),
            (proj_at, 4, rows_proj),
        )
        second_segments = ((0, 1, 4 * rows_conv), (4 * rows_conv, 3, 4 * rows_qkv))
    else:
        first_pieces, first_segments, second_pieces, second_segments, embs = gather_plain(
            flats, embedding, spread, channels
        )
        blocks = head_gather(inputs_own)

    act_first, own, stats_first = call(
        functools.partial(norm_first_kernel, cols=cols, width=width),
        [sds((pixels, channels), BF16), Far(sds((pixels, LANES), BF16)), sds((8, LANES), F32)],
        [ext, far_gains, far_biases, *blocks],
        scratch=[pltpu.VMEM((8, channels), F32)],
        us=2.0,
    )
    if direct:
        first_pieces, token = dp_beside_in_turn(first_straight, second_kept[:TOKEN])
    cots = head_gather(following(cot_own, blocks[2]))
    wide_shape = (channels, 9 * LANES)
    taps_scratch = pltpu.VMEM((pixels + 2 * cols, 9 * LANES), F32)
    flat_scratch = pltpu.VMEM((1, 9 * channels, LANES), BF16)
    n_pieces = len(first_pieces)
    groups = channels // LANES
    if direct:
        part = (groups, LANES // heads, LANES)
        proj_outs = [sds(part, BF16), sds(part, BF16), sds((2, *part), BF16)]
    else:
        proj_outs = [sds((LANES, channels), BF16)]
    first_outs = call(
        functools.partial(
            conv_first_kernel, cols=cols, width=width, count_pieces=n_pieces,
            segments=first_segments,
            emb_at=4 * rows_conv + 8 * rows_ada if direct else None,
        ),
        [
            sds((pixels, LANES), BF16), Far(sds((pixels, LANES), F32)), sds((8, LANES), F32),
            Far(sds(wide_shape, BF16)), Far(sds((2, emb_rows * LANES, LANES), BF16)),
            Far(sds((pixels, channels), BF16), held=False),
        ]
        + proj_outs
        + ([sds((dps, LANES), F32)] if direct else []),
        [ext, far_biases, act_first, far_emb, *first_pieces],
        scratch=[
            flat_scratch,
            taps_scratch,
            pltpu.VMEM((pixels, LANES), F32),
            pltpu.VMEM((groups, LANES, LANES), BF16),
        ],
        us=4.0,
        after=[token] if direct else (),
    )
    act_second_own, normed_second, aux_second, wide_first, ada_full, act_first = first_outs[:6]
    w_proj = first_outs[6 : 6 + len(proj_outs)]
    if direct:
        embs = first_outs[-1]
        w_proj = (w_proj[0], *head_exchange(*w_proj[1:]))
        second_pieces = dp_beside(second_straight)
        mark = []
        act_second_own = following(act_second_own, second_pieces[1], second_straight[1])
    blocks = head_gather(act_second_own, *([second_pieces[3], second_pieces[5]] if direct else []))
    attn_own, act_second, residual, normed_third, aux_third, wide_second, w_qkv = call(
        functools.partial(
            conv_second_kernel, cols=cols, width=width, count_pieces=n_pieces,
            segments=second_segments,
        ),
        [
            sds((pixels, LANES), BF16), Far(sds((pixels, channels), BF16)),
            Far(sds((pixels, LANES), F32)), Far(sds((pixels, LANES), F32)), sds((8, LANES), F32),
            Far(sds(wide_shape, BF16)), sds((channels, 3 * LANES), BF16),
        ],
        [ext, far_gains, far_biases, Far(own), *blocks, *second_pieces],
        scratch=[
            flat_scratch,
            pltpu.VMEM((3, channels, LANES), BF16),
            taps_scratch,
        ],
        us=4.0,
        after=w_proj[1:] if direct else (),
    )
    cot_full, cot_own, cot_att, cot_att_t, rows_weight = call(
        cotangent_kernel,
        [
            Far(sds((pixels, channels), BF16)), Far(sds((pixels, LANES), BF16)),
            sds((pixels, LANES), BF16), sds((LANES, pixels), F32), sds((LANES, channels), BF16),
        ],
        [None, *cots, *w_proj],
    )
    blocks = head_gather(attn_own, cot_att)
    whole_scratch = pltpu.VMEM((pixels, channels), F32)
    shifted_scratch = pltpu.VMEM((pixels, 9 * LANES), BF16)
    split_outs = [sds((pixels, LANES), F32)] + [sds((pixels, LANES), BF16)] * 3
    *parts, attn_full, grads_qkv, attended = call(
        functools.partial(attention_kernel, cols=cols),
        split_outs
        + [
            Far(sds((pixels, channels), BF16)), Far(sds((pixels, 3 * LANES), BF16)),
            Far(sds((pixels, LANES), BF16)),
        ],
        [ext, *blocks, w_qkv, cot_att, cot_att_t],
        scratch=[
            pltpu.VMEM((pixels, 3 * LANES), BF16),
            pltpu.VMEM((LANES, pixels), BF16),
            pltpu.VMEM((LANES, pixels), BF16),
            pltpu.VMEM((pixels, 2 * LANES), F32),
            whole_scratch,
        ],
        us=15.0,
    )
    parts, _ = head_reduce(ext, parts)
    grad_outs = proj_outs if direct else [sds((groups, LANES, LANES), F32)]
    out_all = call(
        out_partial_kernel,
        [sds((rows, channels), F32)] + [sds((rows, channels), BF16)] * 3 + grad_outs,
        [None, far_biases, Far(attended), rows_weight, Far(residual), Far(cot_full)],
        scratch=[whole_scratch],
        us=2.0,
    )
    out_parts, grad_proj = (out_all[:4], out_all[4:])
    if direct:
        grad_proj = (grad_proj[0], *head_exchange(*grad_proj[1:]))
    n_dests = dps if direct else 1

    def grad_outs(size):
        size = size // n_dests
        if not direct:
            return [sds((size, LANES), F32)]
        one = sds((size, LANES), BF16)
        return [sds((size, LANES), F32), one, one, one] + [sds((2, size, LANES), BF16)] * 2

    ahead_outs = grad_outs(3 * channels)
    if direct:
        ahead_outs = ahead_outs[:4] + [sds((4, *ahead_outs[1].shape), BF16)]
    ahead_parts = call(
        functools.partial(qkv_grads_kernel, dp_count=n_dests),
        ahead_outs,
        [None, Far(attn_full), Far(grads_qkv)],
        scratch=[pltpu.VMEM((3, channels, LANES), F32)],
        after=out_parts[:1],
    )
    if direct:
        ahead = hop(ahead_parts[4], "dp", 1)
    *parts, grad_res, third, sums_third = call(
        functools.partial(norm_third_back_kernel, cols=cols, width=width),
        split_outs
        + [Far(sds((pixels, LANES), F32)), sds((pixels, LANES), BF16), sds((8, LANES), F32)],
        [
            ext, far_gains, *parts, Far(normed_third), aux_third, Far(cot_own), Far(wide_second),
        ],
        scratch=[shifted_scratch, whole_scratch],
        us=150.0,
        after=ahead_parts[:1],
    )
    if direct:
        parts[3] = following(parts[3], *grad_proj[1:3], ahead)
    out_sums, _ = head_reduce(ext, out_parts)
    (output,) = call(sum_kernel, [sds((rows, channels), BF16)], [None, *out_sums])
    parts, sent = head_reduce(ext, parts)
    flat_grad = pltpu.VMEM((1, 9 * channels, LANES), F32)
    second_parts = call(
        functools.partial(second_grads_kernel, cols=cols, dp_count=n_dests),
        grad_outs(10 * channels),
        [None, third, Far(act_second), *grad_proj],
        scratch=[
            shifted_scratch,
            flat_grad,
            pltpu.VMEM((channels // LANES, LANES, LANES), F32),
        ],
        us=4.0,
        after=sent,
    )
    *parts, first, sums_second = call(
        functools.partial(norm_second_back_kernel, cols=cols, width=width),
        split_outs + [sds((pixels, LANES), BF16), sds((8, LANES), F32)],
        [ext, *parts, Far(normed_second), aux_second, Far(wide_first)],
        scratch=[shifted_scratch, whole_scratch],
        us=150.0,
        after=second_parts[:1],
    )
    if direct:
        second_pairs = dp_pairs(second_parts)
    parts, sent = head_reduce(ext, parts, second_pairs[:1] if direct else ())
    *first_parts, emb_part = call(
        functools.partial(first_grads_kernel, cols=cols, dp_count=n_dests),
        grad_outs(9 * channels) + [sds((emb_rows, LANES), F32)],
        [ext, first, Far(act_first), sums_second, Far(ada_full)],
        scratch=[shifted_scratch, flat_grad],
        us=3.0,
        after=sent,
    )
    table_rows = 16 + 2 * dps
    early = [emb_part]
    if direct:
        first_early, first_late = (hop(pair, "dp", 1) for pair in first_parts[4:6])
        (near_pair,) = call(
            near_both_kernel,
            [sds((2, rows_second, LANES), BF16)],
            [
                None, second_pairs[0], second_parts[1], second_parts[3], ahead, ahead_parts[1],
                ahead_parts[3],
            ],
            us=0.6,
            after=sent,
        )
        early += [near_pair, second_pairs[1]]
        second_near = hop(near_pair, "dp", 2)
    kept_rows, near, pair, table = call(
        functools.partial(norm_first_back_kernel, cols=cols, width=width),
        [
            sds((rows, LANES), F32), sds((rows, LANES), BF16), sds((2, rows, LANES), BF16),
            sds((table_rows, LANES), F32),
        ],
        [
            ext, far_gains, far_biases, *parts, Far(own), stats_first, Far(grad_res), sums_third,
            sums_second,
        ],
        scratch=[pltpu.VMEM((pixels, LANES), F32)],
        us=40.0,
        after=early,
    )
    small_outs = [
        sds(gains.shape, F32), sds(biases.shape, F32), sds(flats[3].shape, F32),
        sds(embedding.shape, F32),
    ]
    small_scratch = [
        pltpu.VMEM((dps, 8 * LANES), F32),
        pltpu.VMEM((16, channels), F32),
        pltpu.VMEM((LANES, 8 * LANES), F32),
    ]
    if direct:
        beside = hop(table, "dp", 1)
        (far_block,) = call(
            far_both_kernel,
            [sds((rows_second, LANES), BF16)],
            [None, second_parts[2], second_pairs[1], ahead_parts[2], ahead, second_near],
            us=0.6,
            after=[kept_rows],
        )
        second_left = [
            second_parts[0], second_pairs[1], ahead_parts[0], ahead, second_near,
            hop(far_block, "dp", 4),
        ]
        size = 4 * rows_conv + 2 * table_rows
        near_pair, table = call(
            near_table_kernel,
            [sds((2, size, LANES), BF16), sds(table.shape, F32)],
            [None, first_early, first_parts[1], first_parts[3], table, beside],
            us=0.6,
        )
        first_near = hop(near_pair, "dp", 2)
        far_block, table = call(
            far_table_kernel,
            [sds((size, LANES), BF16), sds(table.shape, F32)],
            [None, first_parts[2], first_late, first_near, table],
            us=0.6,
            after=[far_block],
        )
        first_left = [first_parts[0], first_late, first_near, hop(far_block, "dp", 4)]
    (grad_inputs,) = call(
        rows_join_kernel,
        [sds((rows, channels), F32)],
        [None, kept_rows, *head_exchange(near, pair)],
    )
    if direct:
        second_own, near, pair, pj = call(
            functools.partial(split_second_kernel, rows_conv=rows_conv, rows_qkv=rows_qkv),
            [
                sds((rows_b, LANES), F32), sds((rows_b, LANES), BF16),
                sds((2, rows_b, LANES), BF16), sds((4 * rows_proj, LANES), F32),
            ],
            [None, *second_left],
            scratch=[pltpu.VMEM((rows_second, LANES), F32)],
        )
        second_blocks = head_exchange(near, pair)
        second_grad, qkv_grad, proj_grad = call(
            functools.partial(join_second_kernel, rows_conv=rows_conv, rows_qkv=rows_qkv),
            [sds(flats[i].shape, F32) for i in (1, 2, 4)],
            [None, second_own, *second_blocks, pj],
        )
        lines = table_rows + emb_rows
        kept, near, pair, table = call(
            functools.partial(split_first_kernel, rows_conv=rows_conv),
            [
                sds((rows_conv, LANES), F32), sds((rows_conv + 2 * lines, LANES), BF16),
                sds((2, rows_conv + 2 * lines, LANES), BF16), sds((lines, LANES), F32),
            ],
            [None, *first_left, table, emb_part],
            scratch=[pltpu.VMEM((4 * rows_conv, LANES), F32)],
            after=second_blocks[:2],
        )
        first_blocks = head_exchange(near, pair, output, grad_inputs, second_grad)
        first_grad, grad_gains, grad_biases, ada_grad, grad_embedding = call(
            functools.partial(join_first_kernel, rows_conv=rows_conv),
            [sds(flats[0].shape, F32)] + small_outs,
            [None, kept, *first_blocks, table, embs, far_emb],
            scratch=small_scratch + [pltpu.VMEM((lines, LANES), F32)] * 3,
        )
    else:
        table = jnp.concatenate([lax.psum(table, "dp"), emb_part])
        grad_gains, grad_biases, ada_grad, grad_embedding = call(
            small_grads_kernel,
            small_outs,
            [ext, embs, far_emb, *head_gather(table)],
            scratch=small_scratch,
        )
        first_grad, second_grad, qkv_grad, proj_grad = scatter_plain(
            first_parts[0], second_parts[0], ahead_parts[0], spread, channels
        )
    return (
        output.reshape(inputs.shape),
        grad_inputs.reshape(inputs.shape),
        grad_embedding,
        grad_gains,
        grad_biases,
        first_grad.reshape(-1),
        second_grad.reshape(-1),
        qkv_grad.reshape(-1),
        ada_grad.reshape(-1),
        proj_grad.reshape(-1),
    )


def gather_plain(flats, embedding, spread, channels):
    heads = lax.axis_size("head")

    def columns(flat, groups):
        blocks = flat.astype(BF16).reshape(-1, groups, LANES)
        return blocks

    def own_columns(blocks):
        got = lax.all_to_all(blocks, "head", split_axis=1, concat_axis=0, tiled=True)
        return lax.all_gather(got[:, 0], "dp", axis=0, tiled=True)

    first, second = (own_columns(columns(flats[i], heads).reshape(-1, heads, 1, LANES))[:, 0] for i in (0, 1))
    qkv = columns(flats[2], 12).reshape(-1, heads, 2, 3, HD)
    qkv = jnp.swapaxes(qkv, 2, 3).reshape(-1, heads, 3, LANES)
    qkv = jnp.swapaxes(own_columns(qkv), 0, 1).reshape(-1, LANES)
    ada = columns(flats[3], 8).reshape(-1, 2, heads, LANES)
    ada = jnp.swapaxes(own_columns(jnp.swapaxes(ada, 1, 2)), 0, 1).reshape(-1, LANES)
    proj = lax.ppermute(flats[4].astype(BF16), ("dp", "head"), spread)
    proj = lax.all_gather(proj, "dp", axis=0, tiled=True).reshape(-1, channels // LANES, LANES)
    proj = jnp.swapaxes(proj, 0, 1).reshape(-1, LANES)
    embs = lax.all_gather(embedding, "dp", axis=0, tiled=True).astype(F32)
    embs = embs.reshape(embs.shape[0], -1, flats[3].shape[0] // 8)
    embs = lax.dynamic_index_in_dim(
        embs, lax.axis_index("dp") * heads + lax.axis_index("head"), 1, False
    )
    first_piece = jnp.concatenate([first, ada, proj])
    second_piece = jnp.concatenate([second, qkv])
    proj_at = 9 * channels + ada.shape[0]
    return (
        [first_piece],
        (
            (0, 1, 9 * channels),
            (9 * channels, 2, ada.shape[0] // 2),
            (proj_at, channels // LANES, LANES),
        ),
        [second_piece],
        ((0, 1, 9 * channels), (9 * channels, 3, channels)),
        embs,
    )


def scatter_plain(first, second, qkv, spread, channels):
    heads = lax.axis_size("head")

    def rows_of(grad):
        part = lax.psum_scatter(grad, "dp", scatter_dimension=0, tiled=True)
        return lax.all_to_all(part[:, None], "head", split_axis=0, concat_axis=1, tiled=True)

    def conv(grad):
        return rows_of(grad[:, None])

    qkv = jnp.swapaxes(qkv.reshape(3, channels, LANES), 0, 1)
    qkv = rows_of(qkv).reshape(-1, heads, 3, 2, HD)
    qkv = jnp.swapaxes(qkv, 2, 3)
    proj = jnp.swapaxes(second[9 * channels :].reshape(-1, LANES, LANES), 0, 1)
    proj = lax.psum_scatter(proj, "dp", scatter_dimension=0, tiled=True)
    proj = lax.ppermute(proj, ("dp", "head"), [(j, i) for i, j in spread])
    return (conv(first), conv(second[: 9 * channels]), qkv, proj)


def solution(mesh):
    flat = P(("dp", "head"))
    image = P("dp", "head", None, None)
    return jax.shard_map(
        body,
        mesh=mesh,
        in_specs=(image, P("dp", None), P("dp", None), image, P(), P(), flat, flat, flat, flat, flat),
        out_specs=(image, image, P("dp", None), P(), P(), flat, flat, flat, flat, flat),
        check_vma=False,
    )
```

```python
import functools
import math

import jax
import jax.numpy as jnp
from jax import lax
from jax.experimental import pallas as pl
from jax.experimental.pallas import tpu as pltpu
from jax.sharding import PartitionSpec as P

HD = 64
TOKEN = 96
STEP = 512
PROJ_PARTS = 2
MARK = 64
GROUPS = 32
EPS = 1e-05
MASKED = -1e30
LANES = 128
F32 = jnp.float32
BF16 = jnp.bfloat16
VMEM_SPEC = pl.BlockSpec(memory_space=pltpu.VMEM)
SMEM_SPEC = pl.BlockSpec(memory_space=pltpu.SMEM)


def sds(shape, dtype):
    return jax.ShapeDtypeStruct(shape, dtype)


class Far:
    def __init__(self, array, held=True, pinned=False):
        self.array = pltpu.with_memory_space_constraint(array, pltpu.HBM) if pinned else array
        self.held = held


class Fetch:
    def __init__(self, source, ref, sem):
        self.copy = pltpu.make_async_copy(source, ref, sem)
        self.ref = ref
        self.copy.start()

    def get(self):
        self.copy.wait()
        return self.ref


class Store:
    def __init__(self, dest, ref, sem):
        self.dest = dest
        self.ref = ref
        self.sem = sem
        self.copy = None

    def send(self, source=None):
        self.copy = pltpu.make_async_copy(self.ref if source is None else source, self.dest, self.sem)
        self.copy.start()


def call(kernel, outs, args, scratch=(), us=1.0, vmem=24, after=()):
    scalars = args[0] is not None
    args = list(args) if scalars else list(args[1:])
    arrays = [arg.array if isinstance(arg, Far) else arg for arg in args]
    results = [out.array if isinstance(out, Far) else out for out in outs]
    far_in = [isinstance(arg, Far) for arg in args]
    far_out = [isinstance(out, Far) for out in outs]
    held = [
        pltpu.VMEM(x.array.shape, x.array.dtype)
        for x in list(args) + list(outs)
        if isinstance(x, Far) and x.held
    ]
    copies = sum(far_in) + sum(far_out)

    def run(*refs):
        ins = refs[: len(args)]
        begin = len(args) + len(after)
        dests = refs[begin : begin + len(outs)]
        begin += len(outs)
        buffers = iter(refs[begin : begin + len(held)])
        begin += len(held)
        sems = refs[begin] if copies else None
        rest = refs[begin + (1 if copies else 0) :]
        count = 0
        given = []
        for ref, far in zip(ins, far_in):
            if far:
                ref = Fetch(ref, next(buffers), sems.at[count])
                count += 1
            given.append(ref)
        stores = []
        for ref, out in zip(dests, outs):
            if isinstance(out, Far):
                ref = Store(ref, next(buffers) if out.held else None, sems.at[count])
                stores.append(ref)
                count += 1
            given.append(ref)
        kernel(*([] if scalars else [None]), *given, *rest)
        for store in stores:
            store.copy.wait()

    hbm = pl.BlockSpec(memory_space=pltpu.HBM)
    anywhere = pl.BlockSpec(memory_space=pl.ANY)
    return pl.pallas_call(
        run,
        out_shape=tuple(results),
        in_specs=[
            hbm if far else SMEM_SPEC if scalars and i == 0 else VMEM_SPEC
            for i, far in enumerate(far_in)
        ]
        + [anywhere for _ in after],
        out_specs=tuple(hbm if far else VMEM_SPEC for far in far_out),
        scratch_shapes=held
        + ([pltpu.SemaphoreType.DMA((copies,))] if copies else [])
        + list(scratch),
        compiler_params=pltpu.CompilerParams(vmem_limit_bytes=vmem * 1024 * 1024),
        cost_estimate=pl.CostEstimate(
            flops=int(3e7 * us),
            bytes_accessed=1024,
            transcendentals=0,
        ),
    )(*arrays, *after)


def following(value, *earlier):
    return lax.optimization_barrier((value, *earlier))[0]


def hop(value, axis, bit):
    count = lax.axis_size(axis)
    return lax.ppermute(value, axis, [(i, i ^ bit) for i in range(count)])


def head_gather(block, *earlier):
    far = hop(block, "head", 2)
    near = hop(block, "head", 1)
    return (block, near, far, hop(following(far, *earlier) if earlier else far, "head", 1))


def head_exchange(near_block, far_pair, *earlier):
    far = hop(far_pair, "head", 2)
    near = hop(near_block, "head", 1)
    return (near, far, hop(following(far, *earlier) if earlier else far, "head", 1))


def add_kernel(ext, first, second, out):
    out[...] = (first[...].astype(F32) + second[...].astype(F32)).astype(out.dtype)


def head_reduce(ext, blocks, after=()):
    kept, near_block, far_block, corner = blocks
    corner = hop(corner, "head", 1)
    (far_block,) = call(
        add_kernel, [sds(far_block.shape, BF16)], [None, far_block, corner], us=0.7, after=after
    )
    return ((kept, hop(near_block, "head", 1), hop(far_block, "head", 2)), [far_block])


def mm(left, right, left_dim, right_dim):
    return lax.dot_general(
        left, right, (((left_dim,), (right_dim,)), ((), ())), preferred_element_type=F32
    )


def lane_block(index):
    return pl.ds(pl.multiple_of(index * LANES, LANES), LANES)


def row_block(index, rows):
    return pl.ds(pl.multiple_of(index * rows, rows), rows)


def pixel_place(rows, lanes, cols, start=0):
    pixel = lax.broadcasted_iota(jnp.int32, (rows, lanes), 0) + start
    shift = cols.bit_length() - 1
    return (lax.shift_right_logical(pixel, shift), lax.bitwise_and(pixel, cols - 1))


def valid_of(ext, rows, lanes, cols, start=0):
    place_row, place_col = pixel_place(rows, lanes, cols, start)
    inside = jnp.logical_and(place_row < ext[0, 0], place_col < ext[0, 1])
    return jnp.where(inside, 1.0, 0.0).astype(F32)


def group_total(first, second, width):
    lanes = first.shape[-1]
    pick = lax.broadcasted_iota(jnp.int32, (8, lanes), 0)
    both = jnp.where(pick == 0, first, jnp.where(pick == 1, second, 0.0))
    shift = width.bit_length() - 1
    left = lax.shift_right_logical(lax.broadcasted_iota(jnp.int32, (lanes, lanes), 0), shift)
    right = lax.shift_right_logical(lax.broadcasted_iota(jnp.int32, (lanes, lanes), 1), shift)
    same = jnp.where(left == right, 1.0, 0.0).astype(F32)
    total = lax.dot_general(
        both,
        same,
        (((1,), (0,)), ((), ())),
        precision=lax.Precision.HIGHEST,
        preferred_element_type=F32,
    )
    return (total[0:1], total[1:2])


def pixel_count(ext, width):
    return (ext[0, 0] * ext[0, 1] * width).astype(F32)


def col_sum(value):
    return jnp.sum(value, axis=0, keepdims=True)


def head_rank():
    return lax.axis_index("head")


def norm_stats(value, valid, count, width):
    masked = value * valid
    total, square = group_total(col_sum(masked), col_sum(masked * value), width)
    center = total / count
    return (center, lax.rsqrt(square / count - center * center + EPS))


def norm_back(grad, normed, inverse, valid, count, width):
    first, second = group_total(col_sum(grad), col_sum(grad * normed), width)
    return (grad - valid * ((first + normed * second) * (1.0 / count))) * inverse


def silu_grad(value):
    gate = jax.nn.sigmoid(value)
    return gate * (1.0 + value * (1.0 - gate))


def place_pieces(dest, pieces, start, groups, rows):
    for k, piece in enumerate(pieces):
        part = lax.axis_index("dp") ^ k if len(pieces) > 1 else 0
        for group in range(groups):
            begin = start + group * rows
            dest[group, pl.ds(pl.multiple_of(part * rows, rows), rows), :] = piece[
                begin : begin + rows, :
            ]


def taps_side_by_side(flat, wide):
    channels = wide.shape[0]
    for tap in range(9):
        wide[:, tap * LANES : (tap + 1) * LANES] = flat[0, tap * channels : (tap + 1) * channels, :]


def conv_taps(act, wide, taps, cols):
    pixels = act.shape[0]
    lanes = wide.shape[1]
    taps[0:cols, :] = jnp.zeros((cols, lanes), F32)
    taps[pixels + cols :, :] = jnp.zeros((cols, lanes), F32)
    step = STEP

    def one(i, carry):
        begin = pl.multiple_of(i * step, step)
        taps[pl.ds(pl.multiple_of(begin + cols, cols), step), :] = mm(
            act[pl.ds(begin, step), :], wide[...], 1, 0
        )
        return carry

    lax.fori_loop(0, pixels // step, one, 0)


def conv_sum(taps, begin, rows, cols):
    def column(side):
        return sum(
            taps[
                pl.ds(pl.multiple_of(begin + up * cols, cols), rows),
                (up * 3 + side) * LANES : (up * 3 + side + 1) * LANES,
            ]
            for up in range(3)
        )

    place_col = pixel_place(rows, LANES, cols)[1]
    left = jnp.where(place_col > 0, pltpu.roll(column(0), 1, 0), 0.0)
    right = jnp.where(place_col < cols - 1, pltpu.roll(column(2), rows - 1, 0), 0.0)
    return column(1) + left + right


def shifted_grads(grad, dest, cols):
    pixels = grad.shape[0]
    place_col = pixel_place(pixels, LANES, cols)[1]
    sides = (
        jnp.where(place_col < cols - 1, pltpu.roll(grad, pixels - 1, 0), 0.0),
        grad,
        jnp.where(place_col > 0, pltpu.roll(grad, 1, 0), 0.0),
    )
    blank = jnp.zeros((cols, LANES), BF16)
    for side, value in enumerate(sides):
        low = value.astype(BF16)
        for up in range(3):
            lanes = slice((up * 3 + side) * LANES, (up * 3 + side + 1) * LANES)
            if up == 0:
                dest[0 : pixels - cols, lanes] = low[cols:, :]
                dest[pixels - cols :, lanes] = blank
            elif up == 1:
                dest[:, lanes] = low
            else:
                dest[cols:, lanes] = low[0 : pixels - cols, :]
                dest[0:cols, lanes] = blank


def partial_sums(left, right, whole, outs):
    step = STEP

    def one(i, carry):
        rows = pl.ds(pl.multiple_of(i * step, step), step)
        whole[rows, :] = mm(left[rows, :], right[...], 1, 1)
        return carry

    lax.fori_loop(0, left.shape[0] // step, one, 0)
    rank = head_rank()
    for k, out in enumerate(outs):
        out[...] = whole[:, lane_block(rank ^ k)].astype(out.dtype)


def strided(ref, begin, stride):
    return ref[pl.ds(begin, ref.shape[0] // stride, stride=stride), :]


def put_rows(dest, begin, value):
    rows = value.shape[0]
    dest[begin : begin + rows, :] = value.astype(BF16)
    return begin + rows


def first_out_kernel(ext, first, ada, proj, kept, near, pair, parts):
    rank = head_rank()
    first, ada = (first.get(), ada.get())
    for k, dest in enumerate((kept, near, pair.at[0], pair.at[1])):
        at = put_rows(dest, 0, strided(first, rank ^ k, 4))
        for side in range(2):
            at = put_rows(dest, at, strided(ada, 4 * side + (rank ^ k), 8))
    proj = proj.get()
    at = 0
    for g in range(4):
        at = put_rows(parts, at, strided(proj, g, 4))


def second_out_kernel(ext, second, qkv, image, kept, near, far):
    rank = head_rank()
    second, qkv, image = (second.get(), qkv.get(), image.get())
    low_half = lax.broadcasted_iota(jnp.int32, (qkv.shape[0] // 12, LANES), 1) < HD
    rows = image.shape[0]
    groups = image.shape[1] // LANES
    for g in range(groups):
        far[g * rows : (g + 1) * rows, :] = image[:, g * LANES : (g + 1) * LANES]
    begin = groups * rows
    size = kept.shape[0]
    blocks = (kept, near, far.at[pl.ds(begin, size)], far.at[pl.ds(begin + size, size)])
    for k, dest in enumerate(blocks):
        at = put_rows(dest, 0, strided(second, rank ^ k, 4))
        part = [strided(qkv, (rank ^ k) * 3 + g, 12) for g in range(3)]
        at = put_rows(dest, at, jnp.where(low_half, part[0], part[1]))
        at = put_rows(dest, at, pltpu.roll(jnp.where(low_half, part[2], part[0]), HD, 1))
        put_rows(dest, at, jnp.where(low_half, part[1], part[2]))


def join_blocks(dest, blocks, segments):
    rank = head_rank()
    for k, block in enumerate(blocks):
        at, begin = (0, 0)
        for rows in segments:
            place = pl.ds(pl.multiple_of(begin + (rank ^ k) * rows, 16), rows)
            dest[place, :] = block[at : at + rows, :]
            at += rows
            begin += 4 * rows
    return 4 * sum(segments)


def first_piece_kernel(ext, kept, near, far, corner, emb, proj, piece, line, *, segments):
    at = join_blocks(piece, (kept, near, far.at[0], corner.at[1]), segments)
    emb = emb.get()
    line[...] = jnp.zeros(line.shape, F32)
    for j in range(emb.shape[1] // LANES):
        line[j : j + 1, :] = emb[0:1, j * LANES : (j + 1) * LANES].astype(F32)
    piece[at : at + 16, :] = line[...].astype(BF16)
    piece[at + 16 :, :] = proj[...]


def second_piece_kernel(ext, kept, near, far, corner, piece, *, segments):
    size = kept.shape[0]
    begin = far.shape[0] - 2 * size
    blocks = (kept, near, far.at[pl.ds(begin, size)], corner.at[pl.ds(begin + size, size)])
    join_blocks(piece, blocks, segments)


def dp_stepwise(piece):
    far = hop(piece, "dp", 4)
    return [piece, hop(piece, "dp", 2), far, hop(far, "dp", 2)]


def dp_beside(straight):
    near = [hop(value, "dp", 1) for value in straight]
    return [value for pair in zip(straight, near) for value in pair]


def dp_beside_in_turn(straight, token):
    own, two, four, six = straight
    own = hop(own, "dp", 1)
    two_near = hop(following(two, own), "dp", 1)
    token = hop(following(token, two_near), "head", 1)
    four_near = hop(four, "dp", 1)
    six_near = hop(following(six, token, four_near), "dp", 1)
    near = (own, two_near, four_near, six_near)
    return ([value for pair in zip(straight, near) for value in pair], token)


def norm_first_kernel(ext, gains, biases, *refs, cols, width):
    blocks = refs[0:4]
    act, own_out, stats, held = refs[4:]
    own = own_out.ref
    rank = head_rank()
    rows, channels = blocks[0].shape
    count = pixel_count(ext, width)
    total = jnp.zeros((1, channels), F32)
    square = jnp.zeros((1, channels), F32)
    def whole(block):
        if block.shape[1] == channels:
            return block[...].astype(F32)
        parts = [block[g * rows : (g + 1) * rows, :] for g in range(channels // LANES)]
        return jnp.concatenate(parts, axis=1).astype(F32)

    for k, block in enumerate(blocks):
        if block.shape[1] == channels:
            own[row_block(rank ^ k, rows), :] = block[:, lane_block(rank)]
        else:
            own[row_block(rank ^ k, rows), :] = block[row_block(rank, rows), :]
    own_out.send()
    for k, block in enumerate(blocks):
        value = whole(block)
        masked = value * valid_of(ext, rows, channels, cols, (rank ^ k) * rows)
        total = total + col_sum(masked)
        square = square + col_sum(masked * value)
    total, square = group_total(total, square, width)
    center = total / count
    inverse = lax.rsqrt(square / count - center * center + EPS)
    held[0:1, :] = center
    held[1:2, :] = inverse
    gain, bias = (gains.get()[0:1, :], biases.get()[0:1, :])
    for k, block in enumerate(blocks):
        peer = rank ^ k
        pre = (whole(block) - center) * inverse * gain + bias
        valid = valid_of(ext, rows, channels, cols, peer * rows)
        act[row_block(peer, rows), :] = (pre * jax.nn.sigmoid(pre) * valid).astype(BF16)
    stats[...] = held[:, lane_block(rank)]


def conv_first_kernel(ext, biases, act, emb, *refs, cols, width, count_pieces, segments, emb_at):
    pieces = refs[0:count_pieces]
    act_out, normed_out, aux, wide_out, ada_out, act_far = refs[count_pieces : count_pieces + 6]
    w_proj = refs[count_pieces + 6 : -4 if emb_at is None else -5]
    flat, taps, hidden, proj = refs[-4:]
    rank = head_rank()
    pixels = act.shape[0]
    act_far.send(act)
    place_pieces(flat, pieces, *segments[0])
    wide = wide_out.ref
    taps_side_by_side(flat, wide)
    wide_out.send()
    ada = ada_out.ref
    place_pieces(ada, pieces, *segments[1])
    ada_out.send()
    place_pieces(proj, pieces, *segments[2])
    if len(w_proj) == 1:
        for g in range(proj.shape[0]):
            w_proj[0][:, g * LANES : (g + 1) * LANES] = proj[g]
    else:
        kept, near, pair = w_proj
        for k, dest in enumerate((kept, near, pair.at[0], pair.at[1])):
            for g in range(proj.shape[0]):
                dest[g] = proj[g, row_block(rank ^ k, dest.shape[1]), :]
    if emb_at is not None:
        table = refs[-5]
        place = lax.axis_index("dp")
        table[...] = jnp.zeros(table.shape, F32)
        for k, piece in enumerate(pieces):
            lines = piece[emb_at : emb_at + 16, :].astype(F32)
            mine = lax.broadcasted_iota(jnp.int32, lines.shape, 0) == place
            table[pl.ds(place ^ k, 1), :] = col_sum(jnp.where(mine, lines, 0.0))
    conv_taps(act, wide, taps, cols)
    biases = biases.get()
    bias = biases[1:2, lane_block(rank)]
    step = 256
    for i in range(pixels // step):
        hidden[i * step : (i + 1) * step, :] = conv_sum(taps, i * step, step, cols) + bias
    value = hidden[...]
    valid = valid_of(ext, pixels, LANES, cols)
    center, inverse = norm_stats(value, valid, pixel_count(ext, width), width)
    normed = (value - center) * inverse
    normed_out.ref[...] = normed
    normed_out.send()
    emb_value = emb.get()[...].astype(F32)
    emb_act = (emb_value * jax.nn.sigmoid(emb_value)).astype(BF16).astype(F32)
    mods = []
    for side in range(2):
        mod = biases[2 + side : 3 + side, lane_block(rank)]
        for j in range(emb_act.shape[1] // LANES):
            lanes = slice(j * LANES, (j + 1) * LANES)
            row = jnp.broadcast_to(emb_act[:, lanes], (16, LANES)).astype(BF16)
            mod = mod + mm(row, ada[side, lanes, :], 1, 0)[0:1]
        mods.append(mod)
    pre = normed * (1.0 + mods[0]) + mods[1]
    act_out[...] = (pre * jax.nn.sigmoid(pre) * valid).astype(BF16)
    aux[...] = jnp.zeros(aux.shape, F32)
    aux[0:1, :] = inverse
    aux[1:2, :] = mods[0]
    aux[2:3, :] = mods[1]


def conv_second_kernel(ext, gains, biases, own, *refs, cols, width, count_pieces, segments):
    blocks = refs[0:4]
    pieces = refs[4 : 4 + count_pieces]
    attn_in, act_out, residual_out, normed_out, aux, wide_out, w_qkv = refs[4 + count_pieces : -3]
    flat, qkv, taps = refs[-3:]
    rank = head_rank()
    act, wide, residual = (act_out.ref, wide_out.ref, residual_out.ref)
    pixels = act.shape[0]
    for k, block in enumerate(blocks):
        act[:, lane_block(rank ^ k)] = block[...]
    act_out.send()
    place_pieces(flat, pieces, *segments[0])
    taps_side_by_side(flat, wide)
    wide_out.send()
    place_pieces(qkv, pieces, *segments[1])
    for g in range(3):
        w_qkv[:, g * LANES : (g + 1) * LANES] = qkv[g]
    conv_taps(act, wide, taps, cols)
    gains, biases, own = (gains.get(), biases.get(), own.get())
    bias = biases[4:5, lane_block(rank)]
    step = 256
    for i in range(pixels // step):
        rows = slice(i * step, (i + 1) * step)
        third = conv_sum(taps, i * step, step, cols) + bias
        valid = valid_of(ext, step, LANES, cols, i * step)
        residual[rows, :] = own[rows, :].astype(F32) + valid * third
    residual_out.send()
    value = residual[...]
    valid = valid_of(ext, pixels, LANES, cols)
    center, inverse = norm_stats(value, valid, pixel_count(ext, width), width)
    normed = (value - center) * inverse
    normed_out.ref[...] = normed
    normed_out.send()
    attn_in[...] = (
        normed * gains[1:2, lane_block(rank)] + biases[5:6, lane_block(rank)]
    ).astype(BF16)
    aux[...] = jnp.broadcast_to(inverse, aux.shape)


def cotangent_kernel(ext, *refs):
    cots = refs[0:4]
    full_out, own_out, att, att_t, rows_weight = refs[-5:]
    rank = head_rank()
    rows = cots[0].shape[0]
    for k, cot in enumerate(cots):
        at = row_block(rank ^ k, rows)
        full_out.ref[at, :] = cot[...]
        own_out.ref[at, :] = cot[:, lane_block(rank)]
    full_out.send()
    own_out.send()
    weights = refs[4:-5]
    if len(weights) == 1:
        rows_weight[...] = weights[0][...]
    else:
        kept, near, far, corner = weights
        count = len(cots)
        size = LANES // (count * PROJ_PARTS)
        for k, block in enumerate((kept, near, far.at[0], corner.at[1])):
            for part in range(PROJ_PARTS):
                at = pl.ds(pl.multiple_of((part * count + (rank ^ k)) * size, 16), size)
                for g in range(block.shape[0]):
                    lanes = slice(g * LANES, (g + 1) * LANES)
                    rows_weight[at, lanes] = block[g, part * size : (part + 1) * size, :]
    for i in range(4):
        at = slice(i * rows, (i + 1) * rows)
        grad = mm(full_out.ref[at, :], rows_weight[...], 1, 1).astype(BF16)
        att[at, :] = grad
        att_t[:, at] = grad.astype(F32).T


def attention_kernel(ext, *refs, cols):
    blocks = refs[0:4]
    wide, cot_att, cot_att_t = refs[4:7]
    outs = refs[7:11]
    full_out, grads_out, attended_out = refs[11:14]
    qkv, keys_t, values_t, grad_kv, whole = refs[14:]
    attn_full, grads, attended = (full_out.ref, grads_out.ref, attended_out.ref)
    rank = head_rank()
    pixels = attn_full.shape[0]
    scale = 1.0 / math.sqrt(HD)
    for k in range(4):
        attn_full[:, lane_block(rank ^ k)] = blocks[k][...]
    full_out.send()
    step = 256
    qkv[...] = mm(attn_full[...], wide[...], 1, 0).astype(BF16)
    for i in range(pixels // step):
        at = slice(i * step, (i + 1) * step)
        keys_t[:, at] = qkv[at, LANES : 2 * LANES].astype(F32).T.astype(BF16)
        values_t[:, at] = qkv[at, 2 * LANES :].astype(F32).T.astype(BF16)
    lane = lax.broadcasted_iota(jnp.int32, (pixels, LANES), 1)
    sublane = lax.broadcasted_iota(jnp.int32, (LANES, pixels), 0)
    key_row, key_col = pixel_place(pixels, pixels, cols)
    key_valid = jnp.logical_and(key_row < ext[0, 0], key_col < ext[0, 1])
    att_sum = jnp.zeros((LANES, pixels), F32)
    query_sum = jnp.zeros((LANES, pixels), F32)
    for h in range(LANES // HD):
        mine = lax.shift_right_logical(lane, 6) == h
        mine_t = lax.shift_right_logical(sublane, 6) == h
        query = jnp.where(mine, qkv[:, 0:LANES], jnp.zeros((pixels, LANES), BF16))
        cot = jnp.where(mine, cot_att[...], jnp.zeros((pixels, LANES), BF16))
        scores = mm(qkv[:, LANES : 2 * LANES], query, 1, 1) * scale
        scores = jnp.where(key_valid, scores, MASKED)
        top = jnp.max(scores, axis=0, keepdims=True)
        expo = jnp.exp(scores - top)
        probs = expo * (1.0 / col_sum(expo))
        probs_low = probs.astype(BF16)
        att = mm(jnp.where(mine_t, values_t[...], jnp.zeros((LANES, pixels), BF16)), probs_low, 1, 0)
        att_sum = att_sum + att
        row_dot = col_sum(att * cot_att_t[...])
        grad_probs = mm(qkv[:, 2 * LANES :], cot, 1, 1)
        grad_scores = (probs * (grad_probs - row_dot)).astype(BF16)
        grad_values = mm(probs_low, cot, 1, 0)
        grad_keys = mm(grad_scores, query, 1, 0)
        if h == 0:
            grad_kv[:, LANES:] = grad_values
            grad_kv[:, 0:LANES] = grad_keys
        else:
            grad_kv[:, LANES:] += grad_values
            grad_kv[:, 0:LANES] += grad_keys
        query_sum = query_sum + mm(
            jnp.where(mine_t, keys_t[...], jnp.zeros((LANES, pixels), BF16)), grad_scores, 1, 0
        )
    attended[...] = att_sum.T.astype(BF16)
    grads[:, 0:LANES] = (query_sum.T * scale).astype(BF16)
    attended_out.send()
    grads[:, LANES : 2 * LANES] = (grad_kv[:, 0:LANES] * scale).astype(BF16)
    grads[:, 2 * LANES :] = grad_kv[:, LANES:].astype(BF16)
    grads_out.send()
    partial_sums(grads, wide, whole, outs)


def out_partial_kernel(ext, biases, attended, rows_weight, residual, cot, *refs):
    outs = refs[0:4]
    grads = refs[4:-1]
    whole = refs[-1]
    rank = head_rank()
    rows = outs[0].shape[0]
    attended = attended.get()
    for i in range(4):
        at = slice(i * rows, (i + 1) * rows)
        whole[at, :] = mm(attended[at, :], rows_weight[...], 1, 0)
    bias = biases.get()[6:7, lane_block(rank)]
    whole[:, lane_block(rank)] += residual.get()[...] + bias
    for k, out in enumerate(outs):
        out[...] = whole[row_block(rank ^ k, rows), :].astype(out.dtype)
    whole[0:LANES, :] = mm(attended[...], cot.get()[...], 0, 0)
    if len(grads) == 1:
        for g in range(grads[0].shape[0]):
            grads[0][g] = whole[0:LANES, g * LANES : (g + 1) * LANES]
    else:
        kept, near, pair = grads
        count = len(outs)
        size = LANES // (count * PROJ_PARTS)
        for k, dest in enumerate((kept, near, pair.at[0], pair.at[1])):
            for part in range(PROJ_PARTS):
                at = row_block(part * count + (rank ^ k), size)
                for g in range(dest.shape[0]):
                    dest[g, part * size : (part + 1) * size, :] = whole[
                        at, g * LANES : (g + 1) * LANES
                    ].astype(BF16)


def sum_kernel(ext, first, second, third, out):
    out[...] = (first[...] + second[...].astype(F32) + third[...].astype(F32)).astype(out.dtype)


def norm_third_back_kernel(ext, gains, kept, near, far, normed, inverse, cot, wide, *refs, cols, width):
    outs = refs[0:4]
    grad_res, third_out, sums, shifted, whole = refs[4:]
    rank = head_rank()
    pixels = kept.shape[0]
    grad = kept[...] + near[...].astype(F32) + far[...].astype(F32)
    normed, gains, cot = (normed.get()[...], gains.get(), cot.get())
    valid = valid_of(ext, pixels, LANES, cols)
    back = norm_back(
        grad * gains[1:2, lane_block(rank)], normed, inverse[0:1, :], valid,
        pixel_count(ext, width), width,
    )
    cot_value = cot[...].astype(F32)
    residual = cot_value + back
    grad_res.ref[...] = residual
    grad_res.send()
    third = (valid * residual).astype(BF16)
    third_out[...] = third
    third = third.astype(F32)
    shifted_grads(third, shifted, cols)
    sums[...] = jnp.zeros(sums.shape, F32)
    sums[0:1, :] = col_sum(grad * normed)
    sums[1:2, :] = col_sum(grad)
    sums[2:3, :] = col_sum(third)
    sums[3:4, :] = col_sum(cot_value)
    partial_sums(shifted, wide.get(), whole, outs)


def norm_second_back_kernel(ext, kept, near, far, normed, aux, wide, *refs, cols, width):
    outs = refs[0:4]
    first_out, sums, shifted, whole = refs[4:]
    pixels = kept.shape[0]
    grad_act = kept[...] + near[...].astype(F32) + far[...].astype(F32)
    normed = normed.get()[...]
    valid = valid_of(ext, pixels, LANES, cols)
    inverse, scale, shift = (aux[0:1, :], aux[1:2, :], aux[2:3, :])
    grad_pre = grad_act * valid * silu_grad(normed * (1.0 + scale) + shift)
    back = norm_back(
        grad_pre * (1.0 + scale), normed, inverse, valid, pixel_count(ext, width), width
    )
    first = back.astype(BF16)
    first_out[...] = first
    first = first.astype(F32)
    shifted_grads(first, shifted, cols)
    sums[...] = jnp.zeros(sums.shape, F32)
    sums[0:1, :] = col_sum(grad_pre * normed).astype(BF16).astype(F32)
    sums[1:2, :] = col_sum(grad_pre).astype(BF16).astype(F32)
    sums[2:3, :] = col_sum(first)
    partial_sums(shifted, wide.get(), whole, outs)


def norm_first_back_kernel(
    ext, gains, biases, kept, near, far, own, stats, grad_res, sums_third, sums_second, *refs,
    cols, width,
):
    out_kept, out_near, out_pair, table, held = refs
    rank = head_rank()
    pixels = kept.shape[0]
    rows = out_kept.shape[0]
    grad_act = kept[...] + near[...].astype(F32) + far[...].astype(F32)
    valid = valid_of(ext, pixels, LANES, cols)
    center, inverse = (stats[0:1, :], stats[1:2, :])
    normed = (own.get()[...].astype(F32) - center) * inverse
    gain = gains.get()[0:1, lane_block(rank)]
    bias = biases.get()[0:1, lane_block(rank)]
    grad_pre = grad_act * valid * silu_grad(normed * gain + bias)
    back = norm_back(grad_pre * gain, normed, inverse, valid, pixel_count(ext, width), width)
    held[...] = grad_res.get()[...] + back
    out_kept[...] = held[row_block(rank, rows), :]
    out_near[...] = held[row_block(rank ^ 1, rows), :].astype(BF16)
    for k in (2, 3):
        out_pair[k - 2] = held[row_block(rank ^ k, rows), :].astype(BF16)
    table[...] = jnp.zeros(table.shape, F32)
    table[0:1, :] = col_sum(grad_pre * normed)
    table[1:2, :] = sums_third[0:1, :]
    table[2:3, :] = col_sum(grad_pre)
    table[3:4, :] = sums_second[2:3, :]
    table[4:6, :] = sums_second[0:2, :]
    table[6:7, :] = sums_third[2:3, :]
    table[7:8, :] = sums_third[1:2, :]
    table[8:9, :] = sums_third[3:4, :]
    table[pl.ds(16 + 2 * lax.axis_index("dp"), 2), :] = sums_second[0:2, :]


def put_exact(dest, begin, value):
    rows = value.shape[0]
    high = value.astype(BF16)
    dest[begin : begin + rows, :] = high
    dest[begin + rows : begin + 2 * rows, :] = (value - high.astype(F32)).astype(BF16)


def get_exact(source, begin, rows):
    high = source[begin : begin + rows, :].astype(F32)
    return high + source[begin + rows : begin + 2 * rows, :].astype(F32)


def rows_join_kernel(ext, kept, near, far, corner, out):
    rank = head_rank()
    for k, block in enumerate((kept, near, far.at[0], corner.at[1])):
        out[:, lane_block(rank ^ k)] = block[...].astype(F32)


def taps_grad(act, shifted, flat):
    channels = act.shape[1]
    for i in range(channels // LANES):
        part = mm(act[:, i * LANES : (i + 1) * LANES], shifted[...], 0, 0)
        for tap in range(9):
            flat[0, tap * channels + i * LANES : tap * channels + (i + 1) * LANES, :] = part[
                :, tap * LANES : (tap + 1) * LANES
            ]


def dp_parts(dests, sources, dp_count):
    place = lax.axis_index("dp") if dp_count > 1 else 0
    for k, dest in enumerate(dests):
        at = 0
        for source in sources:
            size = source.shape[1] // dp_count
            for g in range(source.shape[0]):
                dest[at : at + size, :] = source[g, row_block(place ^ k, size), :].astype(dest.dtype)
                at += size


def qkv_grads_kernel(ext, attn, grads, *refs, dp_count):
    dests = refs[0:-1]
    qkv = refs[-1]
    part = mm(attn.get()[...], grads.get()[...], 0, 0)
    for g in range(3):
        qkv[g] = part[:, g * LANES : (g + 1) * LANES]
    if dp_count > 1:
        own, two, four, six, pairs = dests
        dests = (own, pairs.at[3], two, pairs.at[0], four, pairs.at[2], six, pairs.at[1])
    dp_parts(dests, (qkv,), dp_count)


def second_grads_kernel(ext, third, act, *refs, cols, dp_count):
    grad_proj = refs[0 : 4 if dp_count > 1 else 1]
    dests = refs[len(grad_proj) : -3]
    shifted, flat, proj = refs[-3:]
    shifted_grads(third[...].astype(F32), shifted, cols)
    act = act.get()
    taps_grad(act, shifted, flat)
    if len(grad_proj) == 1:
        proj[...] = grad_proj[0][...]
    else:
        kept, near, far, corner = grad_proj
        rank = head_rank()
        for k, block in enumerate((kept, near, far.at[0], corner.at[1])):
            size = block.shape[1]
            for g in range(proj.shape[0]):
                proj[g, row_block(rank ^ k, size), :] = block[g].astype(F32)
    dp_parts(split_dests(dests), (flat, proj), dp_count)


def split_dests(dests):
    if len(dests) == 1:
        return dests
    own, two, four, six, first_pair, second_pair = dests
    return (
        own, second_pair.at[1], two, first_pair.at[0], four, second_pair.at[0], six, first_pair.at[1]
    )


def first_grads_kernel(ext, first, act, sums, ada, *refs, cols, dp_count):
    dests = refs[0:-3]
    emb_part, shifted, flat = refs[-3:]
    shifted_grads(first[...].astype(F32), shifted, cols)
    taps_grad(act.get(), shifted, flat)
    dp_parts(split_dests(dests), (flat,), dp_count)
    ada = ada.get()
    for j in range(emb_part.shape[0]):
        row = jnp.zeros((1, LANES), F32)
        for side in range(2):
            mod = jnp.broadcast_to(sums[side : side + 1, :], (16, LANES)).astype(BF16)
            row = row + mm(mod, ada[side, j * LANES : (j + 1) * LANES, :], 1, 1)[0:1]
        emb_part[j : j + 1, :] = row


def near_kernel(ext, other, two, six, out):
    size = two.shape[0]
    for k, mine in enumerate((two, six)):
        out[k, 0:size, :] = (mine[...].astype(F32) + other[k].astype(F32)).astype(BF16)


def near_both_kernel(ext, other, two, six, ahead, ahead_two, ahead_six, out):
    size = two.shape[0]
    near_kernel(ext, other, two, six, out.at[:, pl.ds(0, size)])
    near_kernel(ext, ahead, ahead_two, ahead_six, out.at[:, pl.ds(size, ahead_two.shape[0])])


def near_table_kernel(ext, other, two, six, table, beside, out, total):
    size = two.shape[0]
    for k, mine in enumerate((two, six)):
        out[k * size : (k + 1) * size, :] = (
            mine[...].astype(F32) + other[k].astype(F32)
        ).astype(BF16)
    total[...] = table[...] + beside[...]
    put_exact(out, 2 * size, total[...])


def far_kernel(ext, four, late, near, out):
    size = four.shape[0]
    value = four[...].astype(F32) + late[0].astype(F32) + near[1, 0:size, :].astype(F32)
    out[0:size, :] = value.astype(BF16)


def far_both_kernel(ext, four, late, ahead_four, ahead, near, out):
    size = four.shape[0]
    far_kernel(ext, four, late, near, out)
    rows = pl.ds(size, ahead_four.shape[0])
    far_kernel(ext, ahead_four, ahead.at[pl.ds(2, 2)], near.at[:, rows], out.at[rows])


def far_table_kernel(ext, four, late, near, table, out, total):
    size = four.shape[0]
    value = four[...].astype(F32) + late[0].astype(F32) + near[size : 2 * size, :].astype(F32)
    out[0:size, :] = value.astype(BF16)
    total[...] = table[...] + get_exact(near, 2 * size, table.shape[0])
    put_exact(out, size, total[...])


def dp_pairs(parts):
    early = hop(parts[4], "dp", 1)
    return (early, hop(parts[5], "dp", 1))


def split_second_kernel(
    ext, own, late, ahead_own, ahead, straight, far, kept, near, pair, proj, held, *,
    rows_conv, rows_qkv,
):
    rank = head_rank()
    size = own.shape[0]
    held[...] = straight[0].astype(F32) + far[...].astype(F32)
    held[0:size, :] += own[...] + late[1].astype(F32)
    held[size:, :] += ahead_own[...] + ahead[3].astype(F32)
    for k, dest in enumerate((kept, near, pair.at[0], pair.at[1])):
        peer = rank ^ k
        dest[0:rows_conv, :] = held[row_block(peer, rows_conv), :].astype(dest.dtype)
        for g in range(3):
            begin = size + g * 4 * rows_qkv
            dest[rows_conv + g * rows_qkv : rows_conv + (g + 1) * rows_qkv, :] = held[
                pl.ds(pl.multiple_of(begin + peer * rows_qkv, 8), rows_qkv), :
            ].astype(dest.dtype)
    proj[...] = held[4 * rows_conv : size, :]


def split_first_kernel(
    ext, own, late, straight, far, table, emb_part, kept, near, pair, total, held, *, rows_conv
):
    rank = head_rank()
    size = held.shape[0]
    lines = table.shape[0]
    held[...] = own[...] + sum(
        part[0:size, :].astype(F32) for part in (late.at[1], straight, far)
    )
    total[0:lines, :] = table[...] + get_exact(far, size, lines)
    total[lines:, :] = emb_part[...]
    kept[...] = held[row_block(rank, rows_conv), :]
    for k, dest in enumerate((near, pair.at[0], pair.at[1])):
        dest[0:rows_conv, :] = held[row_block(rank ^ (k + 1), rows_conv), :].astype(BF16)
        put_exact(dest, rows_conv, total[...])


def join_second_kernel(ext, kept, near, far, corner, proj, conv_out, qkv_out, proj_out, *, rows_conv, rows_qkv):
    rank = head_rank()
    rows_proj = proj.shape[0] // 4
    low_half = lax.broadcasted_iota(jnp.int32, (rows_qkv, LANES), 1) < HD
    for k, block in enumerate((kept, near, far.at[0], corner.at[1])):
        peer = rank ^ k
        conv_out[pl.ds(peer, rows_conv, stride=4), :] = block[0:rows_conv, :].astype(F32)
        part = [
            block[rows_conv + g * rows_qkv : rows_conv + (g + 1) * rows_qkv, :].astype(F32)
            for g in range(3)
        ]
        keys = pltpu.roll(part[1], HD, 1)
        mixed = (
            jnp.where(low_half, part[0], keys),
            jnp.where(low_half, part[2], part[0]),
            jnp.where(low_half, keys, part[2]),
        )
        for g in range(3):
            qkv_out[pl.ds(peer * 3 + g, rows_qkv, stride=12), :] = mixed[g]
    for g in range(4):
        proj_out[pl.ds(g, rows_proj, stride=4), :] = proj[
            g * rows_proj : (g + 1) * rows_proj, :
        ].astype(F32)


def join_first_kernel(
    ext, kept, near, far, corner, total, embs, emb, conv_out, *refs, rows_conv
):
    rank = head_rank()
    outs, (mods, table, held, t1, t2, t3) = (refs[:4], refs[4:])
    blocks = (near, far.at[0], corner.at[1])
    conv_out[pl.ds(rank, rows_conv, stride=4), :] = kept[...]
    for k, (block, other) in enumerate(zip(blocks, (t1, t2, t3))):
        conv_out[pl.ds(rank ^ (k + 1), rows_conv, stride=4), :] = block[0:rows_conv, :].astype(F32)
        other[...] = get_exact(block, rows_conv, other.shape[0])
    small_grads_kernel(ext, embs, emb, total, t1, t2, t3, *outs, mods, table, held)


def small_grads_kernel(ext, embs, emb, t0, t1, t2, t3, gains_out, biases_out, ada_out, emb_out, mods, table, held):
    rank = head_rank()
    images = embs.shape[0]
    for k, block in enumerate((t0, t1, t2, t3)):
        table[:, lane_block(rank ^ k)] = block[0:16, :]
        for side in range(2):
            mods[:, lane_block(side * 4 + (rank ^ k))] = block[pl.ds(16 + side, images, stride=2), :]
    gains_out[...] = table[0:2, :]
    biases_out[...] = table[2:9, :]
    value = embs[...]
    part = mm((value * jax.nn.sigmoid(value)).astype(BF16), mods[...].astype(BF16), 0, 0)
    rows = ada_out.shape[0] // 8
    if part.shape[0] != rows:
        held[...] = part
        part = held[row_block(rank, rows), :]
    for g in range(8):
        ada_out[pl.ds(g, rows, stride=8), :] = part[:, g * LANES : (g + 1) * LANES]
    value = emb.get()[...].astype(F32)
    slope = silu_grad(value)
    begin = 16 + 2 * images
    for j in range(value.shape[1] // LANES):
        lanes = slice(j * LANES, (j + 1) * LANES)
        total = sum(block[begin + j : begin + j + 1, :] for block in (t0, t1, t2, t3))
        emb_out[:, lanes] = total * slope[:, lanes]


def body(
    inputs, embedding, extent, cotangent, gains, biases,
    conv_first, conv_second, qkv_master, ada_master, proj_master,
):
    heads = lax.axis_size("head")
    dps = lax.axis_size("dp")
    batch, row_count, cols, channels = inputs.shape
    rows = row_count * cols
    pixels = rows * heads
    width = channels // GROUPS
    emb_rows = embedding.shape[1] // LANES
    ext = extent
    direct = dps == 8
    flats = [
        master.reshape(-1, LANES)
        for master in (conv_first, conv_second, qkv_master, ada_master, proj_master)
    ]
    rows_conv = flats[0].shape[0] // 4
    rows_qkv = flats[2].shape[0] // 12
    rows_ada = flats[3].shape[0] // 8
    rows_proj = flats[4].shape[0] // 4
    far_gains, far_biases, far_emb = (Far(x, pinned=True) for x in (gains, biases, embedding))
    spread = [(i, (i % dps) * heads + i // dps) for i in range(dps * heads)]
    inputs_own = inputs.reshape(rows, channels)
    cot_own = cotangent.reshape(rows, channels)
    if direct:
        rows_a = rows_conv + 2 * rows_ada
        rows_b = rows_conv + 3 * rows_qkv
        far_flats = [Far(flat, pinned=True) for flat in flats]
        kept, near, pair, pj = call(
            first_out_kernel,
            [
                sds((rows_a, LANES), BF16), sds((rows_a, LANES), BF16),
                sds((2, rows_a, LANES), BF16), sds((4 * rows_proj, LANES), BF16),
            ],
            [None, far_flats[0], far_flats[3], far_flats[4]],
        )
        (first_piece,) = call(
            functools.partial(first_piece_kernel, segments=(rows_conv, rows_ada, rows_ada)),
            [sds((4 * rows_conv + 8 * rows_ada + 16 + 4 * rows_proj, LANES), BF16)],
            [None, kept, *head_exchange(near, pair), far_emb, pj],
            scratch=[pltpu.VMEM((16, LANES), F32)],
        )
        second_kept, near, far = call(
            second_out_kernel,
            [
                sds((rows_b, LANES), BF16), sds((rows_b, LANES), BF16),
                sds((channels // LANES * rows + 2 * rows_b, LANES), BF16),
            ],
            [None, far_flats[1], far_flats[2], Far(inputs_own, pinned=True)],
        )
        far = hop(far, "head", 2)
        corner = hop(far, "head", 1)
        blocks = (inputs_own, hop(inputs_own, "head", 1), far, corner)
        rows_second = 4 * rows_conv + 12 * rows_qkv + 4 * rows_proj
        (second_piece,) = call(
            functools.partial(second_piece_kernel, segments=(rows_conv,) + (rows_qkv,) * 3),
            [sds((rows_second - 4 * rows_proj, LANES), BF16)],
            [None, second_kept, hop(near, "head", 1), far, corner],
        )
        first_straight = dp_stepwise(first_piece)
        second_straight = dp_stepwise(second_piece)
        proj_at = 4 * rows_conv + 8 * rows_ada + 16
        first_segments = (
            (0, 1, 4 * rows_conv),
            (4 * rows_conv, 2, 4 * rows_ada),
            (proj_at, 4, rows_proj),
        )
        second_segments = ((0, 1, 4 * rows_conv), (4 * rows_conv, 3, 4 * rows_qkv))
    else:
        first_pieces, first_segments, second_pieces, second_segments, embs = gather_plain(
            flats, embedding, spread, channels
        )
        blocks = head_gather(inputs_own)

    act_first, own, stats_first = call(
        functools.partial(norm_first_kernel, cols=cols, width=width),
        [sds((pixels, channels), BF16), Far(sds((pixels, LANES), BF16)), sds((8, LANES), F32)],
        [ext, far_gains, far_biases, *blocks],
        scratch=[pltpu.VMEM((8, channels), F32)],
        us=2.0,
    )
    if direct:
        first_pieces, token = dp_beside_in_turn(first_straight, second_kept[:TOKEN])
    cots = head_gather(following(cot_own, blocks[2]))
    wide_shape = (channels, 9 * LANES)
    taps_scratch = pltpu.VMEM((pixels + 2 * cols, 9 * LANES), F32)
    flat_scratch = pltpu.VMEM((1, 9 * channels, LANES), BF16)
    n_pieces = len(first_pieces)
    groups = channels // LANES
    if direct:
        part = (groups, LANES // heads, LANES)
        proj_outs = [sds(part, BF16), sds(part, BF16), sds((2, *part), BF16)]
    else:
        proj_outs = [sds((LANES, channels), BF16)]
    first_outs = call(
        functools.partial(
            conv_first_kernel, cols=cols, width=width, count_pieces=n_pieces,
            segments=first_segments,
            emb_at=4 * rows_conv + 8 * rows_ada if direct else None,
        ),
        [
            sds((pixels, LANES), BF16), Far(sds((pixels, LANES), F32)), sds((8, LANES), F32),
            Far(sds(wide_shape, BF16)), Far(sds((2, emb_rows * LANES, LANES), BF16)),
            Far(sds((pixels, channels), BF16), held=False),
        ]
        + proj_outs
        + ([sds((dps, LANES), F32)] if direct else []),
        [ext, far_biases, act_first, far_emb, *first_pieces],
        scratch=[
            flat_scratch,
            taps_scratch,
            pltpu.VMEM((pixels, LANES), F32),
            pltpu.VMEM((groups, LANES, LANES), BF16),
        ],
        us=4.0,
        after=[token] if direct else (),
    )
    act_second_own, normed_second, aux_second, wide_first, ada_full, act_first = first_outs[:6]
    w_proj = first_outs[6 : 6 + len(proj_outs)]
    if direct:
        embs = first_outs[-1]
        w_proj = (w_proj[0], *head_exchange(*w_proj[1:]))
        second_pieces = dp_beside(second_straight)
        mark = []
        act_second_own = following(act_second_own, second_pieces[1], second_straight[1])
    blocks = head_gather(act_second_own, *([second_pieces[3], second_pieces[5]] if direct else []))
    attn_own, act_second, residual, normed_third, aux_third, wide_second, w_qkv = call(
        functools.partial(
            conv_second_kernel, cols=cols, width=width, count_pieces=n_pieces,
            segments=second_segments,
        ),
        [
            sds((pixels, LANES), BF16), Far(sds((pixels, channels), BF16)),
            Far(sds((pixels, LANES), F32)), Far(sds((pixels, LANES), F32)), sds((8, LANES), F32),
            Far(sds(wide_shape, BF16)), sds((channels, 3 * LANES), BF16),
        ],
        [ext, far_gains, far_biases, Far(own), *blocks, *second_pieces],
        scratch=[
            flat_scratch,
            pltpu.VMEM((3, channels, LANES), BF16),
            taps_scratch,
        ],
        us=4.0,
        after=w_proj[1:] if direct else (),
    )
    cot_full, cot_own, cot_att, cot_att_t, rows_weight = call(
        cotangent_kernel,
        [
            Far(sds((pixels, channels), BF16)), Far(sds((pixels, LANES), BF16)),
            sds((pixels, LANES), BF16), sds((LANES, pixels), F32), sds((LANES, channels), BF16),
        ],
        [None, *cots, *w_proj],
    )
    blocks = head_gather(attn_own, cot_att)
    whole_scratch = pltpu.VMEM((pixels, channels), F32)
    shifted_scratch = pltpu.VMEM((pixels, 9 * LANES), BF16)
    split_outs = [sds((pixels, LANES), F32)] + [sds((pixels, LANES), BF16)] * 3
    *parts, attn_full, grads_qkv, attended = call(
        functools.partial(attention_kernel, cols=cols),
        split_outs
        + [
            Far(sds((pixels, channels), BF16)), Far(sds((pixels, 3 * LANES), BF16)),
            Far(sds((pixels, LANES), BF16)),
        ],
        [ext, *blocks, w_qkv, cot_att, cot_att_t],
        scratch=[
            pltpu.VMEM((pixels, 3 * LANES), BF16),
            pltpu.VMEM((LANES, pixels), BF16),
            pltpu.VMEM((LANES, pixels), BF16),
            pltpu.VMEM((pixels, 2 * LANES), F32),
            whole_scratch,
        ],
        us=15.0,
    )
    parts, _ = head_reduce(ext, parts)
    grad_outs = proj_outs if direct else [sds((groups, LANES, LANES), F32)]
    out_all = call(
        out_partial_kernel,
        [sds((rows, channels), F32)] + [sds((rows, channels), BF16)] * 3 + grad_outs,
        [None, far_biases, Far(attended), rows_weight, Far(residual), Far(cot_full)],
        scratch=[whole_scratch],
        us=2.0,
    )
    out_parts, grad_proj = (out_all[:4], out_all[4:])
    if direct:
        grad_proj = (grad_proj[0], *head_exchange(*grad_proj[1:]))
    n_dests = dps if direct else 1

    def grad_outs(size):
        size = size // n_dests
        if not direct:
            return [sds((size, LANES), F32)]
        one = sds((size, LANES), BF16)
        return [sds((size, LANES), F32), one, one, one] + [sds((2, size, LANES), BF16)] * 2

    ahead_outs = grad_outs(3 * channels)
    if direct:
        ahead_outs = ahead_outs[:4] + [sds((4, *ahead_outs[1].shape), BF16)]
    ahead_parts = call(
        functools.partial(qkv_grads_kernel, dp_count=n_dests),
        ahead_outs,
        [None, Far(attn_full), Far(grads_qkv)],
        scratch=[pltpu.VMEM((3, channels, LANES), F32)],
        after=out_parts[:1],
    )
    if direct:
        ahead = hop(ahead_parts[4], "dp", 1)
    *parts, grad_res, third, sums_third = call(
        functools.partial(norm_third_back_kernel, cols=cols, width=width),
        split_outs
        + [Far(sds((pixels, LANES), F32)), sds((pixels, LANES), BF16), sds((8, LANES), F32)],
        [
            ext, far_gains, *parts, Far(normed_third), aux_third, Far(cot_own), Far(wide_second),
        ],
        scratch=[shifted_scratch, whole_scratch],
        us=150.0,
        after=ahead_parts[:1],
    )
    if direct:
        parts[3] = following(parts[3], *grad_proj[1:3], ahead)
    out_sums, _ = head_reduce(ext, out_parts)
    (output,) = call(sum_kernel, [sds((rows, channels), BF16)], [None, *out_sums])
    parts, sent = head_reduce(ext, parts)
    flat_grad = pltpu.VMEM((1, 9 * channels, LANES), F32)
    second_parts = call(
        functools.partial(second_grads_kernel, cols=cols, dp_count=n_dests),
        grad_outs(10 * channels),
        [None, third, Far(act_second), *grad_proj],
        scratch=[
            shifted_scratch,
            flat_grad,
            pltpu.VMEM((channels // LANES, LANES, LANES), F32),
        ],
        us=4.0,
        after=sent,
    )
    *parts, first, sums_second = call(
        functools.partial(norm_second_back_kernel, cols=cols, width=width),
        split_outs + [sds((pixels, LANES), BF16), sds((8, LANES), F32)],
        [ext, *parts, Far(normed_second), aux_second, Far(wide_first)],
        scratch=[shifted_scratch, whole_scratch],
        us=150.0,
        after=second_parts[:1],
    )
    if direct:
        second_pairs = dp_pairs(second_parts)
    parts, sent = head_reduce(ext, parts, second_pairs[:1] if direct else ())
    *first_parts, emb_part = call(
        functools.partial(first_grads_kernel, cols=cols, dp_count=n_dests),
        grad_outs(9 * channels) + [sds((emb_rows, LANES), F32)],
        [ext, first, Far(act_first), sums_second, Far(ada_full)],
        scratch=[shifted_scratch, flat_grad],
        us=3.0,
        after=sent,
    )
    table_rows = 16 + 2 * dps
    early = [emb_part]
    if direct:
        first_early, first_late = (hop(pair, "dp", 1) for pair in first_parts[4:6])
        (near_pair,) = call(
            near_both_kernel,
            [sds((2, rows_second, LANES), BF16)],
            [
                None, second_pairs[0], second_parts[1], second_parts[3], ahead, ahead_parts[1],
                ahead_parts[3],
            ],
            us=0.6,
            after=sent,
        )
        early += [near_pair, second_pairs[1]]
        second_near = hop(near_pair, "dp", 2)
    kept_rows, near, pair, table = call(
        functools.partial(norm_first_back_kernel, cols=cols, width=width),
        [
            sds((rows, LANES), F32), sds((rows, LANES), BF16), sds((2, rows, LANES), BF16),
            sds((table_rows, LANES), F32),
        ],
        [
            ext, far_gains, far_biases, *parts, Far(own), stats_first, Far(grad_res), sums_third,
            sums_second,
        ],
        scratch=[pltpu.VMEM((pixels, LANES), F32)],
        us=40.0,
        after=early,
    )
    small_outs = [
        sds(gains.shape, F32), sds(biases.shape, F32), sds(flats[3].shape, F32),
        sds(embedding.shape, F32),
    ]
    small_scratch = [
        pltpu.VMEM((dps, 8 * LANES), F32),
        pltpu.VMEM((16, channels), F32),
        pltpu.VMEM((LANES, 8 * LANES), F32),
    ]
    if direct:
        beside = hop(table, "dp", 1)
        (far_block,) = call(
            far_both_kernel,
            [sds((rows_second, LANES), BF16)],
            [None, second_parts[2], second_pairs[1], ahead_parts[2], ahead, second_near],
            us=0.6,
            after=[kept_rows],
        )
        second_left = [
            second_parts[0], second_pairs[1], ahead_parts[0], ahead, second_near,
            hop(far_block, "dp", 4),
        ]
        size = 4 * rows_conv + 2 * table_rows
        near_pair, table = call(
            near_table_kernel,
            [sds((4 * rows_conv + size, LANES), BF16), sds(table.shape, F32)],
            [None, first_early, first_parts[1], first_parts[3], table, beside],
            us=0.6,
        )
        first_near = hop(near_pair, "dp", 2)
        far_block, table = call(
            far_table_kernel,
            [sds((size, LANES), BF16), sds(table.shape, F32)],
            [None, first_parts[2], first_late, first_near, table],
            us=0.6,
            after=[far_block],
        )
        first_left = [first_parts[0], first_late, first_near, hop(far_block, "dp", 4)]
    (grad_inputs,) = call(
        rows_join_kernel,
        [sds((rows, channels), F32)],
        [None, kept_rows, *head_exchange(near, pair)],
    )
    if direct:
        second_own, near, pair, pj = call(
            functools.partial(split_second_kernel, rows_conv=rows_conv, rows_qkv=rows_qkv),
            [
                sds((rows_b, LANES), F32), sds((rows_b, LANES), BF16),
                sds((2, rows_b, LANES), BF16), sds((4 * rows_proj, LANES), F32),
            ],
            [None, *second_left],
            scratch=[pltpu.VMEM((rows_second, LANES), F32)],
        )
        second_blocks = head_exchange(near, pair)
        second_grad, qkv_grad, proj_grad = call(
            functools.partial(join_second_kernel, rows_conv=rows_conv, rows_qkv=rows_qkv),
            [sds(flats[i].shape, F32) for i in (1, 2, 4)],
            [None, second_own, *second_blocks, pj],
        )
        lines = table_rows + emb_rows
        kept, near, pair, table = call(
            functools.partial(split_first_kernel, rows_conv=rows_conv),
            [
                sds((rows_conv, LANES), F32), sds((rows_conv + 2 * lines, LANES), BF16),
                sds((2, rows_conv + 2 * lines, LANES), BF16), sds((lines, LANES), F32),
            ],
            [None, *first_left, table, emb_part],
            scratch=[pltpu.VMEM((4 * rows_conv, LANES), F32)],
            after=second_blocks[:2],
        )
        first_blocks = head_exchange(near, pair, output, grad_inputs, second_grad)
        first_grad, grad_gains, grad_biases, ada_grad, grad_embedding = call(
            functools.partial(join_first_kernel, rows_conv=rows_conv),
            [sds(flats[0].shape, F32)] + small_outs,
            [None, kept, *first_blocks, table, embs, far_emb],
            scratch=small_scratch + [pltpu.VMEM((lines, LANES), F32)] * 3,
        )
    else:
        table = jnp.concatenate([lax.psum(table, "dp"), emb_part])
        grad_gains, grad_biases, ada_grad, grad_embedding = call(
            small_grads_kernel,
            small_outs,
            [ext, embs, far_emb, *head_gather(table)],
            scratch=small_scratch,
        )
        first_grad, second_grad, qkv_grad, proj_grad = scatter_plain(
            first_parts[0], second_parts[0], ahead_parts[0], spread, channels
        )
    return (
        output.reshape(inputs.shape),
        grad_inputs.reshape(inputs.shape),
        grad_embedding,
        grad_gains,
        grad_biases,
        first_grad.reshape(-1),
        second_grad.reshape(-1),
        qkv_grad.reshape(-1),
        ada_grad.reshape(-1),
        proj_grad.reshape(-1),
    )


def gather_plain(flats, embedding, spread, channels):
    heads = lax.axis_size("head")

    def columns(flat, groups):
        blocks = flat.astype(BF16).reshape(-1, groups, LANES)
        return blocks

    def own_columns(blocks):
        got = lax.all_to_all(blocks, "head", split_axis=1, concat_axis=0, tiled=True)
        return lax.all_gather(got[:, 0], "dp", axis=0, tiled=True)

    first, second = (own_columns(columns(flats[i], heads).reshape(-1, heads, 1, LANES))[:, 0] for i in (0, 1))
    qkv = columns(flats[2], 12).reshape(-1, heads, 2, 3, HD)
    qkv = jnp.swapaxes(qkv, 2, 3).reshape(-1, heads, 3, LANES)
    qkv = jnp.swapaxes(own_columns(qkv), 0, 1).reshape(-1, LANES)
    ada = columns(flats[3], 8).reshape(-1, 2, heads, LANES)
    ada = jnp.swapaxes(own_columns(jnp.swapaxes(ada, 1, 2)), 0, 1).reshape(-1, LANES)
    proj = lax.ppermute(flats[4].astype(BF16), ("dp", "head"), spread)
    proj = lax.all_gather(proj, "dp", axis=0, tiled=True).reshape(-1, channels // LANES, LANES)
    proj = jnp.swapaxes(proj, 0, 1).reshape(-1, LANES)
    embs = lax.all_gather(embedding, "dp", axis=0, tiled=True).astype(F32)
    embs = embs.reshape(embs.shape[0], -1, flats[3].shape[0] // 8)
    embs = lax.dynamic_index_in_dim(
        embs, lax.axis_index("dp") * heads + lax.axis_index("head"), 1, False
    )
    first_piece = jnp.concatenate([first, ada, proj])
    second_piece = jnp.concatenate([second, qkv])
    proj_at = 9 * channels + ada.shape[0]
    return (
        [first_piece],
        (
            (0, 1, 9 * channels),
            (9 * channels, 2, ada.shape[0] // 2),
            (proj_at, channels // LANES, LANES),
        ),
        [second_piece],
        ((0, 1, 9 * channels), (9 * channels, 3, channels)),
        embs,
    )


def scatter_plain(first, second, qkv, spread, channels):
    heads = lax.axis_size("head")

    def rows_of(grad):
        part = lax.psum_scatter(grad, "dp", scatter_dimension=0, tiled=True)
        return lax.all_to_all(part[:, None], "head", split_axis=0, concat_axis=1, tiled=True)

    def conv(grad):
        return rows_of(grad[:, None])

    qkv = jnp.swapaxes(qkv.reshape(3, channels, LANES), 0, 1)
    qkv = rows_of(qkv).reshape(-1, heads, 3, 2, HD)
    qkv = jnp.swapaxes(qkv, 2, 3)
    proj = jnp.swapaxes(second[9 * channels :].reshape(-1, LANES, LANES), 0, 1)
    proj = lax.psum_scatter(proj, "dp", scatter_dimension=0, tiled=True)
    proj = lax.ppermute(proj, ("dp", "head"), [(j, i) for i, j in spread])
    return (conv(first), conv(second[: 9 * channels]), qkv, proj)


def solution(mesh):
    flat = P(("dp", "head"))
    image = P("dp", "head", None, None)
    return jax.shard_map(
        body,
        mesh=mesh,
        in_specs=(image, P("dp", None), P("dp", None), image, P(), P(), flat, flat, flat, flat, flat),
        out_specs=(image, image, P("dp", None), P(), P(), flat, flat, flat, flat, flat),
        check_vma=False,
    )
```

```python
import functools
import math

import jax
import jax.numpy as jnp
from jax import lax
from jax.experimental import pallas as pl
from jax.experimental.pallas import tpu as pltpu
from jax.sharding import PartitionSpec as P

HD = 64
TOKEN = 96
STEP = 512
PROJ_PARTS = 2
MARK = 64
GROUPS = 32
EPS = 1e-05
MASKED = -1e30
LANES = 128
F32 = jnp.float32
BF16 = jnp.bfloat16
VMEM_SPEC = pl.BlockSpec(memory_space=pltpu.VMEM)
SMEM_SPEC = pl.BlockSpec(memory_space=pltpu.SMEM)


def sds(shape, dtype):
    return jax.ShapeDtypeStruct(shape, dtype)


class Far:
    def __init__(self, array, held=True, pinned=False):
        self.array = pltpu.with_memory_space_constraint(array, pltpu.HBM) if pinned else array
        self.held = held


class Fetch:
    def __init__(self, source, ref, sem):
        self.copy = pltpu.make_async_copy(source, ref, sem)
        self.ref = ref
        self.copy.start()

    def get(self):
        self.copy.wait()
        return self.ref


class Store:
    def __init__(self, dest, ref, sem):
        self.dest = dest
        self.ref = ref
        self.sem = sem
        self.copy = None

    def send(self, source=None):
        self.copy = pltpu.make_async_copy(self.ref if source is None else source, self.dest, self.sem)
        self.copy.start()


def call(kernel, outs, args, scratch=(), us=1.0, vmem=24, after=()):
    scalars = args[0] is not None
    args = list(args) if scalars else list(args[1:])
    arrays = [arg.array if isinstance(arg, Far) else arg for arg in args]
    results = [out.array if isinstance(out, Far) else out for out in outs]
    far_in = [isinstance(arg, Far) for arg in args]
    far_out = [isinstance(out, Far) for out in outs]
    held = [
        pltpu.VMEM(x.array.shape, x.array.dtype)
        for x in list(args) + list(outs)
        if isinstance(x, Far) and x.held
    ]
    copies = sum(far_in) + sum(far_out)

    def run(*refs):
        ins = refs[: len(args)]
        begin = len(args) + len(after)
        dests = refs[begin : begin + len(outs)]
        begin += len(outs)
        buffers = iter(refs[begin : begin + len(held)])
        begin += len(held)
        sems = refs[begin] if copies else None
        rest = refs[begin + (1 if copies else 0) :]
        count = 0
        given = []
        for ref, far in zip(ins, far_in):
            if far:
                ref = Fetch(ref, next(buffers), sems.at[count])
                count += 1
            given.append(ref)
        stores = []
        for ref, out in zip(dests, outs):
            if isinstance(out, Far):
                ref = Store(ref, next(buffers) if out.held else None, sems.at[count])
                stores.append(ref)
                count += 1
            given.append(ref)
        kernel(*([] if scalars else [None]), *given, *rest)
        for store in stores:
            store.copy.wait()

    hbm = pl.BlockSpec(memory_space=pltpu.HBM)
    anywhere = pl.BlockSpec(memory_space=pl.ANY)
    return pl.pallas_call(
        run,
        out_shape=tuple(results),
        in_specs=[
            hbm if far else SMEM_SPEC if scalars and i == 0 else VMEM_SPEC
            for i, far in enumerate(far_in)
        ]
        + [anywhere for _ in after],
        out_specs=tuple(hbm if far else VMEM_SPEC for far in far_out),
        scratch_shapes=held
        + ([pltpu.SemaphoreType.DMA((copies,))] if copies else [])
        + list(scratch),
        compiler_params=pltpu.CompilerParams(vmem_limit_bytes=vmem * 1024 * 1024),
        cost_estimate=pl.CostEstimate(
            flops=int(3e7 * us),
            bytes_accessed=1024,
            transcendentals=0,
        ),
    )(*arrays, *after)


def following(value, *earlier):
    return lax.optimization_barrier((value, *earlier))[0]


def hop(value, axis, bit):
    count = lax.axis_size(axis)
    return lax.ppermute(value, axis, [(i, i ^ bit) for i in range(count)])


def head_gather(block, *earlier):
    far = hop(block, "head", 2)
    near = hop(block, "head", 1)
    return (block, near, far, hop(following(far, *earlier) if earlier else far, "head", 1))


def head_exchange(near_block, far_pair, *earlier):
    far = hop(far_pair, "head", 2)
    near = hop(near_block, "head", 1)
    return (near, far, hop(following(far, *earlier) if earlier else far, "head", 1))


def add_kernel(ext, first, second, out):
    out[...] = (first[...].astype(F32) + second[...].astype(F32)).astype(out.dtype)


def head_reduce(ext, blocks, after=()):
    kept, near_block, far_block, corner = blocks
    corner = hop(corner, "head", 1)
    (far_block,) = call(
        add_kernel, [sds(far_block.shape, BF16)], [None, far_block, corner], us=0.7, after=after
    )
    return ((kept, hop(near_block, "head", 1), hop(far_block, "head", 2)), [far_block])


def mm(left, right, left_dim, right_dim):
    return lax.dot_general(
        left, right, (((left_dim,), (right_dim,)), ((), ())), preferred_element_type=F32
    )


def lane_block(index):
    return pl.ds(pl.multiple_of(index * LANES, LANES), LANES)


def row_block(index, rows):
    return pl.ds(pl.multiple_of(index * rows, rows), rows)


def pixel_place(rows, lanes, cols, start=0):
    pixel = lax.broadcasted_iota(jnp.int32, (rows, lanes), 0) + start
    shift = cols.bit_length() - 1
    return (lax.shift_right_logical(pixel, shift), lax.bitwise_and(pixel, cols - 1))


def valid_of(ext, rows, lanes, cols, start=0):
    place_row, place_col = pixel_place(rows, lanes, cols, start)
    inside = jnp.logical_and(place_row < ext[0, 0], place_col < ext[0, 1])
    return jnp.where(inside, 1.0, 0.0).astype(F32)


def group_total(first, second, width):
    lanes = first.shape[-1]
    pick = lax.broadcasted_iota(jnp.int32, (8, lanes), 0)
    both = jnp.where(pick == 0, first, jnp.where(pick == 1, second, 0.0))
    shift = width.bit_length() - 1
    left = lax.shift_right_logical(lax.broadcasted_iota(jnp.int32, (lanes, lanes), 0), shift)
    right = lax.shift_right_logical(lax.broadcasted_iota(jnp.int32, (lanes, lanes), 1), shift)
    same = jnp.where(left == right, 1.0, 0.0).astype(F32)
    total = lax.dot_general(
        both,
        same,
        (((1,), (0,)), ((), ())),
        precision=lax.Precision.HIGHEST,
        preferred_element_type=F32,
    )
    return (total[0:1], total[1:2])


def pixel_count(ext, width):
    return (ext[0, 0] * ext[0, 1] * width).astype(F32)


def col_sum(value):
    return jnp.sum(value, axis=0, keepdims=True)


def head_rank():
    return lax.axis_index("head")


def norm_stats(value, valid, count, width):
    masked = value * valid
    total, square = group_total(col_sum(masked), col_sum(masked * value), width)
    center = total / count
    return (center, lax.rsqrt(square / count - center * center + EPS))


def norm_back(grad, normed, inverse, valid, count, width):
    first, second = group_total(col_sum(grad), col_sum(grad * normed), width)
    return (grad - valid * ((first + normed * second) * (1.0 / count))) * inverse


def silu_grad(value):
    gate = jax.nn.sigmoid(value)
    return gate * (1.0 + value * (1.0 - gate))


def place_pieces(dest, pieces, start, groups, rows):
    for k, piece in enumerate(pieces):
        part = lax.axis_index("dp") ^ k if len(pieces) > 1 else 0
        for group in range(groups):
            begin = start + group * rows
            dest[group, pl.ds(pl.multiple_of(part * rows, rows), rows), :] = piece[
                begin : begin + rows, :
            ]


def taps_side_by_side(flat, wide):
    channels = wide.shape[0]
    for tap in range(9):
        wide[:, tap * LANES : (tap + 1) * LANES] = flat[0, tap * channels : (tap + 1) * channels, :]


def conv_taps(act, wide, taps, cols):
    pixels = act.shape[0]
    lanes = wide.shape[1]
    taps[0:cols, :] = jnp.zeros((cols, lanes), F32)
    taps[pixels + cols :, :] = jnp.zeros((cols, lanes), F32)
    step = STEP

    def one(i, carry):
        begin = pl.multiple_of(i * step, step)
        taps[pl.ds(pl.multiple_of(begin + cols, cols), step), :] = mm(
            act[pl.ds(begin, step), :], wide[...], 1, 0
        )
        return carry

    lax.fori_loop(0, pixels // step, one, 0)


def conv_sum(taps, begin, rows, cols):
    def column(side):
        return sum(
            taps[
                pl.ds(pl.multiple_of(begin + up * cols, cols), rows),
                (up * 3 + side) * LANES : (up * 3 + side + 1) * LANES,
            ]
            for up in range(3)
        )

    place_col = pixel_place(rows, LANES, cols)[1]
    left = jnp.where(place_col > 0, pltpu.roll(column(0), 1, 0), 0.0)
    right = jnp.where(place_col < cols - 1, pltpu.roll(column(2), rows - 1, 0), 0.0)
    return column(1) + left + right


def shifted_grads(grad, dest, cols):
    pixels = grad.shape[0]
    place_col = pixel_place(pixels, LANES, cols)[1]
    sides = (
        jnp.where(place_col < cols - 1, pltpu.roll(grad, pixels - 1, 0), 0.0),
        grad,
        jnp.where(place_col > 0, pltpu.roll(grad, 1, 0), 0.0),
    )
    blank = jnp.zeros((cols, LANES), BF16)
    for side, value in enumerate(sides):
        low = value.astype(BF16)
        for up in range(3):
            lanes = slice((up * 3 + side) * LANES, (up * 3 + side + 1) * LANES)
            if up == 0:
                dest[0 : pixels - cols, lanes] = low[cols:, :]
                dest[pixels - cols :, lanes] = blank
            elif up == 1:
                dest[:, lanes] = low
            else:
                dest[cols:, lanes] = low[0 : pixels - cols, :]
                dest[0:cols, lanes] = blank


def partial_sums(left, right, whole, outs):
    step = STEP

    def one(i, carry):
        rows = pl.ds(pl.multiple_of(i * step, step), step)
        whole[rows, :] = mm(left[rows, :], right[...], 1, 1)
        return carry

    lax.fori_loop(0, left.shape[0] // step, one, 0)
    rank = head_rank()
    for k, out in enumerate(outs):
        out[...] = whole[:, lane_block(rank ^ k)].astype(out.dtype)


def two_sums(left, right, both, blocks):
    rank = head_rank()
    for i, (k, out) in enumerate(blocks):
        both[i * LANES : (i + 1) * LANES, :] = right[row_block(rank ^ k, LANES), :]
    part = mm(left[...], both[...], 1, 1)
    for i, (k, out) in enumerate(blocks):
        out[...] = part[:, i * LANES : (i + 1) * LANES].astype(out.dtype)


def rest_attention_kernel(ext, grads, wide, kept, upper, lower, near, both):
    two_sums(grads.get(), wide, both, ((0, kept), (1, near)))
    rows = upper.shape[0]
    upper[...] = near[0:rows, :]
    lower[...] = near[rows:, :]


def strided(ref, begin, stride):
    return ref[pl.ds(begin, ref.shape[0] // stride, stride=stride), :]


def put_rows(dest, begin, value):
    rows = value.shape[0]
    dest[begin : begin + rows, :] = value.astype(BF16)
    return begin + rows


def first_out_kernel(ext, first, ada, proj, kept, near, pair, parts):
    rank = head_rank()
    first, ada = (first.get(), ada.get())
    for k, dest in enumerate((kept, near, pair.at[0], pair.at[1])):
        at = put_rows(dest, 0, strided(first, rank ^ k, 4))
        for side in range(2):
            at = put_rows(dest, at, strided(ada, 4 * side + (rank ^ k), 8))
    proj = proj.get()
    at = 0
    for g in range(4):
        at = put_rows(parts, at, strided(proj, g, 4))


def second_out_kernel(ext, second, qkv, image, kept, near, far):
    rank = head_rank()
    second, qkv, image = (second.get(), qkv.get(), image.get())
    low_half = lax.broadcasted_iota(jnp.int32, (qkv.shape[0] // 12, LANES), 1) < HD
    rows = image.shape[0]
    groups = image.shape[1] // LANES
    for g in range(groups):
        far[g * rows : (g + 1) * rows, :] = image[:, g * LANES : (g + 1) * LANES]
    begin = groups * rows
    size = kept.shape[0]
    blocks = (kept, near, far.at[pl.ds(begin, size)], far.at[pl.ds(begin + size, size)])
    for k, dest in enumerate(blocks):
        at = put_rows(dest, 0, strided(second, rank ^ k, 4))
        part = [strided(qkv, (rank ^ k) * 3 + g, 12) for g in range(3)]
        at = put_rows(dest, at, jnp.where(low_half, part[0], part[1]))
        at = put_rows(dest, at, pltpu.roll(jnp.where(low_half, part[2], part[0]), HD, 1))
        put_rows(dest, at, jnp.where(low_half, part[1], part[2]))


def join_blocks(dest, blocks, segments):
    rank = head_rank()
    for k, block in enumerate(blocks):
        at, begin = (0, 0)
        for rows in segments:
            place = pl.ds(pl.multiple_of(begin + (rank ^ k) * rows, 16), rows)
            dest[place, :] = block[at : at + rows, :]
            at += rows
            begin += 4 * rows
    return 4 * sum(segments)


def first_piece_kernel(ext, kept, near, far, corner, emb, proj, piece, line, *, segments):
    at = join_blocks(piece, (kept, near, far.at[0], corner.at[1]), segments)
    emb = emb.get()
    line[...] = jnp.zeros(line.shape, F32)
    for j in range(emb.shape[1] // LANES):
        line[j : j + 1, :] = emb[0:1, j * LANES : (j + 1) * LANES].astype(F32)
    piece[at : at + 16, :] = line[...].astype(BF16)
    piece[at + 16 :, :] = proj[...]


def second_piece_kernel(ext, kept, near, far, corner, piece, *, segments):
    size = kept.shape[0]
    begin = far.shape[0] - 2 * size
    blocks = (kept, near, far.at[pl.ds(begin, size)], corner.at[pl.ds(begin + size, size)])
    join_blocks(piece, blocks, segments)


def dp_stepwise(piece):
    far = hop(piece, "dp", 4)
    return [piece, hop(piece, "dp", 2), far, hop(far, "dp", 2)]


def dp_beside(straight):
    near = [hop(value, "dp", 1) for value in straight]
    return [value for pair in zip(straight, near) for value in pair]


def dp_beside_in_turn(straight, token):
    own, two, four, six = straight
    own = hop(own, "dp", 1)
    two_near = hop(following(two, own), "dp", 1)
    token = hop(following(token, two_near), "head", 1)
    four_near = hop(four, "dp", 1)
    six_near = hop(following(six, token, four_near), "dp", 1)
    near = (own, two_near, four_near, six_near)
    return ([value for pair in zip(straight, near) for value in pair], token)


def norm_first_kernel(ext, gains, biases, *refs, cols, width):
    blocks = refs[0:4]
    act, own_out, stats, held = refs[4:]
    own = own_out.ref
    rank = head_rank()
    rows, channels = blocks[0].shape
    count = pixel_count(ext, width)
    total = jnp.zeros((1, channels), F32)
    square = jnp.zeros((1, channels), F32)
    def whole(block):
        if block.shape[1] == channels:
            return block[...].astype(F32)
        parts = [block[g * rows : (g + 1) * rows, :] for g in range(channels // LANES)]
        return jnp.concatenate(parts, axis=1).astype(F32)

    for k, block in enumerate(blocks):
        if block.shape[1] == channels:
            own[row_block(rank ^ k, rows), :] = block[:, lane_block(rank)]
        else:
            own[row_block(rank ^ k, rows), :] = block[row_block(rank, rows), :]
    own_out.send()
    for k, block in enumerate(blocks):
        value = whole(block)
        masked = value * valid_of(ext, rows, channels, cols, (rank ^ k) * rows)
        total = total + col_sum(masked)
        square = square + col_sum(masked * value)
    total, square = group_total(total, square, width)
    center = total / count
    inverse = lax.rsqrt(square / count - center * center + EPS)
    held[0:1, :] = center
    held[1:2, :] = inverse
    gain, bias = (gains.get()[0:1, :], biases.get()[0:1, :])
    for k, block in enumerate(blocks):
        peer = rank ^ k
        pre = (whole(block) - center) * inverse * gain + bias
        valid = valid_of(ext, rows, channels, cols, peer * rows)
        act[row_block(peer, rows), :] = (pre * jax.nn.sigmoid(pre) * valid).astype(BF16)
    stats[...] = held[:, lane_block(rank)]


def conv_first_kernel(ext, biases, act, emb, *refs, cols, width, count_pieces, segments, emb_at):
    pieces = refs[0:count_pieces]
    act_out, normed_out, aux, wide_out, ada_out, act_far = refs[count_pieces : count_pieces + 6]
    w_proj = refs[count_pieces + 6 : -4 if emb_at is None else -5]
    flat, taps, hidden, proj = refs[-4:]
    rank = head_rank()
    pixels = act.shape[0]
    act_far.send(act)
    place_pieces(flat, pieces, *segments[0])
    wide = wide_out.ref
    taps_side_by_side(flat, wide)
    wide_out.send()
    ada = ada_out.ref
    place_pieces(ada, pieces, *segments[1])
    ada_out.send()
    place_pieces(proj, pieces, *segments[2])
    if len(w_proj) == 1:
        for g in range(proj.shape[0]):
            w_proj[0][:, g * LANES : (g + 1) * LANES] = proj[g]
    else:
        kept, near, pair = w_proj
        for k, dest in enumerate((kept, near, pair.at[0], pair.at[1])):
            for g in range(proj.shape[0]):
                dest[g] = proj[g, row_block(rank ^ k, dest.shape[1]), :]
    if emb_at is not None:
        table = refs[-5]
        place = lax.axis_index("dp")
        table[...] = jnp.zeros(table.shape, F32)
        for k, piece in enumerate(pieces):
            lines = piece[emb_at : emb_at + 16, :].astype(F32)
            mine = lax.broadcasted_iota(jnp.int32, lines.shape, 0) == place
            table[pl.ds(place ^ k, 1), :] = col_sum(jnp.where(mine, lines, 0.0))
    conv_taps(act, wide, taps, cols)
    biases = biases.get()
    bias = biases[1:2, lane_block(rank)]
    step = 256
    for i in range(pixels // step):
        hidden[i * step : (i + 1) * step, :] = conv_sum(taps, i * step, step, cols) + bias
    value = hidden[...]
    valid = valid_of(ext, pixels, LANES, cols)
    center, inverse = norm_stats(value, valid, pixel_count(ext, width), width)
    normed = (value - center) * inverse
    normed_out.ref[...] = normed
    normed_out.send()
    emb_value = emb.get()[...].astype(F32)
    emb_act = (emb_value * jax.nn.sigmoid(emb_value)).astype(BF16).astype(F32)
    mods = []
    for side in range(2):
        mod = biases[2 + side : 3 + side, lane_block(rank)]
        for j in range(emb_act.shape[1] // LANES):
            lanes = slice(j * LANES, (j + 1) * LANES)
            row = jnp.broadcast_to(emb_act[:, lanes], (16, LANES)).astype(BF16)
            mod = mod + mm(row, ada[side, lanes, :], 1, 0)[0:1]
        mods.append(mod)
    pre = normed * (1.0 + mods[0]) + mods[1]
    act_out[...] = (pre * jax.nn.sigmoid(pre) * valid).astype(BF16)
    aux[...] = jnp.zeros(aux.shape, F32)
    aux[0:1, :] = inverse
    aux[1:2, :] = mods[0]
    aux[2:3, :] = mods[1]


def conv_second_kernel(ext, gains, biases, own, *refs, cols, width, count_pieces, segments):
    blocks = refs[0:4]
    pieces = refs[4 : 4 + count_pieces]
    attn_in, act_out, residual_out, normed_out, aux, wide_out, w_qkv = refs[4 + count_pieces : -3]
    flat, qkv, taps = refs[-3:]
    rank = head_rank()
    act, wide, residual = (act_out.ref, wide_out.ref, residual_out.ref)
    pixels = act.shape[0]
    for k, block in enumerate(blocks):
        act[:, lane_block(rank ^ k)] = block[...]
    act_out.send()
    place_pieces(flat, pieces, *segments[0])
    taps_side_by_side(flat, wide)
    wide_out.send()
    place_pieces(qkv, pieces, *segments[1])
    for g in range(3):
        w_qkv[:, g * LANES : (g + 1) * LANES] = qkv[g]
    conv_taps(act, wide, taps, cols)
    gains, biases, own = (gains.get(), biases.get(), own.get())
    bias = biases[4:5, lane_block(rank)]
    step = 256
    for i in range(pixels // step):
        rows = slice(i * step, (i + 1) * step)
        third = conv_sum(taps, i * step, step, cols) + bias
        valid = valid_of(ext, step, LANES, cols, i * step)
        residual[rows, :] = own[rows, :].astype(F32) + valid * third
    residual_out.send()
    value = residual[...]
    valid = valid_of(ext, pixels, LANES, cols)
    center, inverse = norm_stats(value, valid, pixel_count(ext, width), width)
    normed = (value - center) * inverse
    normed_out.ref[...] = normed
    normed_out.send()
    attn_in[...] = (
        normed * gains[1:2, lane_block(rank)] + biases[5:6, lane_block(rank)]
    ).astype(BF16)
    aux[...] = jnp.broadcast_to(inverse, aux.shape)


def cotangent_kernel(ext, *refs):
    cots = refs[0:4]
    full_out, own_out, att, att_t, rows_weight = refs[-5:]
    rank = head_rank()
    rows = cots[0].shape[0]
    for k, cot in enumerate(cots):
        at = row_block(rank ^ k, rows)
        full_out.ref[at, :] = cot[...]
        own_out.ref[at, :] = cot[:, lane_block(rank)]
    full_out.send()
    own_out.send()
    weights = refs[4:-5]
    if len(weights) == 1:
        rows_weight[...] = weights[0][...]
    else:
        kept, near, far, corner = weights
        count = len(cots)
        size = LANES // (count * PROJ_PARTS)
        for k, block in enumerate((kept, near, far.at[0], corner.at[1])):
            for part in range(PROJ_PARTS):
                at = pl.ds(pl.multiple_of((part * count + (rank ^ k)) * size, 16), size)
                for g in range(block.shape[0]):
                    lanes = slice(g * LANES, (g + 1) * LANES)
                    rows_weight[at, lanes] = block[g, part * size : (part + 1) * size, :]
    for i in range(4):
        at = slice(i * rows, (i + 1) * rows)
        grad = mm(full_out.ref[at, :], rows_weight[...], 1, 1).astype(BF16)
        att[at, :] = grad
        att_t[:, at] = grad.astype(F32).T


def attention_kernel(ext, *refs, cols):
    blocks = refs[0:4]
    wide, cot_att, cot_att_t = refs[4:7]
    across, corner, full_out, grads_out, attended_out = refs[7:12]
    qkv, keys_t, values_t, grad_kv, both = refs[12:]
    attn_full, grads, attended = (full_out.ref, grads_out.ref, attended_out.ref)
    rank = head_rank()
    pixels = attn_full.shape[0]
    scale = 1.0 / math.sqrt(HD)
    for k in range(4):
        attn_full[:, lane_block(rank ^ k)] = blocks[k][...]
    full_out.send()
    step = 256
    qkv[...] = mm(attn_full[...], wide[...], 1, 0).astype(BF16)
    for i in range(pixels // step):
        at = slice(i * step, (i + 1) * step)
        keys_t[:, at] = qkv[at, LANES : 2 * LANES].astype(F32).T.astype(BF16)
        values_t[:, at] = qkv[at, 2 * LANES :].astype(F32).T.astype(BF16)
    lane = lax.broadcasted_iota(jnp.int32, (pixels, LANES), 1)
    sublane = lax.broadcasted_iota(jnp.int32, (LANES, pixels), 0)
    key_row, key_col = pixel_place(pixels, pixels, cols)
    key_valid = jnp.logical_and(key_row < ext[0, 0], key_col < ext[0, 1])
    att_sum = jnp.zeros((LANES, pixels), F32)
    query_sum = jnp.zeros((LANES, pixels), F32)
    for h in range(LANES // HD):
        mine = lax.shift_right_logical(lane, 6) == h
        mine_t = lax.shift_right_logical(sublane, 6) == h
        query = jnp.where(mine, qkv[:, 0:LANES], jnp.zeros((pixels, LANES), BF16))
        cot = jnp.where(mine, cot_att[...], jnp.zeros((pixels, LANES), BF16))
        scores = mm(qkv[:, LANES : 2 * LANES], query, 1, 1) * scale
        scores = jnp.where(key_valid, scores, MASKED)
        top = jnp.max(scores, axis=0, keepdims=True)
        expo = jnp.exp(scores - top)
        probs = expo * (1.0 / col_sum(expo))
        probs_low = probs.astype(BF16)
        att = mm(jnp.where(mine_t, values_t[...], jnp.zeros((LANES, pixels), BF16)), probs_low, 1, 0)
        att_sum = att_sum + att
        row_dot = col_sum(att * cot_att_t[...])
        grad_probs = mm(qkv[:, 2 * LANES :], cot, 1, 1)
        grad_scores = (probs * (grad_probs - row_dot)).astype(BF16)
        grad_values = mm(probs_low, cot, 1, 0)
        grad_keys = mm(grad_scores, query, 1, 0)
        if h == 0:
            grad_kv[:, LANES:] = grad_values
            grad_kv[:, 0:LANES] = grad_keys
        else:
            grad_kv[:, LANES:] += grad_values
            grad_kv[:, 0:LANES] += grad_keys
        query_sum = query_sum + mm(
            jnp.where(mine_t, keys_t[...], jnp.zeros((LANES, pixels), BF16)), grad_scores, 1, 0
        )
    attended[...] = att_sum.T.astype(BF16)
    grads[:, 0:LANES] = (query_sum.T * scale).astype(BF16)
    attended_out.send()
    grads[:, LANES : 2 * LANES] = (grad_kv[:, 0:LANES] * scale).astype(BF16)
    grads[:, 2 * LANES :] = grad_kv[:, LANES:].astype(BF16)
    grads_out.send()
    two_sums(grads, wide, both, ((2, across), (3, corner)))


def out_partial_kernel(ext, biases, attended, rows_weight, residual, cot, *refs):
    outs = refs[0:4]
    grads = refs[4:-1]
    whole = refs[-1]
    rank = head_rank()
    rows = outs[0].shape[0]
    attended = attended.get()
    for i in range(4):
        at = slice(i * rows, (i + 1) * rows)
        whole[at, :] = mm(attended[at, :], rows_weight[...], 1, 0)
    bias = biases.get()[6:7, lane_block(rank)]
    whole[:, lane_block(rank)] += residual.get()[...] + bias
    for k, out in enumerate(outs):
        out[...] = whole[row_block(rank ^ k, rows), :].astype(out.dtype)
    whole[0:LANES, :] = mm(attended[...], cot.get()[...], 0, 0)
    if len(grads) == 1:
        for g in range(grads[0].shape[0]):
            grads[0][g] = whole[0:LANES, g * LANES : (g + 1) * LANES]
    else:
        kept, near, pair = grads
        count = len(outs)
        size = LANES // (count * PROJ_PARTS)
        for k, dest in enumerate((kept, near, pair.at[0], pair.at[1])):
            for part in range(PROJ_PARTS):
                at = row_block(part * count + (rank ^ k), size)
                for g in range(dest.shape[0]):
                    dest[g, part * size : (part + 1) * size, :] = whole[
                        at, g * LANES : (g + 1) * LANES
                    ].astype(BF16)


def sum_kernel(ext, first, second, third, out):
    out[...] = (first[...] + second[...].astype(F32) + third[...].astype(F32)).astype(out.dtype)


def norm_third_back_kernel(ext, gains, kept, upper, lower, far, normed, inverse, cot, wide, *refs, cols, width):
    outs = refs[0:4]
    grad_res, third_out, sums, shifted, whole = refs[4:]
    rank = head_rank()
    pixels = kept.shape[0]
    near = jnp.concatenate([upper[...], lower[...]], axis=0)
    grad = kept[...] + near.astype(F32) + far[...].astype(F32)
    normed, gains, cot = (normed.get()[...], gains.get(), cot.get())
    valid = valid_of(ext, pixels, LANES, cols)
    back = norm_back(
        grad * gains[1:2, lane_block(rank)], normed, inverse[0:1, :], valid,
        pixel_count(ext, width), width,
    )
    cot_value = cot[...].astype(F32)
    residual = cot_value + back
    grad_res.ref[...] = residual
    grad_res.send()
    third = (valid * residual).astype(BF16)
    third_out[...] = third
    third = third.astype(F32)
    shifted_grads(third, shifted, cols)
    sums[...] = jnp.zeros(sums.shape, F32)
    sums[0:1, :] = col_sum(grad * normed)
    sums[1:2, :] = col_sum(grad)
    sums[2:3, :] = col_sum(third)
    sums[3:4, :] = col_sum(cot_value)
    partial_sums(shifted, wide.get(), whole, outs)


def norm_second_back_kernel(ext, kept, near, far, normed, aux, wide, *refs, cols, width):
    outs = refs[0:4]
    first_out, sums, shifted, whole = refs[4:]
    pixels = kept.shape[0]
    grad_act = kept[...] + near[...].astype(F32) + far[...].astype(F32)
    normed = normed.get()[...]
    valid = valid_of(ext, pixels, LANES, cols)
    inverse, scale, shift = (aux[0:1, :], aux[1:2, :], aux[2:3, :])
    grad_pre = grad_act * valid * silu_grad(normed * (1.0 + scale) + shift)
    back = norm_back(
        grad_pre * (1.0 + scale), normed, inverse, valid, pixel_count(ext, width), width
    )
    first = back.astype(BF16)
    first_out[...] = first
    first = first.astype(F32)
    shifted_grads(first, shifted, cols)
    sums[...] = jnp.zeros(sums.shape, F32)
    sums[0:1, :] = col_sum(grad_pre * normed).astype(BF16).astype(F32)
    sums[1:2, :] = col_sum(grad_pre).astype(BF16).astype(F32)
    sums[2:3, :] = col_sum(first)
    partial_sums(shifted, wide.get(), whole, outs)


def norm_first_back_kernel(
    ext, gains, biases, kept, near, far, own, stats, grad_res, sums_third, sums_second, *refs,
    cols, width,
):
    out_kept, out_near, out_pair, table, held = refs
    rank = head_rank()
    pixels = kept.shape[0]
    rows = out_kept.shape[0]
    grad_act = kept[...] + near[...].astype(F32) + far[...].astype(F32)
    valid = valid_of(ext, pixels, LANES, cols)
    center, inverse = (stats[0:1, :], stats[1:2, :])
    normed = (own.get()[...].astype(F32) - center) * inverse
    gain = gains.get()[0:1, lane_block(rank)]
    bias = biases.get()[0:1, lane_block(rank)]
    grad_pre = grad_act * valid * silu_grad(normed * gain + bias)
    back = norm_back(grad_pre * gain, normed, inverse, valid, pixel_count(ext, width), width)
    held[...] = grad_res.get()[...] + back
    out_kept[...] = held[row_block(rank, rows), :]
    out_near[...] = held[row_block(rank ^ 1, rows), :].astype(BF16)
    for k in (2, 3):
        out_pair[k - 2] = held[row_block(rank ^ k, rows), :].astype(BF16)
    table[...] = jnp.zeros(table.shape, F32)
    table[0:1, :] = col_sum(grad_pre * normed)
    table[1:2, :] = sums_third[0:1, :]
    table[2:3, :] = col_sum(grad_pre)
    table[3:4, :] = sums_second[2:3, :]
    table[4:6, :] = sums_second[0:2, :]
    table[6:7, :] = sums_third[2:3, :]
    table[7:8, :] = sums_third[1:2, :]
    table[8:9, :] = sums_third[3:4, :]
    table[pl.ds(16 + 2 * lax.axis_index("dp"), 2), :] = sums_second[0:2, :]


def put_exact(dest, begin, value):
    rows = value.shape[0]
    high = value.astype(BF16)
    dest[begin : begin + rows, :] = high
    dest[begin + rows : begin + 2 * rows, :] = (value - high.astype(F32)).astype(BF16)


def get_exact(source, begin, rows):
    high = source[begin : begin + rows, :].astype(F32)
    return high + source[begin + rows : begin + 2 * rows, :].astype(F32)


def rows_join_kernel(ext, kept, near, far, corner, out):
    rank = head_rank()
    for k, block in enumerate((kept, near, far.at[0], corner.at[1])):
        out[:, lane_block(rank ^ k)] = block[...].astype(F32)


def taps_grad(act, shifted, flat):
    channels = act.shape[1]
    for i in range(channels // LANES):
        part = mm(act[:, i * LANES : (i + 1) * LANES], shifted[...], 0, 0)
        for tap in range(9):
            flat[0, tap * channels + i * LANES : tap * channels + (i + 1) * LANES, :] = part[
                :, tap * LANES : (tap + 1) * LANES
            ]


def dp_parts(dests, sources, dp_count):
    place = lax.axis_index("dp") if dp_count > 1 else 0
    for k, dest in enumerate(dests):
        at = 0
        for source in sources:
            size = source.shape[1] // dp_count
            for g in range(source.shape[0]):
                dest[at : at + size, :] = source[g, row_block(place ^ k, size), :].astype(dest.dtype)
                at += size


def qkv_grads_kernel(ext, attn, grads, *refs, dp_count):
    dests = refs[0:-1]
    qkv = refs[-1]
    part = mm(attn.get()[...], grads.get()[...], 0, 0)
    for g in range(3):
        qkv[g] = part[:, g * LANES : (g + 1) * LANES]
    if dp_count > 1:
        own, two, four, six, pairs = dests
        dests = (own, pairs.at[3], two, pairs.at[0], four, pairs.at[2], six, pairs.at[1])
    dp_parts(dests, (qkv,), dp_count)


def second_grads_kernel(ext, third, act, *refs, cols, dp_count):
    grad_proj = refs[0 : 4 if dp_count > 1 else 1]
    dests = refs[len(grad_proj) : -3]
    shifted, flat, proj = refs[-3:]
    shifted_grads(third[...].astype(F32), shifted, cols)
    act = act.get()
    taps_grad(act, shifted, flat)
    if len(grad_proj) == 1:
        proj[...] = grad_proj[0][...]
    else:
        kept, near, far, corner = grad_proj
        rank = head_rank()
        for k, block in enumerate((kept, near, far.at[0], corner.at[1])):
            size = block.shape[1]
            for g in range(proj.shape[0]):
                proj[g, row_block(rank ^ k, size), :] = block[g].astype(F32)
    dp_parts(split_dests(dests), (flat, proj), dp_count)


def split_dests(dests):
    if len(dests) == 1:
        return dests
    own, two, four, six, first_pair, second_pair = dests
    return (
        own, second_pair.at[1], two, first_pair.at[0], four, second_pair.at[0], six, first_pair.at[1]
    )


def first_grads_kernel(ext, first, act, sums, ada, *refs, cols, dp_count):
    dests = refs[0:-3]
    emb_part, shifted, flat = refs[-3:]
    shifted_grads(first[...].astype(F32), shifted, cols)
    taps_grad(act.get(), shifted, flat)
    dp_parts(split_dests(dests), (flat,), dp_count)
    ada = ada.get()
    for j in range(emb_part.shape[0]):
        row = jnp.zeros((1, LANES), F32)
        for side in range(2):
            mod = jnp.broadcast_to(sums[side : side + 1, :], (16, LANES)).astype(BF16)
            row = row + mm(mod, ada[side, j * LANES : (j + 1) * LANES, :], 1, 1)[0:1]
        emb_part[j : j + 1, :] = row


def near_kernel(ext, other, two, six, out):
    size = two.shape[0]
    for k, mine in enumerate((two, six)):
        out[k, 0:size, :] = (mine[...].astype(F32) + other[k].astype(F32)).astype(BF16)


def near_both_kernel(ext, other, two, six, ahead, ahead_two, ahead_six, out):
    size = two.shape[0]
    near_kernel(ext, other, two, six, out.at[:, pl.ds(0, size)])
    near_kernel(ext, ahead, ahead_two, ahead_six, out.at[:, pl.ds(size, ahead_two.shape[0])])


def near_table_kernel(ext, other, two, six, table, beside, out, total):
    size = two.shape[0]
    for k, mine in enumerate((two, six)):
        out[k * size : (k + 1) * size, :] = (
            mine[...].astype(F32) + other[k].astype(F32)
        ).astype(BF16)
    total[...] = table[...] + beside[...]
    put_exact(out, 2 * size, total[...])


def far_kernel(ext, four, late, near, out):
    size = four.shape[0]
    value = four[...].astype(F32) + late[0].astype(F32) + near[1, 0:size, :].astype(F32)
    out[0:size, :] = value.astype(BF16)


def far_both_kernel(ext, four, late, ahead_four, ahead, near, out):
    size = four.shape[0]
    far_kernel(ext, four, late, near, out)
    rows = pl.ds(size, ahead_four.shape[0])
    far_kernel(ext, ahead_four, ahead.at[pl.ds(2, 2)], near.at[:, rows], out.at[rows])


def far_table_kernel(ext, four, late, near, table, out, total):
    size = four.shape[0]
    value = four[...].astype(F32) + late[0].astype(F32) + near[size : 2 * size, :].astype(F32)
    out[0:size, :] = value.astype(BF16)
    total[...] = table[...] + get_exact(near, 2 * size, table.shape[0])
    put_exact(out, size, total[...])


def dp_pairs(parts):
    early = hop(parts[4], "dp", 1)
    return (early, hop(parts[5], "dp", 1))


def split_second_kernel(
    ext, own, late, ahead_own, ahead, straight, far, kept, near, pair, proj, held, *,
    rows_conv, rows_qkv,
):
    rank = head_rank()
    size = own.shape[0]
    held[...] = straight[0].astype(F32) + far[...].astype(F32)
    held[0:size, :] += own[...] + late[1].astype(F32)
    held[size:, :] += ahead_own[...] + ahead[3].astype(F32)
    for k, dest in enumerate((kept, near, pair.at[0], pair.at[1])):
        peer = rank ^ k
        dest[0:rows_conv, :] = held[row_block(peer, rows_conv), :].astype(dest.dtype)
        for g in range(3):
            begin = size + g * 4 * rows_qkv
            dest[rows_conv + g * rows_qkv : rows_conv + (g + 1) * rows_qkv, :] = held[
                pl.ds(pl.multiple_of(begin + peer * rows_qkv, 8), rows_qkv), :
            ].astype(dest.dtype)
    proj[...] = held[4 * rows_conv : size, :]


def split_first_kernel(
    ext, own, late, straight, far, table, emb_part, kept, near, pair, total, held, *, rows_conv
):
    rank = head_rank()
    size = held.shape[0]
    lines = table.shape[0]
    held[...] = own[...] + sum(
        part[0:size, :].astype(F32) for part in (late.at[1], straight, far)
    )
    total[0:lines, :] = table[...] + get_exact(far, size, lines)
    total[lines:, :] = emb_part[...]
    kept[...] = held[row_block(rank, rows_conv), :]
    for k, dest in enumerate((near, pair.at[0], pair.at[1])):
        dest[0:rows_conv, :] = held[row_block(rank ^ (k + 1), rows_conv), :].astype(BF16)
        put_exact(dest, rows_conv, total[...])


def join_second_kernel(ext, kept, near, far, corner, proj, conv_out, qkv_out, proj_out, *, rows_conv, rows_qkv):
    rank = head_rank()
    rows_proj = proj.shape[0] // 4
    low_half = lax.broadcasted_iota(jnp.int32, (rows_qkv, LANES), 1) < HD
    for k, block in enumerate((kept, near, far.at[0], corner.at[1])):
        peer = rank ^ k
        conv_out[pl.ds(peer, rows_conv, stride=4), :] = block[0:rows_conv, :].astype(F32)
        part = [
            block[rows_conv + g * rows_qkv : rows_conv + (g + 1) * rows_qkv, :].astype(F32)
            for g in range(3)
        ]
        keys = pltpu.roll(part[1], HD, 1)
        mixed = (
            jnp.where(low_half, part[0], keys),
            jnp.where(low_half, part[2], part[0]),
            jnp.where(low_half, keys, part[2]),
        )
        for g in range(3):
            qkv_out[pl.ds(peer * 3 + g, rows_qkv, stride=12), :] = mixed[g]
    for g in range(4):
        proj_out[pl.ds(g, rows_proj, stride=4), :] = proj[
            g * rows_proj : (g + 1) * rows_proj, :
        ].astype(F32)


def join_first_kernel(
    ext, kept, near, far, corner, total, embs, emb, conv_out, *refs, rows_conv
):
    rank = head_rank()
    outs, (mods, table, held, t1, t2, t3) = (refs[:4], refs[4:])
    blocks = (near, far.at[0], corner.at[1])
    conv_out[pl.ds(rank, rows_conv, stride=4), :] = kept[...]
    for k, (block, other) in enumerate(zip(blocks, (t1, t2, t3))):
        conv_out[pl.ds(rank ^ (k + 1), rows_conv, stride=4), :] = block[0:rows_conv, :].astype(F32)
        other[...] = get_exact(block, rows_conv, other.shape[0])
    small_grads_kernel(ext, embs, emb, total, t1, t2, t3, *outs, mods, table, held)


def small_grads_kernel(ext, embs, emb, t0, t1, t2, t3, gains_out, biases_out, ada_out, emb_out, mods, table, held):
    rank = head_rank()
    images = embs.shape[0]
    for k, block in enumerate((t0, t1, t2, t3)):
        table[:, lane_block(rank ^ k)] = block[0:16, :]
        for side in range(2):
            mods[:, lane_block(side * 4 + (rank ^ k))] = block[pl.ds(16 + side, images, stride=2), :]
    gains_out[...] = table[0:2, :]
    biases_out[...] = table[2:9, :]
    value = embs[...]
    part = mm((value * jax.nn.sigmoid(value)).astype(BF16), mods[...].astype(BF16), 0, 0)
    rows = ada_out.shape[0] // 8
    if part.shape[0] != rows:
        held[...] = part
        part = held[row_block(rank, rows), :]
    for g in range(8):
        ada_out[pl.ds(g, rows, stride=8), :] = part[:, g * LANES : (g + 1) * LANES]
    value = emb.get()[...].astype(F32)
    slope = silu_grad(value)
    begin = 16 + 2 * images
    for j in range(value.shape[1] // LANES):
        lanes = slice(j * LANES, (j + 1) * LANES)
        total = sum(block[begin + j : begin + j + 1, :] for block in (t0, t1, t2, t3))
        emb_out[:, lanes] = total * slope[:, lanes]


def body(
    inputs, embedding, extent, cotangent, gains, biases,
    conv_first, conv_second, qkv_master, ada_master, proj_master,
):
    heads = lax.axis_size("head")
    dps = lax.axis_size("dp")
    batch, row_count, cols, channels = inputs.shape
    rows = row_count * cols
    pixels = rows * heads
    width = channels // GROUPS
    emb_rows = embedding.shape[1] // LANES
    ext = extent
    direct = dps == 8
    flats = [
        master.reshape(-1, LANES)
        for master in (conv_first, conv_second, qkv_master, ada_master, proj_master)
    ]
    rows_conv = flats[0].shape[0] // 4
    rows_qkv = flats[2].shape[0] // 12
    rows_ada = flats[3].shape[0] // 8
    rows_proj = flats[4].shape[0] // 4
    far_gains, far_biases, far_emb = (Far(x, pinned=True) for x in (gains, biases, embedding))
    spread = [(i, (i % dps) * heads + i // dps) for i in range(dps * heads)]
    inputs_own = inputs.reshape(rows, channels)
    cot_own = cotangent.reshape(rows, channels)
    if direct:
        rows_a = rows_conv + 2 * rows_ada
        rows_b = rows_conv + 3 * rows_qkv
        far_flats = [Far(flat, pinned=True) for flat in flats]
        kept, near, pair, pj = call(
            first_out_kernel,
            [
                sds((rows_a, LANES), BF16), sds((rows_a, LANES), BF16),
                sds((2, rows_a, LANES), BF16), sds((4 * rows_proj, LANES), BF16),
            ],
            [None, far_flats[0], far_flats[3], far_flats[4]],
        )
        (first_piece,) = call(
            functools.partial(first_piece_kernel, segments=(rows_conv, rows_ada, rows_ada)),
            [sds((4 * rows_conv + 8 * rows_ada + 16 + 4 * rows_proj, LANES), BF16)],
            [None, kept, *head_exchange(near, pair), far_emb, pj],
            scratch=[pltpu.VMEM((16, LANES), F32)],
        )
        second_kept, near, far = call(
            second_out_kernel,
            [
                sds((rows_b, LANES), BF16), sds((rows_b, LANES), BF16),
                sds((channels // LANES * rows + 2 * rows_b, LANES), BF16),
            ],
            [None, far_flats[1], far_flats[2], Far(inputs_own, pinned=True)],
        )
        far = hop(far, "head", 2)
        corner = hop(far, "head", 1)
        blocks = (inputs_own, hop(inputs_own, "head", 1), far, corner)
        rows_second = 4 * rows_conv + 12 * rows_qkv + 4 * rows_proj
        (second_piece,) = call(
            functools.partial(second_piece_kernel, segments=(rows_conv,) + (rows_qkv,) * 3),
            [sds((rows_second - 4 * rows_proj, LANES), BF16)],
            [None, second_kept, hop(near, "head", 1), far, corner],
        )
        first_straight = dp_stepwise(first_piece)
        second_straight = dp_stepwise(second_piece)
        proj_at = 4 * rows_conv + 8 * rows_ada + 16
        first_segments = (
            (0, 1, 4 * rows_conv),
            (4 * rows_conv, 2, 4 * rows_ada),
            (proj_at, 4, rows_proj),
        )
        second_segments = ((0, 1, 4 * rows_conv), (4 * rows_conv, 3, 4 * rows_qkv))
    else:
        first_pieces, first_segments, second_pieces, second_segments, embs = gather_plain(
            flats, embedding, spread, channels
        )
        blocks = head_gather(inputs_own)

    act_first, own, stats_first = call(
        functools.partial(norm_first_kernel, cols=cols, width=width),
        [sds((pixels, channels), BF16), Far(sds((pixels, LANES), BF16)), sds((8, LANES), F32)],
        [ext, far_gains, far_biases, *blocks],
        scratch=[pltpu.VMEM((8, channels), F32)],
        us=2.0,
    )
    if direct:
        first_pieces, token = dp_beside_in_turn(first_straight, second_kept[:TOKEN])
    cots = head_gather(following(cot_own, blocks[2]))
    wide_shape = (channels, 9 * LANES)
    taps_scratch = pltpu.VMEM((pixels + 2 * cols, 9 * LANES), F32)
    flat_scratch = pltpu.VMEM((1, 9 * channels, LANES), BF16)
    n_pieces = len(first_pieces)
    groups = channels // LANES
    if direct:
        part = (groups, LANES // heads, LANES)
        proj_outs = [sds(part, BF16), sds(part, BF16), sds((2, *part), BF16)]
    else:
        proj_outs = [sds((LANES, channels), BF16)]
    first_outs = call(
        functools.partial(
            conv_first_kernel, cols=cols, width=width, count_pieces=n_pieces,
            segments=first_segments,
            emb_at=4 * rows_conv + 8 * rows_ada if direct else None,
        ),
        [
            sds((pixels, LANES), BF16), Far(sds((pixels, LANES), F32)), sds((8, LANES), F32),
            Far(sds(wide_shape, BF16)), Far(sds((2, emb_rows * LANES, LANES), BF16)),
            Far(sds((pixels, channels), BF16), held=False),
        ]
        + proj_outs
        + ([sds((dps, LANES), F32)] if direct else []),
        [ext, far_biases, act_first, far_emb, *first_pieces],
        scratch=[
            flat_scratch,
            taps_scratch,
            pltpu.VMEM((pixels, LANES), F32),
            pltpu.VMEM((groups, LANES, LANES), BF16),
        ],
        us=4.0,
        after=[token] if direct else (),
    )
    act_second_own, normed_second, aux_second, wide_first, ada_full, act_first = first_outs[:6]
    w_proj = first_outs[6 : 6 + len(proj_outs)]
    if direct:
        embs = first_outs[-1]
        w_proj = (w_proj[0], *head_exchange(*w_proj[1:]))
        second_pieces = dp_beside(second_straight)
        mark = []
        act_second_own = following(act_second_own, second_pieces[1], second_straight[1])
    blocks = head_gather(act_second_own, *([second_pieces[3], second_pieces[5]] if direct else []))
    attn_own, act_second, residual, normed_third, aux_third, wide_second, w_qkv = call(
        functools.partial(
            conv_second_kernel, cols=cols, width=width, count_pieces=n_pieces,
            segments=second_segments,
        ),
        [
            sds((pixels, LANES), BF16), Far(sds((pixels, channels), BF16)),
            Far(sds((pixels, LANES), F32)), Far(sds((pixels, LANES), F32)), sds((8, LANES), F32),
            Far(sds(wide_shape, BF16)), sds((channels, 3 * LANES), BF16),
        ],
        [ext, far_gains, far_biases, Far(own), *blocks, *second_pieces],
        scratch=[
            flat_scratch,
            pltpu.VMEM((3, channels, LANES), BF16),
            taps_scratch,
        ],
        us=4.0,
        after=w_proj[1:] if direct else (),
    )
    cot_full, cot_own, cot_att, cot_att_t, rows_weight = call(
        cotangent_kernel,
        [
            Far(sds((pixels, channels), BF16)), Far(sds((pixels, LANES), BF16)),
            sds((pixels, LANES), BF16), sds((LANES, pixels), F32), sds((LANES, channels), BF16),
        ],
        [None, *cots, *w_proj],
    )
    blocks = head_gather(attn_own, cot_att)
    whole_scratch = pltpu.VMEM((pixels, channels), F32)
    shifted_scratch = pltpu.VMEM((pixels, 9 * LANES), BF16)
    split_outs = [sds((pixels, LANES), F32)] + [sds((pixels, LANES), BF16)] * 3
    across, corner, attn_full, grads_qkv, attended = call(
        functools.partial(attention_kernel, cols=cols),
        [sds((pixels, LANES), BF16)] * 2
        + [
            Far(sds((pixels, channels), BF16)), Far(sds((pixels, 3 * LANES), BF16)),
            Far(sds((pixels, LANES), BF16)),
        ],
        [ext, *blocks, w_qkv, cot_att, cot_att_t],
        scratch=[
            pltpu.VMEM((pixels, 3 * LANES), BF16),
            pltpu.VMEM((LANES, pixels), BF16),
            pltpu.VMEM((LANES, pixels), BF16),
            pltpu.VMEM((pixels, 2 * LANES), F32),
            pltpu.VMEM((2 * LANES, 3 * LANES), BF16),
        ],
        us=15.0,
    )
    (across,) = call(
        add_kernel, [sds(across.shape, BF16)], [None, across, hop(corner, "head", 1)], us=0.7
    )
    far = hop(across, "head", 2)
    grad_outs = proj_outs if direct else [sds((groups, LANES, LANES), F32)]
    out_all = call(
        out_partial_kernel,
        [sds((rows, channels), F32)] + [sds((rows, channels), BF16)] * 3 + grad_outs,
        [None, far_biases, Far(attended), rows_weight, Far(residual), Far(cot_full)],
        scratch=[whole_scratch],
        us=2.0,
    )
    out_parts, grad_proj = (out_all[:4], out_all[4:])
    kept, *near = call(
        rest_attention_kernel,
        [sds((pixels, LANES), F32)] + [sds((pixels // 2, LANES), BF16)] * 2,
        [None, Far(grads_qkv), w_qkv],
        scratch=[pltpu.VMEM((pixels, LANES), BF16), pltpu.VMEM((2 * LANES, 3 * LANES), BF16)],
        after=out_parts[:1],
    )
    parts = (kept, *(hop(half, "head", 1) for half in near), far)
    if direct:
        grad_proj = (grad_proj[0], *head_exchange(*grad_proj[1:]))
    n_dests = dps if direct else 1

    def grad_outs(size):
        size = size // n_dests
        if not direct:
            return [sds((size, LANES), F32)]
        one = sds((size, LANES), BF16)
        return [sds((size, LANES), F32), one, one, one] + [sds((2, size, LANES), BF16)] * 2

    ahead_outs = grad_outs(3 * channels)
    if direct:
        ahead_outs = ahead_outs[:4] + [sds((4, *ahead_outs[1].shape), BF16)]
    ahead_parts = call(
        functools.partial(qkv_grads_kernel, dp_count=n_dests),
        ahead_outs,
        [None, Far(attn_full), Far(grads_qkv)],
        scratch=[pltpu.VMEM((3, channels, LANES), F32)],
        after=out_parts[:1],
    )
    if direct:
        ahead = hop(ahead_parts[4], "dp", 1)
    *parts, grad_res, third, sums_third = call(
        functools.partial(norm_third_back_kernel, cols=cols, width=width),
        split_outs
        + [Far(sds((pixels, LANES), F32)), sds((pixels, LANES), BF16), sds((8, LANES), F32)],
        [
            ext, far_gains, *parts, Far(normed_third), aux_third, Far(cot_own), Far(wide_second),
        ],
        scratch=[shifted_scratch, whole_scratch],
        us=150.0,
        after=ahead_parts[:1],
    )
    if direct:
        parts[3] = following(parts[3], *grad_proj[1:3], ahead)
    out_sums, _ = head_reduce(ext, out_parts)
    (output,) = call(sum_kernel, [sds((rows, channels), BF16)], [None, *out_sums])
    parts, sent = head_reduce(ext, parts)
    flat_grad = pltpu.VMEM((1, 9 * channels, LANES), F32)
    second_parts = call(
        functools.partial(second_grads_kernel, cols=cols, dp_count=n_dests),
        grad_outs(10 * channels),
        [None, third, Far(act_second), *grad_proj],
        scratch=[
            shifted_scratch,
            flat_grad,
            pltpu.VMEM((channels // LANES, LANES, LANES), F32),
        ],
        us=4.0,
        after=sent,
    )
    *parts, first, sums_second = call(
        functools.partial(norm_second_back_kernel, cols=cols, width=width),
        split_outs + [sds((pixels, LANES), BF16), sds((8, LANES), F32)],
        [ext, *parts, Far(normed_second), aux_second, Far(wide_first)],
        scratch=[shifted_scratch, whole_scratch],
        us=150.0,
        after=second_parts[:1],
    )
    if direct:
        second_pairs = dp_pairs(second_parts)
    parts, sent = head_reduce(ext, parts, second_pairs[:1] if direct else ())
    *first_parts, emb_part = call(
        functools.partial(first_grads_kernel, cols=cols, dp_count=n_dests),
        grad_outs(9 * channels) + [sds((emb_rows, LANES), F32)],
        [ext, first, Far(act_first), sums_second, Far(ada_full)],
        scratch=[shifted_scratch, flat_grad],
        us=3.0,
        after=sent,
    )
    table_rows = 16 + 2 * dps
    early = [emb_part]
    if direct:
        first_early, first_late = (hop(pair, "dp", 1) for pair in first_parts[4:6])
        (near_pair,) = call(
            near_both_kernel,
            [sds((2, rows_second, LANES), BF16)],
            [
                None, second_pairs[0], second_parts[1], second_parts[3], ahead, ahead_parts[1],
                ahead_parts[3],
            ],
            us=0.6,
            after=sent,
        )
        early += [near_pair, second_pairs[1]]
        second_near = hop(near_pair, "dp", 2)
    kept_rows, near, pair, table = call(
        functools.partial(norm_first_back_kernel, cols=cols, width=width),
        [
            sds((rows, LANES), F32), sds((rows, LANES), BF16), sds((2, rows, LANES), BF16),
            sds((table_rows, LANES), F32),
        ],
        [
            ext, far_gains, far_biases, *parts, Far(own), stats_first, Far(grad_res), sums_third,
            sums_second,
        ],
        scratch=[pltpu.VMEM((pixels, LANES), F32)],
        us=40.0,
        after=early,
    )
    small_outs = [
        sds(gains.shape, F32), sds(biases.shape, F32), sds(flats[3].shape, F32),
        sds(embedding.shape, F32),
    ]
    small_scratch = [
        pltpu.VMEM((dps, 8 * LANES), F32),
        pltpu.VMEM((16, channels), F32),
        pltpu.VMEM((LANES, 8 * LANES), F32),
    ]
    if direct:
        beside = hop(table, "dp", 1)
        (far_block,) = call(
            far_both_kernel,
            [sds((rows_second, LANES), BF16)],
            [None, second_parts[2], second_pairs[1], ahead_parts[2], ahead, second_near],
            us=0.6,
            after=[kept_rows],
        )
        second_left = [
            second_parts[0], second_pairs[1], ahead_parts[0], ahead, second_near,
            hop(far_block, "dp", 4),
        ]
        size = 4 * rows_conv + 2 * table_rows
        near_pair, table = call(
            near_table_kernel,
            [sds((4 * rows_conv + size, LANES), BF16), sds(table.shape, F32)],
            [None, first_early, first_parts[1], first_parts[3], table, beside],
            us=0.6,
        )
        first_near = hop(near_pair, "dp", 2)
        far_block, table = call(
            far_table_kernel,
            [sds((size, LANES), BF16), sds(table.shape, F32)],
            [None, first_parts[2], first_late, first_near, table],
            us=0.6,
            after=[far_block],
        )
        first_left = [first_parts[0], first_late, first_near, hop(far_block, "dp", 4)]
    (grad_inputs,) = call(
        rows_join_kernel,
        [sds((rows, channels), F32)],
        [None, kept_rows, *head_exchange(near, pair)],
    )
    if direct:
        second_own, near, pair, pj = call(
            functools.partial(split_second_kernel, rows_conv=rows_conv, rows_qkv=rows_qkv),
            [
                sds((rows_b, LANES), F32), sds((rows_b, LANES), BF16),
                sds((2, rows_b, LANES), BF16), sds((4 * rows_proj, LANES), F32),
            ],
            [None, *second_left],
            scratch=[pltpu.VMEM((rows_second, LANES), F32)],
        )
        second_blocks = head_exchange(near, pair)
        second_grad, qkv_grad, proj_grad = call(
            functools.partial(join_second_kernel, rows_conv=rows_conv, rows_qkv=rows_qkv),
            [sds(flats[i].shape, F32) for i in (1, 2, 4)],
            [None, second_own, *second_blocks, pj],
        )
        lines = table_rows + emb_rows
        kept, near, pair, table = call(
            functools.partial(split_first_kernel, rows_conv=rows_conv),
            [
                sds((rows_conv, LANES), F32), sds((rows_conv + 2 * lines, LANES), BF16),
                sds((2, rows_conv + 2 * lines, LANES), BF16), sds((lines, LANES), F32),
            ],
            [None, *first_left, table, emb_part],
            scratch=[pltpu.VMEM((4 * rows_conv, LANES), F32)],
            after=second_blocks[:2],
        )
        first_blocks = head_exchange(near, pair, output, grad_inputs, second_grad)
        first_grad, grad_gains, grad_biases, ada_grad, grad_embedding = call(
            functools.partial(join_first_kernel, rows_conv=rows_conv),
            [sds(flats[0].shape, F32)] + small_outs,
            [None, kept, *first_blocks, table, embs, far_emb],
            scratch=small_scratch + [pltpu.VMEM((lines, LANES), F32)] * 3,
        )
    else:
        table = jnp.concatenate([lax.psum(table, "dp"), emb_part])
        grad_gains, grad_biases, ada_grad, grad_embedding = call(
            small_grads_kernel,
            small_outs,
            [ext, embs, far_emb, *head_gather(table)],
            scratch=small_scratch,
        )
        first_grad, second_grad, qkv_grad, proj_grad = scatter_plain(
            first_parts[0], second_parts[0], ahead_parts[0], spread, channels
        )
    return (
        output.reshape(inputs.shape),
        grad_inputs.reshape(inputs.shape),
        grad_embedding,
        grad_gains,
        grad_biases,
        first_grad.reshape(-1),
        second_grad.reshape(-1),
        qkv_grad.reshape(-1),
        ada_grad.reshape(-1),
        proj_grad.reshape(-1),
    )


def gather_plain(flats, embedding, spread, channels):
    heads = lax.axis_size("head")

    def columns(flat, groups):
        blocks = flat.astype(BF16).reshape(-1, groups, LANES)
        return blocks

    def own_columns(blocks):
        got = lax.all_to_all(blocks, "head", split_axis=1, concat_axis=0, tiled=True)
        return lax.all_gather(got[:, 0], "dp", axis=0, tiled=True)

    first, second = (own_columns(columns(flats[i], heads).reshape(-1, heads, 1, LANES))[:, 0] for i in (0, 1))
    qkv = columns(flats[2], 12).reshape(-1, heads, 2, 3, HD)
    qkv = jnp.swapaxes(qkv, 2, 3).reshape(-1, heads, 3, LANES)
    qkv = jnp.swapaxes(own_columns(qkv), 0, 1).reshape(-1, LANES)
    ada = columns(flats[3], 8).reshape(-1, 2, heads, LANES)
    ada = jnp.swapaxes(own_columns(jnp.swapaxes(ada, 1, 2)), 0, 1).reshape(-1, LANES)
    proj = lax.ppermute(flats[4].astype(BF16), ("dp", "head"), spread)
    proj = lax.all_gather(proj, "dp", axis=0, tiled=True).reshape(-1, channels // LANES, LANES)
    proj = jnp.swapaxes(proj, 0, 1).reshape(-1, LANES)
    embs = lax.all_gather(embedding, "dp", axis=0, tiled=True).astype(F32)
    embs = embs.reshape(embs.shape[0], -1, flats[3].shape[0] // 8)
    embs = lax.dynamic_index_in_dim(
        embs, lax.axis_index("dp") * heads + lax.axis_index("head"), 1, False
    )
    first_piece = jnp.concatenate([first, ada, proj])
    second_piece = jnp.concatenate([second, qkv])
    proj_at = 9 * channels + ada.shape[0]
    return (
        [first_piece],
        (
            (0, 1, 9 * channels),
            (9 * channels, 2, ada.shape[0] // 2),
            (proj_at, channels // LANES, LANES),
        ),
        [second_piece],
        ((0, 1, 9 * channels), (9 * channels, 3, channels)),
        embs,
    )


def scatter_plain(first, second, qkv, spread, channels):
    heads = lax.axis_size("head")

    def rows_of(grad):
        part = lax.psum_scatter(grad, "dp", scatter_dimension=0, tiled=True)
        return lax.all_to_all(part[:, None], "head", split_axis=0, concat_axis=1, tiled=True)

    def conv(grad):
        return rows_of(grad[:, None])

    qkv = jnp.swapaxes(qkv.reshape(3, channels, LANES), 0, 1)
    qkv = rows_of(qkv).reshape(-1, heads, 3, 2, HD)
    qkv = jnp.swapaxes(qkv, 2, 3)
    proj = jnp.swapaxes(second[9 * channels :].reshape(-1, LANES, LANES), 0, 1)
    proj = lax.psum_scatter(proj, "dp", scatter_dimension=0, tiled=True)
    proj = lax.ppermute(proj, ("dp", "head"), [(j, i) for i, j in spread])
    return (conv(first), conv(second[: 9 * channels]), qkv, proj)


def solution(mesh):
    flat = P(("dp", "head"))
    image = P("dp", "head", None, None)
    return jax.shard_map(
        body,
        mesh=mesh,
        in_specs=(image, P("dp", None), P("dp", None), image, P(), P(), flat, flat, flat, flat, flat),
        out_specs=(image, image, P("dp", None), P(), P(), flat, flat, flat, flat, flat),
        check_vma=False,
    )
```
